32 devices in a mesh: section: 2 (over x), ctx: 4 (over z), wt: 4 (over y, core).
Axes of the slice: x: 2, y: 2, z: 4, core: 2. Of those that a mesh axis runs over, the one named last changes fastest.
Arguments:
- boundary: bfloat16 [2, 3, 2048, 1024], P('section', None, ('wt', 'ctx')), may hold values from -6 to 6
- lengths: int32 [3, 4, 4], replicated, may hold values from 1 to 256, 512 in all within a row
- valid: int32 [3, 2048], P(None, ('wt', 'ctx')), may hold values from 0 to 1, as said below
- w_qkv: bfloat16 [2, 1024, 3072], P('section', 'wt'), may hold values from -0.1875 to 0.1875
- w_out: bfloat16 [2, 1024, 1024], P('section', 'wt'), may hold values from -1 to 1
- w_in: bfloat16 [2, 1024, 4096], P('section', 'wt'), may hold values from -0.1875 to 0.1875
- w_down: bfloat16 [2, 4096, 1024], P('section', 'wt'), may hold values from -0.09375 to 0.09375
- bias_in: bfloat16 [2, 4096], P('section', 'wt'), may hold values from -2 to 2
- vectors: bfloat16 [2, 8, 1024], P('section', None, 'wt'), may hold values from -1 to 2
Outputs:
- results: bfloat16 [2, 3, 2048, 1024], P('section', None, ('wt', 'ctx'))
- grad_qkv: float32 [2, 1024, 3072], P('section', 'wt')
- grad_out: float32 [2, 1024, 1024], P('section', 'wt')
- grad_in: float32 [2, 1024, 4096], P('section', 'wt')
- grad_down: float32 [2, 4096, 1024], P('section', 'wt')
- grad_bias_in: float32 [2, 4096], P('section', 'wt')
- grad_vectors: float32 [2, 8, 1024], P('section', None, 'wt')
The draws below stay inside these ranges and needn't reach their ends.
Inputs may be any that keep to these rules, and one draw needn't show every extreme that they name: Each pack's 4 lengths in natural order sum to 512; one of them is 256. `valid`: the last row of every micro-batch is 1.
All inputs are finite; a program needn't handle non-finite values.
Results may differ from the reference program's by a relative error of at most 0.022.
Values may be sent and summed in bfloat16 or wider, within the bound.
A program may use at most 256 MiB of HBM per device.

```python
import math
import jax
import jax.numpy as jnp
import numpy as np
from jax import lax

D = 1024
HEADS = 16
HEAD = 64
FF = 4096
TD = 128
MICRO = 3
LOSS_SCALE = 1024
PACK = 512
MOST = 256
DOCS = 4
ROWS = 2048
N_SECTION = 2
N_CTX = 4
N_WT = 4


def draw_valid(key, part):
    key = jax.random.fold_in(key, 5)
    picks = jax.random.randint(key, (MICRO, ROWS), 0, 1000)
    row_index = jnp.arange(ROWS, dtype=jnp.int32)
    limits = 200 + 800 * row_index // (ROWS - 1)
    return (picks < limits[None, :]).astype(jnp.int32)


def draw_vectors(key, part):
    key = jax.random.fold_in(key, 11)
    gain_key, shift_key = jax.random.split(key)
    row_index = jnp.arange(8)
    is_gain = (row_index == 3) | (row_index == 6)
    gains = jax.random.uniform(gain_key, (N_SECTION, 8, D), minval=0.6, maxval=1.4)
    shifts = jnp.clip(0.3 * jax.random.normal(shift_key, (N_SECTION, 8, D)), -1.0, 1.0)
    return jnp.where(is_gain[None, :, None], gains, shifts).astype(jnp.float32).astype(jnp.bfloat16)


def block_levels(stream_key, dims, pieces, low, largest):
    loudness, own = 1.0, jax.random.fold_in(stream_key, 6)
    for position, blocks in pieces:
        steps = jnp.exp(jax.random.uniform(jax.random.fold_in(own, position), (blocks,), jnp.float32, low / len(pieces), largest / len(pieces)))
        loudness = loudness * jnp.repeat(steps, dims[position] // blocks).reshape([-1 if axis == position else 1 for axis in range(len(dims))])
    return loudness


def length_profile(count, total, most, lean):
    weights = [(1 << 20) // math.isqrt(rank ** lean) + 1 for rank in range(2, count + 1)]
    rest, holding = total - most - (count - 1), [1] * (count - 1)
    while rest > 0:
        free = [i for i in range(count - 1) if holding[i] < most]
        pool, left = sum([weights[i] for i in free]), rest
        for i in free:
            addition = min(most - holding[i], max(1, left * weights[i] // pool), rest)
            holding[i] = holding[i] + addition
            rest = rest - addition
    return np.array([most] + holding)


def ragged_sizes(stream_key, amount, total, limit, skew):
    if amount == 2:
        one = jax.random.randint(stream_key, (), max(1, total - limit), min(limit, total - 1) + 1)
        return jnp.stack([one, total - one])
    sizes = jnp.asarray(length_profile(amount, total, limit, skew), jnp.int32)
    pairs = (amount - 1) // 2
    source_of, sink = sizes[1:1 + 2 * pairs:2], sizes[2:2 + 2 * pairs:2]
    room = jnp.minimum(source_of - 1, limit - sink)
    moved = jax.random.randint(jax.random.fold_in(stream_key, 1), (pairs,), 0, 1 << 20) % (room + 1)
    sizes = sizes.at[1:1 + 2 * pairs:2].set(source_of - moved).at[2:2 + 2 * pairs:2].set(sink + moved)
    return sizes[jax.random.permutation(jax.random.fold_in(stream_key, 2), amount)]


def centred(stream_key, shape, deviation, reach, pieces=(), held_as=jnp.bfloat16):
    entries = jax.random.normal(stream_key, shape, jnp.float32) * deviation
    if len(pieces) > 0:
        entries = block_levels(stream_key, shape, pieces, -0.22, 0.18) * entries
    return jnp.clip(entries, min=-reach, max=reach).astype(held_as)


def setup_inputs(seed: int = 0) -> dict:
    key_of = jax.random.split(jax.random.key(seed), 10)
    boundary = centred(key_of[0], (N_SECTION, MICRO, ROWS, D), 1.0, 6.0, ((0, 2), (2, 16)))
    lengths = jax.vmap(lambda own: ragged_sizes(own, DOCS, PACK, MOST, 1))(jax.random.split(key_of[1], MICRO * N_WT)).reshape((MICRO, N_WT, DOCS)).astype(jnp.int32)
    valid = draw_valid(jax.random.fold_in(key_of[9], 71), 0)
    w_qkv = centred(key_of[3], (N_SECTION, D, 3 * D), D ** -0.5, 0.1875, ((0, 2), (1, 4)))
    w_out = centred(key_of[4], (N_SECTION, D, D), (D // 32) ** -0.5, 1.0, ((0, 2), (1, 4)))
    w_in = centred(key_of[5], (N_SECTION, D, FF), D ** -0.5, 0.1875, ((0, 2), (1, 4)))
    w_down = centred(key_of[6], (N_SECTION, FF, D), FF ** -0.5, 0.09375, ((0, 2), (1, 4)))
    bias_in = centred(key_of[7], (N_SECTION, FF), 0.5, 2.0, ((0, 2), (1, 4)))
    vectors = draw_vectors(jax.random.fold_in(key_of[9], 71), 0)
    return dict(boundary=boundary, lengths=lengths, valid=valid, w_qkv=w_qkv, w_out=w_out, w_in=w_in, w_down=w_down, bias_in=bias_in, vectors=vectors)


@jax.custom_vjp
def low(v):
    return lax.optimization_barrier(v.astype(jnp.bfloat16)).astype(jnp.float32)

@jax.custom_vjp
def low_back(v):
    return v

def low_keep(v):
    return (low(v), None)

def low_pass(kept, grad):
    return (grad,)

def back_keep(v):
    return (v, None)

def back_low(kept, grad):
    return (low(grad),)
low.defvjp(low_keep, low_pass)
low_back.defvjp(back_keep, back_low)

def both_round(values):
    return low_back(low(values))

def precise(left, right):
    return jnp.dot(left, right, precision=lax.Precision.HIGHEST)

def layer_norm(values, gain, shift):
    center = lax.optimization_barrier(jnp.mean(values, axis=-1, keepdims=True))
    offset = values - center
    spread = lax.optimization_barrier(jnp.mean(offset * offset, axis=-1, keepdims=True))
    return offset * lax.rsqrt(spread + 1e-05) * gain + shift

def pack_ids(length_row):
    ends = jnp.cumsum(length_row).astype(jnp.int32)
    places = jnp.arange(PACK, dtype=jnp.int32)
    natural = lax.optimization_barrier(jnp.sum((places[:, None] >= ends[None, :]).astype(jnp.int32), axis=1)).astype(jnp.int32)
    return natural.reshape(TD, N_CTX).T.reshape(PACK)

def attend(queries, keys, values, ids):
    block = min(512, PACK)
    query_heads = queries.reshape(PACK // block, block, HEADS, HEAD)
    id_blocks = ids.reshape(PACK // block, block)
    key_heads = keys.reshape(PACK, HEADS, HEAD)
    value_heads = values.reshape(PACK, HEADS, HEAD)

    def query_block(items):
        query_part, id_part = items
        scores = jnp.einsum('qhd,khd->hqk', query_part, key_heads, precision=lax.Precision.HIGHEST) * HEAD ** (-0.5)
        scores = low_back(scores)
        same = id_part[:, None] == ids[None, :]
        scores = jnp.where(same[None], scores, -1000000000.0)
        probs = jax.nn.softmax(scores, axis=-1)
        mixed = jnp.einsum('hqk,khd->qhd', low(probs), value_heads, precision=lax.Precision.HIGHEST)
        return mixed.reshape(block, D)
    mixed_all = lax.map(jax.checkpoint(query_block), (query_heads, id_blocks))
    return mixed_all.reshape(PACK, D)

def layer(states, ids, weight_qkv, weight_out, weight_in, weight_down, in_bias, vector_rows):
    states_low = low(states)
    projected = precise(states_low, weight_qkv)
    queries = both_round(projected[:, :D] + vector_rows[0])
    keys = both_round(projected[:, D:2 * D])
    values = both_round(projected[:, 2 * D:] + vector_rows[1])
    mixed = both_round(attend(queries, keys, values, ids))
    branch = low_back(precise(mixed, weight_out) + vector_rows[2])
    first = layer_norm(states + branch, vector_rows[3], vector_rows[4])
    hidden_pre = low_back(precise(low(first), weight_in) + in_bias)
    hidden_low = low(jax.nn.gelu(hidden_pre, approximate=False))
    second = low_back(precise(hidden_low, weight_down) + vector_rows[5])
    return layer_norm(first + second, vector_rows[6], vector_rows[7])

def reference(boundary, lengths, valid, w_qkv, w_out, w_in, w_down, bias_in, vectors):
    packs = MICRO * N_WT
    first_in = boundary[0].astype(jnp.float32).reshape(packs, PACK, D)
    teacher = boundary[1].astype(jnp.float32).reshape(packs, PACK, D)
    covered = valid.astype(jnp.float32).reshape(packs, PACK)
    ids_all = jax.vmap(pack_ids)(lengths.reshape(packs, DOCS))
    count = jnp.sum(covered)
    factor = LOSS_SCALE / count
    weights = tuple((item.astype(jnp.float32) for item in (w_qkv, w_out, w_in, w_down, bias_in, vectors)))

    def objective(inputs, weight_qkv, weight_out, weight_in, weight_down, in_bias, vector_rows):

        def one_pack(items):
            states, ids, target, marks = items
            middle = layer(states, ids, weight_qkv[0], weight_out[0], weight_in[0], weight_down[0], in_bias[0], vector_rows[0])
            middle = low_back(low(middle))
            final = layer(middle, ids, weight_qkv[1], weight_out[1], weight_in[1], weight_down[1], in_bias[1], vector_rows[1])
            distance = final - target
            return (final, jnp.sum(marks[:, None] * distance * distance))
        finals, errors = lax.map(one_pack, (inputs, ids_all, teacher, covered))
        return (factor * 0.5 * jnp.sum(errors), finals)
    value, pull, finals = jax.vjp(objective, first_in, *weights, has_aux=True)
    grads = pull(jnp.ones_like(value))
    input_grad = grads[0].reshape(MICRO, ROWS, D)
    results = jnp.stack([input_grad, finals.reshape(MICRO, ROWS, D)]).astype(jnp.bfloat16)
    return (results, grads[1], grads[2], grads[3], grads[4], grads[5], grads[6])
```

```python
import functools

import jax
import jax.numpy as jnp
from jax import lax
from jax.experimental import pallas as pl
from jax.experimental.pallas import tpu as pltpu
from jax.sharding import PartitionSpec as P

HEADS = 16
LOSS_SCALE = 1024


def shifted(block, axis, distance):
    devices = range(lax.axis_size(axis))
    route = [(i - distance, i) for i in devices if i - distance in devices]
    return lax.ppermute(block, axis, route)


def as_sent(x):

    def short(part):
        return part.astype(jnp.bfloat16) if part.dtype == jnp.float32 else part

    return jax.tree.map(short, x)


def layer_norm(values, gain, shift):
    center = jnp.mean(values, axis=-1, keepdims=True)
    offset = values - center
    spread = jnp.mean(offset * offset, axis=-1, keepdims=True)
    return offset * lax.rsqrt(spread + 1e-05) * gain + shift


def exact_gelu(values):
    return jax.nn.gelu(values, approximate=False)


def dealt_ids(length_row, pack_size, ctx_count):
    ends = jnp.cumsum(length_row)
    places = jnp.arange(pack_size, dtype=jnp.int32)
    natural = jnp.sum((places[:, None] >= ends[None, :]).astype(jnp.int32), axis=1)
    return natural.reshape(pack_size // ctx_count, ctx_count).T.reshape(pack_size)


def split_blocks(full_kv, ids_keys):
    block = min(512, full_kv.shape[0])
    count_blocks = full_kv.shape[0] // block
    return (
        full_kv.reshape(count_blocks, block, full_kv.shape[1]),
        ids_keys.reshape(count_blocks, block),
    )


def split_kv(block_kv, heads):
    half = block_kv.shape[1] // 2
    keys = block_kv[:, :half].reshape(block_kv.shape[0], heads, -1)
    values = block_kv[:, half:].reshape(block_kv.shape[0], heads, -1)
    return (keys, values)


def block_scores(queries, keys, ids_query, ids_keys, scale):
    scores = jnp.einsum("qhd,khd->hqk", queries, keys, preferred_element_type=jnp.float32) * scale
    same = ids_query[:, None] == ids_keys[None, :]
    return jnp.where(same[None], scores, -1000000000.0)


def attend_forward(queries, full_kv, ids_query, ids_keys, heads, scale):
    blocks, id_blocks = split_blocks(full_kv, ids_keys)
    query_rows = queries.shape[0]

    def total_step(carry, items):
        run_max, run_sum = carry
        keys, values = split_kv(items[0], heads)
        scores = block_scores(queries, keys, ids_query, items[1], scale)
        new_max = jnp.maximum(run_max, jnp.max(scores, axis=-1))
        run_sum = run_sum * jnp.exp(run_max - new_max) + jnp.sum(
            jnp.exp(scores - new_max[..., None]), axis=-1
        )
        return ((new_max, run_sum), None)

    start = (
        jnp.full((heads, query_rows), -1e30, jnp.float32),
        jnp.zeros((heads, query_rows), jnp.float32),
    )
    (run_max, run_sum), _ = lax.scan(total_step, start, (blocks, id_blocks))
    log_total = run_max + jnp.log(run_sum)

    def mix_step(carry, items):
        keys, values = split_kv(items[0], heads)
        scores = block_scores(queries, keys, ids_query, items[1], scale)
        probs = jnp.exp(scores - log_total[..., None]).astype(jnp.bfloat16)
        return (
            carry + jnp.einsum("hqk,khd->qhd", probs, values, preferred_element_type=jnp.float32),
            None,
        )

    mixed, _ = lax.scan(mix_step, jnp.zeros(queries.shape, jnp.float32), (blocks, id_blocks))
    return (mixed.reshape(query_rows, -1), log_total)


def attend_backward(queries, full_kv, ids_query, ids_keys, mixed_grad, log_total, heads, scale):
    blocks, id_blocks = split_blocks(full_kv, ids_keys)
    grad_heads = mixed_grad.reshape(queries.shape)

    def inner_step(carry, items):
        keys, values = split_kv(items[0], heads)
        scores = block_scores(queries, keys, ids_query, items[1], scale)
        probs = jnp.exp(scores - log_total[..., None])
        prob_grad = jnp.einsum(
            "qhd,khd->hqk", grad_heads, values, preferred_element_type=jnp.float32
        )
        return (carry + jnp.sum(probs * prob_grad, axis=-1), None)

    inner, _ = lax.scan(inner_step, jnp.zeros(log_total.shape, jnp.float32), (blocks, id_blocks))

    def grad_step(carry, items):
        keys, values = split_kv(items[0], heads)
        scores = block_scores(queries, keys, ids_query, items[1], scale)
        probs = jnp.exp(scores - log_total[..., None])
        prob_grad = jnp.einsum(
            "qhd,khd->hqk", grad_heads, values, preferred_element_type=jnp.float32
        )
        score_grad = (probs * (prob_grad - inner[..., None])).astype(jnp.bfloat16)
        carry = (
            carry
            + jnp.einsum("hqk,khd->qhd", score_grad, keys, preferred_element_type=jnp.float32)
            * scale
        )
        key_grad = (
            jnp.einsum("hqk,qhd->khd", score_grad, queries, preferred_element_type=jnp.float32)
            * scale
        )
        value_grad = jnp.einsum(
            "hqk,qhd->khd",
            probs.astype(jnp.bfloat16),
            grad_heads,
            preferred_element_type=jnp.float32,
        )
        block = keys.shape[0]
        return (
            carry,
            jnp.concatenate([key_grad.reshape(block, -1), value_grad.reshape(block, -1)], axis=1),
        )

    query_grad, partial_kv = lax.scan(
        grad_step, jnp.zeros(queries.shape, jnp.float32), (blocks, id_blocks)
    )
    query_grad = query_grad.reshape(queries.shape[0], -1)
    return (query_grad, partial_kv.reshape(-1, partial_kv.shape[-1]), inner)


def shards(boundary, lengths, valid, w_qkv, w_out, w_in, w_down, bias_in, vectors):
    section_at = lax.axis_index("section")
    ctx_count = lax.axis_size("ctx")
    ctx_at = lax.axis_index("ctx")
    wt_at = lax.axis_index("wt")
    micro_count = boundary.shape[1]
    row_count = boundary.shape[2]
    width = boundary.shape[3]
    pack_size = row_count * ctx_count
    head_size = width // HEADS
    scale = head_size ** (-0.5)
    gathered = (
        lax.all_gather(w_qkv[0], "wt", axis=0, tiled=True),
        lax.all_gather(w_out[0], "wt", axis=0, tiled=True),
        lax.all_gather(w_in[0], "wt", axis=0, tiled=True),
        lax.all_gather(w_down[0], "wt", axis=0, tiled=True),
        lax.all_gather(bias_in[0], "wt", axis=0, tiled=True),
        lax.all_gather(vectors[0], "wt", axis=1, tiled=True),
    )
    weight_qkv, weight_out, weight_in, weight_down, in_bias, vector_rows = gathered
    in_bias = in_bias.astype(jnp.float32)
    vector_rows = vector_rows.astype(jnp.float32)
    qkv_bias = jnp.concatenate([vector_rows[0], jnp.zeros((width,), jnp.float32), vector_rows[1]])
    my_lengths = lax.dynamic_index_in_dim(lengths, wt_at, 1, keepdims=False)

    def ids_of(length_row):
        return dealt_ids(length_row, pack_size, ctx_count)

    pack_ids = jax.vmap(ids_of)(my_lengths)
    query_ids = lax.dynamic_slice_in_dim(pack_ids, ctx_at * row_count, row_count, 1)
    count = lax.psum(jnp.sum(valid.astype(jnp.float32)), ("ctx", "wt"))
    factor = LOSS_SCALE / count
    empty_rows = jnp.zeros((row_count, width), jnp.bfloat16)
    arriving = empty_rows
    kept_list = []
    cotangents = []
    final_states = []
    for tick_at in range(micro_count + 1):
        own_input = boundary[0, tick_at] if tick_at < micro_count else empty_rows
        inputs = jnp.where(section_at == 0, own_input, arriving)
        micro_here = jnp.clip(tick_at - section_at, 0, micro_count - 1)
        ids_keys = lax.dynamic_index_in_dim(pack_ids, micro_here, 0, keepdims=False)
        ids_query = lax.dynamic_index_in_dim(query_ids, micro_here, 0, keepdims=False)
        residual = inputs.astype(jnp.float32)
        projected = jnp.dot(inputs, weight_qkv, preferred_element_type=jnp.float32) + qkv_bias
        layer_queries = (
            projected[:, :width].astype(jnp.bfloat16).reshape(row_count, HEADS, head_size)
        )
        layer_local_kv = projected[:, width:].astype(jnp.bfloat16)
        layer_full_kv = lax.all_gather(layer_local_kv, "ctx", axis=0, tiled=True)
        mixed, layer_log_total = attend_forward(
            layer_queries, layer_full_kv, ids_query, ids_keys, HEADS, scale
        )
        layer_mixed_low = mixed.astype(jnp.bfloat16)
        branch = (
            jnp.dot(layer_mixed_low, weight_out, preferred_element_type=jnp.float32)
            + vector_rows[2]
        )
        layer_summed = residual + branch
        first = layer_norm(layer_summed, vector_rows[3], vector_rows[4])
        layer_first_low = first.astype(jnp.bfloat16)
        layer_hidden_pre = (
            jnp.dot(layer_first_low, weight_in, preferred_element_type=jnp.float32) + in_bias
        )
        layer_hidden_low = exact_gelu(layer_hidden_pre).astype(jnp.bfloat16)
        layer_second = first + (
            jnp.dot(layer_hidden_low, weight_down, preferred_element_type=jnp.float32)
            + vector_rows[5]
        )
        output = layer_norm(layer_second, vector_rows[6], vector_rows[7])
        layer_kept = (
            inputs,
            layer_queries,
            layer_local_kv,
            layer_full_kv,
            layer_mixed_low,
            layer_log_total,
            layer_summed,
            layer_first_low,
            layer_hidden_pre,
            layer_hidden_low,
            layer_second,
            ids_keys,
            ids_query,
        )
        output, kept = (output, layer_kept)
        kept_list.append(kept)
        if tick_at > 0:
            teacher = boundary[0, tick_at - 1].astype(jnp.float32)
            covered = valid[tick_at - 1].astype(jnp.float32)[:, None]
            cotangents.append(factor * covered * (output - teacher))
            final_states.append(output.astype(jnp.bfloat16))
        else:
            cotangents.append(jnp.zeros((row_count, width), jnp.float32))
        if tick_at < micro_count:
            arriving = shifted(output.astype(jnp.bfloat16), "section", 1)
    returning = empty_rows
    totals = None
    input_grads = [None] * micro_count
    for back_at in range(micro_count + 1):
        forward_at = micro_count - back_at
        grad_output = jnp.where(
            section_at == 1, cotangents[forward_at], returning.astype(jnp.float32)
        )
        (
            layer_inputs,
            queries,
            local_kv,
            full_kv,
            mixed_low,
            log_total,
            summed,
            first_low,
            hidden_pre,
            hidden_low,
            second,
            layer_ids_keys,
            layer_ids_query,
        ) = kept_list[forward_at]
        full_kv = lax.all_gather(local_kv, "ctx", axis=0, tiled=True)
        _, pull_last = jax.vjp(layer_norm, second, vector_rows[6], vector_rows[7])
        grad_second, grad_gain_two, grad_shift_two = pull_last(grad_output)
        down_low = grad_second.astype(jnp.bfloat16)
        layer_grad_down = jnp.einsum(
            "rf,rd->fd", hidden_low, down_low, preferred_element_type=jnp.float32
        )
        grad_bias_two = jnp.sum(down_low.astype(jnp.float32), axis=0)
        _, pull_gelu = jax.vjp(exact_gelu, hidden_pre)
        (grad_pre,) = pull_gelu(
            jnp.einsum("rd,fd->rf", down_low, weight_down, preferred_element_type=jnp.float32)
        )
        pre_low = grad_pre.astype(jnp.bfloat16)
        layer_grad_in = jnp.einsum(
            "rd,rf->df", first_low, pre_low, preferred_element_type=jnp.float32
        )
        layer_grad_bias_in = jnp.sum(pre_low.astype(jnp.float32), axis=0)
        grad_first = grad_second + jnp.einsum(
            "rf,df->rd", pre_low, weight_in, preferred_element_type=jnp.float32
        )
        _, pull_first = jax.vjp(layer_norm, summed, vector_rows[3], vector_rows[4])
        grad_summed, grad_gain_one, grad_shift_one = pull_first(grad_first)
        branch_low = grad_summed.astype(jnp.bfloat16)
        layer_grad_out = jnp.einsum(
            "rd,re->de", mixed_low, branch_low, preferred_element_type=jnp.float32
        )
        grad_bias_out = jnp.sum(branch_low.astype(jnp.float32), axis=0)
        mixed_grad = jnp.einsum(
            "re,de->rd", branch_low, weight_out, preferred_element_type=jnp.float32
        ).astype(jnp.bfloat16)
        query_grad, partial_kv, inner = attend_backward(
            queries, full_kv, layer_ids_query, layer_ids_keys, mixed_grad, log_total, HEADS, scale
        )
        kv_grad = lax.psum_scatter(
            partial_kv.astype(jnp.bfloat16), "ctx", scatter_dimension=0, tiled=True
        )
        query_low = query_grad.astype(jnp.bfloat16)
        projected_grad = jnp.concatenate([query_low, kv_grad], axis=1)
        layer_grad_qkv = jnp.einsum(
            "rd,re->de", layer_inputs, projected_grad, preferred_element_type=jnp.float32
        )
        vector_grad = jnp.stack(
            [
                jnp.sum(query_low.astype(jnp.float32), axis=0),
                jnp.sum(kv_grad[:, width:].astype(jnp.float32), axis=0),
                grad_bias_out,
                grad_gain_one,
                grad_shift_one,
                grad_bias_two,
                grad_gain_two,
                grad_shift_two,
            ]
        )
        grad_inputs = grad_summed + jnp.einsum(
            "re,de->rd", projected_grad, weight_qkv, preferred_element_type=jnp.float32
        )
        grad_inputs, grads = (
            grad_inputs,
            (
                layer_grad_qkv,
                layer_grad_out,
                layer_grad_in,
                layer_grad_down,
                layer_grad_bias_in,
                vector_grad,
            ),
        )
        totals = grads if totals is None else jax.tree.map(jnp.add, totals, grads)
        if forward_at < micro_count:
            input_grads[forward_at] = grad_inputs
        if back_at < micro_count:
            returning = shifted(grad_inputs.astype(jnp.bfloat16), "section", -1)
    results = jnp.stack(
        [
            jnp.where(section_at == 0, input_grads[index].astype(jnp.bfloat16), final_states[index])
            for index in range(micro_count)
        ]
    )[None]
    shares = (
        lax.psum_scatter(
            totals[0].astype(jnp.bfloat16), "wt", scatter_dimension=0, tiled=True
        ).astype(jnp.float32),
        lax.psum_scatter(
            totals[1].astype(jnp.bfloat16), "wt", scatter_dimension=0, tiled=True
        ).astype(jnp.float32),
        lax.psum_scatter(
            totals[2].astype(jnp.bfloat16), "wt", scatter_dimension=0, tiled=True
        ).astype(jnp.float32),
        lax.psum_scatter(
            totals[3].astype(jnp.bfloat16), "wt", scatter_dimension=0, tiled=True
        ).astype(jnp.float32),
        lax.psum_scatter(
            totals[4].astype(jnp.bfloat16), "wt", scatter_dimension=0, tiled=True
        ).astype(jnp.float32),
        lax.psum_scatter(
            totals[5].astype(jnp.bfloat16), "wt", scatter_dimension=1, tiled=True
        ).astype(jnp.float32),
    )
    shares = jax.tree.map(lambda part: part.astype(jnp.float32), lax.psum(as_sent(shares), "ctx"))
    grad_qkv, grad_out, grad_in, grad_down, grad_bias_in, grad_vectors = shares
    return (
        results,
        grad_qkv[None],
        grad_out[None],
        grad_in[None],
        grad_down[None],
        grad_bias_in[None],
        grad_vectors[None],
    )


PAIR = 128
FAR = -1000000000.0
VMEM = pltpu.VMEM


def dot(left, right, dims=((1,), (0,))):
    return lax.dot_general(left, right, (dims, ((), ())), preferred_element_type=jnp.float32)


def head_lanes(size):
    lane = lax.broadcasted_iota(jnp.int32, (1, PAIR), 1)
    return [lane // size == index for index in range(PAIR // size)]


def only(mask, values):
    return jnp.where(mask, values, jnp.zeros_like(values))


def attend_kernel(size, ids_row, ids_col, states, weight, bias, qkv, mixed):
    local = mixed.shape[2]
    projected = dot(states[0], weight[...]) + bias[...]
    qkv[0] = projected.astype(jnp.bfloat16)
    same = ids_col[0] == ids_row[0]
    masks = head_lanes(size)
    for pair in range(local // PAIR):
        at = pair * PAIR
        q = qkv[0, :, at : at + PAIR] * jnp.bfloat16(size**-0.5)
        k = qkv[0, :, local + at : local + at + PAIR]
        v = qkv[0, :, 2 * local + at : 2 * local + at + PAIR]
        total = None
        for mask in masks:
            scores = jnp.where(same, dot(only(mask, k), q, ((1,), (1,))), FAR)
            probs = jnp.exp(scores - jnp.max(scores, axis=0, keepdims=True))
            scale = 1.0 / jnp.sum(probs, axis=0, keepdims=True)
            low = (probs * scale).astype(jnp.bfloat16)
            term = dot(only(mask, v), low, ((0,), (0,)))
            total = term if total is None else total + term
        mixed[0, :, at : at + PAIR] = total.T.astype(jnp.bfloat16)


def attend_heads(states, weight, bias, ids, size):
    packs, rows, width = states.shape
    local = weight.shape[1] // 3
    whole = lambda *shape: pl.BlockSpec(shape, lambda m: (0,) * len(shape))
    block = lambda *shape: pl.BlockSpec((1,) + shape, lambda m: (m, 0, 0))
    return pl.pallas_call(
        functools.partial(attend_kernel, size),
        grid=(packs,),
        in_specs=[
            block(1, rows),
            block(rows, 1),
            block(rows, width),
            whole(width, 3 * local),
            whole(1, 3 * local),
        ],
        out_specs=[block(rows, 3 * local), block(rows, local)],
        out_shape=[
            jax.ShapeDtypeStruct((packs, rows, 3 * local), jnp.bfloat16),
            jax.ShapeDtypeStruct((packs, rows, local), jnp.bfloat16),
        ],
        compiler_params=pltpu.CompilerParams(vmem_limit_bytes=48 * 2**20),
        name="attend_heads",
    )(ids[:, None, :], ids[:, :, None], states, weight, bias)


def attend_back_kernel(size, ids_row, ids_col, qkv, mixed_grad, weight, projected_grad, part):
    local = mixed_grad.shape[2]
    same = ids_col[0] == ids_row[0]
    masks = head_lanes(size)
    scale = jnp.bfloat16(size**-0.5)
    for pair in range(local // PAIR):
        at = pair * PAIR
        q = qkv[0, :, at : at + PAIR] * scale
        k = qkv[0, :, local + at : local + at + PAIR]
        v = qkv[0, :, 2 * local + at : 2 * local + at + PAIR]
        grad = mixed_grad[0, :, at : at + PAIR]
        totals = [None] * 3
        for mask in masks:
            own_k = only(mask, k)
            scores = jnp.where(same, dot(own_k, q, ((1,), (1,))), FAR)
            probs = jnp.exp(scores - jnp.max(scores, axis=0, keepdims=True))
            probs = probs * (1.0 / jnp.sum(probs, axis=0, keepdims=True))
            prob_grad = dot(only(mask, v), grad, ((1,), (1,)))
            inner = jnp.sum(probs * prob_grad, axis=0, keepdims=True)
            score_grad = (probs * (prob_grad - inner)).astype(jnp.bfloat16)
            terms = (
                dot(own_k, score_grad, ((0,), (0,))),
                dot(score_grad, only(mask, q)),
                dot(probs.astype(jnp.bfloat16), only(mask, grad)),
            )
            totals = [t if o is None else o + t for o, t in zip(totals, terms)]
        query_grad = totals[0].T * size**-0.5
        projected_grad[0, :, at : at + PAIR] = query_grad.astype(jnp.bfloat16)
        projected_grad[0, :, local + at : local + at + PAIR] = totals[1].astype(jnp.bfloat16)
        projected_grad[0, :, 2 * local + at : 2 * local + at + PAIR] = totals[2].astype(
            jnp.bfloat16
        )
    part[0] = dot(projected_grad[0], weight[...], ((1,), (1,))).astype(jnp.bfloat16)


def attend_heads_back(qkv, mixed_grad, weight, ids, size):
    packs, rows, local = mixed_grad.shape
    width = weight.shape[0]
    whole = lambda *shape: pl.BlockSpec(shape, lambda m: (0,) * len(shape))
    block = lambda *shape: pl.BlockSpec((1,) + shape, lambda m: (m, 0, 0))
    return pl.pallas_call(
        functools.partial(attend_back_kernel, size),
        grid=(packs,),
        in_specs=[
            block(1, rows),
            block(rows, 1),
            block(rows, 3 * local),
            block(rows, local),
            whole(width, 3 * local),
        ],
        out_specs=[block(rows, 3 * local), block(rows, width)],
        out_shape=[
            jax.ShapeDtypeStruct((packs, rows, 3 * local), jnp.bfloat16),
            jax.ShapeDtypeStruct((packs, rows, width), jnp.bfloat16),
        ],
        compiler_params=pltpu.CompilerParams(vmem_limit_bytes=48 * 2**20),
        name="attend_heads_back",
    )(ids[:, None, :], ids[:, :, None], qkv, mixed_grad, weight)


def normal_tail(values):
    size = jnp.abs(values)
    bell = jnp.exp(-0.5 * values * values)
    t = 1.0 / (1.0 + 0.3275911 * (2.0**-0.5) * size)
    poly = t * (
        0.254829592
        + t * (-0.284496736 + t * (1.421413741 + t * (-1.453152027 + t * 1.061405429)))
    )
    tail = 0.5 * poly * bell
    return (jnp.where(values >= 0, 1.0 - tail, tail), bell)


def gelu_both(values):
    below, bell = normal_tail(values)
    return (values * below, below + values * bell * 0.3989422804014327)


def norm_parts(values):
    center = jnp.mean(values, axis=-1, keepdims=True)
    offset = values - center
    spread = jnp.mean(offset * offset, axis=-1, keepdims=True)
    inverse = lax.rsqrt(spread + 1e-05)
    return (offset * inverse, inverse)


def norm_back(grad, gain, normal, inverse):
    inner = grad * gain
    mean = jnp.mean(inner, axis=-1, keepdims=True)
    along = jnp.mean(inner * normal, axis=-1, keepdims=True)
    return inverse * (inner - mean - normal * along)


def relay(boundary, lengths, valid, w_qkv, w_out, w_in, w_down, bias_in, vectors):
    section_at = lax.axis_index("section")
    count_ctx = lax.axis_size("ctx")
    ctx_at = lax.axis_index("ctx")
    wt_at = lax.axis_index("wt")
    micro, rows, width = boundary.shape[1:]
    pack = rows * count_ctx
    size = width // HEADS
    local = width // lax.axis_size("wt")
    tokens = micro * rows
    swap = [
        (c * count_ctx + w, w * count_ctx + c) for c in range(count_ctx) for w in range(count_ctx)
    ]

    def swapped(block):
        return lax.ppermute(block, ("ctx", "wt"), swap)

    def gather_rows(block):
        return lax.all_gather(block, "wt", axis=1, tiled=True)

    def scatter_rows(block):
        return lax.psum_scatter(block, "wt", scatter_dimension=1, tiled=True)

    def rows_of_heads(block):
        split = block.reshape(micro, count_ctx, rows, local)
        return lax.all_to_all(split, "wt", 1, 3, tiled=True).reshape(tokens, width)

    def heads_of_rows(block):
        split = block.reshape(micro, 1, rows, width)
        return lax.all_to_all(split, "wt", 3, 1, tiled=True).reshape(micro, pack, local)

    own = swapped(boundary[0])
    shard = w_qkv[0].reshape(local, 3, count_ctx, local)
    weight_qkv = lax.all_to_all(shard, "wt", 2, 0, tiled=True).reshape(width, 3 * local)
    weight_out = lax.all_gather(w_out[0], "wt", axis=0, tiled=True)
    weight_in = lax.all_gather(w_in[0], "wt", axis=0, tiled=True)
    weight_down = lax.all_gather(w_down[0], "wt", axis=0, tiled=True)
    small = jnp.concatenate([vectors[0], bias_in[0].reshape(-1, local)], axis=0)
    small = lax.all_gather(small, "wt", axis=0)
    vector_rows = small[:, :8].transpose(1, 0, 2).reshape(8, width).astype(jnp.float32)
    in_bias = small[:, 8:].reshape(-1).astype(jnp.float32)
    own_rows = vectors[0].astype(jnp.float32)
    qkv_bias = jnp.concatenate([own_rows[0], jnp.zeros((local,), jnp.float32), own_rows[1]])[None]
    my_lengths = lax.dynamic_index_in_dim(lengths, ctx_at, 1, keepdims=False)
    ids = jax.vmap(lambda row: dealt_ids(row, pack, count_ctx))(my_lengths)
    marks = lax.all_gather(valid, ("wt", "ctx"), axis=1, tiled=True)
    count = jnp.sum(marks.astype(jnp.float32))
    at = (ctx_at * count_ctx + wt_at) * rows
    marks = lax.dynamic_slice_in_dim(marks, at, rows, 1).reshape(tokens, 1).astype(jnp.float32)
    factor = LOSS_SCALE / count

    def forward(states):
        full = gather_rows(states.reshape(micro, rows, width))
        qkv, mixed = attend_heads(full, weight_qkv, qkv_bias, ids, size)
        mixed = rows_of_heads(mixed)
        summed = states.astype(jnp.float32) + (dot(mixed, weight_out) + vector_rows[2])
        normal_one, inverse_one = norm_parts(summed)
        first = normal_one * vector_rows[3] + vector_rows[4]
        first_low = first.astype(jnp.bfloat16)
        hidden, slope = gelu_both(dot(first_low, weight_in) + in_bias)
        hidden = hidden.astype(jnp.bfloat16)
        second = first + (dot(hidden, weight_down) + vector_rows[5])
        normal_two, inverse_two = norm_parts(second)
        output = normal_two * vector_rows[6] + vector_rows[7]
        kept = (full, qkv, mixed, normal_one, inverse_one, first_low, hidden, slope)
        return (output, kept + (normal_two, inverse_two))

    def backward(grad, kept):
        full, qkv, mixed, normal_one, inverse_one, first_low, hidden, slope = kept[:8]
        normal_two, inverse_two = kept[8:]
        grad_second = norm_back(grad, vector_rows[6], normal_two, inverse_two)
        down_low = grad_second.astype(jnp.bfloat16)
        pre_low = (dot(down_low, weight_down, ((1,), (1,))) * slope).astype(jnp.bfloat16)
        grad_first = grad_second + dot(pre_low, weight_in, ((1,), (1,)))
        grad_summed = norm_back(grad_first, vector_rows[3], normal_one, inverse_one)
        branch_low = grad_summed.astype(jnp.bfloat16)
        mixed_grad = dot(branch_low, weight_out, ((1,), (1,))).astype(jnp.bfloat16)
        mixed_grad = heads_of_rows(mixed_grad)
        projected_grad, part = attend_heads_back(qkv, mixed_grad, weight_qkv, ids, size)
        grad_states = grad_summed + scatter_rows(part).reshape(tokens, width)

        def weight_grads():
            along = ((0,), (0,))
            flat = projected_grad.reshape(-1, 3 * local)
            total = lambda values: jnp.sum(values.astype(jnp.float32), axis=0)
            bias_qkv = total(flat)
            rows_local = jnp.stack([bias_qkv[:local], bias_qkv[2 * local :]])
            rows_whole = jnp.stack(
                [
                    total(branch_low),
                    total(grad_first * normal_one),
                    total(grad_first),
                    total(down_low),
                    total(grad * normal_two),
                    total(grad),
                ]
            )
            return (
                dot(full.reshape(-1, width), flat, along),
                dot(mixed, branch_low, along),
                dot(first_low, pre_low, along),
                dot(hidden, down_low, along),
                total(pre_low),
                rows_local,
                rows_whole,
            )

        return (grad_states, weight_grads)

    states = own.reshape(tokens, width)
    output, _ = forward(states)
    arrived = shifted(output.astype(jnp.bfloat16), "section", 1)
    states = jnp.where(section_at == 0, states, arrived)
    output, kept = forward(states)
    distance = output - own.reshape(tokens, width).astype(jnp.float32)
    cotangent = factor * marks * distance
    grad_states, _ = backward(cotangent, kept)
    returned = shifted(grad_states.astype(jnp.bfloat16), "section", -1)
    cotangent = jnp.where(section_at == 1, cotangent, returned.astype(jnp.float32))
    grad_states, weight_grads = backward(cotangent, kept)
    results = jnp.where(section_at == 0, grad_states, output).astype(jnp.bfloat16)
    results = swapped(results.reshape(micro, rows, width))[None]
    grads = weight_grads()
    low = lambda part: part.astype(jnp.bfloat16)
    qkv_back = low(grads[0]).reshape(count_ctx, local, 3, 1, local)
    qkv_back = lax.all_to_all(qkv_back, "wt", 0, 3, tiled=True).reshape(local, 3 * width)
    out_back, in_back, down_back = [
        lax.psum_scatter(low(part), "wt", scatter_dimension=0, tiled=True) for part in grads[1:4]
    ]
    bias_back = lax.psum_scatter(grads[4], "wt", scatter_dimension=0, tiled=True)
    whole_back = lax.psum_scatter(grads[6], "wt", scatter_dimension=1, tiled=True)
    rows_back = jnp.concatenate([grads[5], whole_back])
    shares = lax.psum((qkv_back, out_back, in_back, down_back, bias_back, rows_back), "ctx")
    shares = tuple(part.astype(jnp.float32)[None] for part in shares)
    return (results,) + shares


def solution(mesh):
    in_specs = (
        P("section", None, ("wt", "ctx"), None),
        P(),
        P(None, ("wt", "ctx")),
        P("section", "wt", None),
        P("section", "wt", None),
        P("section", "wt", None),
        P("section", "wt", None),
        P("section", "wt"),
        P("section", None, "wt"),
    )
    out_specs = (
        P("section", None, ("wt", "ctx"), None),
        P("section", "wt", None),
        P("section", "wt", None),
        P("section", "wt", None),
        P("section", "wt", None),
        P("section", "wt"),
        P("section", None, "wt"),
    )
    square = mesh.shape["ctx"] == mesh.shape["wt"]
    return jax.shard_map(relay if square else shards, mesh=mesh, in_specs=in_specs, out_specs=out_specs, check_vma=False)
```

```python
import functools

import jax
import jax.numpy as jnp
from jax import lax
from jax.experimental import pallas as pl
from jax.experimental.pallas import tpu as pltpu
from jax.sharding import PartitionSpec as P

HEADS = 16
LOSS_SCALE = 1024


def shifted(block, axis, distance):
    devices = range(lax.axis_size(axis))
    route = [(i - distance, i) for i in devices if i - distance in devices]
    return lax.ppermute(block, axis, route)


def as_sent(x):

    def short(part):
        return part.astype(jnp.bfloat16) if part.dtype == jnp.float32 else part

    return jax.tree.map(short, x)


def layer_norm(values, gain, shift):
    center = jnp.mean(values, axis=-1, keepdims=True)
    offset = values - center
    spread = jnp.mean(offset * offset, axis=-1, keepdims=True)
    return offset * lax.rsqrt(spread + 1e-05) * gain + shift


def exact_gelu(values):
    return jax.nn.gelu(values, approximate=False)


def dealt_ids(length_row, pack_size, ctx_count):
    ends = jnp.cumsum(length_row)
    places = jnp.arange(pack_size, dtype=jnp.int32)
    natural = jnp.sum((places[:, None] >= ends[None, :]).astype(jnp.int32), axis=1)
    return natural.reshape(pack_size // ctx_count, ctx_count).T.reshape(pack_size)


def split_blocks(full_kv, ids_keys):
    block = min(512, full_kv.shape[0])
    count_blocks = full_kv.shape[0] // block
    return (
        full_kv.reshape(count_blocks, block, full_kv.shape[1]),
        ids_keys.reshape(count_blocks, block),
    )


def split_kv(block_kv, heads):
    half = block_kv.shape[1] // 2
    keys = block_kv[:, :half].reshape(block_kv.shape[0], heads, -1)
    values = block_kv[:, half:].reshape(block_kv.shape[0], heads, -1)
    return (keys, values)


def block_scores(queries, keys, ids_query, ids_keys, scale):
    scores = jnp.einsum("qhd,khd->hqk", queries, keys, preferred_element_type=jnp.float32) * scale
    same = ids_query[:, None] == ids_keys[None, :]
    return jnp.where(same[None], scores, -1000000000.0)


def attend_forward(queries, full_kv, ids_query, ids_keys, heads, scale):
    blocks, id_blocks = split_blocks(full_kv, ids_keys)
    query_rows = queries.shape[0]

    def total_step(carry, items):
        run_max, run_sum = carry
        keys, values = split_kv(items[0], heads)
        scores = block_scores(queries, keys, ids_query, items[1], scale)
        new_max = jnp.maximum(run_max, jnp.max(scores, axis=-1))
        run_sum = run_sum * jnp.exp(run_max - new_max) + jnp.sum(
            jnp.exp(scores - new_max[..., None]), axis=-1
        )
        return ((new_max, run_sum), None)

    start = (
        jnp.full((heads, query_rows), -1e30, jnp.float32),
        jnp.zeros((heads, query_rows), jnp.float32),
    )
    (run_max, run_sum), _ = lax.scan(total_step, start, (blocks, id_blocks))
    log_total = run_max + jnp.log(run_sum)

    def mix_step(carry, items):
        keys, values = split_kv(items[0], heads)
        scores = block_scores(queries, keys, ids_query, items[1], scale)
        probs = jnp.exp(scores - log_total[..., None]).astype(jnp.bfloat16)
        return (
            carry + jnp.einsum("hqk,khd->qhd", probs, values, preferred_element_type=jnp.float32),
            None,
        )

    mixed, _ = lax.scan(mix_step, jnp.zeros(queries.shape, jnp.float32), (blocks, id_blocks))
    return (mixed.reshape(query_rows, -1), log_total)


def attend_backward(queries, full_kv, ids_query, ids_keys, mixed_grad, log_total, heads, scale):
    blocks, id_blocks = split_blocks(full_kv, ids_keys)
    grad_heads = mixed_grad.reshape(queries.shape)

    def inner_step(carry, items):
        keys, values = split_kv(items[0], heads)
        scores = block_scores(queries, keys, ids_query, items[1], scale)
        probs = jnp.exp(scores - log_total[..., None])
        prob_grad = jnp.einsum(
            "qhd,khd->hqk", grad_heads, values, preferred_element_type=jnp.float32
        )
        return (carry + jnp.sum(probs * prob_grad, axis=-1), None)

    inner, _ = lax.scan(inner_step, jnp.zeros(log_total.shape, jnp.float32), (blocks, id_blocks))

    def grad_step(carry, items):
        keys, values = split_kv(items[0], heads)
        scores = block_scores(queries, keys, ids_query, items[1], scale)
        probs = jnp.exp(scores - log_total[..., None])
        prob_grad = jnp.einsum(
            "qhd,khd->hqk", grad_heads, values, preferred_element_type=jnp.float32
        )
        score_grad = (probs * (prob_grad - inner[..., None])).astype(jnp.bfloat16)
        carry = (
            carry
            + jnp.einsum("hqk,khd->qhd", score_grad, keys, preferred_element_type=jnp.float32)
            * scale
        )
        key_grad = (
            jnp.einsum("hqk,qhd->khd", score_grad, queries, preferred_element_type=jnp.float32)
            * scale
        )
        value_grad = jnp.einsum(
            "hqk,qhd->khd",
            probs.astype(jnp.bfloat16),
            grad_heads,
            preferred_element_type=jnp.float32,
        )
        block = keys.shape[0]
        return (
            carry,
            jnp.concatenate([key_grad.reshape(block, -1), value_grad.reshape(block, -1)], axis=1),
        )

    query_grad, partial_kv = lax.scan(
        grad_step, jnp.zeros(queries.shape, jnp.float32), (blocks, id_blocks)
    )
    query_grad = query_grad.reshape(queries.shape[0], -1)
    return (query_grad, partial_kv.reshape(-1, partial_kv.shape[-1]), inner)


def shards(boundary, lengths, valid, w_qkv, w_out, w_in, w_down, bias_in, vectors):
    section_at = lax.axis_index("section")
    ctx_count = lax.axis_size("ctx")
    ctx_at = lax.axis_index("ctx")
    wt_at = lax.axis_index("wt")
    micro_count = boundary.shape[1]
    row_count = boundary.shape[2]
    width = boundary.shape[3]
    pack_size = row_count * ctx_count
    head_size = width // HEADS
    scale = head_size ** (-0.5)
    gathered = (
        lax.all_gather(w_qkv[0], "wt", axis=0, tiled=True),
        lax.all_gather(w_out[0], "wt", axis=0, tiled=True),
        lax.all_gather(w_in[0], "wt", axis=0, tiled=True),
        lax.all_gather(w_down[0], "wt", axis=0, tiled=True),
        lax.all_gather(bias_in[0], "wt", axis=0, tiled=True),
        lax.all_gather(vectors[0], "wt", axis=1, tiled=True),
    )
    weight_qkv, weight_out, weight_in, weight_down, in_bias, vector_rows = gathered
    in_bias = in_bias.astype(jnp.float32)
    vector_rows = vector_rows.astype(jnp.float32)
    qkv_bias = jnp.concatenate([vector_rows[0], jnp.zeros((width,), jnp.float32), vector_rows[1]])
    my_lengths = lax.dynamic_index_in_dim(lengths, wt_at, 1, keepdims=False)

    def ids_of(length_row):
        return dealt_ids(length_row, pack_size, ctx_count)

    pack_ids = jax.vmap(ids_of)(my_lengths)
    query_ids = lax.dynamic_slice_in_dim(pack_ids, ctx_at * row_count, row_count, 1)
    count = lax.psum(jnp.sum(valid.astype(jnp.float32)), ("ctx", "wt"))
    factor = LOSS_SCALE / count
    empty_rows = jnp.zeros((row_count, width), jnp.bfloat16)
    arriving = empty_rows
    kept_list = []
    cotangents = []
    final_states = []
    for tick_at in range(micro_count + 1):
        own_input = boundary[0, tick_at] if tick_at < micro_count else empty_rows
        inputs = jnp.where(section_at == 0, own_input, arriving)
        micro_here = jnp.clip(tick_at - section_at, 0, micro_count - 1)
        ids_keys = lax.dynamic_index_in_dim(pack_ids, micro_here, 0, keepdims=False)
        ids_query = lax.dynamic_index_in_dim(query_ids, micro_here, 0, keepdims=False)
        residual = inputs.astype(jnp.float32)
        projected = jnp.dot(inputs, weight_qkv, preferred_element_type=jnp.float32) + qkv_bias
        layer_queries = (
            projected[:, :width].astype(jnp.bfloat16).reshape(row_count, HEADS, head_size)
        )
        layer_local_kv = projected[:, width:].astype(jnp.bfloat16)
        layer_full_kv = lax.all_gather(layer_local_kv, "ctx", axis=0, tiled=True)
        mixed, layer_log_total = attend_forward(
            layer_queries, layer_full_kv, ids_query, ids_keys, HEADS, scale
        )
        layer_mixed_low = mixed.astype(jnp.bfloat16)
        branch = (
            jnp.dot(layer_mixed_low, weight_out, preferred_element_type=jnp.float32)
            + vector_rows[2]
        )
        layer_summed = residual + branch
        first = layer_norm(layer_summed, vector_rows[3], vector_rows[4])
        layer_first_low = first.astype(jnp.bfloat16)
        layer_hidden_pre = (
            jnp.dot(layer_first_low, weight_in, preferred_element_type=jnp.float32) + in_bias
        )
        layer_hidden_low = exact_gelu(layer_hidden_pre).astype(jnp.bfloat16)
        layer_second = first + (
            jnp.dot(layer_hidden_low, weight_down, preferred_element_type=jnp.float32)
            + vector_rows[5]
        )
        output = layer_norm(layer_second, vector_rows[6], vector_rows[7])
        layer_kept = (
            inputs,
            layer_queries,
            layer_local_kv,
            layer_full_kv,
            layer_mixed_low,
            layer_log_total,
            layer_summed,
            layer_first_low,
            layer_hidden_pre,
            layer_hidden_low,
            layer_second,
            ids_keys,
            ids_query,
        )
        output, kept = (output, layer_kept)
        kept_list.append(kept)
        if tick_at > 0:
            teacher = boundary[0, tick_at - 1].astype(jnp.float32)
            covered = valid[tick_at - 1].astype(jnp.float32)[:, None]
            cotangents.append(factor * covered * (output - teacher))
            final_states.append(output.astype(jnp.bfloat16))
        else:
            cotangents.append(jnp.zeros((row_count, width), jnp.float32))
        if tick_at < micro_count:
            arriving = shifted(output.astype(jnp.bfloat16), "section", 1)
    returning = empty_rows
    totals = None
    input_grads = [None] * micro_count
    for back_at in range(micro_count + 1):
        forward_at = micro_count - back_at
        grad_output = jnp.where(
            section_at == 1, cotangents[forward_at], returning.astype(jnp.float32)
        )
        (
            layer_inputs,
            queries,
            local_kv,
            full_kv,
            mixed_low,
            log_total,
            summed,
            first_low,
            hidden_pre,
            hidden_low,
            second,
            layer_ids_keys,
            layer_ids_query,
        ) = kept_list[forward_at]
        full_kv = lax.all_gather(local_kv, "ctx", axis=0, tiled=True)
        _, pull_last = jax.vjp(layer_norm, second, vector_rows[6], vector_rows[7])
        grad_second, grad_gain_two, grad_shift_two = pull_last(grad_output)
        down_low = grad_second.astype(jnp.bfloat16)
        layer_grad_down = jnp.einsum(
            "rf,rd->fd", hidden_low, down_low, preferred_element_type=jnp.float32
        )
        grad_bias_two = jnp.sum(down_low.astype(jnp.float32), axis=0)
        _, pull_gelu = jax.vjp(exact_gelu, hidden_pre)
        (grad_pre,) = pull_gelu(
            jnp.einsum("rd,fd->rf", down_low, weight_down, preferred_element_type=jnp.float32)
        )
        pre_low = grad_pre.astype(jnp.bfloat16)
        layer_grad_in = jnp.einsum(
            "rd,rf->df", first_low, pre_low, preferred_element_type=jnp.float32
        )
        layer_grad_bias_in = jnp.sum(pre_low.astype(jnp.float32), axis=0)
        grad_first = grad_second + jnp.einsum(
            "rf,df->rd", pre_low, weight_in, preferred_element_type=jnp.float32
        )
        _, pull_first = jax.vjp(layer_norm, summed, vector_rows[3], vector_rows[4])
        grad_summed, grad_gain_one, grad_shift_one = pull_first(grad_first)
        branch_low = grad_summed.astype(jnp.bfloat16)
        layer_grad_out = jnp.einsum(
            "rd,re->de", mixed_low, branch_low, preferred_element_type=jnp.float32
        )
        grad_bias_out = jnp.sum(branch_low.astype(jnp.float32), axis=0)
        mixed_grad = jnp.einsum(
            "re,de->rd", branch_low, weight_out, preferred_element_type=jnp.float32
        ).astype(jnp.bfloat16)
        query_grad, partial_kv, inner = attend_backward(
            queries, full_kv, layer_ids_query, layer_ids_keys, mixed_grad, log_total, HEADS, scale
        )
        kv_grad = lax.psum_scatter(
            partial_kv.astype(jnp.bfloat16), "ctx", scatter_dimension=0, tiled=True
        )
        query_low = query_grad.astype(jnp.bfloat16)
        projected_grad = jnp.concatenate([query_low, kv_grad], axis=1)
        layer_grad_qkv = jnp.einsum(
            "rd,re->de", layer_inputs, projected_grad, preferred_element_type=jnp.float32
        )
        vector_grad = jnp.stack(
            [
                jnp.sum(query_low.astype(jnp.float32), axis=0),
                jnp.sum(kv_grad[:, width:].astype(jnp.float32), axis=0),
                grad_bias_out,
                grad_gain_one,
                grad_shift_one,
                grad_bias_two,
                grad_gain_two,
                grad_shift_two,
            ]
        )
        grad_inputs = grad_summed + jnp.einsum(
            "re,de->rd", projected_grad, weight_qkv, preferred_element_type=jnp.float32
        )
        grad_inputs, grads = (
            grad_inputs,
            (
                layer_grad_qkv,
                layer_grad_out,
                layer_grad_in,
                layer_grad_down,
                layer_grad_bias_in,
                vector_grad,
            ),
        )
        totals = grads if totals is None else jax.tree.map(jnp.add, totals, grads)
        if forward_at < micro_count:
            input_grads[forward_at] = grad_inputs
        if back_at < micro_count:
            returning = shifted(grad_inputs.astype(jnp.bfloat16), "section", -1)
    results = jnp.stack(
        [
            jnp.where(section_at == 0, input_grads[index].astype(jnp.bfloat16), final_states[index])
            for index in range(micro_count)
        ]
    )[None]
    shares = (
        lax.psum_scatter(
            totals[0].astype(jnp.bfloat16), "wt", scatter_dimension=0, tiled=True
        ).astype(jnp.float32),
        lax.psum_scatter(
            totals[1].astype(jnp.bfloat16), "wt", scatter_dimension=0, tiled=True
        ).astype(jnp.float32),
        lax.psum_scatter(
            totals[2].astype(jnp.bfloat16), "wt", scatter_dimension=0, tiled=True
        ).astype(jnp.float32),
        lax.psum_scatter(
            totals[3].astype(jnp.bfloat16), "wt", scatter_dimension=0, tiled=True
        ).astype(jnp.float32),
        lax.psum_scatter(
            totals[4].astype(jnp.bfloat16), "wt", scatter_dimension=0, tiled=True
        ).astype(jnp.float32),
        lax.psum_scatter(
            totals[5].astype(jnp.bfloat16), "wt", scatter_dimension=1, tiled=True
        ).astype(jnp.float32),
    )
    shares = jax.tree.map(lambda part: part.astype(jnp.float32), lax.psum(as_sent(shares), "ctx"))
    grad_qkv, grad_out, grad_in, grad_down, grad_bias_in, grad_vectors = shares
    return (
        results,
        grad_qkv[None],
        grad_out[None],
        grad_in[None],
        grad_down[None],
        grad_bias_in[None],
        grad_vectors[None],
    )


PAIR = 128
FAR = -1000000000.0
MESH = pl.DeviceIdType.MESH


def dot(left, right, dims=((1,), (0,))):
    return lax.dot_general(left, right, (dims, ((), ())), preferred_element_type=jnp.float32)


def head_lanes(size):
    lane = lax.broadcasted_iota(jnp.int32, (1, PAIR), 1)
    return [lane // size == index for index in range(PAIR // size)]


def only(mask, values):
    return jnp.where(mask, values, jnp.zeros_like(values))


def attend_kernel(size, ids_row, ids_col, states, weight, bias, qkv, mixed):
    local = mixed.shape[2]
    projected = dot(states[0], weight[...]) + bias[...]
    qkv[0] = projected.astype(jnp.bfloat16)
    same = ids_col[0] == ids_row[0]
    masks = head_lanes(size)
    for pair in range(local // PAIR):
        at = pair * PAIR
        q = qkv[0, :, at : at + PAIR] * jnp.bfloat16(size**-0.5)
        k = qkv[0, :, local + at : local + at + PAIR]
        v = qkv[0, :, 2 * local + at : 2 * local + at + PAIR]
        total = None
        for mask in masks:
            scores = jnp.where(same, dot(only(mask, k), q, ((1,), (1,))), FAR)
            probs = jnp.exp(scores - jnp.max(scores, axis=0, keepdims=True))
            scale = 1.0 / jnp.sum(probs, axis=0, keepdims=True)
            low = (probs * scale).astype(jnp.bfloat16)
            term = dot(only(mask, v), low, ((0,), (0,)))
            total = term if total is None else total + term
        mixed[0, :, at : at + PAIR] = total.T.astype(jnp.bfloat16)


def attend_heads(states, weight, bias, ids, size):
    packs, rows, width = states.shape
    local = weight.shape[1] // 3
    whole = lambda *shape: pl.BlockSpec(shape, lambda m: (0,) * len(shape))
    block = lambda *shape: pl.BlockSpec((1,) + shape, lambda m: (m, 0, 0))
    return pl.pallas_call(
        functools.partial(attend_kernel, size),
        grid=(packs,),
        in_specs=[
            block(1, rows),
            block(rows, 1),
            block(rows, width),
            whole(width, 3 * local),
            whole(1, 3 * local),
        ],
        out_specs=[block(rows, 3 * local), block(rows, local)],
        out_shape=[
            jax.ShapeDtypeStruct((packs, rows, 3 * local), jnp.bfloat16),
            jax.ShapeDtypeStruct((packs, rows, local), jnp.bfloat16),
        ],
        compiler_params=pltpu.CompilerParams(vmem_limit_bytes=48 * 2**20),
        name="attend_heads",
    )(ids[:, None, :], ids[:, :, None], states, weight, bias)


def attend_back_kernel(size, ids_row, ids_col, qkv, mixed_grad, weight, projected_grad, part):
    local = mixed_grad.shape[2]
    same = ids_col[0] == ids_row[0]
    masks = head_lanes(size)
    scale = jnp.bfloat16(size**-0.5)
    for pair in range(local // PAIR):
        at = pair * PAIR
        q = qkv[0, :, at : at + PAIR] * scale
        k = qkv[0, :, local + at : local + at + PAIR]
        v = qkv[0, :, 2 * local + at : 2 * local + at + PAIR]
        grad = mixed_grad[0, :, at : at + PAIR]
        totals = [None] * 3
        for mask in masks:
            own_k = only(mask, k)
            scores = jnp.where(same, dot(own_k, q, ((1,), (1,))), FAR)
            probs = jnp.exp(scores - jnp.max(scores, axis=0, keepdims=True))
            probs = probs * (1.0 / jnp.sum(probs, axis=0, keepdims=True))
            prob_grad = dot(only(mask, v), grad, ((1,), (1,)))
            inner = jnp.sum(probs * prob_grad, axis=0, keepdims=True)
            score_grad = (probs * (prob_grad - inner)).astype(jnp.bfloat16)
            terms = (
                dot(own_k, score_grad, ((0,), (0,))),
                dot(score_grad, only(mask, q)),
                dot(probs.astype(jnp.bfloat16), only(mask, grad)),
            )
            totals = [t if o is None else o + t for o, t in zip(totals, terms)]
        query_grad = totals[0].T * size**-0.5
        projected_grad[0, :, at : at + PAIR] = query_grad.astype(jnp.bfloat16)
        projected_grad[0, :, local + at : local + at + PAIR] = totals[1].astype(jnp.bfloat16)
        projected_grad[0, :, 2 * local + at : 2 * local + at + PAIR] = totals[2].astype(
            jnp.bfloat16
        )
    part[0] = dot(projected_grad[0], weight[...], ((1,), (1,))).astype(jnp.bfloat16)


def attend_heads_back(qkv, mixed_grad, weight, ids, size):
    packs, rows, local = mixed_grad.shape
    width = weight.shape[0]
    whole = lambda *shape: pl.BlockSpec(shape, lambda m: (0,) * len(shape))
    block = lambda *shape: pl.BlockSpec((1,) + shape, lambda m: (m, 0, 0))
    return pl.pallas_call(
        functools.partial(attend_back_kernel, size),
        grid=(packs,),
        in_specs=[
            block(1, rows),
            block(rows, 1),
            block(rows, 3 * local),
            block(rows, local),
            whole(width, 3 * local),
        ],
        out_specs=[block(rows, 3 * local), block(rows, width)],
        out_shape=[
            jax.ShapeDtypeStruct((packs, rows, 3 * local), jnp.bfloat16),
            jax.ShapeDtypeStruct((packs, rows, width), jnp.bfloat16),
        ],
        compiler_params=pltpu.CompilerParams(vmem_limit_bytes=48 * 2**20),
        name="attend_heads_back",
    )(ids[:, None, :], ids[:, :, None], qkv, mixed_grad, weight)


def normal_tail(values):
    size = jnp.abs(values)
    bell = jnp.exp(-0.5 * values * values)
    t = 1.0 / (1.0 + 0.3275911 * (2.0**-0.5) * size)
    poly = t * (
        0.254829592
        + t * (-0.284496736 + t * (1.421413741 + t * (-1.453152027 + t * 1.061405429)))
    )
    tail = 0.5 * poly * bell
    return (jnp.where(values >= 0, 1.0 - tail, tail), bell)


def gelu_both(values):
    below, bell = normal_tail(values)
    return (values * below, below + values * bell * 0.3989422804014327)


def norm_parts(values):
    center = jnp.mean(values, axis=-1, keepdims=True)
    offset = values - center
    spread = jnp.mean(offset * offset, axis=-1, keepdims=True)
    inverse = lax.rsqrt(spread + 1e-05)
    return (offset * inverse, inverse)


def norm_back(grad, gain, normal, inverse):
    inner = grad * gain
    mean = jnp.mean(inner, axis=-1, keepdims=True)
    along = jnp.mean(inner * normal, axis=-1, keepdims=True)
    return inverse * (inner - mean - normal * along)


CHUNK = 128


def sum_into(target, parts, rows):
    step = 16

    def one(index, carry):
        at = pl.ds(pl.multiple_of(index * step, step), step)
        total = parts[0][at, :].astype(jnp.float32)
        for part in parts[1:]:
            total = total + part[at, :].astype(jnp.float32)
        target[at, :] = total.astype(jnp.bfloat16)
        return carry

    lax.fori_loop(0, rows // step, one, 0)


def chunk_list(local, width, hidden):
    down = [("down", index) for index in range(hidden // 4 // CHUNK)]
    across = [
        ("in", (half, column))
        for column in range(hidden // width)
        for half in range(local // CHUNK)
    ]
    out = [("out", half) for half in range(local // CHUNK)]
    qkv = [("qkv", (half, part)) for part in range(3) for half in range(local // CHUNK)]
    return down + across + out + [("rest", 0)] + qkv


def reduce_kernel(chunks, local, width, hidden, grads, results, buffers, sems):
    near, far, near_in, far_in, across_in, up_in, side_in, total = buffers
    load, load_far, near_send, near_recv, far_send, far_recv = sems[:6]
    across_send, across_recv, up_send, up_recv, side_recv = sems[6:11]
    down_send, down_recv, keep, piece_send, piece_recv = sems[11:]
    z = lax.axis_index("ctx")
    w = lax.axis_index("wt")
    core = lax.rem(w, 2)
    sibling = w + 1 - 2 * core
    across = lax.rem(w + 2, 4)
    across_sibling = lax.rem(sibling + 2, 4)
    partners = (sibling, across, across_sibling)

    barrier = pltpu.get_barrier_semaphore()
    for partner in partners:
        pl.semaphore_signal(barrier, 1, device_id={"wt": partner}, device_id_type=MESH)

    @pl.when(z > 0)
    def _():
        pl.semaphore_signal(barrier, 1, device_id={"ctx": z - 1}, device_id_type=MESH)

    @pl.when(z < 3)
    def _():
        pl.semaphore_signal(barrier, 1, device_id={"ctx": z + 1}, device_id_type=MESH)

    pl.semaphore_wait(barrier, 3 + (z > 0).astype(jnp.int32) + (z < 3).astype(jnp.int32))

    def rows_of(k):
        return 16 if chunks[k][0] == "rest" else CHUNK

    def is_piece(k):
        return chunks[k][0] == "qkv"

    def source(k, j):
        kind, at = chunks[k]
        if kind == "down":
            return grads["down"].at[pl.ds(j * (hidden // 4) + at * CHUNK, CHUNK), :]
        if kind == "in":
            half, column = at
            return grads["in"].at[
                pl.ds(j * local + half * CHUNK, CHUNK), pl.ds(column * width, width)
            ]
        if kind == "out":
            return grads["out"].at[pl.ds(j * local + at * CHUNK, CHUNK), :]
        if kind == "rest":
            return grads["rest"].at[pl.ds(j * 16, 16), :]
        half, part = at
        return grads["qkv"].at[
            pl.ds(j * local + half * CHUNK, CHUNK), pl.ds(part * local, local)
        ]

    def result(k):
        kind, at = chunks[k]
        if kind == "down":
            return results["down"].at[pl.ds(at * CHUNK, CHUNK), :]
        if kind == "out":
            return results["out"].at[pl.ds(at * CHUNK, CHUNK), :]
        if kind == "rest":
            return results["rest"]
        half, column = at
        return results[kind].at[pl.ds(half * CHUNK, CHUNK), pl.ds(column * width, width)]

    def slot(buffer, k):
        return buffer.at[k, pl.ds(0, rows_of(k)), :]

    def remote(source_ref, target_ref, send, recv, **where):
        return pltpu.make_async_remote_copy(
            source_ref, target_ref, send, recv, device_id=where, device_id_type=MESH
        )

    def near_load(k):
        if is_piece(k):
            place = near.at[k, :, pl.ds(w * local, local)]
            return pltpu.make_async_copy(source(k, w), place, load.at[k])
        return pltpu.make_async_copy(source(k, w), slot(near, k), load.at[k])

    def far_load(k):
        return pltpu.make_async_copy(source(k, across), slot(far, k), load_far.at[k])

    def near_copy(k):
        return remote(
            source(k, sibling), slot(near_in, k), near_send.at[k], near_recv.at[k], wt=sibling
        )

    def far_copy(k):
        return remote(
            source(k, across_sibling), slot(far_in, k), far_send.at[k], far_recv.at[k], wt=sibling
        )

    def piece_copy(k, index):
        place = near.at[k, :, pl.ds(w * local, local)]
        at = piece_send.at[k, index], piece_recv.at[k, index]
        return remote(source(k, partners[index]), place, *at, wt=partners[index])

    def across_copy(k):
        return remote(
            slot(far, k), slot(across_in, k), across_send.at[k], across_recv.at[k], wt=across
        )

    def place_of(k, role):
        return role if k % 2 == 0 else 3 - role

    def up_copy(k, role):
        target = place_of(k, 1 if role == 0 else 2)
        return remote(slot(total, k), slot(up_in, k), up_send.at[k], up_recv.at[k], ctx=target)

    def side_copy(k):
        return remote(
            slot(total, k), slot(side_in, k), up_send.at[k], side_recv.at[k], ctx=place_of(k, 1)
        )

    def down_copy(k, role):
        origin = result(k) if role == 3 else slot(total, k)
        at = down_send.at[k, 1 if role == 2 else 0]
        return remote(origin, result(k), at, down_recv.at[k], ctx=place_of(k, role))

    def keep_copy(k):
        return pltpu.make_async_copy(slot(total, k), result(k), keep.at[k])

    def on(k, role, step):
        pl.when(z == place_of(k, role))(step)

    def summands(k):
        if is_piece(k):
            return [slot(near, k)]
        return [slot(near, k), slot(near_in, k), slot(across_in, k)]

    count = len(chunks)
    for k in range(count):
        if not is_piece(k):
            far_copy(k).start()
            far_load(k).start()
            near_copy(k).start()
            near_load(k).start()

    def begin(k):
        if is_piece(k):
            near_load(k).start()
            for index in range(3):
                piece_copy(k, index).start()
            return
        far_load(k).wait()
        far_copy(k).wait_recv()
        sum_into(slot(far, k), [slot(far, k), slot(far_in, k)], rows_of(k))
        across_copy(k).start()

    def settle(k):
        near_load(k).wait()
        if is_piece(k):
            for index in range(3):
                piece_copy(k, index).wait_recv()
        else:
            near_copy(k).wait_recv()
            across_copy(k).wait_recv()
        for role in (0, 3):

            def step(role=role):
                sum_into(slot(total, k), summands(k), rows_of(k))
                up_copy(k, role).start()

            on(k, role, step)

    def aside(k):
        def step():
            up_copy(k, 3).wait_recv()
            sum_into(slot(total, k), summands(k) + [slot(up_in, k)], rows_of(k))
            side_copy(k).start()

        on(k, 2, step)

    def finish(k):
        def step():
            up_copy(k, 0).wait_recv()
            side_copy(k).wait_recv()
            parts = summands(k) + [slot(up_in, k), slot(side_in, k)]
            sum_into(slot(total, k), parts, rows_of(k))
            down_copy(k, 0).start()
            down_copy(k, 2).start()
            keep_copy(k).start()

        on(k, 1, step)

    def forward(k):
        def step():
            down_copy(k, 2).wait_recv()
            down_copy(k, 3).start()

        on(k, 2, step)

    stages = (begin, settle, aside, finish, forward)
    for tick in range(count + len(stages) - 1):
        for lag, stage in enumerate(stages):
            if 0 <= tick - lag < count:
                stage(tick - lag)
    for k in range(count):
        if is_piece(k):
            for index in range(3):
                piece_copy(k, index).wait_send()
        else:
            far_copy(k).wait_send()
            near_copy(k).wait_send()
            across_copy(k).wait_send()

        def ends(role):
            up_copy(k, role).wait_send()
            down_copy(k, role).wait_recv()

        def middle():
            side_copy(k).wait_send()
            down_copy(k, 3).wait_send()

        def owner():
            down_copy(k, 0).wait_send()
            down_copy(k, 2).wait_send()
            keep_copy(k).wait()

        on(k, 0, lambda: ends(0))
        on(k, 3, lambda: ends(3))
        on(k, 2, middle)
        on(k, 1, owner)


def reduce_grads(grad_qkv, grad_out, grad_in, grad_down, rest):
    width = grad_out.shape[0]
    hidden = grad_down.shape[0]
    local = width // 4
    chunks = chunk_list(local, width, hidden)
    count = len(chunks)

    def body(*refs):
        grads = dict(zip(("qkv", "out", "in", "down", "rest"), refs[:5]))
        results = dict(zip(("qkv", "out", "in", "down", "rest"), refs[5:10]))
        reduce_kernel(chunks, local, width, hidden, grads, results, refs[10:18], refs[18:])

    shapes = [
        (local, 3 * width),
        (local, width),
        (local, hidden),
        (hidden // 4, width),
        (16, width),
    ]
    dma = pltpu.SemaphoreType.DMA
    whole = [pltpu.VMEM((count, CHUNK, width), jnp.bfloat16)]
    direct = [pltpu.VMEM((count - 6, CHUNK, width), jnp.bfloat16)]
    return pl.pallas_call(
        body,
        in_specs=[pl.BlockSpec(memory_space=pl.ANY)] * 5,
        out_specs=[pl.BlockSpec(memory_space=pl.ANY)] * 5,
        out_shape=[jax.ShapeDtypeStruct(shape, jnp.bfloat16) for shape in shapes],
        scratch_shapes=whole
        + direct * 4
        + whole * 3
        + [dma((count,))] * 11
        + [dma((count, 2)), dma((count,)), dma((count,)), dma((count, 3)), dma((count, 3))],
        compiler_params=pltpu.CompilerParams(
            collective_id=1, has_side_effects=True, vmem_limit_bytes=60 * 2**20
        ),
        name="reduce_grads",
    )(grad_qkv, grad_out, grad_in, grad_down, rest)


def relay(boundary, lengths, valid, w_qkv, w_out, w_in, w_down, bias_in, vectors):
    section_at = lax.axis_index("section")
    count_ctx = lax.axis_size("ctx")
    ctx_at = lax.axis_index("ctx")
    wt_at = lax.axis_index("wt")
    micro, rows, width = boundary.shape[1:]
    pack = rows * count_ctx
    size = width // HEADS
    local = width // lax.axis_size("wt")
    tokens = micro * rows
    swap = [
        (c * count_ctx + w, w * count_ctx + c) for c in range(count_ctx) for w in range(count_ctx)
    ]

    def swapped(block):
        return lax.ppermute(block, ("ctx", "wt"), swap)

    def gather_rows(block):
        return lax.all_gather(block, "wt", axis=1, tiled=True)

    def scatter_rows(block):
        return lax.psum_scatter(block, "wt", scatter_dimension=1, tiled=True)

    def rows_of_heads(block):
        split = block.reshape(micro, count_ctx, rows, local)
        return lax.all_to_all(split, "wt", 1, 3, tiled=True).reshape(tokens, width)

    def heads_of_rows(block):
        split = block.reshape(micro, 1, rows, width)
        return lax.all_to_all(split, "wt", 3, 1, tiled=True).reshape(micro, pack, local)

    own = swapped(boundary[0])
    shard = w_qkv[0].reshape(local, 3, count_ctx, local)
    weight_qkv = lax.all_to_all(shard, "wt", 2, 0, tiled=True).reshape(width, 3 * local)
    weight_out = lax.all_gather(w_out[0], "wt", axis=0, tiled=True)
    weight_in = lax.all_gather(w_in[0], "wt", axis=0, tiled=True)
    weight_down = lax.all_gather(w_down[0], "wt", axis=0, tiled=True)
    small = jnp.concatenate([vectors[0], bias_in[0].reshape(-1, local)], axis=0)
    small = lax.all_gather(small, "wt", axis=0)
    vector_rows = small[:, :8].transpose(1, 0, 2).reshape(8, width).astype(jnp.float32)
    in_bias = small[:, 8:].reshape(-1).astype(jnp.float32)
    own_rows = vectors[0].astype(jnp.float32)
    qkv_bias = jnp.concatenate([own_rows[0], jnp.zeros((local,), jnp.float32), own_rows[1]])[None]
    my_lengths = lax.dynamic_index_in_dim(lengths, ctx_at, 1, keepdims=False)
    ids = jax.vmap(lambda row: dealt_ids(row, pack, count_ctx))(my_lengths)
    marks = lax.all_gather(valid, ("wt", "ctx"), axis=1, tiled=True)
    count = jnp.sum(marks.astype(jnp.float32))
    at = (ctx_at * count_ctx + wt_at) * rows
    marks = lax.dynamic_slice_in_dim(marks, at, rows, 1).reshape(tokens, 1).astype(jnp.float32)
    factor = LOSS_SCALE / count

    def forward(states):
        full = gather_rows(states.reshape(micro, rows, width))
        qkv, mixed = attend_heads(full, weight_qkv, qkv_bias, ids, size)
        mixed = rows_of_heads(mixed)
        summed = states.astype(jnp.float32) + (dot(mixed, weight_out) + vector_rows[2])
        normal_one, inverse_one = norm_parts(summed)
        first = normal_one * vector_rows[3] + vector_rows[4]
        first_low = first.astype(jnp.bfloat16)
        hidden, slope = gelu_both(dot(first_low, weight_in) + in_bias)
        hidden = hidden.astype(jnp.bfloat16)
        second = first + (dot(hidden, weight_down) + vector_rows[5])
        normal_two, inverse_two = norm_parts(second)
        output = normal_two * vector_rows[6] + vector_rows[7]
        kept = (full, qkv, mixed, normal_one, inverse_one, first_low, hidden, slope)
        return (output, kept + (normal_two, inverse_two))

    def backward(grad, kept):
        full, qkv, mixed, normal_one, inverse_one, first_low, hidden, slope = kept[:8]
        normal_two, inverse_two = kept[8:]
        grad_second = norm_back(grad, vector_rows[6], normal_two, inverse_two)
        down_low = grad_second.astype(jnp.bfloat16)
        pre_low = (dot(down_low, weight_down, ((1,), (1,))) * slope).astype(jnp.bfloat16)
        grad_first = grad_second + dot(pre_low, weight_in, ((1,), (1,)))
        grad_summed = norm_back(grad_first, vector_rows[3], normal_one, inverse_one)
        branch_low = grad_summed.astype(jnp.bfloat16)
        mixed_grad = dot(branch_low, weight_out, ((1,), (1,))).astype(jnp.bfloat16)
        mixed_grad = heads_of_rows(mixed_grad)
        projected_grad, part = attend_heads_back(qkv, mixed_grad, weight_qkv, ids, size)
        grad_states = grad_summed + scatter_rows(part).reshape(tokens, width)

        def weight_grads():
            along = ((0,), (0,))
            flat = projected_grad.reshape(-1, 3 * local)
            total = lambda values: jnp.sum(values.astype(jnp.float32), axis=0)
            bias_qkv = total(flat)
            rows_local = jnp.stack([bias_qkv[:local], bias_qkv[2 * local :]])
            rows_whole = jnp.stack(
                [
                    total(branch_low),
                    total(grad_first * normal_one),
                    total(grad_first),
                    total(down_low),
                    total(grad * normal_two),
                    total(grad),
                ]
            )
            return (
                dot(full.reshape(-1, width), flat, along),
                dot(mixed, branch_low, along),
                dot(first_low, pre_low, along),
                dot(hidden, down_low, along),
                total(pre_low),
                rows_local,
                rows_whole,
            )

        return (grad_states, weight_grads)

    states = own.reshape(tokens, width)
    output, _ = forward(states)
    arrived = shifted(output.astype(jnp.bfloat16), "section", 1)
    states = jnp.where(section_at == 0, states, arrived)
    output, kept = forward(states)
    distance = output - own.reshape(tokens, width).astype(jnp.float32)
    cotangent = factor * marks * distance
    grad_states, _ = backward(cotangent, kept)
    returned = shifted(grad_states.astype(jnp.bfloat16), "section", -1)
    cotangent = jnp.where(section_at == 1, cotangent, returned.astype(jnp.float32))
    grad_states, weight_grads = backward(cotangent, kept)
    results = jnp.where(section_at == 0, grad_states, output).astype(jnp.bfloat16)
    results = swapped(results.reshape(micro, rows, width))[None]
    grads = weight_grads()
    low = lambda part: part.astype(jnp.bfloat16)
    mine = (jnp.arange(4) == wt_at).astype(jnp.float32)[None, :, None]
    rest = jnp.concatenate([grads[5][:, None, :] * mine, grads[6].reshape(6, 4, local)])
    rest = jnp.concatenate([rest, jnp.zeros((8, 4, local), jnp.float32)])
    rest = rest.transpose(1, 0, 2)
    in_rows = jnp.zeros((4, 16, local), jnp.float32)
    in_rows = in_rows.at[:, :4].set(grads[4].reshape(4, -1, local))
    rest = jnp.concatenate([rest, in_rows, jnp.zeros((4, 16, 2 * local), jnp.float32)], axis=2)
    rest = rest.reshape(64, width)
    sums = reduce_grads(*[low(part) for part in grads[:4]], low(rest))
    sums = [part.astype(jnp.float32)[None] for part in sums]
    rest = sums[4]
    bias_back = rest[:, :4, local : 2 * local].reshape(1, -1)
    return (results, *sums[:4], bias_back, rest[:, :8, :local])


def solution(mesh):
    in_specs = (
        P("section", None, ("wt", "ctx"), None),
        P(),
        P(None, ("wt", "ctx")),
        P("section", "wt", None),
        P("section", "wt", None),
        P("section", "wt", None),
        P("section", "wt", None),
        P("section", "wt"),
        P("section", None, "wt"),
    )
    out_specs = (
        P("section", None, ("wt", "ctx"), None),
        P("section", "wt", None),
        P("section", "wt", None),
        P("section", "wt", None),
        P("section", "wt", None),
        P("section", "wt"),
        P("section", None, "wt"),
    )
    square = mesh.shape["ctx"] == mesh.shape["wt"]
    return jax.shard_map(relay if square else shards, mesh=mesh, in_specs=in_specs, out_specs=out_specs, check_vma=False)
```

```python
import functools

import jax
import jax.numpy as jnp
from jax import lax
from jax.experimental import pallas as pl
from jax.experimental.pallas import tpu as pltpu
from jax.sharding import PartitionSpec as P

HEADS = 16
LOSS_SCALE = 1024


def shifted(block, axis, distance):
    devices = range(lax.axis_size(axis))
    route = [(i - distance, i) for i in devices if i - distance in devices]
    return lax.ppermute(block, axis, route)


def as_sent(x):

    def short(part):
        return part.astype(jnp.bfloat16) if part.dtype == jnp.float32 else part

    return jax.tree.map(short, x)


def layer_norm(values, gain, shift):
    center = jnp.mean(values, axis=-1, keepdims=True)
    offset = values - center
    spread = jnp.mean(offset * offset, axis=-1, keepdims=True)
    return offset * lax.rsqrt(spread + 1e-05) * gain + shift


def exact_gelu(values):
    return jax.nn.gelu(values, approximate=False)


def dealt_ids(length_row, pack_size, ctx_count):
    ends = jnp.cumsum(length_row)
    places = jnp.arange(pack_size, dtype=jnp.int32)
    natural = jnp.sum((places[:, None] >= ends[None, :]).astype(jnp.int32), axis=1)
    return natural.reshape(pack_size // ctx_count, ctx_count).T.reshape(pack_size)


def split_blocks(full_kv, ids_keys):
    block = min(512, full_kv.shape[0])
    count_blocks = full_kv.shape[0] // block
    return (
        full_kv.reshape(count_blocks, block, full_kv.shape[1]),
        ids_keys.reshape(count_blocks, block),
    )


def split_kv(block_kv, heads):
    half = block_kv.shape[1] // 2
    keys = block_kv[:, :half].reshape(block_kv.shape[0], heads, -1)
    values = block_kv[:, half:].reshape(block_kv.shape[0], heads, -1)
    return (keys, values)


def block_scores(queries, keys, ids_query, ids_keys, scale):
    scores = jnp.einsum("qhd,khd->hqk", queries, keys, preferred_element_type=jnp.float32) * scale
    same = ids_query[:, None] == ids_keys[None, :]
    return jnp.where(same[None], scores, -1000000000.0)


def attend_forward(queries, full_kv, ids_query, ids_keys, heads, scale):
    blocks, id_blocks = split_blocks(full_kv, ids_keys)
    query_rows = queries.shape[0]

    def total_step(carry, items):
        run_max, run_sum = carry
        keys, values = split_kv(items[0], heads)
        scores = block_scores(queries, keys, ids_query, items[1], scale)
        new_max = jnp.maximum(run_max, jnp.max(scores, axis=-1))
        run_sum = run_sum * jnp.exp(run_max - new_max) + jnp.sum(
            jnp.exp(scores - new_max[..., None]), axis=-1
        )
        return ((new_max, run_sum), None)

    start = (
        jnp.full((heads, query_rows), -1e30, jnp.float32),
        jnp.zeros((heads, query_rows), jnp.float32),
    )
    (run_max, run_sum), _ = lax.scan(total_step, start, (blocks, id_blocks))
    log_total = run_max + jnp.log(run_sum)

    def mix_step(carry, items):
        keys, values = split_kv(items[0], heads)
        scores = block_scores(queries, keys, ids_query, items[1], scale)
        probs = jnp.exp(scores - log_total[..., None]).astype(jnp.bfloat16)
        return (
            carry + jnp.einsum("hqk,khd->qhd", probs, values, preferred_element_type=jnp.float32),
            None,
        )

    mixed, _ = lax.scan(mix_step, jnp.zeros(queries.shape, jnp.float32), (blocks, id_blocks))
    return (mixed.reshape(query_rows, -1), log_total)


def attend_backward(queries, full_kv, ids_query, ids_keys, mixed_grad, log_total, heads, scale):
    blocks, id_blocks = split_blocks(full_kv, ids_keys)
    grad_heads = mixed_grad.reshape(queries.shape)

    def inner_step(carry, items):
        keys, values = split_kv(items[0], heads)
        scores = block_scores(queries, keys, ids_query, items[1], scale)
        probs = jnp.exp(scores - log_total[..., None])
        prob_grad = jnp.einsum(
            "qhd,khd->hqk", grad_heads, values, preferred_element_type=jnp.float32
        )
        return (carry + jnp.sum(probs * prob_grad, axis=-1), None)

    inner, _ = lax.scan(inner_step, jnp.zeros(log_total.shape, jnp.float32), (blocks, id_blocks))

    def grad_step(carry, items):
        keys, values = split_kv(items[0], heads)
        scores = block_scores(queries, keys, ids_query, items[1], scale)
        probs = jnp.exp(scores - log_total[..., None])
        prob_grad = jnp.einsum(
            "qhd,khd->hqk", grad_heads, values, preferred_element_type=jnp.float32
        )
        score_grad = (probs * (prob_grad - inner[..., None])).astype(jnp.bfloat16)
        carry = (
            carry
            + jnp.einsum("hqk,khd->qhd", score_grad, keys, preferred_element_type=jnp.float32)
            * scale
        )
        key_grad = (
            jnp.einsum("hqk,qhd->khd", score_grad, queries, preferred_element_type=jnp.float32)
            * scale
        )
        value_grad = jnp.einsum(
            "hqk,qhd->khd",
            probs.astype(jnp.bfloat16),
            grad_heads,
            preferred_element_type=jnp.float32,
        )
        block = keys.shape[0]
        return (
            carry,
            jnp.concatenate([key_grad.reshape(block, -1), value_grad.reshape(block, -1)], axis=1),
        )

    query_grad, partial_kv = lax.scan(
        grad_step, jnp.zeros(queries.shape, jnp.float32), (blocks, id_blocks)
    )
    query_grad = query_grad.reshape(queries.shape[0], -1)
    return (query_grad, partial_kv.reshape(-1, partial_kv.shape[-1]), inner)


def shards(boundary, lengths, valid, w_qkv, w_out, w_in, w_down, bias_in, vectors):
    section_at = lax.axis_index("section")
    ctx_count = lax.axis_size("ctx")
    ctx_at = lax.axis_index("ctx")
    wt_at = lax.axis_index("wt")
    micro_count = boundary.shape[1]
    row_count = boundary.shape[2]
    width = boundary.shape[3]
    pack_size = row_count * ctx_count
    head_size = width // HEADS
    scale = head_size ** (-0.5)
    gathered = (
        lax.all_gather(w_qkv[0], "wt", axis=0, tiled=True),
        lax.all_gather(w_out[0], "wt", axis=0, tiled=True),
        lax.all_gather(w_in[0], "wt", axis=0, tiled=True),
        lax.all_gather(w_down[0], "wt", axis=0, tiled=True),
        lax.all_gather(bias_in[0], "wt", axis=0, tiled=True),
        lax.all_gather(vectors[0], "wt", axis=1, tiled=True),
    )
    weight_qkv, weight_out, weight_in, weight_down, in_bias, vector_rows = gathered
    in_bias = in_bias.astype(jnp.float32)
    vector_rows = vector_rows.astype(jnp.float32)
    qkv_bias = jnp.concatenate([vector_rows[0], jnp.zeros((width,), jnp.float32), vector_rows[1]])
    my_lengths = lax.dynamic_index_in_dim(lengths, wt_at, 1, keepdims=False)

    def ids_of(length_row):
        return dealt_ids(length_row, pack_size, ctx_count)

    pack_ids = jax.vmap(ids_of)(my_lengths)
    query_ids = lax.dynamic_slice_in_dim(pack_ids, ctx_at * row_count, row_count, 1)
    count = lax.psum(jnp.sum(valid.astype(jnp.float32)), ("ctx", "wt"))
    factor = LOSS_SCALE / count
    empty_rows = jnp.zeros((row_count, width), jnp.bfloat16)
    arriving = empty_rows
    kept_list = []
    cotangents = []
    final_states = []
    for tick_at in range(micro_count + 1):
        own_input = boundary[0, tick_at] if tick_at < micro_count else empty_rows
        inputs = jnp.where(section_at == 0, own_input, arriving)
        micro_here = jnp.clip(tick_at - section_at, 0, micro_count - 1)
        ids_keys = lax.dynamic_index_in_dim(pack_ids, micro_here, 0, keepdims=False)
        ids_query = lax.dynamic_index_in_dim(query_ids, micro_here, 0, keepdims=False)
        residual = inputs.astype(jnp.float32)
        projected = jnp.dot(inputs, weight_qkv, preferred_element_type=jnp.float32) + qkv_bias
        layer_queries = (
            projected[:, :width].astype(jnp.bfloat16).reshape(row_count, HEADS, head_size)
        )
        layer_local_kv = projected[:, width:].astype(jnp.bfloat16)
        layer_full_kv = lax.all_gather(layer_local_kv, "ctx", axis=0, tiled=True)
        mixed, layer_log_total = attend_forward(
            layer_queries, layer_full_kv, ids_query, ids_keys, HEADS, scale
        )
        layer_mixed_low = mixed.astype(jnp.bfloat16)
        branch = (
            jnp.dot(layer_mixed_low, weight_out, preferred_element_type=jnp.float32)
            + vector_rows[2]
        )
        layer_summed = residual + branch
        first = layer_norm(layer_summed, vector_rows[3], vector_rows[4])
        layer_first_low = first.astype(jnp.bfloat16)
        layer_hidden_pre = (
            jnp.dot(layer_first_low, weight_in, preferred_element_type=jnp.float32) + in_bias
        )
        layer_hidden_low = exact_gelu(layer_hidden_pre).astype(jnp.bfloat16)
        layer_second = first + (
            jnp.dot(layer_hidden_low, weight_down, preferred_element_type=jnp.float32)
            + vector_rows[5]
        )
        output = layer_norm(layer_second, vector_rows[6], vector_rows[7])
        layer_kept = (
            inputs,
            layer_queries,
            layer_local_kv,
            layer_full_kv,
            layer_mixed_low,
            layer_log_total,
            layer_summed,
            layer_first_low,
            layer_hidden_pre,
            layer_hidden_low,
            layer_second,
            ids_keys,
            ids_query,
        )
        output, kept = (output, layer_kept)
        kept_list.append(kept)
        if tick_at > 0:
            teacher = boundary[0, tick_at - 1].astype(jnp.float32)
            covered = valid[tick_at - 1].astype(jnp.float32)[:, None]
            cotangents.append(factor * covered * (output - teacher))
            final_states.append(output.astype(jnp.bfloat16))
        else:
            cotangents.append(jnp.zeros((row_count, width), jnp.float32))
        if tick_at < micro_count:
            arriving = shifted(output.astype(jnp.bfloat16), "section", 1)
    returning = empty_rows
    totals = None
    input_grads = [None] * micro_count
    for back_at in range(micro_count + 1):
        forward_at = micro_count - back_at
        grad_output = jnp.where(
            section_at == 1, cotangents[forward_at], returning.astype(jnp.float32)
        )
        (
            layer_inputs,
            queries,
            local_kv,
            full_kv,
            mixed_low,
            log_total,
            summed,
            first_low,
            hidden_pre,
            hidden_low,
            second,
            layer_ids_keys,
            layer_ids_query,
        ) = kept_list[forward_at]
        full_kv = lax.all_gather(local_kv, "ctx", axis=0, tiled=True)
        _, pull_last = jax.vjp(layer_norm, second, vector_rows[6], vector_rows[7])
        grad_second, grad_gain_two, grad_shift_two = pull_last(grad_output)
        down_low = grad_second.astype(jnp.bfloat16)
        layer_grad_down = jnp.einsum(
            "rf,rd->fd", hidden_low, down_low, preferred_element_type=jnp.float32
        )
        grad_bias_two = jnp.sum(down_low.astype(jnp.float32), axis=0)
        _, pull_gelu = jax.vjp(exact_gelu, hidden_pre)
        (grad_pre,) = pull_gelu(
            jnp.einsum("rd,fd->rf", down_low, weight_down, preferred_element_type=jnp.float32)
        )
        pre_low = grad_pre.astype(jnp.bfloat16)
        layer_grad_in = jnp.einsum(
            "rd,rf->df", first_low, pre_low, preferred_element_type=jnp.float32
        )
        layer_grad_bias_in = jnp.sum(pre_low.astype(jnp.float32), axis=0)
        grad_first = grad_second + jnp.einsum(
            "rf,df->rd", pre_low, weight_in, preferred_element_type=jnp.float32
        )
        _, pull_first = jax.vjp(layer_norm, summed, vector_rows[3], vector_rows[4])
        grad_summed, grad_gain_one, grad_shift_one = pull_first(grad_first)
        branch_low = grad_summed.astype(jnp.bfloat16)
        layer_grad_out = jnp.einsum(
            "rd,re->de", mixed_low, branch_low, preferred_element_type=jnp.float32
        )
        grad_bias_out = jnp.sum(branch_low.astype(jnp.float32), axis=0)
        mixed_grad = jnp.einsum(
            "re,de->rd", branch_low, weight_out, preferred_element_type=jnp.float32
        ).astype(jnp.bfloat16)
        query_grad, partial_kv, inner = attend_backward(
            queries, full_kv, layer_ids_query, layer_ids_keys, mixed_grad, log_total, HEADS, scale
        )
        kv_grad = lax.psum_scatter(
            partial_kv.astype(jnp.bfloat16), "ctx", scatter_dimension=0, tiled=True
        )
        query_low = query_grad.astype(jnp.bfloat16)
        projected_grad = jnp.concatenate([query_low, kv_grad], axis=1)
        layer_grad_qkv = jnp.einsum(
            "rd,re->de", layer_inputs, projected_grad, preferred_element_type=jnp.float32
        )
        vector_grad = jnp.stack(
            [
                jnp.sum(query_low.astype(jnp.float32), axis=0),
                jnp.sum(kv_grad[:, width:].astype(jnp.float32), axis=0),
                grad_bias_out,
                grad_gain_one,
                grad_shift_one,
                grad_bias_two,
                grad_gain_two,
                grad_shift_two,
            ]
        )
        grad_inputs = grad_summed + jnp.einsum(
            "re,de->rd", projected_grad, weight_qkv, preferred_element_type=jnp.float32
        )
        grad_inputs, grads = (
            grad_inputs,
            (
                layer_grad_qkv,
                layer_grad_out,
                layer_grad_in,
                layer_grad_down,
                layer_grad_bias_in,
                vector_grad,
            ),
        )
        totals = grads if totals is None else jax.tree.map(jnp.add, totals, grads)
        if forward_at < micro_count:
            input_grads[forward_at] = grad_inputs
        if back_at < micro_count:
            returning = shifted(grad_inputs.astype(jnp.bfloat16), "section", -1)
    results = jnp.stack(
        [
            jnp.where(section_at == 0, input_grads[index].astype(jnp.bfloat16), final_states[index])
            for index in range(micro_count)
        ]
    )[None]
    shares = (
        lax.psum_scatter(
            totals[0].astype(jnp.bfloat16), "wt", scatter_dimension=0, tiled=True
        ).astype(jnp.float32),
        lax.psum_scatter(
            totals[1].astype(jnp.bfloat16), "wt", scatter_dimension=0, tiled=True
        ).astype(jnp.float32),
        lax.psum_scatter(
            totals[2].astype(jnp.bfloat16), "wt", scatter_dimension=0, tiled=True
        ).astype(jnp.float32),
        lax.psum_scatter(
            totals[3].astype(jnp.bfloat16), "wt", scatter_dimension=0, tiled=True
        ).astype(jnp.float32),
        lax.psum_scatter(
            totals[4].astype(jnp.bfloat16), "wt", scatter_dimension=0, tiled=True
        ).astype(jnp.float32),
        lax.psum_scatter(
            totals[5].astype(jnp.bfloat16), "wt", scatter_dimension=1, tiled=True
        ).astype(jnp.float32),
    )
    shares = jax.tree.map(lambda part: part.astype(jnp.float32), lax.psum(as_sent(shares), "ctx"))
    grad_qkv, grad_out, grad_in, grad_down, grad_bias_in, grad_vectors = shares
    return (
        results,
        grad_qkv[None],
        grad_out[None],
        grad_in[None],
        grad_down[None],
        grad_bias_in[None],
        grad_vectors[None],
    )


PAIR = 128
FAR = -1000000000.0
MESH = pl.DeviceIdType.MESH


def dot(left, right, dims=((1,), (0,))):
    return lax.dot_general(left, right, (dims, ((), ())), preferred_element_type=jnp.float32)


def head_lanes(size):
    lane = lax.broadcasted_iota(jnp.int32, (1, PAIR), 1)
    return [lane // size == index for index in range(PAIR // size)]


def only(mask, values):
    return jnp.where(mask, values, jnp.zeros_like(values))


def normal_tail(values):
    size = jnp.abs(values)
    bell = jnp.exp(-0.5 * values * values)
    t = 1.0 / (1.0 + 0.3275911 * (2.0**-0.5) * size)
    poly = t * (
        0.254829592
        + t * (-0.284496736 + t * (1.421413741 + t * (-1.453152027 + t * 1.061405429)))
    )
    tail = 0.5 * poly * bell
    return (jnp.where(values >= 0, 1.0 - tail, tail), bell)


def gelu_both(values):
    below, bell = normal_tail(values)
    return (values * below, below + values * bell * 0.3989422804014327)


def norm_parts(values):
    center = jnp.mean(values, axis=-1, keepdims=True)
    offset = values - center
    spread = jnp.mean(offset * offset, axis=-1, keepdims=True)
    inverse = lax.rsqrt(spread + 1e-05)
    return (offset * inverse, inverse)


def norm_back(grad, gain, normal, inverse):
    inner = grad * gain
    mean = jnp.mean(inner, axis=-1, keepdims=True)
    along = jnp.mean(inner * normal, axis=-1, keepdims=True)
    return inverse * (inner - mean - normal * along)


class Wires:
    def __init__(self, sems):
        self.sems = sems
        self.places = {}

    def at(self, *key):
        return self.sems.at[self.places.setdefault(key, len(self.places))]

    def remote(self, key, source, target, **where):
        return pltpu.make_async_remote_copy(
            source,
            target,
            self.at(key, "send"),
            self.at(key, "recv"),
            device_id=where,
            device_id_type=MESH,
        )

    def local(self, key, source, target):
        return pltpu.make_async_copy(source, target, self.at(key, "local"))


def wt_places():
    w = lax.axis_index("wt")
    core = lax.rem(w, 2)
    sibling = w + 1 - 2 * core
    across = lax.rem(w + 2, 4)
    return w, sibling, across, lax.rem(sibling + 2, 4)


def greet(partners, extra):
    barrier = pltpu.get_barrier_semaphore()
    for partner in partners:
        pl.semaphore_signal(barrier, 1, device_id=partner, device_id_type=MESH)
    waits = len(partners)
    for here, partner in extra:

        @pl.when(here)
        def _():
            pl.semaphore_signal(barrier, 1, device_id=partner, device_id_type=MESH)

        waits = waits + here.astype(jnp.int32)
    pl.semaphore_wait(barrier, waits)


def attend_pack(size, same, qkv, mixed):
    local = mixed.shape[1]
    masks = head_lanes(size)
    for pair in range(local // PAIR):
        at = pair * PAIR
        q = qkv[:, at : at + PAIR] * jnp.bfloat16(size**-0.5)
        k = qkv[:, local + at : local + at + PAIR]
        v = qkv[:, 2 * local + at : 2 * local + at + PAIR]
        total = None
        for mask in masks:
            scores = jnp.where(same, dot(only(mask, k), q, ((1,), (1,))), FAR)
            probs = jnp.exp(scores - jnp.max(scores, axis=0, keepdims=True))
            scale = 1.0 / jnp.sum(probs, axis=0, keepdims=True)
            low = (probs * scale).astype(jnp.bfloat16)
            term = dot(only(mask, v), low, ((0,), (0,)))
            total = term if total is None else total + term
        mixed[:, at : at + PAIR] = total.T.astype(jnp.bfloat16)


def attend_pack_back(size, same, qkv, grad_heads, projected_grad):
    local = grad_heads.shape[1]
    masks = head_lanes(size)
    for pair in range(local // PAIR):
        at = pair * PAIR
        q = qkv[:, at : at + PAIR] * jnp.bfloat16(size**-0.5)
        k = qkv[:, local + at : local + at + PAIR]
        v = qkv[:, 2 * local + at : 2 * local + at + PAIR]
        grad = grad_heads[:, at : at + PAIR]
        totals = [None] * 3
        for mask in masks:
            own_k = only(mask, k)
            scores = jnp.where(same, dot(own_k, q, ((1,), (1,))), FAR)
            probs = jnp.exp(scores - jnp.max(scores, axis=0, keepdims=True))
            probs = probs * (1.0 / jnp.sum(probs, axis=0, keepdims=True))
            prob_grad = dot(only(mask, v), grad, ((1,), (1,)))
            inner = jnp.sum(probs * prob_grad, axis=0, keepdims=True)
            score_grad = (probs * (prob_grad - inner)).astype(jnp.bfloat16)
            terms = (
                dot(own_k, score_grad, ((0,), (0,))),
                dot(score_grad, only(mask, q)),
                dot(probs.astype(jnp.bfloat16), only(mask, grad)),
            )
            totals = [t if o is None else o + t for o, t in zip(totals, terms)]
        query_grad = totals[0].T * size**-0.5
        projected_grad[:, at : at + PAIR] = query_grad.astype(jnp.bfloat16)
        projected_grad[:, local + at : local + at + PAIR] = totals[1].astype(jnp.bfloat16)
        projected_grad[:, 2 * local + at : 2 * local + at + PAIR] = totals[2].astype(jnp.bfloat16)


class Spread:
    def __init__(self, wires, full, mixed, mixed_rows, rows, local):
        self.wires, self.full, self.mixed, self.mixed_rows = wires, full, mixed, mixed_rows
        self.rows, self.local = rows, local
        self.w, self.sibling, self.across, self.across_sibling = wt_places()

    def stripe(self, m, j):
        return self.full.at[m, pl.ds(j * self.rows, self.rows), :]

    def to_sibling(self, m):
        own = self.stripe(m, self.w)
        return self.wires.remote(("sibling", m), own, own, wt=self.sibling)

    def to_across(self, m):
        own = self.stripe(m, self.w)
        return self.wires.remote(("across", m), own, own, wt=self.across)

    def passed(self, m):
        block = self.stripe(m, self.across)
        return self.wires.remote(("passed", m), block, block, wt=self.sibling)

    def send(self, m):
        self.to_across(m).start()
        self.to_sibling(m).start()

    def hand_on(self, m):
        self.to_across(m).wait_recv()
        self.passed(m).start()

    def settle(self, m):
        self.to_sibling(m).wait_recv()
        self.passed(m).wait_recv()

    def back(self, m):
        heads = pl.ds(self.w * self.local, self.local)
        target = self.mixed_rows.at[pl.ds(m * self.rows, self.rows), heads]
        for index, partner in enumerate((self.across, self.across_sibling, self.sibling)):
            block = self.mixed.at[m, pl.ds(partner * self.rows, self.rows), :]
            yield self.wires.remote(("back", m, index), block, target, wt=partner)

    def send_back(self, m):
        for copy in self.back(m):
            copy.start()
        self.own_back(m).start()

    def own_back(self, m):
        heads = pl.ds(self.w * self.local, self.local)
        return self.wires.local(
            ("back", m),
            self.mixed.at[m, pl.ds(self.w * self.rows, self.rows), :],
            self.mixed_rows.at[pl.ds(m * self.rows, self.rows), heads],
        )

    def finish(self, m):
        for copy in (self.to_sibling(m), self.to_across(m), self.passed(m)):
            copy.wait_send()
        for copy in self.back(m):
            copy.wait()
        self.own_back(m).wait()


def project(full, weight, bias, qkv):
    qkv[...] = (dot(full[...], weight[...]) + bias[...]).astype(jnp.bfloat16)


def first_kernel(size, *refs):
    block, shard_qkv, shard_out, shard_in, shard_down, small, marks, bias = refs[:8]
    ids_row, ids_col = refs[8:10]
    own, weight, whole_out, whole_in, whole_down, smalls, own_marks, count = refs[10:18]
    mixed_rows, full, qkv, mixed, marks_wt, marks_ctx, sems = refs[18:]
    micro, rows, width = block.shape
    local = small.shape[1]
    hidden = shard_in.shape[1]
    half = local // 2
    deep = shard_down.shape[0] // 8
    wires = Wires(sems)
    z = lax.axis_index("ctx")
    spread = Spread(wires, full, mixed, mixed_rows, rows, local)
    w, sibling, across, across_sibling = wt_places()
    partners = (across, across_sibling, sibling)
    level = lax.rem(z, 2)
    neighbor = z + 1 - 2 * level
    moves = w != z
    others = [lax.rem(z + step, 4) for step in (1, 2, 3)]
    greet(
        [{"wt": partner} for partner in partners] + [{"ctx": other} for other in others],
        [(moves, {"ctx": w, "wt": z})],
    )

    def swap(m):
        return wires.remote(("swap", m), block.at[m], spread.stripe(m, z), ctx=w, wt=z)

    def stay(m):
        return wires.local(("stay", m), block.at[m], spread.stripe(m, z))

    def swap_marks():
        return wires.remote("swap marks", marks, own_marks, ctx=w, wt=z)

    def head_copy(part, index):
        column = part * width + partners[index] * local
        return wires.remote(
            ("heads", part, index),
            shard_qkv.at[:, pl.ds(column, local)],
            weight.at[pl.ds(w * local, local), pl.ds(part * local, local)],
            wt=partners[index],
        )

    def head_own(part):
        return wires.local(
            ("heads", part),
            shard_qkv.at[:, pl.ds(part * width + w * local, local)],
            weight.at[pl.ds(w * local, local), pl.ds(part * local, local)],
        )

    def small_copy(index):
        return wires.remote(("small", index), small, smalls.at[w], wt=partners[index])

    def marks_copy(index):
        return wires.remote(("marks", index), marks, marks_wt.at[index], wt=partners[index])

    def count_copy(index):
        return wires.remote(("count", index), count, marks_ctx.at[index], ctx=others[index])

    columns = hidden // width
    chunks = 1 + columns + 4

    def piece(k, level):
        if k == 0:
            return shard_out, whole_out, local, level * half, half, 0
        if k <= columns:
            return shard_in, whole_in, local, level * half, half, (k - 1) * width
        at = (level * 4 + k - 1 - columns) * deep
        return shard_down, whole_down, 4 * deep * 2, at, deep, 0

    def from_shard(k, level):
        shard, _, _, at, size, column = piece(k, level)
        return shard.at[pl.ds(at, size), pl.ds(column, width)]

    def in_whole(k, level, j):
        _, whole, stride, at, size, column = piece(k, level)
        return whole.at[pl.ds(j * stride + at, size), pl.ds(column, width)]

    def y_copy(k):
        return wires.remote(
            ("y", k), from_shard(k, level), in_whole(k, level, w), wt=across
        )

    def z_copy(k):
        block = in_whole(k, level, across)
        return wires.remote(("z", k), block, block, ctx=neighbor)

    def core_copy(k, side):
        block = in_whole(k, level if side == 0 else 1 - level, across)
        return wires.remote(("core", k, side), block, block, wt=sibling)

    def shard_sibling(index):
        shard, whole = ((shard_out, whole_out), (shard_in, whole_in), (shard_down, whole_down))[
            index
        ]
        size = shard.shape[0]
        return wires.remote(
            ("shard", index), shard, whole.at[pl.ds(w * size, size), :], wt=sibling
        )

    def shard_own(index):
        shard, whole = ((shard_out, whole_out), (shard_in, whole_in), (shard_down, whole_down))[
            index
        ]
        size = shard.shape[0]
        return wires.local(("shard", index), shard, whole.at[pl.ds(w * size, size), :])

    @pl.when(moves)
    def _():
        for m in range(micro):
            swap(m).start()
        swap_marks().start()

    @pl.when(w == z)
    def _():
        for m in range(micro):
            stay(m).start()
        own_marks[...] = marks[...]

    for part in range(3):
        for index in range(3):
            head_copy(part, index).start()
        head_own(part).start()
    for index in range(3):
        small_copy(index).start()
        marks_copy(index).start()
    smalls[w] = small[...]

    def arrive(m):
        @pl.when(moves)
        def _():
            swap(m).wait_recv()

        @pl.when(w == z)
        def _():
            stay(m).wait()

    def own_copy(m):
        return wires.local(("own", m), spread.stripe(m, w), own.at[m])

    for m in range(micro):
        arrive(m)
        spread.send(m)
        own_copy(m).start()
    for k in range(chunks):
        y_copy(k).start()
    for index in range(3):
        shard_sibling(index).start()
        shard_own(index).start()
    for index in range(3):
        marks_copy(index).wait_recv()
    count[...] = marks[...] + marks_wt[0] + marks_wt[1] + marks_wt[2]
    for index in range(3):
        count_copy(index).start()
    for part in range(3):
        for index in range(3):
            head_copy(part, index).wait_recv()
        head_own(part).wait()
    for m in range(micro):
        spread.hand_on(m)
        spread.settle(m)
        project(full.at[m], weight, bias, qkv.at[0])
        attend_pack(size, ids_col[m] == ids_row[m], qkv.at[0], mixed.at[m])
        spread.send_back(m)
        y_copy(m).wait_recv()
        z_copy(m).start()
        core_copy(m, 0).start()
    for k in range(micro, chunks):
        y_copy(k).wait_recv()
        z_copy(k).start()
        core_copy(k, 0).start()
        z_copy(k - micro).wait_recv()
        core_copy(k - micro, 1).start()
    for k in range(chunks - micro, chunks):
        z_copy(k).wait_recv()
        core_copy(k, 1).start()
    for index in range(3):
        count_copy(index).wait()
    count[...] = count[...] + marks_ctx[0] + marks_ctx[1] + marks_ctx[2]
    for m in range(micro):
        spread.finish(m)
        own_copy(m).wait()
    for part in range(3):
        for index in range(3):
            head_copy(part, index).wait_send()
    for index in range(3):
        small_copy(index).wait()
        marks_copy(index).wait_send()
        shard_sibling(index).wait()
        shard_own(index).wait()
    for k in range(chunks):
        y_copy(k).wait_send()
        z_copy(k).wait_send()
        for side in range(2):
            core_copy(k, side).wait()

    @pl.when(moves)
    def _():
        for m in range(micro):
            swap(m).wait_send()
        swap_marks().wait()


def first_pass(block, shards, small, marks, bias, ids, size):
    micro, rows, width = block.shape
    local = small.shape[1]
    pack = ids.shape[1]
    anywhere = pl.BlockSpec(memory_space=pl.ANY)
    inside = pl.BlockSpec(memory_space=pltpu.VMEM)
    low = lambda *shape: jax.ShapeDtypeStruct(shape, jnp.bfloat16)
    word = jax.ShapeDtypeStruct(marks.shape, jnp.float32)
    return pl.pallas_call(
        functools.partial(first_kernel, size),
        in_specs=[anywhere] * 5 + [inside] * 5,
        out_specs=[anywhere, inside] + [anywhere] * 3 + [inside] * 4,
        out_shape=[
            low(micro, rows, width),
            low(width, 3 * local),
            low(4 * shards[1].shape[0], shards[1].shape[1]),
            low(4 * shards[2].shape[0], shards[2].shape[1]),
            low(4 * shards[3].shape[0], shards[3].shape[1]),
            low(4, *small.shape),
            word,
            word,
            low(micro * rows, width),
        ],
        scratch_shapes=[
            pltpu.VMEM((micro, pack, width), jnp.bfloat16),
            pltpu.VMEM((1, pack, 3 * local), jnp.bfloat16),
            pltpu.VMEM((micro, pack, local), jnp.bfloat16),
            pltpu.VMEM((3,) + marks.shape, jnp.float32),
            pltpu.VMEM((3,) + marks.shape, jnp.float32),
            pltpu.SemaphoreType.DMA((256,)),
        ],
        compiler_params=pltpu.CompilerParams(
            collective_id=2, has_side_effects=True, vmem_limit_bytes=48 * 2**20
        ),
        name="first_pass",
    )(block, *shards, small, marks, bias, ids[:, None, :], ids[:, :, None])


def second_kernel(size, *refs):
    states, leaving, weight, bias, ids_row, ids_col = refs[:6]
    full, qkv, mixed_rows, mixed, sems = refs[6:]
    micro, rows, width = states.shape
    wires = Wires(sems)
    section = lax.axis_index("section")
    spread = Spread(wires, full, mixed, mixed_rows, rows, weight.shape[1] // 3)
    w, sibling, across, across_sibling = wt_places()
    greet(
        [{"wt": partner} for partner in (across, across_sibling, sibling)]
        + [{"section": 1 - section}],
        [],
    )

    def relay_copy(m):
        return wires.remote(("relay", m), leaving.at[m], spread.stripe(m, w), section=1 - section)

    def stay(m):
        return wires.local(("stay", m), states.at[m], spread.stripe(m, w))

    @pl.when(section == 0)
    def _():
        for m in range(micro):
            relay_copy(m).start()
            stay(m).start()

    def arrive(m):
        @pl.when(section == 0)
        def _():
            stay(m).wait()

        @pl.when(section == 1)
        def _():
            relay_copy(m).wait_recv()

        spread.send(m)

    def work(m):
        spread.settle(m)
        project(full.at[m], weight, bias, qkv.at[m])
        attend_pack(size, ids_col[m] == ids_row[m], qkv.at[m], mixed.at[m])
        spread.send_back(m)

    arrive(0)
    arrive(1)
    spread.hand_on(0)
    work(0)
    arrive(2)
    spread.hand_on(1)
    work(1)
    spread.hand_on(2)
    work(2)
    for m in range(micro):
        spread.finish(m)

    @pl.when(section == 0)
    def _():
        for m in range(micro):
            relay_copy(m).wait_send()


def second_pass(states, leaving, weight, bias, ids, size):
    micro, rows, width = states.shape
    local = weight.shape[1] // 3
    pack = ids.shape[1]
    anywhere = pl.BlockSpec(memory_space=pl.ANY)
    inside = pl.BlockSpec(memory_space=pltpu.VMEM)
    low = lambda *shape: jax.ShapeDtypeStruct(shape, jnp.bfloat16)
    return pl.pallas_call(
        functools.partial(second_kernel, size),
        in_specs=[anywhere] * 2 + [inside] * 4,
        out_specs=[inside] * 3,
        out_shape=[
            low(micro, pack, width),
            low(micro, pack, 3 * local),
            low(micro * rows, width),
        ],
        scratch_shapes=[
            pltpu.VMEM((micro, pack, local), jnp.bfloat16),
            pltpu.SemaphoreType.DMA((80,)),
        ],
        compiler_params=pltpu.CompilerParams(
            collective_id=3, has_side_effects=True, vmem_limit_bytes=48 * 2**20
        ),
        name="second_pass",
    )(states, leaving, weight, bias, ids[:, None, :], ids[:, :, None])


def back_kernel(size, returns, *refs):
    rows_grad, skip, qkv, weight, ids_row, ids_col = refs[:6]
    grad_states, projected, returned = refs[6:9]
    heads_grad, part, from_sibling, far, from_across, sems = refs[9:]
    micro, pack, local = heads_grad.shape
    rows = pack // 4
    wires = Wires(sems)
    section = lax.axis_index("section")
    w, sibling, across, across_sibling = wt_places()
    partners = (across, across_sibling, sibling)
    greet(
        [{"wt": partner} for partner in partners]
        + ([{"section": 1 - section}] if returns else []),
        [],
    )

    def heads_copy(m, index):
        return wires.remote(
            ("heads", m, index),
            rows_grad.at[pl.ds(m * rows, rows), pl.ds(partners[index] * local, local)],
            heads_grad.at[m, pl.ds(w * rows, rows), :],
            wt=partners[index],
        )

    def heads_own(m):
        return wires.local(
            ("heads", m),
            rows_grad.at[pl.ds(m * rows, rows), pl.ds(w * local, local)],
            heads_grad.at[m, pl.ds(w * rows, rows), :],
        )

    def stripe(m, j):
        return part.at[m, pl.ds(j * rows, rows), :]

    def sibling_copy(m, index):
        j = (across_sibling, sibling)[index]
        return wires.remote(
            ("sibling", m, index), stripe(m, j), from_sibling.at[m, index], wt=sibling
        )

    def across_copy(m):
        return wires.remote(("across", m), far.at[m], from_across.at[m], wt=across)

    def back_copy(m):
        place = pl.ds(m * rows, rows)
        return wires.remote(
            ("return", m), grad_states.at[place, :], returned.at[place, :], section=1 - section
        )

    for m in range(micro):
        for index in range(3):
            heads_copy(m, index).start()
        heads_own(m).start()

    def work(m):
        for index in range(3):
            heads_copy(m, index).wait_recv()
        heads_own(m).wait()
        same = ids_col[m] == ids_row[m]
        attend_pack_back(size, same, qkv.at[m], heads_grad.at[m], projected.at[m])
        part[m] = dot(projected[m], weight[...], ((1,), (1,))).astype(jnp.bfloat16)
        for index in range(2):
            sibling_copy(m, index).start()

    def cross(m):
        for index in range(2):
            sibling_copy(m, index).wait_recv()
        total = stripe(m, across)[...].astype(jnp.float32) + from_sibling[m, 0].astype(jnp.float32)
        far[m] = total.astype(jnp.bfloat16)
        across_copy(m).start()

    def finish(m):
        across_copy(m).wait_recv()
        place = pl.ds(m * rows, rows)
        total = skip[place, :] + stripe(m, w)[...].astype(jnp.float32)
        total = total + from_sibling[m, 1].astype(jnp.float32)
        total = total + from_across[m].astype(jnp.float32)
        grad_states[place, :] = total.astype(jnp.bfloat16)
        if returns:

            @pl.when(section == 1)
            def _():
                back_copy(m).start()

    work(0)
    cross(0)
    work(1)
    cross(1)
    finish(0)
    work(2)
    cross(2)
    finish(1)
    finish(2)
    for m in range(micro):
        for index in range(3):
            heads_copy(m, index).wait_send()
        for index in range(2):
            sibling_copy(m, index).wait_send()
        across_copy(m).wait_send()
        if returns:

            @pl.when(section == 1)
            def _():
                back_copy(m).wait_send()

            @pl.when(section == 0)
            def _():
                back_copy(m).wait_recv()

    if not returns:
        returned[...] = jnp.zeros_like(returned)


def back_pass(rows_grad, skip, qkv, weight, ids, size, returns):
    micro, pack, local = qkv.shape
    local = local // 3
    tokens, width = rows_grad.shape
    rows = pack // 4
    inside = pl.BlockSpec(memory_space=pltpu.VMEM)
    low = lambda *shape: jax.ShapeDtypeStruct(shape, jnp.bfloat16)
    back = (tokens, width) if returns else (16, PAIR)
    block = pltpu.VMEM((micro, rows, width), jnp.bfloat16)
    return pl.pallas_call(
        functools.partial(back_kernel, size, returns),
        in_specs=[inside] * 6,
        out_specs=[inside] * 3,
        out_shape=[low(tokens, width), low(micro, pack, 3 * local), low(*back)],
        scratch_shapes=[
            pltpu.VMEM((micro, pack, local), jnp.bfloat16),
            pltpu.VMEM((micro, pack, width), jnp.bfloat16),
            pltpu.VMEM((micro, 2, rows, width), jnp.bfloat16),
            block,
            block,
            pltpu.SemaphoreType.DMA((80,)),
        ],
        compiler_params=pltpu.CompilerParams(
            collective_id=4 if returns else 5,
            has_side_effects=True,
            vmem_limit_bytes=48 * 2**20,
        ),
        name="back_pass",
    )(rows_grad, skip, qkv, weight, ids[:, None, :], ids[:, :, None])


CHUNK = 128


def sum_into(target, parts, rows):
    step = 16

    def one(index, carry):
        at = pl.ds(pl.multiple_of(index * step, step), step)
        total = parts[0][at, :].astype(jnp.float32)
        for part in parts[1:]:
            total = total + part[at, :].astype(jnp.float32)
        target[at, :] = total.astype(jnp.bfloat16)
        return carry

    lax.fori_loop(0, rows // step, one, 0)


def chunk_list(local, width, hidden):
    down = [("down", index) for index in range(hidden // 4 // CHUNK)]
    across = [
        ("in", (half, column))
        for column in range(hidden // width)
        for half in range(local // CHUNK)
    ]
    out = [("out", half) for half in range(local // CHUNK)]
    qkv = [("qkv", (half, part)) for part in range(3) for half in range(local // CHUNK)]
    return down + across + out + [("rest", 0)] + qkv


def reduce_kernel(chunks, local, width, hidden, grads, results, buffers, sems):
    near, far, near_in, far_in, across_in, up_in, side_in, total = buffers
    load, load_far, near_send, near_recv, far_send, far_recv = sems[:6]
    across_send, across_recv, up_send, up_recv, side_recv = sems[6:11]
    down_send, down_recv, keep, piece_send, piece_recv = sems[11:]
    z = lax.axis_index("ctx")
    w = lax.axis_index("wt")
    core = lax.rem(w, 2)
    sibling = w + 1 - 2 * core
    across = lax.rem(w + 2, 4)
    across_sibling = lax.rem(sibling + 2, 4)
    partners = (sibling, across, across_sibling)

    barrier = pltpu.get_barrier_semaphore()
    for partner in partners:
        pl.semaphore_signal(barrier, 1, device_id={"wt": partner}, device_id_type=MESH)

    @pl.when(z > 0)
    def _():
        pl.semaphore_signal(barrier, 1, device_id={"ctx": z - 1}, device_id_type=MESH)

    @pl.when(z < 3)
    def _():
        pl.semaphore_signal(barrier, 1, device_id={"ctx": z + 1}, device_id_type=MESH)

    pl.semaphore_wait(barrier, 3 + (z > 0).astype(jnp.int32) + (z < 3).astype(jnp.int32))

    def rows_of(k):
        return 16 if chunks[k][0] == "rest" else CHUNK

    def is_piece(k):
        return chunks[k][0] == "qkv"

    def source(k, j):
        kind, at = chunks[k]
        if kind == "down":
            return grads["down"].at[pl.ds(j * (hidden // 4) + at * CHUNK, CHUNK), :]
        if kind == "in":
            half, column = at
            return grads["in"].at[
                pl.ds(j * local + half * CHUNK, CHUNK), pl.ds(column * width, width)
            ]
        if kind == "out":
            return grads["out"].at[pl.ds(j * local + at * CHUNK, CHUNK), :]
        if kind == "rest":
            return grads["rest"].at[pl.ds(j * 16, 16), :]
        half, part = at
        return grads["qkv"].at[
            pl.ds(j * local + half * CHUNK, CHUNK), pl.ds(part * local, local)
        ]

    def result(k):
        kind, at = chunks[k]
        if kind == "down":
            return results["down"].at[pl.ds(at * CHUNK, CHUNK), :]
        if kind == "out":
            return results["out"].at[pl.ds(at * CHUNK, CHUNK), :]
        if kind == "rest":
            return results["rest"]
        half, column = at
        return results[kind].at[pl.ds(half * CHUNK, CHUNK), pl.ds(column * width, width)]

    def slot(buffer, k):
        return buffer.at[k, pl.ds(0, rows_of(k)), :]

    def remote(source_ref, target_ref, send, recv, **where):
        return pltpu.make_async_remote_copy(
            source_ref, target_ref, send, recv, device_id=where, device_id_type=MESH
        )

    def near_load(k):
        if is_piece(k):
            place = near.at[k, :, pl.ds(w * local, local)]
            return pltpu.make_async_copy(source(k, w), place, load.at[k])
        return pltpu.make_async_copy(source(k, w), slot(near, k), load.at[k])

    def far_load(k):
        return pltpu.make_async_copy(source(k, across), slot(far, k), load_far.at[k])

    def near_copy(k):
        return remote(
            source(k, sibling), slot(near_in, k), near_send.at[k], near_recv.at[k], wt=sibling
        )

    def far_copy(k):
        return remote(
            source(k, across_sibling), slot(far_in, k), far_send.at[k], far_recv.at[k], wt=sibling
        )

    def piece_copy(k, index):
        place = near.at[k, :, pl.ds(w * local, local)]
        at = piece_send.at[k, index], piece_recv.at[k, index]
        return remote(source(k, partners[index]), place, *at, wt=partners[index])

    def across_copy(k):
        return remote(
            slot(far, k), slot(across_in, k), across_send.at[k], across_recv.at[k], wt=across
        )

    def place_of(k, role):
        return role if k % 2 == 0 else 3 - role

    def up_copy(k, role):
        target = place_of(k, 1 if role == 0 else 2)
        return remote(slot(total, k), slot(up_in, k), up_send.at[k], up_recv.at[k], ctx=target)

    def side_copy(k):
        return remote(
            slot(total, k), slot(side_in, k), up_send.at[k], side_recv.at[k], ctx=place_of(k, 1)
        )

    def down_copy(k, role):
        origin = result(k) if role == 3 else slot(total, k)
        at = down_send.at[k, 1 if role == 2 else 0]
        return remote(origin, result(k), at, down_recv.at[k], ctx=place_of(k, role))

    def keep_copy(k):
        return pltpu.make_async_copy(slot(total, k), result(k), keep.at[k])

    def on(k, role, step):
        pl.when(z == place_of(k, role))(step)

    def summands(k):
        if is_piece(k):
            return [slot(near, k)]
        return [slot(near, k), slot(near_in, k), slot(across_in, k)]

    count = len(chunks)
    for k in range(count):
        if not is_piece(k):
            far_copy(k).start()
            far_load(k).start()
            near_copy(k).start()
            near_load(k).start()

    def begin(k):
        if is_piece(k):
            near_load(k).start()
            for index in range(3):
                piece_copy(k, index).start()
            return
        far_load(k).wait()
        far_copy(k).wait_recv()
        sum_into(slot(far, k), [slot(far, k), slot(far_in, k)], rows_of(k))
        across_copy(k).start()

    def settle(k):
        near_load(k).wait()
        if is_piece(k):
            for index in range(3):
                piece_copy(k, index).wait_recv()
        else:
            near_copy(k).wait_recv()
            across_copy(k).wait_recv()
        for role in (0, 3):

            def step(role=role):
                sum_into(slot(total, k), summands(k), rows_of(k))
                up_copy(k, role).start()

            on(k, role, step)

    def aside(k):
        def step():
            up_copy(k, 3).wait_recv()
            sum_into(slot(total, k), summands(k) + [slot(up_in, k)], rows_of(k))
            side_copy(k).start()

        on(k, 2, step)

    def finish(k):
        def step():
            up_copy(k, 0).wait_recv()
            side_copy(k).wait_recv()
            parts = summands(k) + [slot(up_in, k), slot(side_in, k)]
            sum_into(slot(total, k), parts, rows_of(k))
            down_copy(k, 0).start()
            down_copy(k, 2).start()
            keep_copy(k).start()

        on(k, 1, step)

    def forward(k):
        def step():
            down_copy(k, 2).wait_recv()
            down_copy(k, 3).start()

        on(k, 2, step)

    stages = (begin, settle, aside, finish, forward)
    for tick in range(count + len(stages) - 1):
        for lag, stage in enumerate(stages):
            if 0 <= tick - lag < count:
                stage(tick - lag)
    for k in range(count):
        if is_piece(k):
            for index in range(3):
                piece_copy(k, index).wait_send()
        else:
            far_copy(k).wait_send()
            near_copy(k).wait_send()
            across_copy(k).wait_send()

        def ends(role):
            up_copy(k, role).wait_send()
            down_copy(k, role).wait_recv()

        def middle():
            side_copy(k).wait_send()
            down_copy(k, 3).wait_send()

        def owner():
            down_copy(k, 0).wait_send()
            down_copy(k, 2).wait_send()
            keep_copy(k).wait()

        on(k, 0, lambda: ends(0))
        on(k, 3, lambda: ends(3))
        on(k, 2, middle)
        on(k, 1, owner)


def reduce_grads(grad_qkv, grad_out, grad_in, grad_down, rest):
    width = grad_out.shape[0]
    hidden = grad_down.shape[0]
    local = width // 4
    chunks = chunk_list(local, width, hidden)
    count = len(chunks)

    def body(*refs):
        grads = dict(zip(("qkv", "out", "in", "down", "rest"), refs[:5]))
        results = dict(zip(("qkv", "out", "in", "down", "rest"), refs[5:10]))
        reduce_kernel(chunks, local, width, hidden, grads, results, refs[10:18], refs[18:])

    shapes = [
        (local, 3 * width),
        (local, width),
        (local, hidden),
        (hidden // 4, width),
        (16, width),
    ]
    dma = pltpu.SemaphoreType.DMA
    whole = [pltpu.VMEM((count, CHUNK, width), jnp.bfloat16)]
    direct = [pltpu.VMEM((count - 6, CHUNK, width), jnp.bfloat16)]
    return pl.pallas_call(
        body,
        in_specs=[pl.BlockSpec(memory_space=pl.ANY)] * 5,
        out_specs=[pl.BlockSpec(memory_space=pl.ANY)] * 5,
        out_shape=[jax.ShapeDtypeStruct(shape, jnp.bfloat16) for shape in shapes],
        scratch_shapes=whole
        + direct * 4
        + whole * 3
        + [dma((count,))] * 11
        + [dma((count, 2)), dma((count,)), dma((count,)), dma((count, 3)), dma((count, 3))],
        compiler_params=pltpu.CompilerParams(
            collective_id=1, has_side_effects=True, vmem_limit_bytes=60 * 2**20
        ),
        name="reduce_grads",
    )(grad_qkv, grad_out, grad_in, grad_down, rest)


def relay(boundary, lengths, valid, w_qkv, w_out, w_in, w_down, bias_in, vectors):
    section_at = lax.axis_index("section")
    count_ctx = lax.axis_size("ctx")
    ctx_at = lax.axis_index("ctx")
    wt_at = lax.axis_index("wt")
    micro, rows, width = boundary.shape[1:]
    pack = rows * count_ctx
    size = width // HEADS
    local = width // lax.axis_size("wt")
    tokens = micro * rows
    swap = [
        (c * count_ctx + w, w * count_ctx + c) for c in range(count_ctx) for w in range(count_ctx)
    ]

    own_rows = vectors[0].astype(jnp.float32)
    qkv_bias = jnp.concatenate([own_rows[0], jnp.zeros((local,), jnp.float32), own_rows[1]])[None]
    my_lengths = lax.dynamic_index_in_dim(lengths, ctx_at, 1, keepdims=False)
    ids = jax.vmap(lambda row: dealt_ids(row, pack, count_ctx))(my_lengths)
    small = jnp.concatenate([vectors[0], bias_in[0].reshape(-1, local)], axis=0)
    small = jnp.pad(small, ((0, 16 - small.shape[0]), (0, 0)))
    marks = jnp.pad(valid.astype(jnp.float32), ((0, 8 - micro), (0, 0)))
    shards = (w_qkv[0], w_out[0], w_in[0], w_down[0])
    own, weight_qkv, weight_out, weight_in, weight_down, smalls, marks, counts, mixed = first_pass(
        boundary[0], shards, small, marks, qkv_bias, ids, size
    )
    vector_rows = smalls[:, :8].transpose(1, 0, 2).reshape(8, width).astype(jnp.float32)
    in_bias = smalls[:, 8 : 8 + w_in.shape[2] // width].reshape(-1).astype(jnp.float32)
    marks = marks[:micro].reshape(tokens, 1)
    factor = LOSS_SCALE / jnp.sum(counts)
    flat = own.reshape(tokens, width)

    def forward(states, mixed):
        summed = states.astype(jnp.float32) + (dot(mixed, weight_out) + vector_rows[2])
        normal_one, inverse_one = norm_parts(summed)
        first = normal_one * vector_rows[3] + vector_rows[4]
        first_low = first.astype(jnp.bfloat16)
        hidden, slope = gelu_both(dot(first_low, weight_in) + in_bias)
        hidden = hidden.astype(jnp.bfloat16)
        second = first + (dot(hidden, weight_down) + vector_rows[5])
        normal_two, inverse_two = norm_parts(second)
        output = normal_two * vector_rows[6] + vector_rows[7]
        slope = slope.astype(jnp.bfloat16)
        return (
            output,
            (normal_one, inverse_one, first_low, hidden, slope, normal_two, inverse_two),
        )

    def backward(grad, kept):
        normal_one, inverse_one, first_low, hidden, slope, normal_two, inverse_two = kept
        grad_second = norm_back(grad, vector_rows[6], normal_two, inverse_two)
        down_low = grad_second.astype(jnp.bfloat16)
        pre_low = (dot(down_low, weight_down, ((1,), (1,))) * slope).astype(jnp.bfloat16)
        grad_first = grad_second + dot(pre_low, weight_in, ((1,), (1,)))
        grad_summed = norm_back(grad_first, vector_rows[3], normal_one, inverse_one)
        branch_low = grad_summed.astype(jnp.bfloat16)
        mixed_grad = dot(branch_low, weight_out, ((1,), (1,))).astype(jnp.bfloat16)
        return (mixed_grad, grad_summed, (down_low, pre_low, grad_first, branch_low))

    output, _ = forward(flat, mixed)
    leaving = output.astype(jnp.bfloat16).reshape(micro, rows, width)
    full, qkv, mixed = second_pass(own, leaving, weight_qkv, qkv_bias, ids, size)
    states = lax.dynamic_slice_in_dim(full, wt_at * rows, rows, 1).reshape(tokens, width)
    output, kept = forward(states, mixed)
    cotangent = factor * marks * (output - flat.astype(jnp.float32))
    mixed_grad, skip, _ = backward(cotangent, kept)
    _, _, returned = back_pass(mixed_grad, skip, qkv, weight_qkv, ids, size, True)
    cotangent = jnp.where(section_at == 1, cotangent, returned.astype(jnp.float32))
    mixed_grad, skip, grads = backward(cotangent, kept)
    grad_states, projected, _ = back_pass(mixed_grad, skip, qkv, weight_qkv, ids, size, False)
    results = jnp.where(section_at == 0, grad_states, output.astype(jnp.bfloat16))
    results = results.reshape(micro, rows, width)
    results = lax.ppermute(results, ("ctx", "wt"), swap)[None]

    normal_one, _, first_low, hidden, _, normal_two, _ = kept
    down_low, pre_low, grad_first, branch_low = grads
    along = ((0,), (0,))
    total = lambda values: jnp.sum(values.astype(jnp.float32), axis=0)
    projected = projected.reshape(-1, 3 * local)
    bias_qkv = total(projected)
    rows_local = jnp.stack([bias_qkv[:local], bias_qkv[2 * local :]])
    rows_whole = jnp.stack(
        [
            total(branch_low),
            total(grad_first * normal_one),
            total(grad_first),
            total(down_low),
            total(cotangent * normal_two),
            total(cotangent),
        ]
    )
    mine = (jnp.arange(4) == wt_at).astype(jnp.float32)[None, :, None]
    rest = jnp.concatenate([rows_local[:, None, :] * mine, rows_whole.reshape(6, 4, local)])
    rest = jnp.concatenate([rest, jnp.zeros((8, 4, local), jnp.float32)]).transpose(1, 0, 2)
    in_rows = total(pre_low).reshape(4, -1, local)
    in_rows = jnp.pad(in_rows, ((0, 0), (0, 16 - in_rows.shape[1]), (0, 2 * local)))
    rest = jnp.concatenate([rest, in_rows], axis=2).reshape(64, width)
    low = lambda part: part.astype(jnp.bfloat16)
    sums = reduce_grads(
        low(dot(full.reshape(-1, width), projected, along)),
        low(dot(mixed, branch_low, along)),
        low(dot(first_low, pre_low, along)),
        low(dot(hidden, down_low, along)),
        low(rest),
    )
    sums = [part.astype(jnp.float32)[None] for part in sums]
    rest = sums[4]
    in_rows = w_in.shape[2] // width
    bias_back = rest[:, :in_rows, local : 2 * local].reshape(1, -1)
    return (results, *sums[:4], bias_back, rest[:, :8, :local])


def solution(mesh):
    in_specs = (
        P("section", None, ("wt", "ctx"), None),
        P(),
        P(None, ("wt", "ctx")),
        P("section", "wt", None),
        P("section", "wt", None),
        P("section", "wt", None),
        P("section", "wt", None),
        P("section", "wt"),
        P("section", None, "wt"),
    )
    out_specs = (
        P("section", None, ("wt", "ctx"), None),
        P("section", "wt", None),
        P("section", "wt", None),
        P("section", "wt", None),
        P("section", "wt", None),
        P("section", "wt"),
        P("section", None, "wt"),
    )
    square = mesh.shape["ctx"] == mesh.shape["wt"]
    return jax.shard_map(relay if square else shards, mesh=mesh, in_specs=in_specs, out_specs=out_specs, check_vma=False)
```

```python
import functools

import jax
import jax.numpy as jnp
from jax import lax
from jax.experimental import pallas as pl
from jax.experimental.pallas import tpu as pltpu
from jax.sharding import PartitionSpec as P

HEADS = 16
LOSS_SCALE = 1024


def shifted(block, axis, distance):
    devices = range(lax.axis_size(axis))
    route = [(i - distance, i) for i in devices if i - distance in devices]
    return lax.ppermute(block, axis, route)


def as_sent(x):

    def short(part):
        return part.astype(jnp.bfloat16) if part.dtype == jnp.float32 else part

    return jax.tree.map(short, x)


def layer_norm(values, gain, shift):
    center = jnp.mean(values, axis=-1, keepdims=True)
    offset = values - center
    spread = jnp.mean(offset * offset, axis=-1, keepdims=True)
    return offset * lax.rsqrt(spread + 1e-05) * gain + shift


def exact_gelu(values):
    return jax.nn.gelu(values, approximate=False)


def dealt_ids(length_row, pack_size, ctx_count):
    ends = jnp.cumsum(length_row)
    places = jnp.arange(pack_size, dtype=jnp.int32)
    natural = jnp.sum((places[:, None] >= ends[None, :]).astype(jnp.int32), axis=1)
    return natural.reshape(pack_size // ctx_count, ctx_count).T.reshape(pack_size)


def split_blocks(full_kv, ids_keys):
    block = min(512, full_kv.shape[0])
    count_blocks = full_kv.shape[0] // block
    return (
        full_kv.reshape(count_blocks, block, full_kv.shape[1]),
        ids_keys.reshape(count_blocks, block),
    )


def split_kv(block_kv, heads):
    half = block_kv.shape[1] // 2
    keys = block_kv[:, :half].reshape(block_kv.shape[0], heads, -1)
    values = block_kv[:, half:].reshape(block_kv.shape[0], heads, -1)
    return (keys, values)


def block_scores(queries, keys, ids_query, ids_keys, scale):
    scores = jnp.einsum("qhd,khd->hqk", queries, keys, preferred_element_type=jnp.float32) * scale
    same = ids_query[:, None] == ids_keys[None, :]
    return jnp.where(same[None], scores, -1000000000.0)


def attend_forward(queries, full_kv, ids_query, ids_keys, heads, scale):
    blocks, id_blocks = split_blocks(full_kv, ids_keys)
    query_rows = queries.shape[0]

    def total_step(carry, items):
        run_max, run_sum = carry
        keys, values = split_kv(items[0], heads)
        scores = block_scores(queries, keys, ids_query, items[1], scale)
        new_max = jnp.maximum(run_max, jnp.max(scores, axis=-1))
        run_sum = run_sum * jnp.exp(run_max - new_max) + jnp.sum(
            jnp.exp(scores - new_max[..., None]), axis=-1
        )
        return ((new_max, run_sum), None)

    start = (
        jnp.full((heads, query_rows), -1e30, jnp.float32),
        jnp.zeros((heads, query_rows), jnp.float32),
    )
    (run_max, run_sum), _ = lax.scan(total_step, start, (blocks, id_blocks))
    log_total = run_max + jnp.log(run_sum)

    def mix_step(carry, items):
        keys, values = split_kv(items[0], heads)
        scores = block_scores(queries, keys, ids_query, items[1], scale)
        probs = jnp.exp(scores - log_total[..., None]).astype(jnp.bfloat16)
        return (
            carry + jnp.einsum("hqk,khd->qhd", probs, values, preferred_element_type=jnp.float32),
            None,
        )

    mixed, _ = lax.scan(mix_step, jnp.zeros(queries.shape, jnp.float32), (blocks, id_blocks))
    return (mixed.reshape(query_rows, -1), log_total)


def attend_backward(queries, full_kv, ids_query, ids_keys, mixed_grad, log_total, heads, scale):
    blocks, id_blocks = split_blocks(full_kv, ids_keys)
    grad_heads = mixed_grad.reshape(queries.shape)

    def inner_step(carry, items):
        keys, values = split_kv(items[0], heads)
        scores = block_scores(queries, keys, ids_query, items[1], scale)
        probs = jnp.exp(scores - log_total[..., None])
        prob_grad = jnp.einsum(
            "qhd,khd->hqk", grad_heads, values, preferred_element_type=jnp.float32
        )
        return (carry + jnp.sum(probs * prob_grad, axis=-1), None)

    inner, _ = lax.scan(inner_step, jnp.zeros(log_total.shape, jnp.float32), (blocks, id_blocks))

    def grad_step(carry, items):
        keys, values = split_kv(items[0], heads)
        scores = block_scores(queries, keys, ids_query, items[1], scale)
        probs = jnp.exp(scores - log_total[..., None])
        prob_grad = jnp.einsum(
            "qhd,khd->hqk", grad_heads, values, preferred_element_type=jnp.float32
        )
        score_grad = (probs * (prob_grad - inner[..., None])).astype(jnp.bfloat16)
        carry = (
            carry
            + jnp.einsum("hqk,khd->qhd", score_grad, keys, preferred_element_type=jnp.float32)
            * scale
        )
        key_grad = (
            jnp.einsum("hqk,qhd->khd", score_grad, queries, preferred_element_type=jnp.float32)
            * scale
        )
        value_grad = jnp.einsum(
            "hqk,qhd->khd",
            probs.astype(jnp.bfloat16),
            grad_heads,
            preferred_element_type=jnp.float32,
        )
        block = keys.shape[0]
        return (
            carry,
            jnp.concatenate([key_grad.reshape(block, -1), value_grad.reshape(block, -1)], axis=1),
        )

    query_grad, partial_kv = lax.scan(
        grad_step, jnp.zeros(queries.shape, jnp.float32), (blocks, id_blocks)
    )
    query_grad = query_grad.reshape(queries.shape[0], -1)
    return (query_grad, partial_kv.reshape(-1, partial_kv.shape[-1]), inner)


def shards(boundary, lengths, valid, w_qkv, w_out, w_in, w_down, bias_in, vectors):
    section_at = lax.axis_index("section")
    ctx_count = lax.axis_size("ctx")
    ctx_at = lax.axis_index("ctx")
    wt_at = lax.axis_index("wt")
    micro_count = boundary.shape[1]
    row_count = boundary.shape[2]
    width = boundary.shape[3]
    pack_size = row_count * ctx_count
    head_size = width // HEADS
    scale = head_size ** (-0.5)
    gathered = (
        lax.all_gather(w_qkv[0], "wt", axis=0, tiled=True),
        lax.all_gather(w_out[0], "wt", axis=0, tiled=True),
        lax.all_gather(w_in[0], "wt", axis=0, tiled=True),
        lax.all_gather(w_down[0], "wt", axis=0, tiled=True),
        lax.all_gather(bias_in[0], "wt", axis=0, tiled=True),
        lax.all_gather(vectors[0], "wt", axis=1, tiled=True),
    )
    weight_qkv, weight_out, weight_in, weight_down, in_bias, vector_rows = gathered
    in_bias = in_bias.astype(jnp.float32)
    vector_rows = vector_rows.astype(jnp.float32)
    qkv_bias = jnp.concatenate([vector_rows[0], jnp.zeros((width,), jnp.float32), vector_rows[1]])
    my_lengths = lax.dynamic_index_in_dim(lengths, wt_at, 1, keepdims=False)

    def ids_of(length_row):
        return dealt_ids(length_row, pack_size, ctx_count)

    pack_ids = jax.vmap(ids_of)(my_lengths)
    query_ids = lax.dynamic_slice_in_dim(pack_ids, ctx_at * row_count, row_count, 1)
    count = lax.psum(jnp.sum(valid.astype(jnp.float32)), ("ctx", "wt"))
    factor = LOSS_SCALE / count
    empty_rows = jnp.zeros((row_count, width), jnp.bfloat16)
    arriving = empty_rows
    kept_list = []
    cotangents = []
    final_states = []
    for tick_at in range(micro_count + 1):
        own_input = boundary[0, tick_at] if tick_at < micro_count else empty_rows
        inputs = jnp.where(section_at == 0, own_input, arriving)
        micro_here = jnp.clip(tick_at - section_at, 0, micro_count - 1)
        ids_keys = lax.dynamic_index_in_dim(pack_ids, micro_here, 0, keepdims=False)
        ids_query = lax.dynamic_index_in_dim(query_ids, micro_here, 0, keepdims=False)
        residual = inputs.astype(jnp.float32)
        projected = jnp.dot(inputs, weight_qkv, preferred_element_type=jnp.float32) + qkv_bias
        layer_queries = (
            projected[:, :width].astype(jnp.bfloat16).reshape(row_count, HEADS, head_size)
        )
        layer_local_kv = projected[:, width:].astype(jnp.bfloat16)
        layer_full_kv = lax.all_gather(layer_local_kv, "ctx", axis=0, tiled=True)
        mixed, layer_log_total = attend_forward(
            layer_queries, layer_full_kv, ids_query, ids_keys, HEADS, scale
        )
        layer_mixed_low = mixed.astype(jnp.bfloat16)
        branch = (
            jnp.dot(layer_mixed_low, weight_out, preferred_element_type=jnp.float32)
            + vector_rows[2]
        )
        layer_summed = residual + branch
        first = layer_norm(layer_summed, vector_rows[3], vector_rows[4])
        layer_first_low = first.astype(jnp.bfloat16)
        layer_hidden_pre = (
            jnp.dot(layer_first_low, weight_in, preferred_element_type=jnp.float32) + in_bias
        )
        layer_hidden_low = exact_gelu(layer_hidden_pre).astype(jnp.bfloat16)
        layer_second = first + (
            jnp.dot(layer_hidden_low, weight_down, preferred_element_type=jnp.float32)
            + vector_rows[5]
        )
        output = layer_norm(layer_second, vector_rows[6], vector_rows[7])
        layer_kept = (
            inputs,
            layer_queries,
            layer_local_kv,
            layer_full_kv,
            layer_mixed_low,
            layer_log_total,
            layer_summed,
            layer_first_low,
            layer_hidden_pre,
            layer_hidden_low,
            layer_second,
            ids_keys,
            ids_query,
        )
        output, kept = (output, layer_kept)
        kept_list.append(kept)
        if tick_at > 0:
            teacher = boundary[0, tick_at - 1].astype(jnp.float32)
            covered = valid[tick_at - 1].astype(jnp.float32)[:, None]
            cotangents.append(factor * covered * (output - teacher))
            final_states.append(output.astype(jnp.bfloat16))
        else:
            cotangents.append(jnp.zeros((row_count, width), jnp.float32))
        if tick_at < micro_count:
            arriving = shifted(output.astype(jnp.bfloat16), "section", 1)
    returning = empty_rows
    totals = None
    input_grads = [None] * micro_count
    for back_at in range(micro_count + 1):
        forward_at = micro_count - back_at
        grad_output = jnp.where(
            section_at == 1, cotangents[forward_at], returning.astype(jnp.float32)
        )
        (
            layer_inputs,
            queries,
            local_kv,
            full_kv,
            mixed_low,
            log_total,
            summed,
            first_low,
            hidden_pre,
            hidden_low,
            second,
            layer_ids_keys,
            layer_ids_query,
        ) = kept_list[forward_at]
        full_kv = lax.all_gather(local_kv, "ctx", axis=0, tiled=True)
        _, pull_last = jax.vjp(layer_norm, second, vector_rows[6], vector_rows[7])
        grad_second, grad_gain_two, grad_shift_two = pull_last(grad_output)
        down_low = grad_second.astype(jnp.bfloat16)
        layer_grad_down = jnp.einsum(
            "rf,rd->fd", hidden_low, down_low, preferred_element_type=jnp.float32
        )
        grad_bias_two = jnp.sum(down_low.astype(jnp.float32), axis=0)
        _, pull_gelu = jax.vjp(exact_gelu, hidden_pre)
        (grad_pre,) = pull_gelu(
            jnp.einsum("rd,fd->rf", down_low, weight_down, preferred_element_type=jnp.float32)
        )
        pre_low = grad_pre.astype(jnp.bfloat16)
        layer_grad_in = jnp.einsum(
            "rd,rf->df", first_low, pre_low, preferred_element_type=jnp.float32
        )
        layer_grad_bias_in = jnp.sum(pre_low.astype(jnp.float32), axis=0)
        grad_first = grad_second + jnp.einsum(
            "rf,df->rd", pre_low, weight_in, preferred_element_type=jnp.float32
        )
        _, pull_first = jax.vjp(layer_norm, summed, vector_rows[3], vector_rows[4])
        grad_summed, grad_gain_one, grad_shift_one = pull_first(grad_first)
        branch_low = grad_summed.astype(jnp.bfloat16)
        layer_grad_out = jnp.einsum(
            "rd,re->de", mixed_low, branch_low, preferred_element_type=jnp.float32
        )
        grad_bias_out = jnp.sum(branch_low.astype(jnp.float32), axis=0)
        mixed_grad = jnp.einsum(
            "re,de->rd", branch_low, weight_out, preferred_element_type=jnp.float32
        ).astype(jnp.bfloat16)
        query_grad, partial_kv, inner = attend_backward(
            queries, full_kv, layer_ids_query, layer_ids_keys, mixed_grad, log_total, HEADS, scale
        )
        kv_grad = lax.psum_scatter(
            partial_kv.astype(jnp.bfloat16), "ctx", scatter_dimension=0, tiled=True
        )
        query_low = query_grad.astype(jnp.bfloat16)
        projected_grad = jnp.concatenate([query_low, kv_grad], axis=1)
        layer_grad_qkv = jnp.einsum(
            "rd,re->de", layer_inputs, projected_grad, preferred_element_type=jnp.float32
        )
        vector_grad = jnp.stack(
            [
                jnp.sum(query_low.astype(jnp.float32), axis=0),
                jnp.sum(kv_grad[:, width:].astype(jnp.float32), axis=0),
                grad_bias_out,
                grad_gain_one,
                grad_shift_one,
                grad_bias_two,
                grad_gain_two,
                grad_shift_two,
            ]
        )
        grad_inputs = grad_summed + jnp.einsum(
            "re,de->rd", projected_grad, weight_qkv, preferred_element_type=jnp.float32
        )
        grad_inputs, grads = (
            grad_inputs,
            (
                layer_grad_qkv,
                layer_grad_out,
                layer_grad_in,
                layer_grad_down,
                layer_grad_bias_in,
                vector_grad,
            ),
        )
        totals = grads if totals is None else jax.tree.map(jnp.add, totals, grads)
        if forward_at < micro_count:
            input_grads[forward_at] = grad_inputs
        if back_at < micro_count:
            returning = shifted(grad_inputs.astype(jnp.bfloat16), "section", -1)
    results = jnp.stack(
        [
            jnp.where(section_at == 0, input_grads[index].astype(jnp.bfloat16), final_states[index])
            for index in range(micro_count)
        ]
    )[None]
    shares = (
        lax.psum_scatter(
            totals[0].astype(jnp.bfloat16), "wt", scatter_dimension=0, tiled=True
        ).astype(jnp.float32),
        lax.psum_scatter(
            totals[1].astype(jnp.bfloat16), "wt", scatter_dimension=0, tiled=True
        ).astype(jnp.float32),
        lax.psum_scatter(
            totals[2].astype(jnp.bfloat16), "wt", scatter_dimension=0, tiled=True
        ).astype(jnp.float32),
        lax.psum_scatter(
            totals[3].astype(jnp.bfloat16), "wt", scatter_dimension=0, tiled=True
        ).astype(jnp.float32),
        lax.psum_scatter(
            totals[4].astype(jnp.bfloat16), "wt", scatter_dimension=0, tiled=True
        ).astype(jnp.float32),
        lax.psum_scatter(
            totals[5].astype(jnp.bfloat16), "wt", scatter_dimension=1, tiled=True
        ).astype(jnp.float32),
    )
    shares = jax.tree.map(lambda part: part.astype(jnp.float32), lax.psum(as_sent(shares), "ctx"))
    grad_qkv, grad_out, grad_in, grad_down, grad_bias_in, grad_vectors = shares
    return (
        results,
        grad_qkv[None],
        grad_out[None],
        grad_in[None],
        grad_down[None],
        grad_bias_in[None],
        grad_vectors[None],
    )


PAIR = 128
FAR = -1000000000.0
MESH = pl.DeviceIdType.MESH


def dot(left, right, dims=((1,), (0,))):
    return lax.dot_general(left, right, (dims, ((), ())), preferred_element_type=jnp.float32)


def head_lanes(size):
    lane = lax.broadcasted_iota(jnp.int32, (1, PAIR), 1)
    return [lane // size == index for index in range(PAIR // size)]


def only(mask, values):
    return jnp.where(mask, values, jnp.zeros_like(values))


def normal_tail(values):
    size = jnp.abs(values)
    bell = jnp.exp(-0.5 * values * values)
    t = 1.0 / (1.0 + 0.3275911 * (2.0**-0.5) * size)
    poly = t * (
        0.254829592
        + t * (-0.284496736 + t * (1.421413741 + t * (-1.453152027 + t * 1.061405429)))
    )
    tail = 0.5 * poly * bell
    return (jnp.where(values >= 0, 1.0 - tail, tail), bell)


def gelu_both(values):
    below, bell = normal_tail(values)
    return (values * below, below + values * bell * 0.3989422804014327)


def norm_parts(values):
    center = jnp.mean(values, axis=-1, keepdims=True)
    offset = values - center
    spread = jnp.mean(offset * offset, axis=-1, keepdims=True)
    inverse = lax.rsqrt(spread + 1e-05)
    return (offset * inverse, inverse)


def norm_back(grad, gain, normal, inverse):
    inner = grad * gain
    mean = jnp.mean(inner, axis=-1, keepdims=True)
    along = jnp.mean(inner * normal, axis=-1, keepdims=True)
    return inverse * (inner - mean - normal * along)


class Wires:
    def __init__(self, sems):
        self.sems = sems
        self.places = {}

    def at(self, *key):
        return self.sems.at[self.places.setdefault(key, len(self.places))]

    def remote(self, key, source, target, **where):
        return pltpu.make_async_remote_copy(
            source,
            target,
            self.at(key, "send"),
            self.at(key, "recv"),
            device_id=where,
            device_id_type=MESH,
        )

    def local(self, key, source, target):
        return pltpu.make_async_copy(source, target, self.at(key, "local"))


def wt_places():
    w = lax.axis_index("wt")
    core = lax.rem(w, 2)
    sibling = w + 1 - 2 * core
    across = lax.rem(w + 2, 4)
    return w, sibling, across, lax.rem(sibling + 2, 4)


def turned(place):
    return 2 * lax.rem(place, 2) + place // 2


def greet(partners, extra):
    barrier = pltpu.get_barrier_semaphore()
    for partner in partners:
        pl.semaphore_signal(barrier, 1, device_id=partner, device_id_type=MESH)
    waits = len(partners)
    for here, partner in extra:

        @pl.when(here)
        def _():
            pl.semaphore_signal(barrier, 1, device_id=partner, device_id_type=MESH)

        waits = waits + here.astype(jnp.int32)
    pl.semaphore_wait(barrier, waits)


def attend_pack(size, same, qkv, mixed):
    local = mixed.shape[1]
    masks = head_lanes(size)
    for pair in range(local // PAIR):
        at = pair * PAIR
        q = qkv[:, at : at + PAIR] * jnp.bfloat16(size**-0.5)
        k = qkv[:, local + at : local + at + PAIR]
        v = qkv[:, 2 * local + at : 2 * local + at + PAIR]
        total = None
        for mask in masks:
            scores = jnp.where(same, dot(only(mask, k), q, ((1,), (1,))), FAR)
            probs = jnp.exp(scores - jnp.max(scores, axis=0, keepdims=True))
            scale = 1.0 / jnp.sum(probs, axis=0, keepdims=True)
            low = (probs * scale).astype(jnp.bfloat16)
            term = dot(only(mask, v), low, ((0,), (0,)))
            total = term if total is None else total + term
        mixed[:, at : at + PAIR] = total.T.astype(jnp.bfloat16)


def attend_pack_back(size, same, qkv, grad_heads, projected_grad):
    local = grad_heads.shape[1]
    masks = head_lanes(size)
    for pair in range(local // PAIR):
        at = pair * PAIR
        q = qkv[:, at : at + PAIR] * jnp.bfloat16(size**-0.5)
        k = qkv[:, local + at : local + at + PAIR]
        v = qkv[:, 2 * local + at : 2 * local + at + PAIR]
        grad = grad_heads[:, at : at + PAIR]
        totals = [None] * 3
        for mask in masks:
            own_k = only(mask, k)
            scores = jnp.where(same, dot(own_k, q, ((1,), (1,))), FAR)
            probs = jnp.exp(scores - jnp.max(scores, axis=0, keepdims=True))
            probs = probs * (1.0 / jnp.sum(probs, axis=0, keepdims=True))
            prob_grad = dot(only(mask, v), grad, ((1,), (1,)))
            inner = jnp.sum(probs * prob_grad, axis=0, keepdims=True)
            score_grad = (probs * (prob_grad - inner)).astype(jnp.bfloat16)
            terms = (
                dot(own_k, score_grad, ((0,), (0,))),
                dot(score_grad, only(mask, q)),
                dot(probs.astype(jnp.bfloat16), only(mask, grad)),
            )
            totals = [t if o is None else o + t for o, t in zip(totals, terms)]
        query_grad = totals[0].T * size**-0.5
        projected_grad[:, at : at + PAIR] = query_grad.astype(jnp.bfloat16)
        projected_grad[:, local + at : local + at + PAIR] = totals[1].astype(jnp.bfloat16)
        projected_grad[:, 2 * local + at : 2 * local + at + PAIR] = totals[2].astype(jnp.bfloat16)


class Spread:
    def __init__(self, wires, full, mixed, mixed_rows, rows, local):
        self.wires, self.full, self.mixed, self.mixed_rows = wires, full, mixed, mixed_rows
        self.rows, self.local = rows, local
        self.w, self.sibling, self.across, self.across_sibling = wt_places()

    def stripe(self, m, j):
        return self.full.at[m, pl.ds(j * self.rows, self.rows), :]

    def to_sibling(self, m):
        own = self.stripe(m, self.w)
        return self.wires.remote(("sibling", m), own, own, wt=self.sibling)

    def to_across(self, m):
        own = self.stripe(m, self.w)
        return self.wires.remote(("across", m), own, own, wt=self.across)

    def passed(self, m):
        block = self.stripe(m, self.across)
        return self.wires.remote(("passed", m), block, block, wt=self.sibling)

    def send(self, m):
        self.to_across(m).start()
        self.to_sibling(m).start()

    def hand_on(self, m):
        self.to_across(m).wait_recv()
        self.passed(m).start()

    def settle(self, m):
        self.to_sibling(m).wait_recv()
        self.passed(m).wait_recv()

    def back(self, m):
        heads = pl.ds(self.w * self.local, self.local)
        target = self.mixed_rows.at[pl.ds(m * self.rows, self.rows), heads]
        for index, partner in enumerate((self.across, self.across_sibling, self.sibling)):
            block = self.mixed.at[m, pl.ds(partner * self.rows, self.rows), :]
            yield self.wires.remote(("back", m, index), block, target, wt=partner)

    def send_back(self, m):
        for copy in self.back(m):
            copy.start()
        self.own_back(m).start()

    def own_back(self, m):
        heads = pl.ds(self.w * self.local, self.local)
        return self.wires.local(
            ("back", m),
            self.mixed.at[m, pl.ds(self.w * self.rows, self.rows), :],
            self.mixed_rows.at[pl.ds(m * self.rows, self.rows), heads],
        )

    def finish(self, m):
        for copy in (self.to_sibling(m), self.to_across(m), self.passed(m)):
            copy.wait_send()
        for copy in self.back(m):
            copy.wait()
        self.own_back(m).wait()


def project(full, weight, bias, qkv):
    qkv[...] = (dot(full[...], weight[...]) + bias[...]).astype(jnp.bfloat16)


def first_kernel(size, *refs):
    block, shard_qkv, shard_out, shard_in, shard_down, small, marks, bias = refs[:8]
    ids_row, ids_col = refs[8:10]
    own, weight, whole_out, whole_in, whole_down, smalls, own_marks, count = refs[10:18]
    mixed_rows, full, qkv, mixed, marks_wt, marks_ctx = refs[18:24]
    held_out, held_in, held_down, sems = refs[24:]
    micro, rows, width = block.shape
    local = small.shape[1]
    hidden = shard_in.shape[1]
    half = local // 2
    deep = shard_down.shape[0] // 8
    wires = Wires(sems)
    z = lax.axis_index("ctx")
    spread = Spread(wires, full, mixed, mixed_rows, rows, local)
    w, sibling, across, across_sibling = wt_places()
    partners = (across, across_sibling, sibling)
    level = lax.rem(z, 2)
    neighbor = z + 1 - 2 * level
    moves = w != turned(z)
    others = [lax.rem(z + step, 4) for step in (1, 2, 3)]
    greet(
        [{"wt": partner} for partner in partners] + [{"ctx": other} for other in others],
        [(moves, {"ctx": turned(w), "wt": turned(z)})],
    )

    def swap(m):
        return wires.remote(
            ("swap", m), block.at[m], spread.stripe(m, turned(z)), ctx=turned(w), wt=turned(z)
        )

    def stay(m):
        return wires.local(("stay", m), block.at[m], spread.stripe(m, w))

    def swap_marks():
        return wires.remote("swap marks", marks, own_marks, ctx=turned(w), wt=turned(z))

    def head_copy(part, index):
        column = part * width + partners[index] * local
        return wires.remote(
            ("heads", part, index),
            shard_qkv.at[:, pl.ds(column, local)],
            weight.at[pl.ds(w * local, local), pl.ds(part * local, local)],
            wt=partners[index],
        )

    def head_own(part):
        return wires.local(
            ("heads", part),
            shard_qkv.at[:, pl.ds(part * width + w * local, local)],
            weight.at[pl.ds(w * local, local), pl.ds(part * local, local)],
        )

    def small_copy(index):
        return wires.remote(("small", index), small, smalls.at[w], wt=partners[index])

    def marks_copy(index):
        return wires.remote(("marks", index), marks, marks_wt.at[index], wt=partners[index])

    def count_copy(index):
        return wires.remote(("count", index), count, marks_ctx.at[index], ctx=others[index])

    columns = hidden // width
    chunks = 1 + columns + 4

    def piece(k, level):
        if k == 0:
            return shard_out, whole_out, local, level * half, half, 0
        if k <= columns:
            return shard_in, whole_in, local, level * half, half, (k - 1) * width
        at = (level * 4 + k - 1 - columns) * deep
        return shard_down, whole_down, 4 * deep * 2, at, deep, 0

    def from_shard(k, level):
        shard, _, _, at, size, column = piece(k, level)
        return shard.at[pl.ds(at, size), pl.ds(column, width)]

    def in_whole(k, level, j):
        _, whole, stride, at, size, column = piece(k, level)
        return whole.at[pl.ds(j * stride + at, size), pl.ds(column, width)]

    def y_copy(k):
        return wires.remote(
            ("y", k), from_shard(k, level), in_whole(k, level, w), wt=across
        )

    def z_copy(k):
        block = in_whole(k, level, across)
        return wires.remote(("z", k), block, block, ctx=neighbor)

    def core_copy(k, side):
        block = in_whole(k, level if side == 0 else 1 - level, across)
        return wires.remote(("core", k, side), block, block, wt=sibling)

    def shard_sibling(index):
        shard, whole = ((shard_out, whole_out), (shard_in, whole_in), (shard_down, whole_down))[
            index
        ]
        size = shard.shape[0]
        return wires.remote(
            ("shard", index), shard, whole.at[pl.ds(w * size, size), :], wt=sibling
        )

    def shard_own(index):
        shard, whole = ((shard_out, whole_out), (shard_in, whole_in), (shard_down, whole_down))[
            index
        ]
        size = shard.shape[0]
        held = (held_out, held_in, held_down)[index]
        place = whole.at[pl.ds(w * size, size), :]
        return (
            wires.local(("shard in", index), shard, held),
            wires.local(("shard own", index), held, place),
        )

    @pl.when(moves)
    def _():
        for m in range(micro):
            swap(m).start()
        swap_marks().start()

    @pl.when(w == turned(z))
    def _():
        for m in range(micro):
            stay(m).start()
        own_marks[...] = marks[...]

    for part in range(3):
        for index in range(3):
            head_copy(part, index).start()
        head_own(part).start()
    for index in range(3):
        small_copy(index).start()
        marks_copy(index).start()
    smalls[w] = small[...]

    def arrive(m):
        @pl.when(moves)
        def _():
            swap(m).wait_recv()

        @pl.when(w == turned(z))
        def _():
            stay(m).wait()

    def own_copy(m):
        return wires.local(("own", m), spread.stripe(m, w), own.at[m])

    for m in range(micro):
        arrive(m)
        spread.send(m)
        own_copy(m).start()
    for k in range(chunks):
        y_copy(k).start()
    for index in range(3):
        shard_sibling(index).start()
        shard_own(index)[0].start()
    for index in range(3):
        shard_own(index)[0].wait()
        shard_own(index)[1].start()
    for index in range(3):
        marks_copy(index).wait_recv()
    count[...] = marks[...] + marks_wt[0] + marks_wt[1] + marks_wt[2]
    for index in range(3):
        count_copy(index).start()
    for part in range(3):
        for index in range(3):
            head_copy(part, index).wait_recv()
        head_own(part).wait()
    for m in range(micro):
        spread.hand_on(m)
        spread.settle(m)
        project(full.at[m], weight, bias, qkv.at[0])
        attend_pack(size, ids_col[m] == ids_row[m], qkv.at[0], mixed.at[m])
        spread.send_back(m)
        y_copy(m).wait_recv()
        z_copy(m).start()
        core_copy(m, 0).start()
    for k in range(micro, chunks):
        y_copy(k).wait_recv()
        z_copy(k).start()
        core_copy(k, 0).start()
        z_copy(k - micro).wait_recv()
        core_copy(k - micro, 1).start()
    for k in range(chunks - micro, chunks):
        z_copy(k).wait_recv()
        core_copy(k, 1).start()
    for index in range(3):
        count_copy(index).wait()
    count[...] = count[...] + marks_ctx[0] + marks_ctx[1] + marks_ctx[2]
    for m in range(micro):
        spread.finish(m)
        own_copy(m).wait()
    for part in range(3):
        for index in range(3):
            head_copy(part, index).wait_send()
    for index in range(3):
        small_copy(index).wait()
        marks_copy(index).wait_send()
        shard_sibling(index).wait()
        shard_own(index)[1].wait()
    for k in range(chunks):
        y_copy(k).wait_send()
        z_copy(k).wait_send()
        for side in range(2):
            core_copy(k, side).wait()

    @pl.when(moves)
    def _():
        for m in range(micro):
            swap(m).wait_send()
        swap_marks().wait()


def first_pass(block, shards, small, marks, bias, ids, size):
    micro, rows, width = block.shape
    local = small.shape[1]
    pack = ids.shape[1]
    anywhere = pl.BlockSpec(memory_space=pl.ANY)
    inside = pl.BlockSpec(memory_space=pltpu.VMEM)
    low = lambda *shape: jax.ShapeDtypeStruct(shape, jnp.bfloat16)
    word = jax.ShapeDtypeStruct(marks.shape, jnp.float32)
    return pl.pallas_call(
        functools.partial(first_kernel, size),
        in_specs=[anywhere] * 5 + [inside] * 5,
        out_specs=[anywhere, inside] + [anywhere] * 3 + [inside] * 4,
        out_shape=[
            low(micro, rows, width),
            low(width, 3 * local),
            low(4 * shards[1].shape[0], shards[1].shape[1]),
            low(4 * shards[2].shape[0], shards[2].shape[1]),
            low(4 * shards[3].shape[0], shards[3].shape[1]),
            low(4, *small.shape),
            word,
            word,
            low(micro * rows, width),
        ],
        scratch_shapes=[
            pltpu.VMEM((micro, pack, width), jnp.bfloat16),
            pltpu.VMEM((1, pack, 3 * local), jnp.bfloat16),
            pltpu.VMEM((micro, pack, local), jnp.bfloat16),
            pltpu.VMEM((3,) + marks.shape, jnp.float32),
            pltpu.VMEM((3,) + marks.shape, jnp.float32),
        ]
        + [pltpu.VMEM(shard.shape, jnp.bfloat16) for shard in shards[1:]]
        + [
            pltpu.SemaphoreType.DMA((256,)),
        ],
        compiler_params=pltpu.CompilerParams(
            collective_id=2, has_side_effects=True, vmem_limit_bytes=48 * 2**20
        ),
        name="first_pass",
    )(block, *shards, small, marks, bias, ids[:, None, :], ids[:, :, None])


def second_kernel(size, *refs):
    states, leaving, weight, bias, ids_row, ids_col = refs[:6]
    full, qkv, mixed_rows, mixed, sems = refs[6:]
    micro, rows, width = states.shape
    wires = Wires(sems)
    section = lax.axis_index("section")
    spread = Spread(wires, full, mixed, mixed_rows, rows, weight.shape[1] // 3)
    w, sibling, across, across_sibling = wt_places()
    greet(
        [{"wt": partner} for partner in (across, across_sibling, sibling)]
        + [{"section": 1 - section}],
        [],
    )

    def relay_copy(m):
        return wires.remote(("relay", m), leaving.at[m], spread.stripe(m, w), section=1 - section)

    def stay(m):
        return wires.local(("stay", m), states.at[m], spread.stripe(m, w))

    @pl.when(section == 0)
    def _():
        for m in range(micro):
            relay_copy(m).start()
            stay(m).start()

    def arrive(m):
        @pl.when(section == 0)
        def _():
            stay(m).wait()

        @pl.when(section == 1)
        def _():
            relay_copy(m).wait_recv()

        spread.send(m)

    def work(m):
        spread.settle(m)
        project(full.at[m], weight, bias, qkv.at[m])
        attend_pack(size, ids_col[m] == ids_row[m], qkv.at[m], mixed.at[m])
        spread.send_back(m)

    arrive(0)
    arrive(1)
    spread.hand_on(0)
    work(0)
    arrive(2)
    spread.hand_on(1)
    work(1)
    spread.hand_on(2)
    work(2)
    for m in range(micro):
        spread.finish(m)

    @pl.when(section == 0)
    def _():
        for m in range(micro):
            relay_copy(m).wait_send()


def second_pass(states, leaving, weight, bias, ids, size):
    micro, rows, width = states.shape
    local = weight.shape[1] // 3
    pack = ids.shape[1]
    anywhere = pl.BlockSpec(memory_space=pl.ANY)
    inside = pl.BlockSpec(memory_space=pltpu.VMEM)
    low = lambda *shape: jax.ShapeDtypeStruct(shape, jnp.bfloat16)
    return pl.pallas_call(
        functools.partial(second_kernel, size),
        in_specs=[anywhere] * 2 + [inside] * 4,
        out_specs=[inside] * 3,
        out_shape=[
            low(micro, pack, width),
            low(micro, pack, 3 * local),
            low(micro * rows, width),
        ],
        scratch_shapes=[
            pltpu.VMEM((micro, pack, local), jnp.bfloat16),
            pltpu.SemaphoreType.DMA((80,)),
        ],
        compiler_params=pltpu.CompilerParams(
            collective_id=3, has_side_effects=True, vmem_limit_bytes=48 * 2**20
        ),
        name="second_pass",
    )(states, leaving, weight, bias, ids[:, None, :], ids[:, :, None])


class Back:
    def __init__(self, wires, size, refs):
        self.wires, self.size = wires, size
        self.rows_grad, self.skip, self.qkv, self.weight, self.ids = refs[:5]
        self.projected, self.grad_states = refs[5:7]
        self.heads_grad, self.part, self.from_sibling, self.far, self.from_across = refs[7:]
        self.micro, self.pack, self.local = self.heads_grad.shape
        self.rows = self.pack // 4
        self.w, self.sibling, self.across, self.across_sibling = wt_places()
        self.partners = (self.across, self.across_sibling, self.sibling)

    def place(self, m):
        return pl.ds(m * self.rows, self.rows)

    def heads_copy(self, m, index):
        column = pl.ds(self.partners[index] * self.local, self.local)
        return self.wires.remote(
            ("heads", m, index),
            self.rows_grad.at[self.place(m), column],
            self.heads_grad.at[m, pl.ds(self.w * self.rows, self.rows), :],
            wt=self.partners[index],
        )

    def heads_own(self, m):
        return self.wires.local(
            ("heads", m),
            self.rows_grad.at[self.place(m), pl.ds(self.w * self.local, self.local)],
            self.heads_grad.at[m, pl.ds(self.w * self.rows, self.rows), :],
        )

    def stripe(self, m, j):
        return self.part.at[m, pl.ds(j * self.rows, self.rows), :]

    def sibling_copy(self, m, index):
        j = (self.across_sibling, self.sibling)[index]
        return self.wires.remote(
            ("to sibling", m, index),
            self.stripe(m, j),
            self.from_sibling.at[m, index],
            wt=self.sibling,
        )

    def across_copy(self, m):
        return self.wires.remote(
            ("to across", m), self.far.at[m], self.from_across.at[m], wt=self.across
        )

    def begin(self, m):
        for index in range(3):
            self.heads_copy(m, index).start()
        self.heads_own(m).start()

    def arrive(self, m):
        for index in range(3):
            self.heads_copy(m, index).wait_recv()
        self.heads_own(m).wait()

    def work(self, m, following=None):
        self.arrive(m)
        if following is not None:
            self.begin(following)
        ids_row, ids_col = self.ids
        whole = pl.ds(m * self.pack, self.pack)
        projected = self.projected.at[whole, :]
        same = ids_col[m] == ids_row[m]
        attend_pack_back(self.size, same, self.qkv.at[m], self.heads_grad.at[m], projected)
        product = dot(projected[...], self.weight[...], ((1,), (1,)))
        self.part[m] = product.astype(jnp.bfloat16)
        for index in range(2):
            self.sibling_copy(m, index).start()

    def cross(self, m):
        for index in range(2):
            self.sibling_copy(m, index).wait_recv()
        total = self.stripe(m, self.across)[...].astype(jnp.float32)
        total = total + self.from_sibling[m, 0].astype(jnp.float32)
        self.far[m] = total.astype(jnp.bfloat16)
        self.across_copy(m).start()

    def finish(self, m):
        self.across_copy(m).wait_recv()
        total = self.skip[self.place(m), :] + self.stripe(m, self.w)[...].astype(jnp.float32)
        total = total + self.from_sibling[m, 1].astype(jnp.float32)
        total = total + self.from_across[m].astype(jnp.float32)
        self.grad_states[self.place(m), :] = total.astype(jnp.bfloat16)

    def end(self, m):
        for index in range(3):
            self.heads_copy(m, index).wait_send()
        for index in range(2):
            self.sibling_copy(m, index).wait_send()
        self.across_copy(m).wait_send()


def back_scratch(micro, pack, local, width):
    block = pltpu.VMEM((micro, pack // 4, width), jnp.bfloat16)
    return [
        pltpu.VMEM((micro, pack, local), jnp.bfloat16),
        pltpu.VMEM((micro, pack, width), jnp.bfloat16),
        pltpu.VMEM((micro, 2, pack // 4, width), jnp.bfloat16),
        block,
        block,
    ]


def swap_back(wires, rows, source, target, m, moves):
    z, w = lax.axis_index("ctx"), lax.axis_index("wt")
    block = source.at[pl.ds(m * rows, rows), :]
    if moves:
        return wires.remote(("home", m), block, target.at[m], ctx=turned(w), wt=turned(z))
    return wires.local(("home", m), block, target.at[m])


def back_kernel(size, *refs):
    returned, grad_states, projected = refs[6:9]
    wires = Wires(refs[-1])
    section = lax.axis_index("section")
    back = Back(wires, size, refs[:4] + (refs[4:6], projected, grad_states) + refs[9:-1])
    greet([{"wt": partner} for partner in back.partners] + [{"section": 1 - section}], [])
    back.begin(0)

    def back_copy(m):
        place = back.place(m)
        return wires.remote(
            ("return", m), grad_states.at[place, :], returned.at[place, :], section=1 - section
        )

    def finish(m):
        back.finish(m)

        @pl.when(section == 1)
        def _():
            back_copy(m).start()

    back.work(0, 1)
    back.cross(0)
    back.work(1, 2)
    back.cross(1)
    finish(0)
    back.work(2)
    back.cross(2)
    finish(1)
    finish(2)
    for m in range(back.micro):
        back.end(m)

        @pl.when(section == 1)
        def _():
            back_copy(m).wait_send()

        @pl.when(section == 0)
        def _():
            back_copy(m).wait_recv()


def back_pass(rows_grad, skip, qkv, weight, ids, size):
    micro, pack, local = qkv.shape
    local = local // 3
    tokens, width = rows_grad.shape
    inside = pl.BlockSpec(memory_space=pltpu.VMEM)
    low = lambda *shape: jax.ShapeDtypeStruct(shape, jnp.bfloat16)
    return pl.pallas_call(
        functools.partial(back_kernel, size),
        in_specs=[inside] * 6,
        out_specs=inside,
        out_shape=low(tokens, width),
        scratch_shapes=[
            pltpu.VMEM((tokens, width), jnp.bfloat16),
            pltpu.VMEM((micro * pack, 3 * local), jnp.bfloat16),
        ]
        + back_scratch(micro, pack, local, width)
        + [pltpu.SemaphoreType.DMA((96,))],
        compiler_params=pltpu.CompilerParams(
            collective_id=4, has_side_effects=True, vmem_limit_bytes=48 * 2**20
        ),
        name="back_pass",
    )(rows_grad, skip, qkv, weight, ids[:, None, :], ids[:, :, None])


CHUNK = 128
RING = 6
LAGS = (0, 3, 5, 7, 9)


def sum_into(target, parts, rows):
    step = 16

    def one(index, carry):
        at = pl.ds(pl.multiple_of(index * step, step), step)
        total = parts[0][at, :].astype(jnp.float32)
        for part in parts[1:]:
            total = total + part[at, :].astype(jnp.float32)
        target[at, :] = total.astype(jnp.bfloat16)
        return carry

    lax.fori_loop(0, rows // step, one, 0)


def chunk_list(local, width, hidden):
    down = [("down", row, CHUNK, 0) for row in range(0, hidden // 4, CHUNK)]
    across = [
        ("in", row, CHUNK, column)
        for column in range(hidden // width)
        for row in range(0, local, CHUNK)
    ]
    out = [("out", row, CHUNK, 0) for row in range(0, local, CHUNK)]
    qkv = [("qkv", row, CHUNK, part) for part in range(2) for row in range(0, local, CHUNK)]
    qkv += [("qkv", row, CHUNK // 2, 2) for row in range(0, local - CHUNK // 2, CHUNK // 2)]
    qkv += [("qkv", row, CHUNK // 4, 2) for row in range(local - CHUNK // 2, local, CHUNK // 4)]
    return down + across + out + [("rest", 0, 16, 0)] + qkv


def starts_of(chunks):
    rows = [chunk[2] for chunk in chunks]
    starts = [sum(rows[:k]) for k in range(len(rows) + 1)]
    return starts, [sum(rows[k % 2 : k : 2]) for k in range(len(rows) + 2)]


def last_kernel(chunks, size, *refs):
    rows_grad, skip, qkv_all, weight, ids_row, ids_col, full_all, rest = refs[:8]
    hidden, pre, first, mixed, down, branch, final = refs[8:15]
    home = refs[15]
    results = dict(zip(("qkv", "out", "in", "down", "rest"), refs[16:21]))
    grad_states, projected, full, product = refs[21:25]
    downs, ins, outs, down_both, pre_both, branch_both, rest_in = refs[25:32]
    near, far, across_in, up_in, side_in = refs[32:37]
    wires = Wires(refs[-1])
    z, section = lax.axis_index("ctx"), lax.axis_index("section")
    given = (rows_grad, skip, qkv_all, weight, (ids_row, ids_col))
    back = Back(wires, size, given + (projected, grad_states) + refs[37:-1])
    w, sibling, across, across_sibling = wt_places()
    partners = (sibling, across, across_sibling)
    tokens, width = down.shape
    count = len(chunks)
    local = back.local
    deep = hidden.shape[1] // 4
    starts, sides_at = starts_of(chunks)
    moves = w != turned(z)
    greet(
        [{"wt": partner} for partner in partners],
        [
            (moves, {"ctx": turned(w), "wt": turned(z)}),
            (z > 0, {"ctx": z - 1}),
            (z < 3, {"ctx": z + 1}),
        ],
    )

    def both(key, source, target, at, columns, theirs):
        mine = (pl.ds(0, tokens), at)
        other = (pl.ds(tokens, tokens), at)
        return (
            wires.local(key, source.at[:, columns], target.at[mine]),
            wires.remote(key, source.at[:, theirs], target.at[other], wt=sibling),
        )

    def sides(key, source, block, target):
        for side, (j, k) in enumerate(((w, sibling), (across, across_sibling))):
            yield from both(
                key + (side,),
                source,
                target,
                pl.ds(side * CHUNK, CHUNK),
                pl.ds(block(j), CHUNK),
                pl.ds(block(k), CHUNK),
            )

    def down_block(index):
        return sides(
            ("down", index), hidden, lambda j: j * deep + index * CHUNK, downs.at[index]
        )

    def in_block(half):
        return sides(("in", half), first, lambda j: j * local + half * CHUNK, ins.at[half])

    def out_block(half):
        return sides(("out", half), mixed, lambda j: j * local + half * CHUNK, outs.at[half])

    def whole(key, source, target, column):
        at = pl.ds(column * width, width)
        return both((key, column), source, target, at, at, at)

    def rest_copies():
        for side, k in enumerate((sibling, across_sibling)):
            yield wires.remote(
                ("rest", side), rest.at[pl.ds(k * 16, 16), :], rest_in.at[side], wt=sibling
            )

    halves = local // CHUNK
    columns = hidden.shape[1] // width
    loads = [lambda: whole("down", down, down_both, 0)]
    loads += [lambda index=index: down_block(index) for index in range(deep // CHUNK)]
    loads += [lambda half=half: in_block(half) for half in range(halves)]
    loads += [lambda at=at: whole("pre", pre, pre_both, at) for at in range(columns)]
    loads += [lambda: whole("branch", branch, branch_both, 0)]
    loads += [lambda half=half: out_block(half) for half in range(halves)]

    def full_copy():
        return wires.local("full", full_all, full)

    def needs(k):
        kind, row, _, column = chunks[k]
        index = row // CHUNK
        if kind == "down":
            return ([whole("down", down, down_both, 0)] if index == 0 else []) + [
                down_block(index)
            ]
        if kind == "in":
            return [whole("pre", pre, pre_both, column)] * (index == 0) + [
                in_block(index)
            ] * (column == 0)
        return [whole("branch", branch, branch_both, 0)] * (index == 0) + [out_block(index)]

    def operands(k):
        kind, row, _, column = chunks[k]
        index = row // CHUNK
        if kind == "down":
            return downs[index], down_both[...]
        if kind == "in":
            return ins[index], pre_both[:, column * width : (column + 1) * width]
        return outs[index], branch_both[...]

    def is_piece(k):
        return chunks[k][0] == "qkv"

    def rows_of(k):
        return chunks[k][2]

    def slot(buffer, k):
        return buffer.at[pl.ds(starts[k], rows_of(k)), :]

    def beside_slot(k):
        return side_in.at[pl.ds(sides_at[k], rows_of(k)), :]

    def result(k):
        kind, row, rows, column = chunks[k]
        if kind == "rest":
            return results["rest"]
        return results[kind].at[pl.ds(row, rows), pl.ds(column * width, width)]

    def piece(k, j):
        _, row, rows, part = chunks[k]
        return product.at[part, pl.ds(j * local + row, rows), :]

    def piece_place(k):
        return near.at[pl.ds(starts[k], rows_of(k)), pl.ds(w * local, local)]

    def piece_copy(k, index):
        place = piece_place(k)
        return wires.remote(
            ("piece", k, index), piece(k, partners[index]), place, wt=partners[index]
        )

    def piece_own(k):
        return wires.local(("piece", k), piece(k, w), piece_place(k))

    def across_copy(k):
        source = far.at[k % RING, pl.ds(0, rows_of(k)), :]
        return wires.remote(("chunk", k), source, slot(across_in, k), wt=across)

    def place_of(k, role):
        return role if k % 2 == 0 else 3 - role

    def up_copy(k, role):
        target = place_of(k, 1 if role == 0 else 2)
        return wires.remote(("up", k), slot(near, k), slot(up_in, k), ctx=target)

    def side_copy(k):
        return wires.remote(("side", k), slot(near, k), beside_slot(k), ctx=place_of(k, 1))

    def down_copy(k, role):
        origin = result(k) if role == 3 else slot(near, k)
        return pltpu.make_async_remote_copy(
            origin,
            result(k),
            wires.at("down send", k, 1 if role == 2 else 0),
            wires.at("down recv", k),
            device_id={"ctx": place_of(k, role)},
            device_id_type=MESH,
        )

    def keep_copy(k):
        return wires.local(("keep", k), slot(near, k), result(k))

    def on(k, role, step):
        pl.when(z == place_of(k, role))(step)

    def summands(k):
        if is_piece(k):
            return [slot(near, k)]
        return [slot(near, k), slot(across_in, k)]

    def begin(k):
        kind, row, _, column = chunks[k]
        if is_piece(k):
            if row == 0:
                at = pl.ds(column * local, local)
                grad = dot(full[...], projected[:, at], ((0,), (0,)))
                product[column] = grad.astype(jnp.bfloat16)
            for partner in range(3):
                piece_copy(k, partner).start()
            piece_own(k).start()
            return
        if k >= RING:
            across_copy(k - RING).wait_send()
        if kind == "rest":
            for copy in rest_copies():
                copy.wait_recv()
            ones = jnp.ones((16, projected.shape[0]), jnp.bfloat16)
            sums = dot(ones, projected[...])
            row = lax.broadcasted_iota(jnp.int32, (16, local), 0)
            own = jnp.where(row == 0, sums[:, :local], 0.0)
            own = own + jnp.where(row == 1, sums[:, 2 * local :], 0.0)
            own = jnp.concatenate([own, jnp.zeros((16, width - local), jnp.float32)], axis=1)
            own = own + rest[pl.ds(w * 16, 16), :] + rest_in[0]
            other = rest[pl.ds(across * 16, 16), :] + rest_in[1]
            slot(near, k)[...] = own.astype(jnp.bfloat16)
            far[k % RING, pl.ds(0, 16), :] = other.astype(jnp.bfloat16)
        else:
            for copies in needs(k):
                for index, copy in enumerate(copies):
                    (copy.wait if index % 2 == 0 else copy.wait_recv)()
            left, right = operands(k)
            grad = dot(left, right, ((0,), (0,))).astype(jnp.bfloat16)
            slot(near, k)[...] = grad[:CHUNK]
            far[k % RING] = grad[CHUNK:]
        across_copy(k).start()

    def settle(k):
        if is_piece(k):
            for index in range(3):
                piece_copy(k, index).wait_recv()
            piece_own(k).wait()
        else:
            across_copy(k).wait_recv()
        for role in (0, 3):

            def step(role=role):
                if not is_piece(k):
                    sum_into(slot(near, k), summands(k), rows_of(k))
                up_copy(k, role).start()

            on(k, role, step)

    def aside(k):
        def step():
            up_copy(k, 3).wait_recv()
            sum_into(slot(near, k), summands(k) + [slot(up_in, k)], rows_of(k))
            side_copy(k).start()

        on(k, 2, step)

    def finish(k):
        def step():
            up_copy(k, 0).wait_recv()
            side_copy(k).wait_recv()
            parts = summands(k) + [slot(up_in, k), beside_slot(k)]
            sum_into(slot(near, k), parts, rows_of(k))
            down_copy(k, 0).start()
            down_copy(k, 2).start()
            keep_copy(k).start()

        on(k, 1, step)

    def forward(k):
        def step():
            down_copy(k, 2).wait_recv()
            down_copy(k, 3).start()

        on(k, 2, step)

    def go_home(m, source, here, do):
        @pl.when(moves & here)
        def _():
            do(swap_back(wires, back.rows, source, home, m, True))

        @pl.when((w == turned(z)) & here)
        def _():
            do(swap_back(wires, back.rows, source, home, m, False))

    def done(m):
        back.finish(m)
        go_home(m, grad_states, section == 0, lambda copy: copy.start())

    def final_home(m):
        go_home(m, final, section == 1, lambda copy: copy.start())

    tail = count - 9
    beside = {
        1: [lambda: back.work(0)],
        3: [lambda: back.work(1)],
        5: [lambda: back.work(2)],
        8: [lambda: final_home(0)],
        12: [lambda: final_home(1)],
        16: [lambda: final_home(2)],
        tail: [lambda: back.cross(0)],
        tail + 1: [lambda: back.cross(1)],
        tail + 3: [lambda: back.cross(2), lambda: done(0)],
        tail + 5: [lambda: done(1)],
        tail + 7: [lambda: done(2)],
    }

    for m in range(back.micro):
        back.begin(m)
    for copy in rest_copies():
        copy.start()
    for load in loads:
        for copy in load():
            copy.start()
    full_copy().start()
    stages = (begin, settle, aside, finish, forward)
    for tick in range(count + LAGS[-1]):
        if tick < count and chunks[tick][0] == "qkv" and chunks[tick - 1][0] != "qkv":
            full_copy().wait()
        for lag, stage in zip(LAGS, stages):
            if 0 <= tick - lag < count:
                stage(tick - lag)
        for step in beside.get(tick, []):
            step()
    for m in range(back.micro):
        back.end(m)
        go_home(m, grad_states, z >= 0, lambda copy: copy.wait())
    for copy in rest_copies():
        copy.wait_send()
    for load in loads:
        for index, copy in enumerate(load()):
            if index % 2 == 1:
                copy.wait_send()
    direct = [k for k in range(count) if not is_piece(k)]
    for k in direct[-RING:]:
        across_copy(k).wait_send()
    for k in range(count):
        if is_piece(k):
            for index in range(3):
                piece_copy(k, index).wait_send()

        def ends(role):
            up_copy(k, role).wait_send()
            down_copy(k, role).wait_recv()

        def middle():
            side_copy(k).wait_send()
            down_copy(k, 3).wait_send()

        def owner():
            down_copy(k, 0).wait_send()
            down_copy(k, 2).wait_send()
            keep_copy(k).wait()

        on(k, 0, lambda: ends(0))
        on(k, 3, lambda: ends(3))
        on(k, 2, middle)
        on(k, 1, owner)


def last_pass(rows_grad, skip, qkv, weight, ids, full, rest, operands, final, size):
    micro, pack, local = qkv.shape
    local = local // 3
    tokens, width = rows_grad.shape
    hidden = operands[0].shape[1]
    chunks = chunk_list(local, width, hidden)
    count = len(chunks)
    direct = sum(chunk[0] != "qkv" for chunk in chunks)
    starts, sides_at = starts_of(chunks)
    inside = pl.BlockSpec(memory_space=pltpu.VMEM)
    anywhere = pl.BlockSpec(memory_space=pl.ANY)
    low = lambda *shape: jax.ShapeDtypeStruct(shape, jnp.bfloat16)
    room = lambda *shape: pltpu.VMEM(shape, jnp.bfloat16)
    halves = local // CHUNK
    return pl.pallas_call(
        functools.partial(last_kernel, chunks, size),
        in_specs=[inside] * 6 + [anywhere, inside] + [anywhere] * 7,
        out_specs=[anywhere] * 6,
        out_shape=[
            low(micro, pack // 4, width),
            low(local, 3 * width),
            low(local, width),
            low(local, hidden),
            low(hidden // 4, width),
            low(16, width),
        ],
        scratch_shapes=[
            room(tokens, width),
            room(micro * pack, 3 * local),
            room(micro * pack, width),
            room(3, width, local),
            room(hidden // 4 // CHUNK, 2 * tokens, 2 * CHUNK),
            room(halves, 2 * tokens, 2 * CHUNK),
            room(halves, 2 * tokens, 2 * CHUNK),
            room(2 * tokens, width),
            room(2 * tokens, hidden),
            room(2 * tokens, width),
            pltpu.VMEM((2, 16, width), jnp.float32),
            room(starts[count], width),
            room(RING, CHUNK, width),
            room(starts[direct], width),
            room(starts[count], width),
            room(max(sides_at[count:]), width),
        ]
        + back_scratch(micro, pack, local, width)
        + [pltpu.SemaphoreType.DMA((720,))],
        compiler_params=pltpu.CompilerParams(
            collective_id=1, has_side_effects=True, vmem_limit_bytes=62 * 2**20
        ),
        name="last_pass",
    )(
        rows_grad,
        skip,
        qkv,
        weight,
        ids[:, None, :],
        ids[:, :, None],
        full.reshape(micro * pack, width),
        rest,
        *operands,
        final,
    )


def relay(boundary, lengths, valid, w_qkv, w_out, w_in, w_down, bias_in, vectors):
    section_at = lax.axis_index("section")
    count_ctx = lax.axis_size("ctx")
    ctx_at = lax.axis_index("ctx")
    wt_at = lax.axis_index("wt")
    micro, rows, width = boundary.shape[1:]
    pack = rows * count_ctx
    size = width // HEADS
    local = width // lax.axis_size("wt")
    tokens = micro * rows
    own_rows = vectors[0].astype(jnp.float32)
    qkv_bias = jnp.concatenate([own_rows[0], jnp.zeros((local,), jnp.float32), own_rows[1]])[None]
    my_lengths = lax.dynamic_index_in_dim(lengths, turned(ctx_at), 1, keepdims=False)
    ids = jax.vmap(lambda row: dealt_ids(row, pack, count_ctx))(my_lengths)
    ids = ids.reshape(micro, 2, 2, rows).swapaxes(1, 2).reshape(micro, pack)
    small = jnp.concatenate([vectors[0], bias_in[0].reshape(-1, local)], axis=0)
    small = jnp.pad(small, ((0, 16 - small.shape[0]), (0, 0)))
    marks = jnp.pad(valid.astype(jnp.float32), ((0, 8 - micro), (0, 0)))
    shards = (w_qkv[0], w_out[0], w_in[0], w_down[0])
    own, weight_qkv, weight_out, weight_in, weight_down, smalls, marks, counts, mixed = first_pass(
        boundary[0], shards, small, marks, qkv_bias, ids, size
    )
    vector_rows = smalls[:, :8].transpose(1, 0, 2).reshape(8, width).astype(jnp.float32)
    in_bias = smalls[:, 8 : 8 + w_in.shape[2] // width].reshape(-1).astype(jnp.float32)
    marks = marks[:micro].reshape(tokens, 1)
    factor = LOSS_SCALE / jnp.sum(counts)
    flat = own.reshape(tokens, width)

    def forward(states, mixed):
        summed = states.astype(jnp.float32) + (dot(mixed, weight_out) + vector_rows[2])
        normal_one, inverse_one = norm_parts(summed)
        first = normal_one * vector_rows[3] + vector_rows[4]
        first_low = first.astype(jnp.bfloat16)
        hidden, slope = gelu_both(dot(first_low, weight_in) + in_bias)
        hidden = lax.optimization_barrier(hidden.astype(jnp.bfloat16))
        second = first + (dot(hidden, weight_down) + vector_rows[5])
        normal_two, inverse_two = norm_parts(second)
        output = normal_two * vector_rows[6] + vector_rows[7]
        slope = slope.astype(jnp.bfloat16)
        return (
            output,
            (normal_one, inverse_one, first_low, hidden, slope, normal_two, inverse_two),
        )

    def backward(grad, kept):
        normal_one, inverse_one, first_low, hidden, slope, normal_two, inverse_two = kept
        grad_second = norm_back(grad, vector_rows[6], normal_two, inverse_two)
        down_low = grad_second.astype(jnp.bfloat16)
        pre_low = (dot(down_low, weight_down, ((1,), (1,))) * slope).astype(jnp.bfloat16)
        pre_low = lax.optimization_barrier(pre_low)
        grad_first = grad_second + dot(pre_low, weight_in, ((1,), (1,)))
        grad_summed = norm_back(grad_first, vector_rows[3], normal_one, inverse_one)
        branch_low = grad_summed.astype(jnp.bfloat16)
        mixed_grad = dot(branch_low, weight_out, ((1,), (1,))).astype(jnp.bfloat16)
        return (mixed_grad, grad_summed, (down_low, pre_low, grad_first, branch_low))

    output, _ = forward(flat, mixed)
    leaving = output.astype(jnp.bfloat16).reshape(micro, rows, width)
    full, qkv, mixed = second_pass(own, leaving, weight_qkv, qkv_bias, ids, size)
    states = lax.dynamic_slice_in_dim(full, wt_at * rows, rows, 1).reshape(tokens, width)
    output, kept = forward(states, mixed)
    cotangent = factor * marks * (output - flat.astype(jnp.float32))
    mixed_grad, skip, _ = backward(cotangent, kept)
    returned = back_pass(mixed_grad, skip, qkv, weight_qkv, ids, size)
    cotangent = jnp.where(section_at == 1, cotangent, returned.astype(jnp.float32))
    mixed_grad, skip, grads = backward(cotangent, kept)
    normal_one, _, first_low, hidden, _, normal_two, _ = kept
    down_low, pre_low, grad_first, branch_low = grads
    along = ((0,), (0,))
    total = lambda values: jnp.sum(values.astype(jnp.float32), axis=0)
    rows_whole = jnp.stack(
        [
            total(branch_low),
            total(grad_first * normal_one),
            total(grad_first),
            total(down_low),
            total(cotangent * normal_two),
            total(cotangent),
        ]
    )
    rest = rows_whole.reshape(6, 4, local)
    rest = jnp.pad(rest, ((2, 8), (0, 0), (0, 0))).transpose(1, 0, 2)
    in_rows = total(pre_low).reshape(4, -1, local)
    in_rows = jnp.pad(in_rows, ((0, 0), (0, 16 - in_rows.shape[1]), (0, 2 * local)))
    rest = jnp.concatenate([rest, in_rows], axis=2).reshape(64, width)
    operands = (hidden, pre_low, first_low, mixed, down_low, branch_low)
    final = output.astype(jnp.bfloat16)
    home, *sums = last_pass(
        mixed_grad, skip, qkv, weight_qkv, ids, full, rest, operands, final, size
    )
    sums = [part.astype(jnp.float32)[None] for part in sums]
    rest = sums[4]
    in_rows = w_in.shape[2] // width
    bias_back = rest[:, :in_rows, local : 2 * local].reshape(1, -1)
    return (home[None], *sums[:4], bias_back, rest[:, :8, :local])


def solution(mesh):
    in_specs = (
        P("section", None, ("wt", "ctx"), None),
        P(),
        P(None, ("wt", "ctx")),
        P("section", "wt", None),
        P("section", "wt", None),
        P("section", "wt", None),
        P("section", "wt", None),
        P("section", "wt"),
        P("section", None, "wt"),
    )
    out_specs = (
        P("section", None, ("wt", "ctx"), None),
        P("section", "wt", None),
        P("section", "wt", None),
        P("section", "wt", None),
        P("section", "wt", None),
        P("section", "wt"),
        P("section", None, "wt"),
    )
    square = mesh.shape["ctx"] == mesh.shape["wt"] == 4
    return jax.shard_map(relay if square else shards, mesh=mesh, in_specs=in_specs, out_specs=out_specs, check_vma=False)
```

```python
import functools

import jax
import jax.numpy as jnp
from jax import lax
from jax.experimental import pallas as pl
from jax.experimental.pallas import tpu as pltpu
from jax.sharding import PartitionSpec as P

HEADS = 16
LOSS_SCALE = 1024


def shifted(block, axis, distance):
    devices = range(lax.axis_size(axis))
    route = [(i - distance, i) for i in devices if i - distance in devices]
    return lax.ppermute(block, axis, route)


def as_sent(x):

    def short(part):
        return part.astype(jnp.bfloat16) if part.dtype == jnp.float32 else part

    return jax.tree.map(short, x)


def layer_norm(values, gain, shift):
    center = jnp.mean(values, axis=-1, keepdims=True)
    offset = values - center
    spread = jnp.mean(offset * offset, axis=-1, keepdims=True)
    return offset * lax.rsqrt(spread + 1e-05) * gain + shift


def exact_gelu(values):
    return jax.nn.gelu(values, approximate=False)


def dealt_ids(length_row, pack_size, ctx_count):
    ends = jnp.cumsum(length_row)
    places = jnp.arange(pack_size, dtype=jnp.int32)
    natural = jnp.sum((places[:, None] >= ends[None, :]).astype(jnp.int32), axis=1)
    return natural.reshape(pack_size // ctx_count, ctx_count).T.reshape(pack_size)


def split_blocks(full_kv, ids_keys):
    block = min(512, full_kv.shape[0])
    count_blocks = full_kv.shape[0] // block
    return (
        full_kv.reshape(count_blocks, block, full_kv.shape[1]),
        ids_keys.reshape(count_blocks, block),
    )


def split_kv(block_kv, heads):
    half = block_kv.shape[1] // 2
    keys = block_kv[:, :half].reshape(block_kv.shape[0], heads, -1)
    values = block_kv[:, half:].reshape(block_kv.shape[0], heads, -1)
    return (keys, values)


def block_scores(queries, keys, ids_query, ids_keys, scale):
    scores = jnp.einsum("qhd,khd->hqk", queries, keys, preferred_element_type=jnp.float32) * scale
    same = ids_query[:, None] == ids_keys[None, :]
    return jnp.where(same[None], scores, -1000000000.0)


def attend_forward(queries, full_kv, ids_query, ids_keys, heads, scale):
    blocks, id_blocks = split_blocks(full_kv, ids_keys)
    query_rows = queries.shape[0]

    def total_step(carry, items):
        run_max, run_sum = carry
        keys, values = split_kv(items[0], heads)
        scores = block_scores(queries, keys, ids_query, items[1], scale)
        new_max = jnp.maximum(run_max, jnp.max(scores, axis=-1))
        run_sum = run_sum * jnp.exp(run_max - new_max) + jnp.sum(
            jnp.exp(scores - new_max[..., None]), axis=-1
        )
        return ((new_max, run_sum), None)

    start = (
        jnp.full((heads, query_rows), -1e30, jnp.float32),
        jnp.zeros((heads, query_rows), jnp.float32),
    )
    (run_max, run_sum), _ = lax.scan(total_step, start, (blocks, id_blocks))
    log_total = run_max + jnp.log(run_sum)

    def mix_step(carry, items):
        keys, values = split_kv(items[0], heads)
        scores = block_scores(queries, keys, ids_query, items[1], scale)
        probs = jnp.exp(scores - log_total[..., None]).astype(jnp.bfloat16)
        return (
            carry + jnp.einsum("hqk,khd->qhd", probs, values, preferred_element_type=jnp.float32),
            None,
        )

    mixed, _ = lax.scan(mix_step, jnp.zeros(queries.shape, jnp.float32), (blocks, id_blocks))
    return (mixed.reshape(query_rows, -1), log_total)


def attend_backward(queries, full_kv, ids_query, ids_keys, mixed_grad, log_total, heads, scale):
    blocks, id_blocks = split_blocks(full_kv, ids_keys)
    grad_heads = mixed_grad.reshape(queries.shape)

    def inner_step(carry, items):
        keys, values = split_kv(items[0], heads)
        scores = block_scores(queries, keys, ids_query, items[1], scale)
        probs = jnp.exp(scores - log_total[..., None])
        prob_grad = jnp.einsum(
            "qhd,khd->hqk", grad_heads, values, preferred_element_type=jnp.float32
        )
        return (carry + jnp.sum(probs * prob_grad, axis=-1), None)

    inner, _ = lax.scan(inner_step, jnp.zeros(log_total.shape, jnp.float32), (blocks, id_blocks))

    def grad_step(carry, items):
        keys, values = split_kv(items[0], heads)
        scores = block_scores(queries, keys, ids_query, items[1], scale)
        probs = jnp.exp(scores - log_total[..., None])
        prob_grad = jnp.einsum(
            "qhd,khd->hqk", grad_heads, values, preferred_element_type=jnp.float32
        )
        score_grad = (probs * (prob_grad - inner[..., None])).astype(jnp.bfloat16)
        carry = (
            carry
            + jnp.einsum("hqk,khd->qhd", score_grad, keys, preferred_element_type=jnp.float32)
            * scale
        )
        key_grad = (
            jnp.einsum("hqk,qhd->khd", score_grad, queries, preferred_element_type=jnp.float32)
            * scale
        )
        value_grad = jnp.einsum(
            "hqk,qhd->khd",
            probs.astype(jnp.bfloat16),
            grad_heads,
            preferred_element_type=jnp.float32,
        )
        block = keys.shape[0]
        return (
            carry,
            jnp.concatenate([key_grad.reshape(block, -1), value_grad.reshape(block, -1)], axis=1),
        )

    query_grad, partial_kv = lax.scan(
        grad_step, jnp.zeros(queries.shape, jnp.float32), (blocks, id_blocks)
    )
    query_grad = query_grad.reshape(queries.shape[0], -1)
    return (query_grad, partial_kv.reshape(-1, partial_kv.shape[-1]), inner)


def shards(boundary, lengths, valid, w_qkv, w_out, w_in, w_down, bias_in, vectors):
    section_at = lax.axis_index("section")
    ctx_count = lax.axis_size("ctx")
    ctx_at = lax.axis_index("ctx")
    wt_at = lax.axis_index("wt")
    micro_count = boundary.shape[1]
    row_count = boundary.shape[2]
    width = boundary.shape[3]
    pack_size = row_count * ctx_count
    head_size = width // HEADS
    scale = head_size ** (-0.5)
    gathered = (
        lax.all_gather(w_qkv[0], "wt", axis=0, tiled=True),
        lax.all_gather(w_out[0], "wt", axis=0, tiled=True),
        lax.all_gather(w_in[0], "wt", axis=0, tiled=True),
        lax.all_gather(w_down[0], "wt", axis=0, tiled=True),
        lax.all_gather(bias_in[0], "wt", axis=0, tiled=True),
        lax.all_gather(vectors[0], "wt", axis=1, tiled=True),
    )
    weight_qkv, weight_out, weight_in, weight_down, in_bias, vector_rows = gathered
    in_bias = in_bias.astype(jnp.float32)
    vector_rows = vector_rows.astype(jnp.float32)
    qkv_bias = jnp.concatenate([vector_rows[0], jnp.zeros((width,), jnp.float32), vector_rows[1]])
    my_lengths = lax.dynamic_index_in_dim(lengths, wt_at, 1, keepdims=False)

    def ids_of(length_row):
        return dealt_ids(length_row, pack_size, ctx_count)

    pack_ids = jax.vmap(ids_of)(my_lengths)
    query_ids = lax.dynamic_slice_in_dim(pack_ids, ctx_at * row_count, row_count, 1)
    count = lax.psum(jnp.sum(valid.astype(jnp.float32)), ("ctx", "wt"))
    factor = LOSS_SCALE / count
    empty_rows = jnp.zeros((row_count, width), jnp.bfloat16)
    arriving = empty_rows
    kept_list = []
    cotangents = []
    final_states = []
    for tick_at in range(micro_count + 1):
        own_input = boundary[0, tick_at] if tick_at < micro_count else empty_rows
        inputs = jnp.where(section_at == 0, own_input, arriving)
        micro_here = jnp.clip(tick_at - section_at, 0, micro_count - 1)
        ids_keys = lax.dynamic_index_in_dim(pack_ids, micro_here, 0, keepdims=False)
        ids_query = lax.dynamic_index_in_dim(query_ids, micro_here, 0, keepdims=False)
        residual = inputs.astype(jnp.float32)
        projected = jnp.dot(inputs, weight_qkv, preferred_element_type=jnp.float32) + qkv_bias
        layer_queries = (
            projected[:, :width].astype(jnp.bfloat16).reshape(row_count, HEADS, head_size)
        )
        layer_local_kv = projected[:, width:].astype(jnp.bfloat16)
        layer_full_kv = lax.all_gather(layer_local_kv, "ctx", axis=0, tiled=True)
        mixed, layer_log_total = attend_forward(
            layer_queries, layer_full_kv, ids_query, ids_keys, HEADS, scale
        )
        layer_mixed_low = mixed.astype(jnp.bfloat16)
        branch = (
            jnp.dot(layer_mixed_low, weight_out, preferred_element_type=jnp.float32)
            + vector_rows[2]
        )
        layer_summed = residual + branch
        first = layer_norm(layer_summed, vector_rows[3], vector_rows[4])
        layer_first_low = first.astype(jnp.bfloat16)
        layer_hidden_pre = (
            jnp.dot(layer_first_low, weight_in, preferred_element_type=jnp.float32) + in_bias
        )
        layer_hidden_low = exact_gelu(layer_hidden_pre).astype(jnp.bfloat16)
        layer_second = first + (
            jnp.dot(layer_hidden_low, weight_down, preferred_element_type=jnp.float32)
            + vector_rows[5]
        )
        output = layer_norm(layer_second, vector_rows[6], vector_rows[7])
        layer_kept = (
            inputs,
            layer_queries,
            layer_local_kv,
            layer_full_kv,
            layer_mixed_low,
            layer_log_total,
            layer_summed,
            layer_first_low,
            layer_hidden_pre,
            layer_hidden_low,
            layer_second,
            ids_keys,
            ids_query,
        )
        output, kept = (output, layer_kept)
        kept_list.append(kept)
        if tick_at > 0:
            teacher = boundary[0, tick_at - 1].astype(jnp.float32)
            covered = valid[tick_at - 1].astype(jnp.float32)[:, None]
            cotangents.append(factor * covered * (output - teacher))
            final_states.append(output.astype(jnp.bfloat16))
        else:
            cotangents.append(jnp.zeros((row_count, width), jnp.float32))
        if tick_at < micro_count:
            arriving = shifted(output.astype(jnp.bfloat16), "section", 1)
    returning = empty_rows
    totals = None
    input_grads = [None] * micro_count
    for back_at in range(micro_count + 1):
        forward_at = micro_count - back_at
        grad_output = jnp.where(
            section_at == 1, cotangents[forward_at], returning.astype(jnp.float32)
        )
        (
            layer_inputs,
            queries,
            local_kv,
            full_kv,
            mixed_low,
            log_total,
            summed,
            first_low,
            hidden_pre,
            hidden_low,
            second,
            layer_ids_keys,
            layer_ids_query,
        ) = kept_list[forward_at]
        full_kv = lax.all_gather(local_kv, "ctx", axis=0, tiled=True)
        _, pull_last = jax.vjp(layer_norm, second, vector_rows[6], vector_rows[7])
        grad_second, grad_gain_two, grad_shift_two = pull_last(grad_output)
        down_low = grad_second.astype(jnp.bfloat16)
        layer_grad_down = jnp.einsum(
            "rf,rd->fd", hidden_low, down_low, preferred_element_type=jnp.float32
        )
        grad_bias_two = jnp.sum(down_low.astype(jnp.float32), axis=0)
        _, pull_gelu = jax.vjp(exact_gelu, hidden_pre)
        (grad_pre,) = pull_gelu(
            jnp.einsum("rd,fd->rf", down_low, weight_down, preferred_element_type=jnp.float32)
        )
        pre_low = grad_pre.astype(jnp.bfloat16)
        layer_grad_in = jnp.einsum(
            "rd,rf->df", first_low, pre_low, preferred_element_type=jnp.float32
        )
        layer_grad_bias_in = jnp.sum(pre_low.astype(jnp.float32), axis=0)
        grad_first = grad_second + jnp.einsum(
            "rf,df->rd", pre_low, weight_in, preferred_element_type=jnp.float32
        )
        _, pull_first = jax.vjp(layer_norm, summed, vector_rows[3], vector_rows[4])
        grad_summed, grad_gain_one, grad_shift_one = pull_first(grad_first)
        branch_low = grad_summed.astype(jnp.bfloat16)
        layer_grad_out = jnp.einsum(
            "rd,re->de", mixed_low, branch_low, preferred_element_type=jnp.float32
        )
        grad_bias_out = jnp.sum(branch_low.astype(jnp.float32), axis=0)
        mixed_grad = jnp.einsum(
            "re,de->rd", branch_low, weight_out, preferred_element_type=jnp.float32
        ).astype(jnp.bfloat16)
        query_grad, partial_kv, inner = attend_backward(
            queries, full_kv, layer_ids_query, layer_ids_keys, mixed_grad, log_total, HEADS, scale
        )
        kv_grad = lax.psum_scatter(
            partial_kv.astype(jnp.bfloat16), "ctx", scatter_dimension=0, tiled=True
        )
        query_low = query_grad.astype(jnp.bfloat16)
        projected_grad = jnp.concatenate([query_low, kv_grad], axis=1)
        layer_grad_qkv = jnp.einsum(
            "rd,re->de", layer_inputs, projected_grad, preferred_element_type=jnp.float32
        )
        vector_grad = jnp.stack(
            [
                jnp.sum(query_low.astype(jnp.float32), axis=0),
                jnp.sum(kv_grad[:, width:].astype(jnp.float32), axis=0),
                grad_bias_out,
                grad_gain_one,
                grad_shift_one,
                grad_bias_two,
                grad_gain_two,
                grad_shift_two,
            ]
        )
        grad_inputs = grad_summed + jnp.einsum(
            "re,de->rd", projected_grad, weight_qkv, preferred_element_type=jnp.float32
        )
        grad_inputs, grads = (
            grad_inputs,
            (
                layer_grad_qkv,
                layer_grad_out,
                layer_grad_in,
                layer_grad_down,
                layer_grad_bias_in,
                vector_grad,
            ),
        )
        totals = grads if totals is None else jax.tree.map(jnp.add, totals, grads)
        if forward_at < micro_count:
            input_grads[forward_at] = grad_inputs
        if back_at < micro_count:
            returning = shifted(grad_inputs.astype(jnp.bfloat16), "section", -1)
    results = jnp.stack(
        [
            jnp.where(section_at == 0, input_grads[index].astype(jnp.bfloat16), final_states[index])
            for index in range(micro_count)
        ]
    )[None]
    shares = (
        lax.psum_scatter(
            totals[0].astype(jnp.bfloat16), "wt", scatter_dimension=0, tiled=True
        ).astype(jnp.float32),
        lax.psum_scatter(
            totals[1].astype(jnp.bfloat16), "wt", scatter_dimension=0, tiled=True
        ).astype(jnp.float32),
        lax.psum_scatter(
            totals[2].astype(jnp.bfloat16), "wt", scatter_dimension=0, tiled=True
        ).astype(jnp.float32),
        lax.psum_scatter(
            totals[3].astype(jnp.bfloat16), "wt", scatter_dimension=0, tiled=True
        ).astype(jnp.float32),
        lax.psum_scatter(
            totals[4].astype(jnp.bfloat16), "wt", scatter_dimension=0, tiled=True
        ).astype(jnp.float32),
        lax.psum_scatter(
            totals[5].astype(jnp.bfloat16), "wt", scatter_dimension=1, tiled=True
        ).astype(jnp.float32),
    )
    shares = jax.tree.map(lambda part: part.astype(jnp.float32), lax.psum(as_sent(shares), "ctx"))
    grad_qkv, grad_out, grad_in, grad_down, grad_bias_in, grad_vectors = shares
    return (
        results,
        grad_qkv[None],
        grad_out[None],
        grad_in[None],
        grad_down[None],
        grad_bias_in[None],
        grad_vectors[None],
    )


PAIR = 128
FAR = -1000000000.0
MESH = pl.DeviceIdType.MESH


def dot(left, right, dims=((1,), (0,))):
    return lax.dot_general(left, right, (dims, ((), ())), preferred_element_type=jnp.float32)


def head_lanes(size):
    lane = lax.broadcasted_iota(jnp.int32, (1, PAIR), 1)
    return [lane // size == index for index in range(PAIR // size)]


def only(mask, values):
    return jnp.where(mask, values, jnp.zeros_like(values))


def normal_tail(values):
    size = jnp.abs(values)
    bell = jnp.exp(-0.5 * values * values)
    t = 1.0 / (1.0 + 0.3275911 * (2.0**-0.5) * size)
    poly = t * (
        0.254829592
        + t * (-0.284496736 + t * (1.421413741 + t * (-1.453152027 + t * 1.061405429)))
    )
    tail = 0.5 * poly * bell
    return (jnp.where(values >= 0, 1.0 - tail, tail), bell)


def gelu_both(values):
    below, bell = normal_tail(values)
    return (values * below, below + values * bell * 0.3989422804014327)


def norm_parts(values):
    center = jnp.mean(values, axis=-1, keepdims=True)
    offset = values - center
    spread = jnp.mean(offset * offset, axis=-1, keepdims=True)
    inverse = lax.rsqrt(spread + 1e-05)
    return (offset * inverse, inverse)


def norm_back(grad, gain, normal, inverse):
    inner = grad * gain
    mean = jnp.mean(inner, axis=-1, keepdims=True)
    along = jnp.mean(inner * normal, axis=-1, keepdims=True)
    return inverse * (inner - mean - normal * along)


class Wires:
    def __init__(self, sems):
        self.sems = sems
        self.places = {}

    def at(self, *key):
        return self.sems.at[self.places.setdefault(key, len(self.places))]

    def remote(self, key, source, target, **where):
        return pltpu.make_async_remote_copy(
            source,
            target,
            self.at(key, "send"),
            self.at(key, "recv"),
            device_id=where,
            device_id_type=MESH,
        )

    def local(self, key, source, target):
        return pltpu.make_async_copy(source, target, self.at(key, "local"))


def wt_places():
    w = lax.axis_index("wt")
    core = lax.rem(w, 2)
    sibling = w + 1 - 2 * core
    across = lax.rem(w + 2, 4)
    return w, sibling, across, lax.rem(sibling + 2, 4)


def turned(place):
    return 2 * lax.rem(place, 2) + place // 2


def stripe_of(z, w):
    return 2 * lax.rem(w, 2) + lax.rem(w // 2 + z, 2)


def plane_place(z, w):
    plane = turned(w)
    return dict(ctx=plane, wt=2 * lax.rem(z + plane, 2) + z // 2)


def home_place(z, w):
    return dict(ctx=stripe_of(z, w), wt=turned(z))


def is_moving(z, w):
    place = home_place(z, w)
    return (place["ctx"] != z) | (place["wt"] != w)


def greet(partners, extra, meanwhile=lambda: None):
    barrier = pltpu.get_barrier_semaphore()
    for partner in partners:
        pl.semaphore_signal(barrier, 1, device_id=partner, device_id_type=MESH)
    waits = len(partners)
    for here, partner in extra:

        @pl.when(here)
        def _():
            pl.semaphore_signal(barrier, 1, device_id=partner, device_id_type=MESH)

        waits = waits + here.astype(jnp.int32)
    meanwhile()
    pl.semaphore_wait(barrier, waits)


def attend_pack(size, same, qkv, mixed):
    local = mixed.shape[1]
    masks = head_lanes(size)
    for pair in range(local // PAIR):
        at = pair * PAIR
        q = qkv[:, at : at + PAIR] * jnp.bfloat16(size**-0.5)
        k = qkv[:, local + at : local + at + PAIR]
        v = qkv[:, 2 * local + at : 2 * local + at + PAIR]
        total = None
        for mask in masks:
            scores = jnp.where(same, dot(only(mask, k), q, ((1,), (1,))), FAR)
            probs = jnp.exp(scores - jnp.max(scores, axis=0, keepdims=True))
            scale = 1.0 / jnp.sum(probs, axis=0, keepdims=True)
            low = (probs * scale).astype(jnp.bfloat16)
            term = dot(only(mask, v), low, ((0,), (0,)))
            total = term if total is None else total + term
        mixed[:, at : at + PAIR] = total.T.astype(jnp.bfloat16)


def attend_pack_back(size, same, qkv, grad_heads, projected_grad):
    local = grad_heads.shape[1]
    masks = head_lanes(size)
    for pair in range(local // PAIR):
        at = pair * PAIR
        q = qkv[:, at : at + PAIR] * jnp.bfloat16(size**-0.5)
        k = qkv[:, local + at : local + at + PAIR]
        v = qkv[:, 2 * local + at : 2 * local + at + PAIR]
        grad = grad_heads[:, at : at + PAIR]
        totals = [None] * 3
        for mask in masks:
            own_k = only(mask, k)
            scores = jnp.where(same, dot(own_k, q, ((1,), (1,))), FAR)
            probs = jnp.exp(scores - jnp.max(scores, axis=0, keepdims=True))
            probs = probs * (1.0 / jnp.sum(probs, axis=0, keepdims=True))
            prob_grad = dot(only(mask, v), grad, ((1,), (1,)))
            inner = jnp.sum(probs * prob_grad, axis=0, keepdims=True)
            score_grad = (probs * (prob_grad - inner)).astype(jnp.bfloat16)
            terms = (
                dot(own_k, score_grad, ((0,), (0,))),
                dot(score_grad, only(mask, q)),
                dot(probs.astype(jnp.bfloat16), only(mask, grad)),
            )
            totals = [t if o is None else o + t for o, t in zip(totals, terms)]
        query_grad = totals[0].T * size**-0.5
        projected_grad[:, at : at + PAIR] = query_grad.astype(jnp.bfloat16)
        projected_grad[:, local + at : local + at + PAIR] = totals[1].astype(jnp.bfloat16)
        projected_grad[:, 2 * local + at : 2 * local + at + PAIR] = totals[2].astype(jnp.bfloat16)


class Spread:
    def __init__(self, wires, full, mixed, mixed_rows, rows, local):
        self.wires, self.full, self.mixed, self.mixed_rows = wires, full, mixed, mixed_rows
        self.rows, self.local = rows, local
        self.w, self.sibling, self.across, self.across_sibling = wt_places()

    def stripe(self, m, j):
        return self.full.at[m, pl.ds(j * self.rows, self.rows), :]

    def to_sibling(self, m):
        own = self.stripe(m, self.w)
        return self.wires.remote(("sibling", m), own, own, wt=self.sibling)

    def to_across(self, m):
        own = self.stripe(m, self.w)
        return self.wires.remote(("across", m), own, own, wt=self.across)

    def passed(self, m):
        block = self.stripe(m, self.across)
        return self.wires.remote(("passed", m), block, block, wt=self.sibling)

    def send(self, m):
        self.to_across(m).start()
        self.to_sibling(m).start()

    def hand_on(self, m):
        self.to_across(m).wait_recv()
        self.passed(m).start()

    def settle(self, m):
        self.to_sibling(m).wait_recv()
        self.passed(m).wait_recv()

    def back(self, m):
        heads = pl.ds(self.w * self.local, self.local)
        target = self.mixed_rows.at[pl.ds(m * self.rows, self.rows), heads]
        for index, partner in enumerate((self.across, self.across_sibling, self.sibling)):
            block = self.mixed.at[m, pl.ds(partner * self.rows, self.rows), :]
            yield self.wires.remote(("back", m, index), block, target, wt=partner)

    def send_back(self, m):
        for copy in self.back(m):
            copy.start()
        self.own_back(m).start()

    def own_back(self, m):
        heads = pl.ds(self.w * self.local, self.local)
        return self.wires.local(
            ("back", m),
            self.mixed.at[m, pl.ds(self.w * self.rows, self.rows), :],
            self.mixed_rows.at[pl.ds(m * self.rows, self.rows), heads],
        )

    def finish(self, m):
        for copy in (self.to_sibling(m), self.to_across(m), self.passed(m)):
            copy.wait_send()
        for copy in self.back(m):
            copy.wait()
        self.own_back(m).wait()


def project(full, weight, bias, qkv):
    qkv[...] = (dot(full[...], weight[...]) + bias[...]).astype(jnp.bfloat16)


def first_kernel(size, *refs):
    block, shard_qkv, shard_out, shard_in, shard_down, small, marks, bias = refs[:8]
    ids_row, ids_col = refs[8:10]
    own, weight, whole_out, whole_in, whole_down, smalls, own_marks, count = refs[10:18]
    mixed_rows, full, qkv, mixed, marks_wt, marks_ctx = refs[18:24]
    held_out, held_in, held_down, sems = refs[24:]
    micro, rows, width = block.shape
    local = small.shape[1]
    hidden = shard_in.shape[1]
    half = local // 2
    deep = shard_down.shape[0] // 8
    wires = Wires(sems)
    z = lax.axis_index("ctx")
    spread = Spread(wires, full, mixed, mixed_rows, rows, local)
    w, sibling, across, across_sibling = wt_places()
    partners = (across, across_sibling, sibling)
    level = lax.rem(z, 2)
    neighbor = z + 1 - 2 * level
    moves, place = is_moving(z, w), plane_place(z, w)
    others = [lax.rem(z + step, 4) for step in (1, 2, 3)]
    greet(
        [{"wt": partner} for partner in partners] + [{"ctx": other} for other in others],
        [(moves, place), (moves, home_place(z, w))],
    )

    def swap(m):
        return wires.remote(
            ("swap", m), block.at[m], spread.stripe(m, place["wt"]), **place
        )

    def stay(m):
        return wires.local(("stay", m), block.at[m], spread.stripe(m, w))

    def swap_marks():
        return wires.remote("swap marks", marks, own_marks, **place)

    def head_copy(part, index):
        column = part * width + partners[index] * local
        return wires.remote(
            ("heads", part, index),
            shard_qkv.at[:, pl.ds(column, local)],
            weight.at[pl.ds(w * local, local), pl.ds(part * local, local)],
            wt=partners[index],
        )

    def head_own(part):
        return wires.local(
            ("heads", part),
            shard_qkv.at[:, pl.ds(part * width + w * local, local)],
            weight.at[pl.ds(w * local, local), pl.ds(part * local, local)],
        )

    def small_copy(index):
        return wires.remote(("small", index), small, smalls.at[w], wt=partners[index])

    def marks_copy(index):
        return wires.remote(("marks", index), marks, marks_wt.at[index], wt=partners[index])

    def count_copy(index):
        return wires.remote(("count", index), count, marks_ctx.at[index], ctx=others[index])

    columns = hidden // width
    chunks = 1 + columns + 4

    def piece(k, level):
        if k == 0:
            return shard_out, whole_out, local, level * half, half, 0
        if k <= columns:
            return shard_in, whole_in, local, level * half, half, (k - 1) * width
        at = (level * 4 + k - 1 - columns) * deep
        return shard_down, whole_down, 4 * deep * 2, at, deep, 0

    def from_shard(k, level):
        shard, _, _, at, size, column = piece(k, level)
        return shard.at[pl.ds(at, size), pl.ds(column, width)]

    def in_whole(k, level, j):
        _, whole, stride, at, size, column = piece(k, level)
        return whole.at[pl.ds(j * stride + at, size), pl.ds(column, width)]

    def y_copy(k):
        return wires.remote(
            ("y", k), from_shard(k, level), in_whole(k, level, w), wt=across
        )

    def z_copy(k):
        block = in_whole(k, level, across)
        return wires.remote(("z", k), block, block, ctx=neighbor)

    def core_copy(k, side):
        block = in_whole(k, level if side == 0 else 1 - level, across)
        return wires.remote(("core", k, side), block, block, wt=sibling)

    def shard_sibling(index):
        shard, whole = ((shard_out, whole_out), (shard_in, whole_in), (shard_down, whole_down))[
            index
        ]
        size = shard.shape[0]
        return wires.remote(
            ("shard", index), shard, whole.at[pl.ds(w * size, size), :], wt=sibling
        )

    def shard_own(index):
        shard, whole = ((shard_out, whole_out), (shard_in, whole_in), (shard_down, whole_down))[
            index
        ]
        size = shard.shape[0]
        held = (held_out, held_in, held_down)[index]
        place = whole.at[pl.ds(w * size, size), :]
        return (
            wires.local(("shard in", index), shard, held),
            wires.local(("shard own", index), held, place),
        )

    @pl.when(moves)
    def _():
        for m in range(micro):
            swap(m).start()
        swap_marks().start()

    @pl.when(jnp.logical_not(moves))
    def _():
        for m in range(micro):
            stay(m).start()
        own_marks[...] = marks[...]

    for part in range(3):
        for index in range(3):
            head_copy(part, index).start()
        head_own(part).start()
    for index in range(3):
        small_copy(index).start()
        marks_copy(index).start()
    smalls[w] = small[...]

    def arrive(m):
        @pl.when(moves)
        def _():
            swap(m).wait_recv()

        @pl.when(jnp.logical_not(moves))
        def _():
            stay(m).wait()

    def own_copy(m):
        return wires.local(("own", m), spread.stripe(m, w), own.at[m])

    for m in range(micro):
        arrive(m)
        spread.send(m)
        own_copy(m).start()
    for k in range(chunks):
        y_copy(k).start()
    for index in range(3):
        shard_sibling(index).start()
        shard_own(index)[0].start()
    for index in range(3):
        shard_own(index)[0].wait()
        shard_own(index)[1].start()
    for index in range(3):
        marks_copy(index).wait_recv()
    count[...] = marks[...] + marks_wt[0] + marks_wt[1] + marks_wt[2]
    for index in range(3):
        count_copy(index).start()
    for part in range(3):
        for index in range(3):
            head_copy(part, index).wait_recv()
        head_own(part).wait()
    for m in range(micro):
        spread.hand_on(m)
        spread.settle(m)
        project(full.at[m], weight, bias, qkv.at[0])
        attend_pack(size, ids_col[m] == ids_row[m], qkv.at[0], mixed.at[m])
        spread.send_back(m)
        y_copy(m).wait_recv()
        z_copy(m).start()
        core_copy(m, 0).start()
    for k in range(micro, chunks):
        y_copy(k).wait_recv()
        z_copy(k).start()
        core_copy(k, 0).start()
        z_copy(k - micro).wait_recv()
        core_copy(k - micro, 1).start()
    for k in range(chunks - micro, chunks):
        z_copy(k).wait_recv()
        core_copy(k, 1).start()
    for index in range(3):
        count_copy(index).wait()
    count[...] = count[...] + marks_ctx[0] + marks_ctx[1] + marks_ctx[2]
    for m in range(micro):
        spread.finish(m)
        own_copy(m).wait()
    for part in range(3):
        for index in range(3):
            head_copy(part, index).wait_send()
    for index in range(3):
        small_copy(index).wait()
        marks_copy(index).wait_send()
        shard_sibling(index).wait()
        shard_own(index)[1].wait()
    for k in range(chunks):
        y_copy(k).wait_send()
        z_copy(k).wait_send()
        for side in range(2):
            core_copy(k, side).wait()

    @pl.when(moves)
    def _():
        for m in range(micro):
            swap(m).wait_send()
        swap_marks().wait()


def first_pass(block, shards, small, marks, bias, ids, size):
    micro, rows, width = block.shape
    local = small.shape[1]
    pack = ids.shape[1]
    anywhere = pl.BlockSpec(memory_space=pl.ANY)
    inside = pl.BlockSpec(memory_space=pltpu.VMEM)
    low = lambda *shape: jax.ShapeDtypeStruct(shape, jnp.bfloat16)
    word = jax.ShapeDtypeStruct(marks.shape, jnp.float32)
    return pl.pallas_call(
        functools.partial(first_kernel, size),
        in_specs=[anywhere] * 5 + [inside] * 5,
        out_specs=[anywhere, inside] + [anywhere] * 3 + [inside] * 4,
        out_shape=[
            low(micro, rows, width),
            low(width, 3 * local),
            low(4 * shards[1].shape[0], shards[1].shape[1]),
            low(4 * shards[2].shape[0], shards[2].shape[1]),
            low(4 * shards[3].shape[0], shards[3].shape[1]),
            low(4, *small.shape),
            word,
            word,
            low(micro * rows, width),
        ],
        scratch_shapes=[
            pltpu.VMEM((micro, pack, width), jnp.bfloat16),
            pltpu.VMEM((1, pack, 3 * local), jnp.bfloat16),
            pltpu.VMEM((micro, pack, local), jnp.bfloat16),
            pltpu.VMEM((3,) + marks.shape, jnp.float32),
            pltpu.VMEM((3,) + marks.shape, jnp.float32),
        ]
        + [pltpu.VMEM(shard.shape, jnp.bfloat16) for shard in shards[1:]]
        + [
            pltpu.SemaphoreType.DMA((256,)),
        ],
        compiler_params=pltpu.CompilerParams(
            collective_id=2, has_side_effects=True, vmem_limit_bytes=48 * 2**20
        ),
        name="first_pass",
    )(block, *shards, small, marks, bias, ids[:, None, :], ids[:, :, None])


def second_kernel(size, *refs):
    states, leaving, weight, bias, ids_row, ids_col = refs[:6]
    full, qkv, mixed_rows, mixed, sems = refs[6:]
    micro, rows, width = states.shape
    wires = Wires(sems)
    section = lax.axis_index("section")
    spread = Spread(wires, full, mixed, mixed_rows, rows, weight.shape[1] // 3)
    w, sibling, across, across_sibling = wt_places()
    greet(
        [{"wt": partner} for partner in (across, across_sibling, sibling)]
        + [{"section": 1 - section}],
        [],
    )

    def relay_copy(m):
        return wires.remote(("relay", m), leaving.at[m], spread.stripe(m, w), section=1 - section)

    def stay(m):
        return wires.local(("stay", m), states.at[m], spread.stripe(m, w))

    @pl.when(section == 0)
    def _():
        for m in range(micro):
            relay_copy(m).start()
            stay(m).start()

    def arrive(m):
        @pl.when(section == 0)
        def _():
            stay(m).wait()

        @pl.when(section == 1)
        def _():
            relay_copy(m).wait_recv()

        spread.send(m)

    def work(m):
        spread.settle(m)
        project(full.at[m], weight, bias, qkv.at[m])
        attend_pack(size, ids_col[m] == ids_row[m], qkv.at[m], mixed.at[m])
        spread.send_back(m)

    arrive(0)
    arrive(1)
    spread.hand_on(0)
    work(0)
    arrive(2)
    spread.hand_on(1)
    work(1)
    spread.hand_on(2)
    work(2)
    for m in range(micro):
        spread.finish(m)

    @pl.when(section == 0)
    def _():
        for m in range(micro):
            relay_copy(m).wait_send()


def second_pass(states, leaving, weight, bias, ids, size):
    micro, rows, width = states.shape
    local = weight.shape[1] // 3
    pack = ids.shape[1]
    anywhere = pl.BlockSpec(memory_space=pl.ANY)
    inside = pl.BlockSpec(memory_space=pltpu.VMEM)
    low = lambda *shape: jax.ShapeDtypeStruct(shape, jnp.bfloat16)
    return pl.pallas_call(
        functools.partial(second_kernel, size),
        in_specs=[anywhere] * 2 + [inside] * 4,
        out_specs=[inside] * 3,
        out_shape=[
            low(micro, pack, width),
            low(micro, pack, 3 * local),
            low(micro * rows, width),
        ],
        scratch_shapes=[
            pltpu.VMEM((micro, pack, local), jnp.bfloat16),
            pltpu.SemaphoreType.DMA((80,)),
        ],
        compiler_params=pltpu.CompilerParams(
            collective_id=3, has_side_effects=True, vmem_limit_bytes=48 * 2**20
        ),
        name="second_pass",
    )(states, leaving, weight, bias, ids[:, None, :], ids[:, :, None])


class Back:
    def __init__(self, wires, size, refs):
        self.wires, self.size = wires, size
        self.rows_grad, self.skip, self.qkv, self.weight, self.ids = refs[:5]
        self.projected, self.grad_states = refs[5:7]
        self.heads_grad, self.part, self.from_sibling, self.far, self.from_across = refs[7:]
        self.micro, self.pack, self.local = self.heads_grad.shape
        self.rows = self.pack // 4
        self.w, self.sibling, self.across, self.across_sibling = wt_places()
        self.partners = (self.across, self.across_sibling, self.sibling)

    def place(self, m):
        return pl.ds(m * self.rows, self.rows)

    def heads_copy(self, m, index):
        column = pl.ds(self.partners[index] * self.local, self.local)
        return self.wires.remote(
            ("heads", m, index),
            self.rows_grad.at[self.place(m), column],
            self.heads_grad.at[m, pl.ds(self.w * self.rows, self.rows), :],
            wt=self.partners[index],
        )

    def heads_own(self, m):
        return self.wires.local(
            ("heads", m),
            self.rows_grad.at[self.place(m), pl.ds(self.w * self.local, self.local)],
            self.heads_grad.at[m, pl.ds(self.w * self.rows, self.rows), :],
        )

    def stripe(self, m, j):
        return self.part.at[m, pl.ds(j * self.rows, self.rows), :]

    def sibling_copy(self, m, index):
        j = (self.across_sibling, self.sibling)[index]
        return self.wires.remote(
            ("to sibling", m, index),
            self.stripe(m, j),
            self.from_sibling.at[m, index],
            wt=self.sibling,
        )

    def across_copy(self, m):
        return self.wires.remote(
            ("to across", m), self.far.at[m], self.from_across.at[m], wt=self.across
        )

    def begin(self, m):
        for index in range(3):
            self.heads_copy(m, index).start()
        self.heads_own(m).start()

    def arrive(self, m):
        for index in range(3):
            self.heads_copy(m, index).wait_recv()
        self.heads_own(m).wait()

    def work(self, m, following=None):
        self.arrive(m)
        if following is not None:
            self.begin(following)
        ids_row, ids_col = self.ids
        whole = pl.ds(m * self.pack, self.pack)
        projected = self.projected.at[whole, :]
        same = ids_col[m] == ids_row[m]
        qkv = self.qkv(m)
        attend_pack_back(self.size, same, qkv, self.heads_grad.at[m], projected)
        product = dot(projected[...], self.weight[...], ((1,), (1,)))
        self.part[m] = product.astype(jnp.bfloat16)
        for index in range(2):
            self.sibling_copy(m, index).start()

    def cross(self, m):
        for index in range(2):
            self.sibling_copy(m, index).wait_recv()
        total = self.stripe(m, self.across)[...].astype(jnp.float32)
        total = total + self.from_sibling[m, 0].astype(jnp.float32)
        self.far[m] = total.astype(jnp.bfloat16)
        self.across_copy(m).start()

    def finish(self, m):
        self.across_copy(m).wait_recv()
        total = self.skip[self.place(m), :] + self.stripe(m, self.w)[...].astype(jnp.float32)
        total = total + self.from_sibling[m, 1].astype(jnp.float32)
        total = total + self.from_across[m].astype(jnp.float32)
        self.grad_states[self.place(m), :] = total.astype(jnp.bfloat16)

    def end(self, m):
        for index in range(3):
            self.heads_copy(m, index).wait_send()
        for index in range(2):
            self.sibling_copy(m, index).wait_send()
        self.across_copy(m).wait_send()


def back_scratch(micro, pack, local, width):
    block = pltpu.VMEM((micro, pack // 4, width), jnp.bfloat16)
    return [
        pltpu.VMEM((micro, pack, local), jnp.bfloat16),
        pltpu.VMEM((micro, pack, width), jnp.bfloat16),
        pltpu.VMEM((micro, 2, pack // 4, width), jnp.bfloat16),
        block,
        block,
    ]


def swap_back(wires, rows, source, target, m, moves):
    z, w = lax.axis_index("ctx"), lax.axis_index("wt")
    block = source.at[pl.ds(m * rows, rows), :]
    if moves:
        return wires.remote(("home", m), block, target.at[m], **home_place(z, w))
    return wires.local(("home", m), block, target.at[m])


def back_kernel(size, *refs):
    returned, grad_states, projected = refs[6:9]
    wires = Wires(refs[-1])
    section = lax.axis_index("section")
    qkv = lambda m: refs[2].at[m]
    given = (refs[0], refs[1], qkv, refs[3], refs[4:6])
    back = Back(wires, size, given + (projected, grad_states) + refs[9:-1])
    greet([{"wt": partner} for partner in back.partners] + [{"section": 1 - section}], [])
    back.begin(0)

    def back_copy(m):
        place = back.place(m)
        return wires.remote(
            ("return", m), grad_states.at[place, :], returned.at[place, :], section=1 - section
        )

    def finish(m):
        back.finish(m)

        @pl.when(section == 1)
        def _():
            back_copy(m).start()

    back.work(0, 1)
    back.cross(0)
    back.work(1, 2)
    back.cross(1)
    finish(0)
    back.work(2)
    back.cross(2)
    finish(1)
    finish(2)
    for m in range(back.micro):
        back.end(m)

        @pl.when(section == 1)
        def _():
            back_copy(m).wait_send()

        @pl.when(section == 0)
        def _():
            back_copy(m).wait_recv()


def back_pass(rows_grad, skip, qkv, weight, ids, size):
    micro, pack, local = qkv.shape
    local = local // 3
    tokens, width = rows_grad.shape
    inside = pl.BlockSpec(memory_space=pltpu.VMEM)
    low = lambda *shape: jax.ShapeDtypeStruct(shape, jnp.bfloat16)
    return pl.pallas_call(
        functools.partial(back_kernel, size),
        in_specs=[inside] * 6,
        out_specs=inside,
        out_shape=low(tokens, width),
        scratch_shapes=[
            pltpu.VMEM((tokens, width), jnp.bfloat16),
            pltpu.VMEM((micro * pack, 3 * local), jnp.bfloat16),
        ]
        + back_scratch(micro, pack, local, width)
        + [pltpu.SemaphoreType.DMA((96,))],
        compiler_params=pltpu.CompilerParams(
            collective_id=4, has_side_effects=True, vmem_limit_bytes=48 * 2**20
        ),
        name="back_pass",
    )(rows_grad, skip, qkv, weight, ids[:, None, :], ids[:, :, None])


CHUNK = 128
RING = 6
TILE = 256
LAGS = (2, 4, 6, 8)
AHEAD = 4


def sum_into(target, parts, rows):
    step = 16

    def one(index, carry):
        at = pl.ds(pl.multiple_of(index * step, step), step)
        total = parts[0][at, :].astype(jnp.float32)
        for part in parts[1:]:
            total = total + part[at, :].astype(jnp.float32)
        target[at, :] = total.astype(jnp.bfloat16)
        return carry

    lax.fori_loop(0, rows // step, one, 0)


def chunk_list(local, width, hidden):
    down = [("down", 0, CHUNK // 4, 0), ("down", CHUNK // 4, CHUNK // 4, 0)]
    down += [("down", CHUNK // 2, CHUNK // 2, 0)]
    down += [("down", row, CHUNK, 0) for row in range(CHUNK, hidden // 4, CHUNK)]
    across = [
        ("in", row, CHUNK, column)
        for column in range(hidden // width)
        for row in range(0, local, CHUNK)
    ]
    out = [("out", row, CHUNK // 2, 0) for row in range(0, local - CHUNK // 2, CHUNK // 2)]
    out += [("out", row, CHUNK // 4, 0) for row in range(local - CHUNK // 2, local, CHUNK // 4)]
    qkv = [("qkv", row, CHUNK, part) for part in range(3) for row in range(0, local, CHUNK)]
    return down + across[:3] + qkv + across[3:] + out + [("rest", 0, 16, 0)]


def starts_of(chunks):
    rows = [chunk[2] for chunk in chunks]
    starts = [sum(rows[:k]) for k in range(len(rows) + 1)]
    return starts, [sum(rows[k % 2 : k : 2]) for k in range(len(rows) + 2)]


def last_kernel(chunks, size, *refs):
    weight, ids_row, ids_col, gain, inverse_one, rows_low = refs[:6]
    grad_second, normal_one, qkv_all, full_all, slope = refs[6:11]
    weight_out, weight_in, weight_down = refs[11:14]
    hidden, first, mixed, down, final = refs[14:19]
    home = refs[19]
    results = dict(zip(("qkv", "out", "in", "down", "rest"), refs[20:25]))
    grad_states, projected, full, product = refs[25:29]
    downs, ins, outs, down_both, pre_both, branch_both, rest_in = refs[29:36]
    near, far, across_in, up_in, side_in = refs[36:41]
    skip, normal, slopes, qkv_one, rows_grad, rest = refs[41:47]
    wires = Wires(refs[-1])
    z, section = lax.axis_index("ctx"), lax.axis_index("section")
    tokens, width = down.shape
    count = len(chunks)
    micro = qkv_all.shape[0]

    def qkv_copy(m):
        return wires.local(("pack", m), qkv_all.at[m], qkv_one)

    def qkv_of(m):
        qkv_copy(m).wait()
        return qkv_one

    given = (rows_grad, skip, qkv_of, weight, (ids_row, ids_col))
    back = Back(wires, size, given + (projected, grad_states) + refs[47:-1])
    w, sibling, across, across_sibling = wt_places()
    partners = (sibling, across, across_sibling)
    local = back.local
    deep = hidden.shape[1] // 4
    starts, sides_at = starts_of(chunks)
    moves = is_moving(z, w)
    own_rows = pl.ds(0, tokens)
    blocks = hidden.shape[1] // TILE

    def tile_copies(b):
        low = full.at[pl.ds((b % 2) * TILE, TILE), :]
        if b >= blocks:
            source = weight_out.at[pl.ds((b - blocks) * TILE, TILE), :]
            return [wires.local(("tile", b), source, low)]
        columns = pl.ds(b * TILE, TILE)
        wide = full.at[pl.ds(2 * TILE, width), pl.ds((b % 4) * TILE, TILE)]
        return [
            wires.local(("tile", b), weight_down.at[columns, :], low),
            wires.local(("wide", b), weight_in.at[:, columns], wide),
            wires.local(("slope", b), slope.at[:, columns], slopes.at[b % 2]),
        ]

    def start_tiles(b):
        for copy in tile_copies(b):
            copy.start()

    def skip_copy():
        return wires.local("skip", grad_second, skip)

    def normal_copy():
        return wires.local("normal", normal_one, normal)

    def own_loads():
        start_tiles(0)
        start_tiles(1)
        skip_copy().start()
        normal_copy().start()
        qkv_copy(0).start()

    greet(
        [{"wt": partner} for partner in partners],
        [
            (moves, home_place(z, w)),
            (moves, plane_place(z, w)),
            (z > 0, {"ctx": z - 1}),
            (z < 3, {"ctx": z + 1}),
        ],
        own_loads,
    )

    def step_back(b):
        if b == 0:
            skip_copy().wait()
        for copy in tile_copies(b):
            copy.wait()
        columns = pl.ds(b * TILE, TILE)
        low = full[pl.ds((b % 2) * TILE, TILE), :]
        wide = full[pl.ds(2 * TILE, width), pl.ds((b % 4) * TILE, TILE)]
        grad = dot(down_both[own_rows, :], low, ((1,), (1,)))
        grad = (grad * slopes[b % 2].astype(jnp.float32)).astype(jnp.bfloat16)
        pre_both[own_rows, columns] = grad
        skip[...] += dot(grad, wide, ((1,), (1,)))
        start_tiles(b + 2)
        if (b + 1) * TILE % width == 0:
            to_sibling("pre", pre_both, (b + 1) * TILE // width - 1).start()

    def to_sibling(key, array, column):
        at = pl.ds(column * width, width)
        target = array.at[pl.ds(tokens, tokens), at]
        return wires.remote((key, column), array.at[own_rows, at], target, wt=sibling)

    def step_norm():
        normal_copy().wait()
        ones = jnp.ones((16, tokens), jnp.bfloat16)
        grad_first = skip[...]
        rows = {r: rows_low[r : r + 1, :] for r in (5, 6, 7)}
        rows[3] = jnp.sum(grad_first * normal[...], axis=0, keepdims=True)
        rows[4] = jnp.sum(grad_first, axis=0, keepdims=True)
        grad_summed = norm_back(grad_first, gain[...], normal[...], inverse_one[...])
        skip[...] = grad_summed
        branch = grad_summed.astype(jnp.bfloat16)
        branch_both[own_rows, :] = branch
        to_sibling("branch", branch_both, 0).start()
        rows[2] = dot(ones, branch)[:1]
        sums = dot(ones, pre_both[own_rows, :])[:1]
        rest[...] = jnp.zeros_like(rest)
        for j in range(4):
            for r, row in rows.items():
                rest[j * 16 + r : j * 16 + r + 1, :local] = row[:, j * local : (j + 1) * local]
            for r in range(deep // local):
                at = j * deep + r * local
                rest[j * 16 + r : j * 16 + r + 1, local : 2 * local] = sums[:, at : at + local]
        for copy in rest_copies():
            copy.start()

    def step_out(b):
        for copy in tile_copies(b):
            copy.wait()
        tile = full[pl.ds((b % 2) * TILE, TILE), :]
        grad = dot(branch_both[own_rows, :], tile, ((1,), (1,))).astype(jnp.bfloat16)
        rows_grad[:, pl.ds((b - blocks) * TILE, TILE)] = grad
        if b + 2 < blocks + width // TILE:
            start_tiles(b + 2)

    def last_out():
        for b in range(blocks, blocks + width // TILE):
            step_out(b)
        full_copy().start()
        for m in range(micro):
            back.begin(m)

    def both(key, source, target, at, columns, theirs):
        mine = (pl.ds(0, tokens), at)
        other = (pl.ds(tokens, tokens), at)
        return (
            wires.local(key, source.at[:, columns], target.at[mine]),
            wires.remote(key, source.at[:, theirs], target.at[other], wt=sibling),
        )

    def sides(key, source, block, target):
        for side, (j, k) in enumerate(((w, sibling), (across, across_sibling))):
            yield from both(
                key + (side,),
                source,
                target,
                pl.ds(side * CHUNK, CHUNK),
                pl.ds(block(j), CHUNK),
                pl.ds(block(k), CHUNK),
            )

    def down_block(index):
        return sides(
            ("down", index), hidden, lambda j: j * deep + index * CHUNK, downs.at[index]
        )

    def in_block(half):
        return sides(("in", half), first, lambda j: j * local + half * CHUNK, ins.at[half])

    def out_block(half):
        return sides(("out", half), mixed, lambda j: j * local + half * CHUNK, outs.at[half])

    def whole(key, source, target, column):
        at = pl.ds(column * width, width)
        return both((key, column), source, target, at, at, at)

    def rest_copies():
        for side, k in enumerate((sibling, across_sibling)):
            yield wires.remote(
                ("rest", side), rest.at[pl.ds(k * 16, 16), :], rest_in.at[side], wt=sibling
            )

    halves = local // CHUNK
    columns = hidden.shape[1] // width
    loads = [lambda: whole("down", down, down_both, 0)]
    loads += [lambda index=index: down_block(index) for index in range(deep // CHUNK)]
    loads += [lambda half=half: in_block(half) for half in range(halves)]
    loads += [lambda half=half: out_block(half) for half in range(halves)]

    def full_copy():
        return wires.local("full", full_all, full)

    def needs(k):
        kind, row, _, column = chunks[k]
        index = row // CHUNK
        copies = []
        if kind == "down":
            if index == 0:
                copies += whole("down", down, down_both, 0)
            copies += down_block(index)
        elif kind == "in":
            if column == 0:
                copies += in_block(index)
            if index == 0:
                to_sibling("pre", pre_both, column).wait_recv()
        else:
            copies += out_block(index)
            if index == 0:
                to_sibling("branch", branch_both, 0).wait_recv()
        for index, copy in enumerate(copies):
            (copy.wait if index % 2 == 0 else copy.wait_recv)()

    def operands(k):
        kind, row, _, column = chunks[k]
        index = row // CHUNK
        if kind == "down":
            return downs[index], down_both[...]
        if kind == "in":
            return ins[index], pre_both[:, column * width : (column + 1) * width]
        return outs[index], branch_both[...]

    def is_piece(k):
        return chunks[k][0] == "qkv"

    def rows_of(k):
        return chunks[k][2]

    def slot(buffer, k):
        return buffer.at[pl.ds(starts[k], rows_of(k)), :]

    def beside_slot(k):
        return side_in.at[pl.ds(sides_at[k], rows_of(k)), :]

    def result(k):
        kind, row, rows, column = chunks[k]
        if kind == "rest":
            return results["rest"]
        return results[kind].at[pl.ds(row, rows), pl.ds(column * width, width)]

    def piece(k, j):
        _, row, rows, part = chunks[k]
        return product.at[part, pl.ds(j * local + row, rows), :]

    def piece_place(k):
        return near.at[pl.ds(starts[k], rows_of(k)), pl.ds(w * local, local)]

    def piece_copy(k, index):
        place = piece_place(k)
        return wires.remote(
            ("piece", k, index), piece(k, partners[index]), place, wt=partners[index]
        )

    def piece_own(k):
        return wires.local(("piece", k), piece(k, w), piece_place(k))

    direct = [k for k in range(count) if not is_piece(k)]
    bases = [k for k in direct if chunks[k][1] % CHUNK == 0]

    def base_of(k):
        return max(base for base in bases if base <= k)

    def far_slot(k, rows):
        return far.at[bases.index(base_of(k)) % RING, pl.ds(chunks[k][1] % CHUNK, rows), :]

    def across_copy(k):
        source = far_slot(k, rows_of(k))
        return wires.remote(("chunk", k), source, slot(across_in, k), wt=across)

    def place_of(k, role):
        return role if k % 2 == 0 else 3 - role

    def up_copy(k, role):
        target = place_of(k, 1 if role == 0 else 2)
        return wires.remote(("up", k), slot(near, k), slot(up_in, k), ctx=target)

    def side_copy(k):
        return wires.remote(("side", k), slot(near, k), beside_slot(k), ctx=place_of(k, 1))

    def down_copy(k, role):
        origin = result(k) if role == 3 else slot(near, k)
        return pltpu.make_async_remote_copy(
            origin,
            result(k),
            wires.at("down send", k, 1 if role == 2 else 0),
            wires.at("down recv", k),
            device_id={"ctx": place_of(k, role)},
            device_id_type=MESH,
        )

    def keep_copy(k):
        return wires.local(("keep", k), slot(near, k), result(k))

    def on(k, role, step):
        pl.when(z == place_of(k, role))(step)

    def summands(k):
        if is_piece(k):
            return [slot(near, k)]
        return [slot(near, k), slot(across_in, k)]

    def begin(k):
        kind, row, _, column = chunks[k]
        if is_piece(k):
            if row == 0:
                at = pl.ds(column * local, local)
                grad = dot(full[...], projected[:, at], ((0,), (0,)))
                product[column] = grad.astype(jnp.bfloat16)
            for partner in range(3):
                piece_copy(k, partner).start()
            piece_own(k).start()
            return
        if k in bases:
            order = bases.index(k)
            for old in direct:
                if order >= RING and base_of(old) == bases[order - RING]:
                    across_copy(old).wait_send()
        if kind == "rest":
            for copy in rest_copies():
                copy.wait_recv()
            ones = jnp.ones((16, projected.shape[0]), jnp.bfloat16)
            sums = dot(ones, projected[...])
            row = lax.broadcasted_iota(jnp.int32, (16, local), 0)
            own = jnp.where(row == 0, sums[:, :local], 0.0)
            own = own + jnp.where(row == 1, sums[:, 2 * local :], 0.0)
            own = jnp.concatenate([own, jnp.zeros((16, width - local), jnp.float32)], axis=1)
            own = own + rest[pl.ds(w * 16, 16), :] + rest_in[0]
            other = rest[pl.ds(across * 16, 16), :] + rest_in[1]
            slot(near, k)[...] = own.astype(jnp.bfloat16)
            far_slot(k, 16)[...] = other.astype(jnp.bfloat16)
        elif k in bases:
            needs(k)
            left, right = operands(k)
            grad = dot(left, right, ((0,), (0,))).astype(jnp.bfloat16)
            near[pl.ds(starts[k], CHUNK), :] = grad[:CHUNK]
            far_slot(k, CHUNK)[...] = grad[CHUNK:]
        across_copy(k).start()

    def settle(k):
        if is_piece(k):
            for index in range(3):
                piece_copy(k, index).wait_recv()
            piece_own(k).wait()
        else:
            across_copy(k).wait_recv()
        for role in (0, 3):

            def step(role=role):
                if not is_piece(k):
                    sum_into(slot(near, k), summands(k), rows_of(k))
                up_copy(k, role).start()

            on(k, role, step)

    def aside(k):
        def step():
            up_copy(k, 3).wait_recv()
            sum_into(slot(near, k), summands(k) + [slot(up_in, k)], rows_of(k))
            side_copy(k).start()

        on(k, 2, step)

    def finish(k):
        def step():
            up_copy(k, 0).wait_recv()
            side_copy(k).wait_recv()
            parts = summands(k) + [slot(up_in, k), beside_slot(k)]
            sum_into(slot(near, k), parts, rows_of(k))
            down_copy(k, 0).start()
            down_copy(k, 2).start()
            keep_copy(k).start()

        on(k, 1, step)

    def forward(k):
        def step():
            down_copy(k, 2).wait_recv()
            down_copy(k, 3).start()

        on(k, 2, step)

    def go_home(m, source, here, do):
        @pl.when(moves & here)
        def _():
            do(swap_back(wires, back.rows, source, home, m, True))

        @pl.when(jnp.logical_not(moves) & here)
        def _():
            do(swap_back(wires, back.rows, source, home, m, False))

    def done(m):
        back.finish(m)
        go_home(m, grad_states, section == 0, lambda copy: copy.start())

    def final_home(m):
        go_home(m, final, section == 1, lambda copy: copy.start())

    beside = {
        9: [lambda: back.work(0), lambda: qkv_copy(1).start()],
        10: [lambda: back.work(1), lambda: qkv_copy(2).start()],
        11: [lambda: back.work(2)],
        17: [lambda: final_home(0)],
        18: [lambda: final_home(1)],
        19: [lambda: final_home(2)],
        20: [lambda: back.cross(0)],
        22: [lambda: back.cross(1)],
        24: [lambda: back.cross(2), lambda: done(0)],
        26: [lambda: done(1)],
        28: [lambda: done(2)],
        7: [step_norm, last_out],
    }
    steps = iter(range(blocks))
    for tick, many in enumerate((0, 0, 2, 3, 3, 4, 4)):
        beside[tick] = [functools.partial(step_back, next(steps)) for _ in range(many)]

    for load in loads:
        for copy in load():
            copy.start()
    stages = (settle, aside, finish, forward)
    begun, first_piece = 0, min(k for k in range(count) if is_piece(k))
    for tick in range(count + LAGS[-1]):
        for lag, stage in reversed(list(zip(LAGS, stages))):
            if 0 <= tick - lag < count:
                stage(tick - lag)
        while begun < min(count, tick + 1 + max(0, min(AHEAD, tick - 11))):
            if begun == first_piece:
                full_copy().wait()
            begin(begun)
            begun += 1
        for step in beside.get(tick, []):
            step()
    for m in range(back.micro):
        back.end(m)
        go_home(m, grad_states, z >= 0, lambda copy: copy.wait())
    for copy in rest_copies():
        copy.wait_send()
    for load in loads:
        for index, copy in enumerate(load()):
            if index % 2 == 1:
                copy.wait_send()
    for column in range(columns):
        to_sibling("pre", pre_both, column).wait_send()
    to_sibling("branch", branch_both, 0).wait_send()
    for k in direct:
        if base_of(k) in bases[-RING:]:
            across_copy(k).wait_send()
    for k in range(count):
        if is_piece(k):
            for index in range(3):
                piece_copy(k, index).wait_send()

        def ends(role):
            up_copy(k, role).wait_send()
            down_copy(k, role).wait_recv()

        def middle():
            side_copy(k).wait_send()
            down_copy(k, 3).wait_send()

        def owner():
            down_copy(k, 0).wait_send()
            down_copy(k, 2).wait_send()
            keep_copy(k).wait()

        on(k, 0, lambda: ends(0))
        on(k, 3, lambda: ends(3))
        on(k, 2, middle)
        on(k, 1, owner)


def last_pass(weight, ids, gain, inverse_one, rows_low, arrays, weights, operands, size):
    micro, pack, local = arrays[2].shape
    local = local // 3
    tokens, width = operands[3].shape
    hidden = operands[0].shape[1]
    chunks = chunk_list(local, width, hidden)
    count = len(chunks)
    starts, sides_at = starts_of(chunks)
    inside = pl.BlockSpec(memory_space=pltpu.VMEM)
    anywhere = pl.BlockSpec(memory_space=pl.ANY)
    low = lambda *shape: jax.ShapeDtypeStruct(shape, jnp.bfloat16)
    room = lambda *shape: pltpu.VMEM(shape, jnp.bfloat16)
    halves = local // CHUNK
    return pl.pallas_call(
        functools.partial(last_kernel, chunks, size),
        in_specs=[inside] * 6 + [anywhere] * 13,
        out_specs=[anywhere] * 6,
        out_shape=[
            low(micro, pack // 4, width),
            low(local, 3 * width),
            low(local, width),
            low(local, hidden),
            low(hidden // 4, width),
            low(16, width),
        ],
        scratch_shapes=[
            room(tokens, width),
            room(micro * pack, 3 * local),
            room(micro * pack, width),
            room(3, width, local),
            room(hidden // 4 // CHUNK, 2 * tokens, 2 * CHUNK),
            room(halves, 2 * tokens, 2 * CHUNK),
            room(halves, 2 * tokens, 2 * CHUNK),
            room(2 * tokens, width),
            room(2 * tokens, hidden),
            room(2 * tokens, width),
            pltpu.VMEM((2, 16, width), jnp.float32),
            room(starts[count], width),
            room(RING, CHUNK, width),
            room(starts[count], width),
            room(starts[count], width),
            room(max(sides_at[count:]), width),
            pltpu.VMEM((tokens, width), jnp.float32),
            pltpu.VMEM((tokens, width), jnp.float32),
            room(2, tokens, TILE),
            room(pack, 3 * local),
            room(tokens, width),
            pltpu.VMEM((64, width), jnp.float32),
        ]
        + back_scratch(micro, pack, local, width)
        + [pltpu.SemaphoreType.DMA((900,))],
        compiler_params=pltpu.CompilerParams(
            collective_id=1, has_side_effects=True, vmem_limit_bytes=63 * 2**20
        ),
        name="last_pass",
    )(
        weight,
        ids[:, None, :],
        ids[:, :, None],
        gain,
        inverse_one,
        rows_low,
        *arrays,
        *weights,
        *operands,
    )


def relay(boundary, lengths, valid, w_qkv, w_out, w_in, w_down, bias_in, vectors):
    section_at = lax.axis_index("section")
    count_ctx = lax.axis_size("ctx")
    ctx_at = lax.axis_index("ctx")
    wt_at = lax.axis_index("wt")
    micro, rows, width = boundary.shape[1:]
    pack = rows * count_ctx
    size = width // HEADS
    local = width // lax.axis_size("wt")
    tokens = micro * rows
    own_rows = vectors[0].astype(jnp.float32)
    qkv_bias = jnp.concatenate([own_rows[0], jnp.zeros((local,), jnp.float32), own_rows[1]])[None]
    my_lengths = lax.dynamic_index_in_dim(lengths, turned(ctx_at), 1, keepdims=False)
    ends = jnp.cumsum(my_lengths, axis=1)
    stripes = stripe_of(ctx_at, jnp.arange(count_ctx, dtype=jnp.int32))
    places = jnp.arange(rows, dtype=jnp.int32)[None, :] * count_ctx + stripes[:, None]
    ids = jnp.sum((places.reshape(1, pack, 1) >= ends[:, None, :]).astype(jnp.int32), axis=2)
    small = jnp.concatenate([vectors[0], bias_in[0].reshape(-1, local)], axis=0)
    small = jnp.pad(small, ((0, 16 - small.shape[0]), (0, 0)))
    marks = jnp.pad(valid.astype(jnp.float32), ((0, 8 - micro), (0, 0)))
    shards = (w_qkv[0], w_out[0], w_in[0], w_down[0])
    own, weight_qkv, weight_out, weight_in, weight_down, smalls, marks, counts, mixed = first_pass(
        boundary[0], shards, small, marks, qkv_bias, ids, size
    )
    vector_rows = smalls[:, :8].transpose(1, 0, 2).reshape(8, width).astype(jnp.float32)
    in_bias = smalls[:, 8 : 8 + w_in.shape[2] // width].reshape(-1).astype(jnp.float32)
    marks = marks[:micro].reshape(tokens, 1)
    factor = LOSS_SCALE / jnp.sum(counts)
    flat = own.reshape(tokens, width)

    def forward(states, mixed):
        summed = states.astype(jnp.float32) + (dot(mixed, weight_out) + vector_rows[2])
        normal_one, inverse_one = norm_parts(summed)
        first = normal_one * vector_rows[3] + vector_rows[4]
        first_low = first.astype(jnp.bfloat16)
        hidden, slope = gelu_both(dot(first_low, weight_in) + in_bias)
        hidden = lax.optimization_barrier(hidden.astype(jnp.bfloat16))
        second = first + (dot(hidden, weight_down) + vector_rows[5])
        normal_two, inverse_two = norm_parts(second)
        output = normal_two * vector_rows[6] + vector_rows[7]
        slope = slope.astype(jnp.bfloat16)
        return (
            output,
            (normal_one, inverse_one, first_low, hidden, slope, normal_two, inverse_two),
        )

    def backward(grad, kept):
        normal_one, inverse_one, first_low, hidden, slope, normal_two, inverse_two = kept
        grad_second = norm_back(grad, vector_rows[6], normal_two, inverse_two)
        down_low = grad_second.astype(jnp.bfloat16)
        pre_low = (dot(down_low, weight_down, ((1,), (1,))) * slope).astype(jnp.bfloat16)
        pre_low = lax.optimization_barrier(pre_low)
        grad_first = grad_second + dot(pre_low, weight_in, ((1,), (1,)))
        grad_summed = norm_back(grad_first, vector_rows[3], normal_one, inverse_one)
        branch_low = grad_summed.astype(jnp.bfloat16)
        mixed_grad = dot(branch_low, weight_out, ((1,), (1,))).astype(jnp.bfloat16)
        return (mixed_grad, grad_summed, (down_low, pre_low, grad_first, branch_low))

    output, _ = forward(flat, mixed)
    leaving = output.astype(jnp.bfloat16).reshape(micro, rows, width)
    full, qkv, mixed = second_pass(own, leaving, weight_qkv, qkv_bias, ids, size)
    states = lax.dynamic_slice_in_dim(full, wt_at * rows, rows, 1).reshape(tokens, width)
    output, kept = forward(states, mixed)
    cotangent = factor * marks * (output - flat.astype(jnp.float32))
    mixed_grad, skip, _ = backward(cotangent, kept)
    returned = back_pass(mixed_grad, skip, qkv, weight_qkv, ids, size)
    cotangent = jnp.where(section_at == 1, cotangent, returned.astype(jnp.float32))
    normal_one, inverse_one, first_low, hidden, slope, normal_two, inverse_two = kept
    grad_second = norm_back(cotangent, vector_rows[6], normal_two, inverse_two)
    down_low = grad_second.astype(jnp.bfloat16)
    total = lambda values: jnp.sum(values.astype(jnp.float32), axis=0)
    rows_low = jnp.stack([total(down_low), total(cotangent * normal_two), total(cotangent)])
    home, *sums = last_pass(
        weight_qkv,
        ids,
        vector_rows[3:4],
        inverse_one,
        jnp.pad(rows_low, ((5, 0), (0, 0))),
        (grad_second, normal_one, qkv, full.reshape(-1, width), slope),
        (weight_out, weight_in, weight_down),
        (hidden, first_low, mixed, down_low, output.astype(jnp.bfloat16)),
        size,
    )
    sums = [part.astype(jnp.float32)[None] for part in sums]
    rest = sums[4]
    in_rows = w_in.shape[2] // width
    bias_back = rest[:, :in_rows, local : 2 * local].reshape(1, -1)
    return (home[None], *sums[:4], bias_back, rest[:, :8, :local])


def solution(mesh):
    in_specs = (
        P("section", None, ("wt", "ctx"), None),
        P(),
        P(None, ("wt", "ctx")),
        P("section", "wt", None),
        P("section", "wt", None),
        P("section", "wt", None),
        P("section", "wt", None),
        P("section", "wt"),
        P("section", None, "wt"),
    )
    out_specs = (
        P("section", None, ("wt", "ctx"), None),
        P("section", "wt", None),
        P("section", "wt", None),
        P("section", "wt", None),
        P("section", "wt", None),
        P("section", "wt"),
        P("section", None, "wt"),
    )
    square = mesh.shape["ctx"] == mesh.shape["wt"] == 4
    return jax.shard_map(relay if square else shards, mesh=mesh, in_specs=in_specs, out_specs=out_specs, check_vma=False)
```

```python
import functools

import jax
import jax.numpy as jnp
from jax import lax
from jax.experimental import pallas as pl
from jax.experimental.pallas import tpu as pltpu
from jax.sharding import PartitionSpec as P

HEADS = 16
LOSS_SCALE = 1024


def shifted(block, axis, distance):
    devices = range(lax.axis_size(axis))
    route = [(i - distance, i) for i in devices if i - distance in devices]
    return lax.ppermute(block, axis, route)


def as_sent(x):

    def short(part):
        return part.astype(jnp.bfloat16) if part.dtype == jnp.float32 else part

    return jax.tree.map(short, x)


def layer_norm(values, gain, shift):
    center = jnp.mean(values, axis=-1, keepdims=True)
    offset = values - center
    spread = jnp.mean(offset * offset, axis=-1, keepdims=True)
    return offset * lax.rsqrt(spread + 1e-05) * gain + shift


def exact_gelu(values):
    return jax.nn.gelu(values, approximate=False)


def dealt_ids(length_row, pack_size, ctx_count):
    ends = jnp.cumsum(length_row)
    places = jnp.arange(pack_size, dtype=jnp.int32)
    natural = jnp.sum((places[:, None] >= ends[None, :]).astype(jnp.int32), axis=1)
    return natural.reshape(pack_size // ctx_count, ctx_count).T.reshape(pack_size)


def split_blocks(full_kv, ids_keys):
    block = min(512, full_kv.shape[0])
    count_blocks = full_kv.shape[0] // block
    return (
        full_kv.reshape(count_blocks, block, full_kv.shape[1]),
        ids_keys.reshape(count_blocks, block),
    )


def split_kv(block_kv, heads):
    half = block_kv.shape[1] // 2
    keys = block_kv[:, :half].reshape(block_kv.shape[0], heads, -1)
    values = block_kv[:, half:].reshape(block_kv.shape[0], heads, -1)
    return (keys, values)


def block_scores(queries, keys, ids_query, ids_keys, scale):
    scores = jnp.einsum("qhd,khd->hqk", queries, keys, preferred_element_type=jnp.float32) * scale
    same = ids_query[:, None] == ids_keys[None, :]
    return jnp.where(same[None], scores, -1000000000.0)


def attend_forward(queries, full_kv, ids_query, ids_keys, heads, scale):
    blocks, id_blocks = split_blocks(full_kv, ids_keys)
    query_rows = queries.shape[0]

    def total_step(carry, items):
        run_max, run_sum = carry
        keys, values = split_kv(items[0], heads)
        scores = block_scores(queries, keys, ids_query, items[1], scale)
        new_max = jnp.maximum(run_max, jnp.max(scores, axis=-1))
        run_sum = run_sum * jnp.exp(run_max - new_max) + jnp.sum(
            jnp.exp(scores - new_max[..., None]), axis=-1
        )
        return ((new_max, run_sum), None)

    start = (
        jnp.full((heads, query_rows), -1e30, jnp.float32),
        jnp.zeros((heads, query_rows), jnp.float32),
    )
    (run_max, run_sum), _ = lax.scan(total_step, start, (blocks, id_blocks))
    log_total = run_max + jnp.log(run_sum)

    def mix_step(carry, items):
        keys, values = split_kv(items[0], heads)
        scores = block_scores(queries, keys, ids_query, items[1], scale)
        probs = jnp.exp(scores - log_total[..., None]).astype(jnp.bfloat16)
        return (
            carry + jnp.einsum("hqk,khd->qhd", probs, values, preferred_element_type=jnp.float32),
            None,
        )

    mixed, _ = lax.scan(mix_step, jnp.zeros(queries.shape, jnp.float32), (blocks, id_blocks))
    return (mixed.reshape(query_rows, -1), log_total)


def attend_backward(queries, full_kv, ids_query, ids_keys, mixed_grad, log_total, heads, scale):
    blocks, id_blocks = split_blocks(full_kv, ids_keys)
    grad_heads = mixed_grad.reshape(queries.shape)

    def inner_step(carry, items):
        keys, values = split_kv(items[0], heads)
        scores = block_scores(queries, keys, ids_query, items[1], scale)
        probs = jnp.exp(scores - log_total[..., None])
        prob_grad = jnp.einsum(
            "qhd,khd->hqk", grad_heads, values, preferred_element_type=jnp.float32
        )
        return (carry + jnp.sum(probs * prob_grad, axis=-1), None)

    inner, _ = lax.scan(inner_step, jnp.zeros(log_total.shape, jnp.float32), (blocks, id_blocks))

    def grad_step(carry, items):
        keys, values = split_kv(items[0], heads)
        scores = block_scores(queries, keys, ids_query, items[1], scale)
        probs = jnp.exp(scores - log_total[..., None])
        prob_grad = jnp.einsum(
            "qhd,khd->hqk", grad_heads, values, preferred_element_type=jnp.float32
        )
        score_grad = (probs * (prob_grad - inner[..., None])).astype(jnp.bfloat16)
        carry = (
            carry
            + jnp.einsum("hqk,khd->qhd", score_grad, keys, preferred_element_type=jnp.float32)
            * scale
        )
        key_grad = (
            jnp.einsum("hqk,qhd->khd", score_grad, queries, preferred_element_type=jnp.float32)
            * scale
        )
        value_grad = jnp.einsum(
            "hqk,qhd->khd",
            probs.astype(jnp.bfloat16),
            grad_heads,
            preferred_element_type=jnp.float32,
        )
        block = keys.shape[0]
        return (
            carry,
            jnp.concatenate([key_grad.reshape(block, -1), value_grad.reshape(block, -1)], axis=1),
        )

    query_grad, partial_kv = lax.scan(
        grad_step, jnp.zeros(queries.shape, jnp.float32), (blocks, id_blocks)
    )
    query_grad = query_grad.reshape(queries.shape[0], -1)
    return (query_grad, partial_kv.reshape(-1, partial_kv.shape[-1]), inner)


def shards(boundary, lengths, valid, w_qkv, w_out, w_in, w_down, bias_in, vectors):
    section_at = lax.axis_index("section")
    ctx_count = lax.axis_size("ctx")
    ctx_at = lax.axis_index("ctx")
    wt_at = lax.axis_index("wt")
    micro_count = boundary.shape[1]
    row_count = boundary.shape[2]
    width = boundary.shape[3]
    pack_size = row_count * ctx_count
    head_size = width // HEADS
    scale = head_size ** (-0.5)
    gathered = (
        lax.all_gather(w_qkv[0], "wt", axis=0, tiled=True),
        lax.all_gather(w_out[0], "wt", axis=0, tiled=True),
        lax.all_gather(w_in[0], "wt", axis=0, tiled=True),
        lax.all_gather(w_down[0], "wt", axis=0, tiled=True),
        lax.all_gather(bias_in[0], "wt", axis=0, tiled=True),
        lax.all_gather(vectors[0], "wt", axis=1, tiled=True),
    )
    weight_qkv, weight_out, weight_in, weight_down, in_bias, vector_rows = gathered
    in_bias = in_bias.astype(jnp.float32)
    vector_rows = vector_rows.astype(jnp.float32)
    qkv_bias = jnp.concatenate([vector_rows[0], jnp.zeros((width,), jnp.float32), vector_rows[1]])
    my_lengths = lax.dynamic_index_in_dim(lengths, wt_at, 1, keepdims=False)

    def ids_of(length_row):
        return dealt_ids(length_row, pack_size, ctx_count)

    pack_ids = jax.vmap(ids_of)(my_lengths)
    query_ids = lax.dynamic_slice_in_dim(pack_ids, ctx_at * row_count, row_count, 1)
    count = lax.psum(jnp.sum(valid.astype(jnp.float32)), ("ctx", "wt"))
    factor = LOSS_SCALE / count
    empty_rows = jnp.zeros((row_count, width), jnp.bfloat16)
    arriving = empty_rows
    kept_list = []
    cotangents = []
    final_states = []
    for tick_at in range(micro_count + 1):
        own_input = boundary[0, tick_at] if tick_at < micro_count else empty_rows
        inputs = jnp.where(section_at == 0, own_input, arriving)
        micro_here = jnp.clip(tick_at - section_at, 0, micro_count - 1)
        ids_keys = lax.dynamic_index_in_dim(pack_ids, micro_here, 0, keepdims=False)
        ids_query = lax.dynamic_index_in_dim(query_ids, micro_here, 0, keepdims=False)
        residual = inputs.astype(jnp.float32)
        projected = jnp.dot(inputs, weight_qkv, preferred_element_type=jnp.float32) + qkv_bias
        layer_queries = (
            projected[:, :width].astype(jnp.bfloat16).reshape(row_count, HEADS, head_size)
        )
        layer_local_kv = projected[:, width:].astype(jnp.bfloat16)
        layer_full_kv = lax.all_gather(layer_local_kv, "ctx", axis=0, tiled=True)
        mixed, layer_log_total = attend_forward(
            layer_queries, layer_full_kv, ids_query, ids_keys, HEADS, scale
        )
        layer_mixed_low = mixed.astype(jnp.bfloat16)
        branch = (
            jnp.dot(layer_mixed_low, weight_out, preferred_element_type=jnp.float32)
            + vector_rows[2]
        )
        layer_summed = residual + branch
        first = layer_norm(layer_summed, vector_rows[3], vector_rows[4])
        layer_first_low = first.astype(jnp.bfloat16)
        layer_hidden_pre = (
            jnp.dot(layer_first_low, weight_in, preferred_element_type=jnp.float32) + in_bias
        )
        layer_hidden_low = exact_gelu(layer_hidden_pre).astype(jnp.bfloat16)
        layer_second = first + (
            jnp.dot(layer_hidden_low, weight_down, preferred_element_type=jnp.float32)
            + vector_rows[5]
        )
        output = layer_norm(layer_second, vector_rows[6], vector_rows[7])
        layer_kept = (
            inputs,
            layer_queries,
            layer_local_kv,
            layer_full_kv,
            layer_mixed_low,
            layer_log_total,
            layer_summed,
            layer_first_low,
            layer_hidden_pre,
            layer_hidden_low,
            layer_second,
            ids_keys,
            ids_query,
        )
        output, kept = (output, layer_kept)
        kept_list.append(kept)
        if tick_at > 0:
            teacher = boundary[0, tick_at - 1].astype(jnp.float32)
            covered = valid[tick_at - 1].astype(jnp.float32)[:, None]
            cotangents.append(factor * covered * (output - teacher))
            final_states.append(output.astype(jnp.bfloat16))
        else:
            cotangents.append(jnp.zeros((row_count, width), jnp.float32))
        if tick_at < micro_count:
            arriving = shifted(output.astype(jnp.bfloat16), "section", 1)
    returning = empty_rows
    totals = None
    input_grads = [None] * micro_count
    for back_at in range(micro_count + 1):
        forward_at = micro_count - back_at
        grad_output = jnp.where(
            section_at == 1, cotangents[forward_at], returning.astype(jnp.float32)
        )
        (
            layer_inputs,
            queries,
            local_kv,
            full_kv,
            mixed_low,
            log_total,
            summed,
            first_low,
            hidden_pre,
            hidden_low,
            second,
            layer_ids_keys,
            layer_ids_query,
        ) = kept_list[forward_at]
        full_kv = lax.all_gather(local_kv, "ctx", axis=0, tiled=True)
        _, pull_last = jax.vjp(layer_norm, second, vector_rows[6], vector_rows[7])
        grad_second, grad_gain_two, grad_shift_two = pull_last(grad_output)
        down_low = grad_second.astype(jnp.bfloat16)
        layer_grad_down = jnp.einsum(
            "rf,rd->fd", hidden_low, down_low, preferred_element_type=jnp.float32
        )
        grad_bias_two = jnp.sum(down_low.astype(jnp.float32), axis=0)
        _, pull_gelu = jax.vjp(exact_gelu, hidden_pre)
        (grad_pre,) = pull_gelu(
            jnp.einsum("rd,fd->rf", down_low, weight_down, preferred_element_type=jnp.float32)
        )
        pre_low = grad_pre.astype(jnp.bfloat16)
        layer_grad_in = jnp.einsum(
            "rd,rf->df", first_low, pre_low, preferred_element_type=jnp.float32
        )
        layer_grad_bias_in = jnp.sum(pre_low.astype(jnp.float32), axis=0)
        grad_first = grad_second + jnp.einsum(
            "rf,df->rd", pre_low, weight_in, preferred_element_type=jnp.float32
        )
        _, pull_first = jax.vjp(layer_norm, summed, vector_rows[3], vector_rows[4])
        grad_summed, grad_gain_one, grad_shift_one = pull_first(grad_first)
        branch_low = grad_summed.astype(jnp.bfloat16)
        layer_grad_out = jnp.einsum(
            "rd,re->de", mixed_low, branch_low, preferred_element_type=jnp.float32
        )
        grad_bias_out = jnp.sum(branch_low.astype(jnp.float32), axis=0)
        mixed_grad = jnp.einsum(
            "re,de->rd", branch_low, weight_out, preferred_element_type=jnp.float32
        ).astype(jnp.bfloat16)
        query_grad, partial_kv, inner = attend_backward(
            queries, full_kv, layer_ids_query, layer_ids_keys, mixed_grad, log_total, HEADS, scale
        )
        kv_grad = lax.psum_scatter(
            partial_kv.astype(jnp.bfloat16), "ctx", scatter_dimension=0, tiled=True
        )
        query_low = query_grad.astype(jnp.bfloat16)
        projected_grad = jnp.concatenate([query_low, kv_grad], axis=1)
        layer_grad_qkv = jnp.einsum(
            "rd,re->de", layer_inputs, projected_grad, preferred_element_type=jnp.float32
        )
        vector_grad = jnp.stack(
            [
                jnp.sum(query_low.astype(jnp.float32), axis=0),
                jnp.sum(kv_grad[:, width:].astype(jnp.float32), axis=0),
                grad_bias_out,
                grad_gain_one,
                grad_shift_one,
                grad_bias_two,
                grad_gain_two,
                grad_shift_two,
            ]
        )
        grad_inputs = grad_summed + jnp.einsum(
            "re,de->rd", projected_grad, weight_qkv, preferred_element_type=jnp.float32
        )
        grad_inputs, grads = (
            grad_inputs,
            (
                layer_grad_qkv,
                layer_grad_out,
                layer_grad_in,
                layer_grad_down,
                layer_grad_bias_in,
                vector_grad,
            ),
        )
        totals = grads if totals is None else jax.tree.map(jnp.add, totals, grads)
        if forward_at < micro_count:
            input_grads[forward_at] = grad_inputs
        if back_at < micro_count:
            returning = shifted(grad_inputs.astype(jnp.bfloat16), "section", -1)
    results = jnp.stack(
        [
            jnp.where(section_at == 0, input_grads[index].astype(jnp.bfloat16), final_states[index])
            for index in range(micro_count)
        ]
    )[None]
    shares = (
        lax.psum_scatter(
            totals[0].astype(jnp.bfloat16), "wt", scatter_dimension=0, tiled=True
        ).astype(jnp.float32),
        lax.psum_scatter(
            totals[1].astype(jnp.bfloat16), "wt", scatter_dimension=0, tiled=True
        ).astype(jnp.float32),
        lax.psum_scatter(
            totals[2].astype(jnp.bfloat16), "wt", scatter_dimension=0, tiled=True
        ).astype(jnp.float32),
        lax.psum_scatter(
            totals[3].astype(jnp.bfloat16), "wt", scatter_dimension=0, tiled=True
        ).astype(jnp.float32),
        lax.psum_scatter(
            totals[4].astype(jnp.bfloat16), "wt", scatter_dimension=0, tiled=True
        ).astype(jnp.float32),
        lax.psum_scatter(
            totals[5].astype(jnp.bfloat16), "wt", scatter_dimension=1, tiled=True
        ).astype(jnp.float32),
    )
    shares = jax.tree.map(lambda part: part.astype(jnp.float32), lax.psum(as_sent(shares), "ctx"))
    grad_qkv, grad_out, grad_in, grad_down, grad_bias_in, grad_vectors = shares
    return (
        results,
        grad_qkv[None],
        grad_out[None],
        grad_in[None],
        grad_down[None],
        grad_bias_in[None],
        grad_vectors[None],
    )


PAIR = 128
FAR = -1000000000.0
MESH = pl.DeviceIdType.MESH


def dot(left, right, dims=((1,), (0,))):
    return lax.dot_general(left, right, (dims, ((), ())), preferred_element_type=jnp.float32)


def head_lanes(size):
    lane = lax.broadcasted_iota(jnp.int32, (1, PAIR), 1)
    return [lane // size == index for index in range(PAIR // size)]


def only(mask, values):
    return jnp.where(mask, values, jnp.zeros_like(values))


def normal_tail(values):
    size = jnp.abs(values)
    bell = jnp.exp(-0.5 * values * values)
    t = 1.0 / (1.0 + 0.3275911 * (2.0**-0.5) * size)
    poly = t * (
        0.254829592
        + t * (-0.284496736 + t * (1.421413741 + t * (-1.453152027 + t * 1.061405429)))
    )
    tail = 0.5 * poly * bell
    return (jnp.where(values >= 0, 1.0 - tail, tail), bell)


def gelu_both(values):
    below, bell = normal_tail(values)
    return (values * below, below + values * bell * 0.3989422804014327)


def norm_parts(values):
    center = jnp.mean(values, axis=-1, keepdims=True)
    offset = values - center
    spread = jnp.mean(offset * offset, axis=-1, keepdims=True)
    inverse = lax.rsqrt(spread + 1e-05)
    return (offset * inverse, inverse)


def norm_back(grad, gain, normal, inverse):
    inner = grad * gain
    mean = jnp.mean(inner, axis=-1, keepdims=True)
    along = jnp.mean(inner * normal, axis=-1, keepdims=True)
    return inverse * (inner - mean - normal * along)


class Wires:
    def __init__(self, sems):
        self.sems = sems
        self.places = {}

    def at(self, *key):
        return self.sems.at[self.places.setdefault(key, len(self.places))]

    def remote(self, key, source, target, **where):
        return pltpu.make_async_remote_copy(
            source,
            target,
            self.at(key, "send"),
            self.at(key, "recv"),
            device_id=where,
            device_id_type=MESH,
        )

    def local(self, key, source, target):
        return pltpu.make_async_copy(source, target, self.at(key, "local"))


def wt_places():
    w = lax.axis_index("wt")
    core = lax.rem(w, 2)
    sibling = w + 1 - 2 * core
    across = lax.rem(w + 2, 4)
    return w, sibling, across, lax.rem(sibling + 2, 4)


def turned(place):
    return 2 * lax.rem(place, 2) + place // 2


def stripe_of(z, w):
    return 2 * lax.rem(w, 2) + lax.rem(w // 2 + z, 2)


def plane_place(z, w):
    plane = turned(w)
    return dict(ctx=plane, wt=2 * lax.rem(z + plane, 2) + z // 2)


def home_place(z, w):
    return dict(ctx=stripe_of(z, w), wt=turned(z))


def is_moving(z, w):
    place = home_place(z, w)
    return (place["ctx"] != z) | (place["wt"] != w)


def greet(partners, extra, meanwhile=lambda: None):
    barrier = pltpu.get_barrier_semaphore()
    for partner in partners:
        pl.semaphore_signal(barrier, 1, device_id=partner, device_id_type=MESH)
    waits = len(partners)
    for here, partner in extra:

        @pl.when(here)
        def _():
            pl.semaphore_signal(barrier, 1, device_id=partner, device_id_type=MESH)

        waits = waits + here.astype(jnp.int32)
    meanwhile()
    pl.semaphore_wait(barrier, waits)


def attend_pack(size, same, qkv, mixed):
    local = mixed.shape[1]
    masks = head_lanes(size)
    for pair in range(local // PAIR):
        at = pair * PAIR
        q = qkv[:, at : at + PAIR] * jnp.bfloat16(size**-0.5)
        k = qkv[:, local + at : local + at + PAIR]
        v = qkv[:, 2 * local + at : 2 * local + at + PAIR]
        total = None
        for mask in masks:
            scores = jnp.where(same, dot(only(mask, k), q, ((1,), (1,))), FAR)
            probs = jnp.exp(scores - jnp.max(scores, axis=0, keepdims=True))
            scale = 1.0 / jnp.sum(probs, axis=0, keepdims=True)
            low = (probs * scale).astype(jnp.bfloat16)
            term = dot(only(mask, v), low, ((0,), (0,)))
            total = term if total is None else total + term
        mixed[:, at : at + PAIR] = total.T.astype(jnp.bfloat16)


def attend_pack_back(size, same, qkv, grad_heads, projected_grad):
    local = grad_heads.shape[1]
    masks = head_lanes(size)
    for pair in range(local // PAIR):
        at = pair * PAIR
        q = qkv[:, at : at + PAIR] * jnp.bfloat16(size**-0.5)
        k = qkv[:, local + at : local + at + PAIR]
        v = qkv[:, 2 * local + at : 2 * local + at + PAIR]
        grad = grad_heads[:, at : at + PAIR]
        totals = [None] * 3
        for mask in masks:
            own_k = only(mask, k)
            scores = jnp.where(same, dot(own_k, q, ((1,), (1,))), FAR)
            probs = jnp.exp(scores - jnp.max(scores, axis=0, keepdims=True))
            probs = probs * (1.0 / jnp.sum(probs, axis=0, keepdims=True))
            prob_grad = dot(only(mask, v), grad, ((1,), (1,)))
            inner = jnp.sum(probs * prob_grad, axis=0, keepdims=True)
            score_grad = (probs * (prob_grad - inner)).astype(jnp.bfloat16)
            terms = (
                dot(own_k, score_grad, ((0,), (0,))),
                dot(score_grad, only(mask, q)),
                dot(probs.astype(jnp.bfloat16), only(mask, grad)),
            )
            totals = [t if o is None else o + t for o, t in zip(totals, terms)]
        query_grad = totals[0].T * size**-0.5
        projected_grad[:, at : at + PAIR] = query_grad.astype(jnp.bfloat16)
        projected_grad[:, local + at : local + at + PAIR] = totals[1].astype(jnp.bfloat16)
        projected_grad[:, 2 * local + at : 2 * local + at + PAIR] = totals[2].astype(jnp.bfloat16)


class Spread:
    def __init__(self, wires, full, mixed, mixed_rows, rows, local):
        self.wires, self.full, self.mixed, self.mixed_rows = wires, full, mixed, mixed_rows
        self.rows, self.local = rows, local
        self.w, self.sibling, self.across, self.across_sibling = wt_places()

    def stripe(self, m, j):
        return self.full.at[m, pl.ds(j * self.rows, self.rows), :]

    def to_sibling(self, m):
        own = self.stripe(m, self.w)
        return self.wires.remote(("sibling", m), own, own, wt=self.sibling)

    def to_across(self, m):
        own = self.stripe(m, self.w)
        return self.wires.remote(("across", m), own, own, wt=self.across)

    def passed(self, m):
        block = self.stripe(m, self.across)
        return self.wires.remote(("passed", m), block, block, wt=self.sibling)

    def send(self, m):
        self.to_across(m).start()
        self.to_sibling(m).start()

    def hand_on(self, m):
        self.to_across(m).wait_recv()
        self.passed(m).start()

    def settle(self, m):
        self.to_sibling(m).wait_recv()
        self.passed(m).wait_recv()

    def back(self, m):
        heads = pl.ds(self.w * self.local, self.local)
        target = self.mixed_rows.at[pl.ds(m * self.rows, self.rows), heads]
        for index, partner in enumerate((self.across, self.across_sibling, self.sibling)):
            block = self.mixed.at[m, pl.ds(partner * self.rows, self.rows), :]
            yield self.wires.remote(("back", m, index), block, target, wt=partner)

    def send_back(self, m):
        for copy in self.back(m):
            copy.start()
        self.own_back(m).start()

    def own_back(self, m):
        heads = pl.ds(self.w * self.local, self.local)
        return self.wires.local(
            ("back", m),
            self.mixed.at[m, pl.ds(self.w * self.rows, self.rows), :],
            self.mixed_rows.at[pl.ds(m * self.rows, self.rows), heads],
        )

    def arrived_back(self, m):
        for copy in self.back(m):
            copy.wait_recv()
        self.own_back(m).wait()

    def end(self, m):
        for copy in (self.to_sibling(m), self.to_across(m), self.passed(m)):
            copy.wait_send()
        for copy in self.back(m):
            copy.wait_send()


def project(full, weight, bias, qkv):
    qkv[...] = (dot(full[...], weight[...]) + bias[...]).astype(jnp.bfloat16)


BLOCK = 512


def feed_start(states, mixed, weight_out, rows):
    summed = states.astype(jnp.float32) + (dot(mixed, weight_out) + rows[2:3, :])
    normal, inverse = norm_parts(summed)
    return normal, inverse, normal * rows[3:4, :] + rows[4:5, :]


def feed_forward(at, states, mixed, weights, rows, in_bias, kept):
    weight_out, weight_in, weight_down = weights
    normal, inverse, first = feed_start(states, mixed, weight_out[...], rows)
    kept["normal_one"][at, :] = normal
    kept["inverse_one"][at, :] = inverse
    low = first.astype(jnp.bfloat16)
    kept["first"][at, :] = low
    total = first + rows[5:6, :]
    for column in range(0, weight_in.shape[1], BLOCK):
        columns = pl.ds(column, BLOCK)
        hidden, slope = gelu_both(dot(low, weight_in[:, columns]) + in_bias[:, columns])
        hidden = hidden.astype(jnp.bfloat16)
        kept["hidden"][at, columns] = hidden
        kept["slope"][at, columns] = slope.astype(jnp.bfloat16)
        total = total + dot(hidden, weight_down[columns, :])
    normal, inverse = norm_parts(total)
    kept["normal_two"][at, :] = normal
    kept["inverse_two"][at, :] = inverse
    return normal * rows[6:7, :] + rows[7:8, :]


def feed_backward(at, grad, weights, rows, kept):
    weight_out, weight_in, weight_down = weights
    total = norm_back(grad, rows[6:7, :], kept["normal_two"][at, :], kept["inverse_two"][at, :])
    low = total.astype(jnp.bfloat16)
    for column in range(0, weight_in.shape[1], BLOCK):
        columns = pl.ds(column, BLOCK)
        inner = dot(low, weight_down[columns, :], ((1,), (1,)))
        inner = (inner * kept["slope"][at, columns].astype(jnp.float32)).astype(jnp.bfloat16)
        total = total + dot(inner, weight_in[:, columns], ((1,), (1,)))
    total = norm_back(total, rows[3:4, :], kept["normal_one"][at, :], kept["inverse_one"][at, :])
    branch = total.astype(jnp.bfloat16)
    return total, dot(branch, weight_out[...], ((1,), (1,))).astype(jnp.bfloat16)


def first_kernel(size, *refs):
    block, shard_qkv, shard_out, shard_in, shard_down, small, marks, bias = refs[:8]
    ids_row, ids_col = refs[8:10]
    own, weight, kept_out, kept_in, kept_down, layer_rows, in_bias, own_marks, count = refs[10:19]
    leaving, full, qkv, mixed, marks_wt, marks_ctx = refs[19:25]
    whole_out, whole_in, whole_down, smalls, mixed_rows, first, inner, total, sems = refs[25:]
    micro, rows, width = block.shape
    local = small.shape[1]
    hidden = shard_in.shape[1]
    half = local // 2
    deep = shard_down.shape[0] // 8
    wires = Wires(sems)
    z = lax.axis_index("ctx")
    spread = Spread(wires, full, mixed, mixed_rows, rows, local)
    w, sibling, across, across_sibling = wt_places()
    partners = (across, across_sibling, sibling)
    level = lax.rem(z, 2)
    neighbor = z + 1 - 2 * level
    moves, place = is_moving(z, w), plane_place(z, w)
    others = [lax.rem(z + step, 4) for step in (1, 2, 3)]
    greet(
        [{"wt": partner} for partner in partners] + [{"ctx": other} for other in others],
        [(moves, place), (moves, home_place(z, w))],
    )

    def swap(m):
        return wires.remote(
            ("swap", m), block.at[m], spread.stripe(m, place["wt"]), **place
        )

    def stay(m):
        return wires.local(("stay", m), block.at[m], spread.stripe(m, w))

    def swap_marks():
        return wires.remote("swap marks", marks, own_marks, **place)

    def head_copy(part, index):
        column = part * width + partners[index] * local
        return wires.remote(
            ("heads", part, index),
            shard_qkv.at[:, pl.ds(column, local)],
            weight.at[pl.ds(w * local, local), pl.ds(part * local, local)],
            wt=partners[index],
        )

    def head_own(part):
        return wires.local(
            ("heads", part),
            shard_qkv.at[:, pl.ds(part * width + w * local, local)],
            weight.at[pl.ds(w * local, local), pl.ds(part * local, local)],
        )

    def small_copy(index):
        return wires.remote(("small", index), small, smalls.at[w], wt=partners[index])

    def marks_copy(index):
        return wires.remote(("marks", index), marks, marks_wt.at[index], wt=partners[index])

    def count_copy(index):
        return wires.remote(("count", index), count, marks_ctx.at[index], ctx=others[index])

    columns = hidden // width
    chunks = 1 + columns + 4

    def piece(k, level):
        if k == 0:
            return shard_out, whole_out, local, level * half, half, 0
        if k <= columns:
            return shard_in, whole_in, local, level * half, half, (k - 1) * width
        at = (level * 4 + k - 1 - columns) * deep
        return shard_down, whole_down, 4 * deep * 2, at, deep, 0

    def from_shard(k, level):
        shard, _, _, at, size, column = piece(k, level)
        return shard.at[pl.ds(at, size), pl.ds(column, width)]

    def in_whole(k, level, j):
        _, whole, stride, at, size, column = piece(k, level)
        return whole.at[pl.ds(j * stride + at, size), pl.ds(column, width)]

    def y_copy(k):
        return wires.remote(
            ("y", k), from_shard(k, level), in_whole(k, level, w), wt=across
        )

    def z_copy(k):
        block = in_whole(k, level, across)
        return wires.remote(("z", k), block, block, ctx=neighbor)

    def core_copy(k, side):
        block = in_whole(k, level if side == 0 else 1 - level, across)
        return wires.remote(("core", k, side), block, block, wt=sibling)

    def shard_sibling(index):
        shard, whole = ((shard_out, whole_out), (shard_in, whole_in), (shard_down, whole_down))[
            index
        ]
        size = shard.shape[0]
        return wires.remote(
            ("shard", index), shard, whole.at[pl.ds(w * size, size), :], wt=sibling
        )

    def shard_own(index):
        shard, whole = ((shard_out, whole_out), (shard_in, whole_in), (shard_down, whole_down))[
            index
        ]
        size = shard.shape[0]
        return wires.local(("shard", index), shard, whole.at[pl.ds(w * size, size), :])

    def shard_ready(index):
        shard_own(index).wait()
        shard_sibling(index).wait_recv()

    @pl.when(moves)
    def _():
        swap(0).start()
        swap_marks().start()

    @pl.when(jnp.logical_not(moves))
    def _():
        for m in range(micro):
            stay(m).start()
        own_marks[...] = marks[...]

    for part in range(3):
        for index in range(3):
            head_copy(part, index).start()
        head_own(part).start()
    for index in range(3):
        small_copy(index).start()
        marks_copy(index).start()
    smalls[w] = small[...]

    def arrive(m):
        @pl.when(moves)
        def _():
            swap(m).wait_recv()

        @pl.when(jnp.logical_not(moves))
        def _():
            stay(m).wait()

    def own_copy(m):
        return wires.local(("own", m), spread.stripe(m, w), own.at[m])

    @pl.when(moves)
    def _():
        swap(0).wait_send()
        for m in range(1, micro):
            swap(m).start()

    for m in range(micro):
        arrive(m)
        spread.send(m)
        own_copy(m).start()
    for k in range(micro):
        y_copy(k).start()
    for index in range(3):
        shard_sibling(index).start()
        shard_own(index).start()
    for index in range(3):
        marks_copy(index).wait_recv()
    count[...] = marks[...] + marks_wt[0] + marks_wt[1] + marks_wt[2]
    for index in range(3):
        count_copy(index).start()
    for part in range(3):
        for index in range(3):
            head_copy(part, index).wait_recv()
        head_own(part).wait()
    def passing(k):
        y_copy(k).wait_recv()
        if k + micro < chunks:
            y_copy(k + micro).start()
        z_copy(k).start()
        core_copy(k, 0).start()

    def passed(k):
        z_copy(k).wait_recv()
        core_copy(k, 1).start()

    def stored(k):
        if k == 0:
            return [wires.local(("stored", k), whole_out, kept_out)]
        if k <= columns:
            at = pl.ds((k - 1) * width, width)
            return [wires.local(("stored", k), whole_in.at[:, at], kept_in.at[:, at])]
        return [
            wires.local(("stored", k, row), whole_down.at[at, :], kept_down.at[at, :])
            for row, at in pair_rows(k)
        ]

    def pair_rows(k):
        if (k - columns) % 2 == 1:
            return []
        first_row = (k - 2 - columns) * deep
        return [
            (row, pl.ds(row, 2 * deep)) for row in range(first_row, hidden, 4 * deep)
        ]

    def compute(k):
        core_copy(k, 0).wait_recv()
        core_copy(k, 1).wait_recv()
        if k == 0:
            shard_ready(0)
            for m in range(micro):
                spread.arrived_back(m)
            states = [spread.stripe(m, w)[...] for m in range(micro)]
            states = jnp.concatenate(states, axis=0)
            values = feed_start(states, mixed_rows[...], whole_out[...], layer_rows)[2]
            first[...] = values.astype(jnp.bfloat16)
            total[...] = values + layer_rows[5:6, :]
        elif k <= columns:
            if k == 1:
                shard_ready(1)
            for column in range((k - 1) * width, k * width, BLOCK):
                at = pl.ds(column, BLOCK)
                values = gelu_both(dot(first[...], whole_in[:, at]) + in_bias[:, at])[0]
                inner[:, at] = values.astype(jnp.bfloat16)
        else:
            if k == columns + 1:
                shard_ready(2)
            for _, at in pair_rows(k):
                total[...] += dot(inner[:, at], whole_down[at, :])
        for copy in stored(k):
            copy.start()

    for index in range(3):
        small_copy(index).wait_recv()
    for j in range(4):
        at = pl.ds(j * local, local)
        layer_rows[:, at] = smalls[j, :8, :].astype(jnp.float32)
        for row in range(columns):
            at = pl.ds(j * 8 * deep + row * local, local)
            in_bias[:, at] = smalls[j, 8 + row : 9 + row, :].astype(jnp.float32)
    for m in range(micro):
        spread.hand_on(m)
        spread.settle(m)
        project(full.at[m], weight, bias, qkv.at[0])
        attend_pack(size, ids_col[m] == ids_row[m], qkv.at[0], mixed.at[m])
        spread.send_back(m)
        passing(m)
    passed(0)
    for k in range(micro, chunks):
        passing(k)
        passed(k - 2)
        if k >= micro + 2:
            compute(k - micro - 2)
    passed(chunks - 2)
    for k in range(chunks - micro - 2, chunks):
        if k == chunks - 2:
            passed(chunks - 1)
        compute(k)
    values = norm_parts(total[...])[0] * layer_rows[6:7, :] + layer_rows[7:8, :]
    leaving[...] = values.astype(jnp.bfloat16)
    for index in range(3):
        count_copy(index).wait()
    count[...] = count[...] + marks_ctx[0] + marks_ctx[1] + marks_ctx[2]
    for m in range(micro):
        spread.end(m)
        own_copy(m).wait()
    for part in range(3):
        for index in range(3):
            head_copy(part, index).wait_send()
    for index in range(3):
        small_copy(index).wait_send()
        marks_copy(index).wait_send()
        shard_sibling(index).wait_send()
    for k in range(chunks):
        y_copy(k).wait_send()
        z_copy(k).wait_send()
        for side in range(2):
            core_copy(k, side).wait_send()
        for copy in stored(k):
            copy.wait()

    @pl.when(moves)
    def _():
        for m in range(1, micro):
            swap(m).wait_send()
        swap_marks().wait()


def first_pass(block, shards, small, marks, bias, ids, size):
    micro, rows, width = block.shape
    local = small.shape[1]
    pack = ids.shape[1]
    tokens, hidden = micro * rows, shards[2].shape[1]
    anywhere = pl.BlockSpec(memory_space=pl.ANY)
    inside = pl.BlockSpec(memory_space=pltpu.VMEM)
    low = lambda *shape: jax.ShapeDtypeStruct(shape, jnp.bfloat16)
    word = lambda *shape: jax.ShapeDtypeStruct(shape, jnp.float32)
    room = lambda *shape: pltpu.VMEM(shape, jnp.bfloat16)
    return pl.pallas_call(
        functools.partial(first_kernel, size),
        in_specs=[anywhere] * 5 + [inside] * 5,
        out_specs=[anywhere, inside] + [anywhere] * 3 + [inside] * 5,
        out_shape=[
            low(micro, rows, width),
            low(width, 3 * local),
            low(width, width),
            low(width, hidden),
            low(hidden, width),
            word(8, width),
            word(1, hidden),
            word(*marks.shape),
            word(*marks.shape),
            low(tokens, width),
        ],
        scratch_shapes=[
            room(micro, pack, width),
            room(1, pack, 3 * local),
            room(micro, pack, local),
            pltpu.VMEM((3,) + marks.shape, jnp.float32),
            pltpu.VMEM((3,) + marks.shape, jnp.float32),
            room(width, width),
            room(width, hidden),
            room(hidden, width),
            room(4, *small.shape),
            room(tokens, width),
            room(tokens, width),
            room(tokens, hidden),
            pltpu.VMEM((tokens, width), jnp.float32),
            pltpu.SemaphoreType.DMA((320,)),
        ],
        compiler_params=pltpu.CompilerParams(
            collective_id=2, has_side_effects=True, vmem_limit_bytes=60 * 2**20
        ),
        name="first_pass",
    )(block, *shards, small, marks, bias, ids[:, None, :], ids[:, :, None])


class Back:
    def __init__(self, wires, size, refs):
        self.wires, self.size = wires, size
        self.rows_grad, self.skip, self.qkv, self.weight, self.ids = refs[:5]
        self.projected, self.grad_states = refs[5:7]
        self.heads_grad, self.part, self.from_sibling, self.far, self.from_across = refs[7:]
        self.micro, self.pack, self.local = self.heads_grad.shape
        self.rows = self.pack // 4
        self.w, self.sibling, self.across, self.across_sibling = wt_places()
        self.partners = (self.across, self.across_sibling, self.sibling)

    def place(self, m):
        return pl.ds(m * self.rows, self.rows)

    def heads_copy(self, m, index):
        column = pl.ds(self.partners[index] * self.local, self.local)
        return self.wires.remote(
            ("heads", m, index),
            self.rows_grad.at[self.place(m), column],
            self.heads_grad.at[m, pl.ds(self.w * self.rows, self.rows), :],
            wt=self.partners[index],
        )

    def heads_own(self, m):
        return self.wires.local(
            ("heads", m),
            self.rows_grad.at[self.place(m), pl.ds(self.w * self.local, self.local)],
            self.heads_grad.at[m, pl.ds(self.w * self.rows, self.rows), :],
        )

    def stripe(self, m, j):
        return self.part.at[m, pl.ds(j * self.rows, self.rows), :]

    def sibling_copy(self, m, index):
        j = (self.across_sibling, self.sibling)[index]
        return self.wires.remote(
            ("to sibling", m, index),
            self.stripe(m, j),
            self.from_sibling.at[m, index],
            wt=self.sibling,
        )

    def across_copy(self, m):
        return self.wires.remote(
            ("to across", m), self.far.at[m], self.from_across.at[m], wt=self.across
        )

    def begin(self, m):
        for index in range(3):
            self.heads_copy(m, index).start()
        self.heads_own(m).start()

    def arrive(self, m):
        for index in range(3):
            self.heads_copy(m, index).wait_recv()
        self.heads_own(m).wait()

    def work(self, m, following=None):
        self.arrive(m)
        if following is not None:
            self.begin(following)
        ids_row, ids_col = self.ids
        whole = pl.ds(m * self.pack, self.pack)
        projected = self.projected.at[whole, :]
        same = ids_col[m] == ids_row[m]
        qkv = self.qkv(m)
        attend_pack_back(self.size, same, qkv, self.heads_grad.at[m], projected)
        product = dot(projected[...], self.weight[...], ((1,), (1,)))
        self.part[m] = product.astype(jnp.bfloat16)
        for index in range(2):
            self.sibling_copy(m, index).start()

    def cross(self, m):
        for index in range(2):
            self.sibling_copy(m, index).wait_recv()
        total = self.stripe(m, self.across)[...].astype(jnp.float32)
        total = total + self.from_sibling[m, 0].astype(jnp.float32)
        self.far[m] = total.astype(jnp.bfloat16)
        self.across_copy(m).start()

    def finish(self, m):
        self.across_copy(m).wait_recv()
        total = self.skip[self.place(m), :] + self.stripe(m, self.w)[...].astype(jnp.float32)
        total = total + self.from_sibling[m, 1].astype(jnp.float32)
        total = total + self.from_across[m].astype(jnp.float32)
        self.grad_states[self.place(m), :] = total.astype(jnp.bfloat16)

    def end(self, m):
        for index in range(3):
            self.heads_copy(m, index).wait_send()
        for index in range(2):
            self.sibling_copy(m, index).wait_send()
        self.across_copy(m).wait_send()


def back_scratch(micro, pack, local, width):
    block = pltpu.VMEM((micro, pack // 4, width), jnp.bfloat16)
    return [
        pltpu.VMEM((micro, pack, local), jnp.bfloat16),
        pltpu.VMEM((micro, pack, width), jnp.bfloat16),
        pltpu.VMEM((micro, 2, pack // 4, width), jnp.bfloat16),
        block,
        block,
    ]


def swap_back(wires, rows, source, target, m, moves):
    z, w = lax.axis_index("ctx"), lax.axis_index("wt")
    block = source.at[pl.ds(m * rows, rows), :]
    if moves:
        return wires.remote(("home", m), block, target.at[m], **home_place(z, w))
    return wires.local(("home", m), block, target.at[m])


def mid_kernel(size, *refs):
    states, leaving, weight_out, weight_in, weight_down = refs[:5]
    weight, bias, ids_row, ids_col, layer_rows, in_bias, covered = refs[5:12]
    outs = refs[12:22]
    inverse_one, inverse_two, returned = refs[22:25]
    held = refs[25:28]
    full, qkv, mixed_rows, mixed = refs[28:32]
    saved = dict(zip(SAVED, refs[32:39]))
    skip, rows_grad, projected, grad_states = refs[39:43]
    micro, rows, width = states.shape
    wires = Wires(refs[-1])
    section = lax.axis_index("section")
    spread = Spread(wires, full, mixed, mixed_rows, rows, weight.shape[1] // 3)
    given = (rows_grad, skip, lambda m: qkv.at[m], weight, (ids_row, ids_col))
    back = Back(wires, size, given + (projected, grad_states) + refs[43:-1])
    w = spread.w
    kept = dict(saved, inverse_one=inverse_one, inverse_two=inverse_two)

    def stay(m):
        return wires.local(("stay", m), states.at[m], spread.stripe(m, w))

    def teacher_copy(m):
        return wires.local(("teacher", m), states.at[m], grad_states.at[pl.ds(m * rows, rows), :])

    def weight_copies():
        for index, source in enumerate((weight_out, weight_in, weight_down)):
            yield wires.local(("weight", index), source, held[index])

    def own_loads():
        @pl.when(section == 0)
        def _():
            for m in range(micro):
                stay(m).start()

        for copy in weight_copies():
            copy.start()
        for m in range(micro):
            teacher_copy(m).start()

    greet(
        [{"wt": partner} for partner in back.partners] + [{"section": 1 - section}],
        [],
        own_loads,
    )

    def relay_copy(m):
        return wires.remote(("relay", m), leaving.at[m], spread.stripe(m, w), section=1 - section)

    @pl.when(section == 0)
    def _():
        for m in range(micro):
            relay_copy(m).start()

    def arrive(m):
        @pl.when(section == 0)
        def _():
            stay(m).wait()

        @pl.when(section == 1)
        def _():
            relay_copy(m).wait_recv()

        spread.send(m)

    def attend(m):
        spread.settle(m)
        project(full.at[m], weight, bias, qkv.at[m])
        attend_pack(size, ids_col[m] == ids_row[m], qkv.at[m], mixed.at[m])
        spread.send_back(m)
        for name, source in (("full", full), ("qkv", qkv)):
            store(name, m, source.at[m], outs[OUTS.index(name)].at[m]).start()

    def store(name, m, source, target):
        return wires.local(("store", name, m), source, target)

    def stores(m):
        at = pl.ds(m * rows, rows)
        for name, ref in [("mixed", mixed_rows)] + list(saved.items()):
            yield store(name, m, ref.at[at, :], outs[OUTS.index(name)].at[at, :])

    def feed(m):
        spread.arrived_back(m)
        at = pl.ds(m * rows, rows)
        block = spread.stripe(m, w)[...]
        output = feed_forward(at, block, mixed_rows[at, :], held, layer_rows, in_bias, kept)
        saved["final"][at, :] = output.astype(jnp.bfloat16)
        teacher_copy(m).wait()
        teacher = grad_states[at, :].astype(jnp.float32)
        grad = covered[at, :] * (output - teacher)
        saved["grad"][at, :] = grad
        skip[at, :], rows_grad[at, :] = feed_backward(at, grad, held, layer_rows, kept)
        for copy in stores(m):
            copy.start()
        back.begin(m)

    def back_copy(m):
        place = back.place(m)
        return wires.remote(
            ("return", m), grad_states.at[place, :], returned.at[place, :], section=1 - section
        )

    def finish(m):
        back.finish(m)

        @pl.when(section == 1)
        def _():
            back_copy(m).start()

    arrive(0)
    arrive(1)
    spread.hand_on(0)
    attend(0)
    arrive(2)
    spread.hand_on(1)
    attend(1)
    spread.hand_on(2)
    for copy in weight_copies():
        copy.wait()
    feed(0)
    attend(2)
    feed(1)
    back.work(0)
    back.cross(0)
    feed(2)
    back.work(1)
    back.cross(1)
    finish(0)
    back.work(2)
    back.cross(2)
    finish(1)
    finish(2)
    for m in range(micro):
        spread.end(m)
        back.end(m)
        for name, source in (("full", full), ("qkv", qkv)):
            store(name, m, source.at[m], outs[OUTS.index(name)].at[m]).wait()
        for copy in stores(m):
            copy.wait()

        @pl.when(section == 1)
        def _():
            back_copy(m).wait_send()

        @pl.when(section == 0)
        def _():
            relay_copy(m).wait_send()
            back_copy(m).wait_recv()


SAVED = ("normal_one", "first", "hidden", "slope", "normal_two", "final", "grad")
OUTS = ("full", "qkv", "mixed") + SAVED


def mid_pass(states, leaving, weights, weight, bias, ids, layer_rows, in_bias, covered, size):
    micro, rows, width = states.shape
    local = weight.shape[1] // 3
    pack = ids.shape[1]
    tokens, hidden = micro * rows, weights[1].shape[1]
    anywhere = pl.BlockSpec(memory_space=pl.ANY)
    inside = pl.BlockSpec(memory_space=pltpu.VMEM)
    low = lambda *shape: jax.ShapeDtypeStruct(shape, jnp.bfloat16)
    word = lambda *shape: jax.ShapeDtypeStruct(shape, jnp.float32)
    held = [
        word(tokens, width),
        low(tokens, width),
        low(tokens, hidden),
        low(tokens, hidden),
        word(tokens, width),
        low(tokens, width),
        word(tokens, width),
    ]
    room = lambda shape: pltpu.VMEM(shape.shape, shape.dtype)
    kept = [low(micro, pack, width), low(micro, pack, 3 * local), low(tokens, width)]
    *results, inverse_one, inverse_two, returned = pl.pallas_call(
        functools.partial(mid_kernel, size),
        in_specs=[anywhere] * 5 + [inside] * 7,
        out_specs=[anywhere] * 10 + [inside] * 3,
        out_shape=kept + held + [word(tokens, 1), word(tokens, 1), low(tokens, width)],
        scratch_shapes=[pltpu.VMEM(part.shape, jnp.bfloat16) for part in weights]
        + [room(shape) for shape in kept]
        + [room(low(micro, pack, local))]
        + [room(shape) for shape in held]
        + [
            room(word(tokens, width)),
            room(low(tokens, width)),
            room(low(micro * pack, 3 * local)),
            room(low(tokens, width)),
        ]
        + back_scratch(micro, pack, local, width)
        + [pltpu.SemaphoreType.DMA((200,))],
        compiler_params=pltpu.CompilerParams(
            collective_id=4, has_side_effects=True, vmem_limit_bytes=62 * 2**20
        ),
        name="mid_pass",
    )(
        states,
        leaving,
        *weights,
        weight,
        bias,
        ids[:, None, :],
        ids[:, :, None],
        layer_rows,
        in_bias,
        covered,
    )
    return dict(zip(OUTS, results)), inverse_one, inverse_two, returned


CHUNK = 128
RING = 6
TILE = 256
LAGS = (2, 4, 6, 8)
AHEAD = 4


def sum_into(target, parts, rows):
    step = 16

    def one(index, carry):
        at = pl.ds(pl.multiple_of(index * step, step), step)
        total = parts[0][at, :].astype(jnp.float32)
        for part in parts[1:]:
            total = total + part[at, :].astype(jnp.float32)
        target[at, :] = total.astype(jnp.bfloat16)
        return carry

    lax.fori_loop(0, rows // step, one, 0)


def chunk_list(local, width, hidden):
    down = [("down", 0, CHUNK // 4, 0), ("down", CHUNK // 4, CHUNK // 4, 0)]
    down += [("down", CHUNK // 2, CHUNK // 2, 0)]
    down += [("down", row, CHUNK, 0) for row in range(CHUNK, hidden // 4, CHUNK)]
    across = [
        ("in", row, CHUNK, column)
        for column in range(hidden // width)
        for row in range(0, local, CHUNK)
    ]
    out = [("out", row, CHUNK // 2, 0) for row in range(0, local - CHUNK // 2, CHUNK // 2)]
    out += [("out", row, CHUNK // 4, 0) for row in range(local - CHUNK // 2, local, CHUNK // 4)]
    qkv = [("qkv", row, CHUNK, part) for part in range(3) for row in range(0, local, CHUNK)]
    return down + across[:3] + qkv + across[3:] + out + [("rest", 0, 16, 0)]


def starts_of(chunks):
    rows = [chunk[2] for chunk in chunks]
    starts = [sum(rows[:k]) for k in range(len(rows) + 1)]
    return starts, [sum(rows[k % 2 : k : 2]) for k in range(len(rows) + 2)]


def last_kernel(chunks, size, *refs):
    weight, ids_row, ids_col, gain, inverse_one, rows_low = refs[:6]
    grad_second, normal_one, qkv_all, full_all, slope = refs[6:11]
    weight_out, weight_in, weight_down = refs[11:14]
    hidden, first, mixed, down, final = refs[14:19]
    home = refs[19]
    results = dict(zip(("qkv", "out", "in", "down", "rest"), refs[20:25]))
    grad_states, projected, full, product = refs[25:29]
    downs, ins, outs, down_both, pre_both, branch_both, rest_in = refs[29:36]
    near, far, across_in, up_in, side_in = refs[36:41]
    skip, normal, slopes, qkv_one, rows_grad, rest = refs[41:47]
    wires = Wires(refs[-1])
    z, section = lax.axis_index("ctx"), lax.axis_index("section")
    tokens, width = down.shape
    count = len(chunks)
    micro = qkv_all.shape[0]

    def qkv_copy(m):
        return wires.local(("pack", m), qkv_all.at[m], qkv_one)

    def qkv_of(m):
        qkv_copy(m).wait()
        return qkv_one

    given = (rows_grad, skip, qkv_of, weight, (ids_row, ids_col))
    back = Back(wires, size, given + (projected, grad_states) + refs[47:-1])
    w, sibling, across, across_sibling = wt_places()
    partners = (sibling, across, across_sibling)
    local = back.local
    deep = hidden.shape[1] // 4
    starts, sides_at = starts_of(chunks)
    moves = is_moving(z, w)
    own_rows = pl.ds(0, tokens)
    blocks = hidden.shape[1] // TILE

    def tile_copies(b):
        low = full.at[pl.ds((b % 2) * TILE, TILE), :]
        if b >= blocks:
            source = weight_out.at[pl.ds((b - blocks) * TILE, TILE), :]
            return [wires.local(("tile", b), source, low)]
        columns = pl.ds(b * TILE, TILE)
        wide = full.at[pl.ds(2 * TILE, width), pl.ds((b % 4) * TILE, TILE)]
        return [
            wires.local(("tile", b), weight_down.at[columns, :], low),
            wires.local(("wide", b), weight_in.at[:, columns], wide),
            wires.local(("slope", b), slope.at[:, columns], slopes.at[b % 2]),
        ]

    def start_tiles(b):
        for copy in tile_copies(b):
            copy.start()

    def skip_copy():
        return wires.local("skip", grad_second, skip)

    def normal_copy():
        return wires.local("normal", normal_one, normal)

    def own_loads():
        start_tiles(0)
        start_tiles(1)
        skip_copy().start()
        normal_copy().start()
        qkv_copy(0).start()

    greet(
        [{"wt": partner} for partner in partners],
        [
            (moves, home_place(z, w)),
            (moves, plane_place(z, w)),
            (z > 0, {"ctx": z - 1}),
            (z < 3, {"ctx": z + 1}),
        ],
        own_loads,
    )

    def step_back(b):
        if b == 0:
            skip_copy().wait()
        for copy in tile_copies(b):
            copy.wait()
        columns = pl.ds(b * TILE, TILE)
        low = full[pl.ds((b % 2) * TILE, TILE), :]
        wide = full[pl.ds(2 * TILE, width), pl.ds((b % 4) * TILE, TILE)]
        grad = dot(down_both[own_rows, :], low, ((1,), (1,)))
        grad = (grad * slopes[b % 2].astype(jnp.float32)).astype(jnp.bfloat16)
        pre_both[own_rows, columns] = grad
        skip[...] += dot(grad, wide, ((1,), (1,)))
        start_tiles(b + 2)
        if (b + 1) * TILE % width == 0:
            to_sibling("pre", pre_both, (b + 1) * TILE // width - 1).start()

    def to_sibling(key, array, column):
        at = pl.ds(column * width, width)
        target = array.at[pl.ds(tokens, tokens), at]
        return wires.remote((key, column), array.at[own_rows, at], target, wt=sibling)

    def step_norm():
        normal_copy().wait()
        ones = jnp.ones((16, tokens), jnp.bfloat16)
        grad_first = skip[...]
        rows = {r: rows_low[r : r + 1, :] for r in (5, 6, 7)}
        rows[3] = jnp.sum(grad_first * normal[...], axis=0, keepdims=True)
        rows[4] = jnp.sum(grad_first, axis=0, keepdims=True)
        grad_summed = norm_back(grad_first, gain[...], normal[...], inverse_one[...])
        skip[...] = grad_summed
        branch = grad_summed.astype(jnp.bfloat16)
        branch_both[own_rows, :] = branch
        to_sibling("branch", branch_both, 0).start()
        rows[2] = dot(ones, branch)[:1]
        sums = dot(ones, pre_both[own_rows, :])[:1]
        rest[...] = jnp.zeros_like(rest)
        for j in range(4):
            for r, row in rows.items():
                rest[j * 16 + r : j * 16 + r + 1, :local] = row[:, j * local : (j + 1) * local]
            for r in range(deep // local):
                at = j * deep + r * local
                rest[j * 16 + r : j * 16 + r + 1, local : 2 * local] = sums[:, at : at + local]
        for copy in rest_copies():
            copy.start()

    def step_out(b):
        for copy in tile_copies(b):
            copy.wait()
        tile = full[pl.ds((b % 2) * TILE, TILE), :]
        grad = dot(branch_both[own_rows, :], tile, ((1,), (1,))).astype(jnp.bfloat16)
        rows_grad[:, pl.ds((b - blocks) * TILE, TILE)] = grad
        if b + 2 < blocks + width // TILE:
            start_tiles(b + 2)

    def last_out():
        for b in range(blocks, blocks + width // TILE):
            step_out(b)
        full_copy().start()
        for m in range(micro):
            back.begin(m)

    def both(key, source, target, at, columns, theirs):
        mine = (pl.ds(0, tokens), at)
        other = (pl.ds(tokens, tokens), at)
        return (
            wires.local(key, source.at[:, columns], target.at[mine]),
            wires.remote(key, source.at[:, theirs], target.at[other], wt=sibling),
        )

    def sides(key, source, block, target):
        for side, (j, k) in enumerate(((w, sibling), (across, across_sibling))):
            yield from both(
                key + (side,),
                source,
                target,
                pl.ds(side * CHUNK, CHUNK),
                pl.ds(block(j), CHUNK),
                pl.ds(block(k), CHUNK),
            )

    def down_block(index):
        return sides(
            ("down", index), hidden, lambda j: j * deep + index * CHUNK, downs.at[index]
        )

    def in_block(half):
        return sides(("in", half), first, lambda j: j * local + half * CHUNK, ins.at[half])

    def out_block(half):
        return sides(("out", half), mixed, lambda j: j * local + half * CHUNK, outs.at[half])

    def whole(key, source, target, column):
        at = pl.ds(column * width, width)
        return both((key, column), source, target, at, at, at)

    def rest_copies():
        for side, k in enumerate((sibling, across_sibling)):
            yield wires.remote(
                ("rest", side), rest.at[pl.ds(k * 16, 16), :], rest_in.at[side], wt=sibling
            )

    halves = local // CHUNK
    columns = hidden.shape[1] // width
    loads = [lambda: whole("down", down, down_both, 0)]
    loads += [lambda index=index: down_block(index) for index in range(deep // CHUNK)]
    loads += [lambda half=half: in_block(half) for half in range(halves)]
    loads += [lambda half=half: out_block(half) for half in range(halves)]

    def full_copy():
        return wires.local("full", full_all, full)

    def needs(k):
        kind, row, _, column = chunks[k]
        index = row // CHUNK
        copies = []
        if kind == "down":
            if index == 0:
                copies += whole("down", down, down_both, 0)
            copies += down_block(index)
        elif kind == "in":
            if column == 0:
                copies += in_block(index)
            if index == 0:
                to_sibling("pre", pre_both, column).wait_recv()
        else:
            copies += out_block(index)
            if index == 0:
                to_sibling("branch", branch_both, 0).wait_recv()
        for index, copy in enumerate(copies):
            (copy.wait if index % 2 == 0 else copy.wait_recv)()

    def operands(k):
        kind, row, _, column = chunks[k]
        index = row // CHUNK
        if kind == "down":
            return downs[index], down_both[...]
        if kind == "in":
            return ins[index], pre_both[:, column * width : (column + 1) * width]
        return outs[index], branch_both[...]

    def is_piece(k):
        return chunks[k][0] == "qkv"

    def rows_of(k):
        return chunks[k][2]

    def slot(buffer, k):
        return buffer.at[pl.ds(starts[k], rows_of(k)), :]

    def beside_slot(k):
        return side_in.at[pl.ds(sides_at[k], rows_of(k)), :]

    def result(k):
        kind, row, rows, column = chunks[k]
        if kind == "rest":
            return results["rest"]
        return results[kind].at[pl.ds(row, rows), pl.ds(column * width, width)]

    def piece(k, j):
        _, row, rows, part = chunks[k]
        return product.at[part, pl.ds(j * local + row, rows), :]

    def piece_place(k):
        return near.at[pl.ds(starts[k], rows_of(k)), pl.ds(w * local, local)]

    def piece_copy(k, index):
        place = piece_place(k)
        return wires.remote(
            ("piece", k, index), piece(k, partners[index]), place, wt=partners[index]
        )

    def piece_own(k):
        return wires.local(("piece", k), piece(k, w), piece_place(k))

    direct = [k for k in range(count) if not is_piece(k)]
    bases = [k for k in direct if chunks[k][1] % CHUNK == 0]

    def base_of(k):
        return max(base for base in bases if base <= k)

    def far_slot(k, rows):
        return far.at[bases.index(base_of(k)) % RING, pl.ds(chunks[k][1] % CHUNK, rows), :]

    def across_copy(k):
        source = far_slot(k, rows_of(k))
        return wires.remote(("chunk", k), source, slot(across_in, k), wt=across)

    def place_of(k, role):
        return role if k % 2 == 0 else 3 - role

    def up_copy(k, role):
        target = place_of(k, 1 if role == 0 else 2)
        return wires.remote(("up", k), slot(near, k), slot(up_in, k), ctx=target)

    def side_copy(k):
        return wires.remote(("side", k), slot(near, k), beside_slot(k), ctx=place_of(k, 1))

    def down_copy(k, role):
        origin = result(k) if role == 3 else slot(near, k)
        return pltpu.make_async_remote_copy(
            origin,
            result(k),
            wires.at("down send", k, 1 if role == 2 else 0),
            wires.at("down recv", k),
            device_id={"ctx": place_of(k, role)},
            device_id_type=MESH,
        )

    def keep_copy(k):
        return wires.local(("keep", k), slot(near, k), result(k))

    def on(k, role, step):
        pl.when(z == place_of(k, role))(step)

    def summands(k):
        if is_piece(k):
            return [slot(near, k)]
        return [slot(near, k), slot(across_in, k)]

    def begin(k):
        kind, row, _, column = chunks[k]
        if is_piece(k):
            if row == 0:
                at = pl.ds(column * local, local)
                grad = dot(full[...], projected[:, at], ((0,), (0,)))
                product[column] = grad.astype(jnp.bfloat16)
            for partner in range(3):
                piece_copy(k, partner).start()
            piece_own(k).start()
            return
        if k in bases:
            order = bases.index(k)
            for old in direct:
                if order >= RING and base_of(old) == bases[order - RING]:
                    across_copy(old).wait_send()
        if kind == "rest":
            for copy in rest_copies():
                copy.wait_recv()
            ones = jnp.ones((16, projected.shape[0]), jnp.bfloat16)
            sums = dot(ones, projected[...])
            row = lax.broadcasted_iota(jnp.int32, (16, local), 0)
            own = jnp.where(row == 0, sums[:, :local], 0.0)
            own = own + jnp.where(row == 1, sums[:, 2 * local :], 0.0)
            own = jnp.concatenate([own, jnp.zeros((16, width - local), jnp.float32)], axis=1)
            own = own + rest[pl.ds(w * 16, 16), :] + rest_in[0]
            other = rest[pl.ds(across * 16, 16), :] + rest_in[1]
            slot(near, k)[...] = own.astype(jnp.bfloat16)
            far_slot(k, 16)[...] = other.astype(jnp.bfloat16)
        elif k in bases:
            needs(k)
            left, right = operands(k)
            grad = dot(left, right, ((0,), (0,))).astype(jnp.bfloat16)
            near[pl.ds(starts[k], CHUNK), :] = grad[:CHUNK]
            far_slot(k, CHUNK)[...] = grad[CHUNK:]
        across_copy(k).start()

    def settle(k):
        if is_piece(k):
            for index in range(3):
                piece_copy(k, index).wait_recv()
            piece_own(k).wait()
        else:
            across_copy(k).wait_recv()
        for role in (0, 3):

            def step(role=role):
                if not is_piece(k):
                    sum_into(slot(near, k), summands(k), rows_of(k))
                up_copy(k, role).start()

            on(k, role, step)

    def aside(k):
        def step():
            up_copy(k, 3).wait_recv()
            sum_into(slot(near, k), summands(k) + [slot(up_in, k)], rows_of(k))
            side_copy(k).start()

        on(k, 2, step)

    def finish(k):
        def step():
            up_copy(k, 0).wait_recv()
            side_copy(k).wait_recv()
            parts = summands(k) + [slot(up_in, k), beside_slot(k)]
            sum_into(slot(near, k), parts, rows_of(k))
            down_copy(k, 0).start()
            down_copy(k, 2).start()
            keep_copy(k).start()

        on(k, 1, step)

    def forward(k):
        def step():
            down_copy(k, 2).wait_recv()
            down_copy(k, 3).start()

        on(k, 2, step)

    def go_home(m, source, here, do):
        @pl.when(moves & here)
        def _():
            do(swap_back(wires, back.rows, source, home, m, True))

        @pl.when(jnp.logical_not(moves) & here)
        def _():
            do(swap_back(wires, back.rows, source, home, m, False))

    def done(m):
        back.finish(m)
        go_home(m, grad_states, section == 0, lambda copy: copy.start())

    def final_home(m):
        go_home(m, final, section == 1, lambda copy: copy.start())

    beside = {
        9: [lambda: back.work(0), lambda: qkv_copy(1).start()],
        10: [lambda: back.work(1), lambda: qkv_copy(2).start()],
        11: [lambda: back.work(2)],
        17: [lambda: final_home(0)],
        18: [lambda: final_home(1)],
        19: [lambda: final_home(2)],
        20: [lambda: back.cross(0)],
        22: [lambda: back.cross(1)],
        24: [lambda: back.cross(2), lambda: done(0)],
        26: [lambda: done(1)],
        28: [lambda: done(2)],
        7: [step_norm, last_out],
    }
    steps = iter(range(blocks))
    for tick, many in enumerate((0, 0, 2, 3, 3, 4, 4)):
        beside[tick] = [functools.partial(step_back, next(steps)) for _ in range(many)]

    for load in loads:
        for copy in load():
            copy.start()
    stages = (settle, aside, finish, forward)
    begun, first_piece = 0, min(k for k in range(count) if is_piece(k))
    for tick in range(count + LAGS[-1]):
        for lag, stage in reversed(list(zip(LAGS, stages))):
            if 0 <= tick - lag < count:
                stage(tick - lag)
        while begun < min(count, tick + 1 + max(0, min(AHEAD, tick - 11))):
            if begun == first_piece:
                full_copy().wait()
            begin(begun)
            begun += 1
        for step in beside.get(tick, []):
            step()
    for m in range(back.micro):
        back.end(m)
        go_home(m, grad_states, z >= 0, lambda copy: copy.wait())
    for copy in rest_copies():
        copy.wait_send()
    for load in loads:
        for index, copy in enumerate(load()):
            if index % 2 == 1:
                copy.wait_send()
    for column in range(columns):
        to_sibling("pre", pre_both, column).wait_send()
    to_sibling("branch", branch_both, 0).wait_send()
    for k in direct:
        if base_of(k) in bases[-RING:]:
            across_copy(k).wait_send()
    for k in range(count):
        if is_piece(k):
            for index in range(3):
                piece_copy(k, index).wait_send()

        def ends(role):
            up_copy(k, role).wait_send()
            down_copy(k, role).wait_recv()

        def middle():
            side_copy(k).wait_send()
            down_copy(k, 3).wait_send()

        def owner():
            down_copy(k, 0).wait_send()
            down_copy(k, 2).wait_send()
            keep_copy(k).wait()

        on(k, 0, lambda: ends(0))
        on(k, 3, lambda: ends(3))
        on(k, 2, middle)
        on(k, 1, owner)


def last_pass(weight, ids, gain, inverse_one, rows_low, arrays, weights, operands, size):
    micro, pack, local = arrays[2].shape
    local = local // 3
    tokens, width = operands[3].shape
    hidden = operands[0].shape[1]
    chunks = chunk_list(local, width, hidden)
    count = len(chunks)
    starts, sides_at = starts_of(chunks)
    inside = pl.BlockSpec(memory_space=pltpu.VMEM)
    anywhere = pl.BlockSpec(memory_space=pl.ANY)
    low = lambda *shape: jax.ShapeDtypeStruct(shape, jnp.bfloat16)
    room = lambda *shape: pltpu.VMEM(shape, jnp.bfloat16)
    halves = local // CHUNK
    return pl.pallas_call(
        functools.partial(last_kernel, chunks, size),
        in_specs=[inside] * 6 + [anywhere] * 13,
        out_specs=[anywhere] * 6,
        out_shape=[
            low(micro, pack // 4, width),
            low(local, 3 * width),
            low(local, width),
            low(local, hidden),
            low(hidden // 4, width),
            low(16, width),
        ],
        scratch_shapes=[
            room(tokens, width),
            room(micro * pack, 3 * local),
            room(micro * pack, width),
            room(3, width, local),
            room(hidden // 4 // CHUNK, 2 * tokens, 2 * CHUNK),
            room(halves, 2 * tokens, 2 * CHUNK),
            room(halves, 2 * tokens, 2 * CHUNK),
            room(2 * tokens, width),
            room(2 * tokens, hidden),
            room(2 * tokens, width),
            pltpu.VMEM((2, 16, width), jnp.float32),
            room(starts[count], width),
            room(RING, CHUNK, width),
            room(starts[count], width),
            room(starts[count], width),
            room(max(sides_at[count:]), width),
            pltpu.VMEM((tokens, width), jnp.float32),
            pltpu.VMEM((tokens, width), jnp.float32),
            room(2, tokens, TILE),
            room(pack, 3 * local),
            room(tokens, width),
            pltpu.VMEM((64, width), jnp.float32),
        ]
        + back_scratch(micro, pack, local, width)
        + [pltpu.SemaphoreType.DMA((900,))],
        compiler_params=pltpu.CompilerParams(
            collective_id=1, has_side_effects=True, vmem_limit_bytes=63 * 2**20
        ),
        name="last_pass",
    )(
        weight,
        ids[:, None, :],
        ids[:, :, None],
        gain,
        inverse_one,
        rows_low,
        *arrays,
        *weights,
        *operands,
    )


def relay(boundary, lengths, valid, w_qkv, w_out, w_in, w_down, bias_in, vectors):
    section_at = lax.axis_index("section")
    count_ctx = lax.axis_size("ctx")
    ctx_at = lax.axis_index("ctx")
    wt_at = lax.axis_index("wt")
    micro, rows, width = boundary.shape[1:]
    pack = rows * count_ctx
    size = width // HEADS
    local = width // lax.axis_size("wt")
    tokens = micro * rows
    own_rows = vectors[0].astype(jnp.float32)
    qkv_bias = jnp.concatenate([own_rows[0], jnp.zeros((local,), jnp.float32), own_rows[1]])[None]
    my_lengths = lax.dynamic_index_in_dim(lengths, turned(ctx_at), 1, keepdims=False)
    ends = jnp.cumsum(my_lengths, axis=1)
    stripes = stripe_of(ctx_at, jnp.arange(count_ctx, dtype=jnp.int32))
    places = jnp.arange(rows, dtype=jnp.int32)[None, :] * count_ctx + stripes[:, None]
    ids = jnp.sum((places.reshape(1, pack, 1) >= ends[:, None, :]).astype(jnp.int32), axis=2)
    small = jnp.concatenate([vectors[0], bias_in[0].reshape(-1, local)], axis=0)
    small = jnp.pad(small, ((0, 16 - small.shape[0]), (0, 0)))
    marks = jnp.pad(valid.astype(jnp.float32), ((0, 8 - micro), (0, 0)))
    shards = (w_qkv[0], w_out[0], w_in[0], w_down[0])
    own, weight_qkv, *weights, layer_rows, in_bias, marks, counts, leaving = first_pass(
        boundary[0], shards, small, marks, qkv_bias, ids, size
    )
    factor = LOSS_SCALE / jnp.sum(counts)
    covered = factor * marks[:micro].reshape(tokens, 1)
    leaving = leaving.reshape(micro, rows, width)
    kept, inverse_one, inverse_two, returned = mid_pass(
        own, leaving, weights, weight_qkv, qkv_bias, ids, layer_rows, in_bias, covered, size
    )
    cotangent = jnp.where(section_at == 1, kept["grad"], returned.astype(jnp.float32))
    normal_two = kept["normal_two"]
    grad_second = norm_back(cotangent, layer_rows[6], normal_two, inverse_two)
    down_low = grad_second.astype(jnp.bfloat16)
    total = lambda values: jnp.sum(values.astype(jnp.float32), axis=0)
    rows_low = jnp.stack([total(down_low), total(cotangent * normal_two), total(cotangent)])
    home, *sums = last_pass(
        weight_qkv,
        ids,
        layer_rows[3:4],
        inverse_one,
        jnp.pad(rows_low, ((5, 0), (0, 0))),
        (
            grad_second,
            kept["normal_one"],
            kept["qkv"],
            kept["full"].reshape(-1, width),
            kept["slope"],
        ),
        weights,
        (kept["hidden"], kept["first"], kept["mixed"], down_low, kept["final"]),
        size,
    )
    sums = [part.astype(jnp.float32)[None] for part in sums]
    rest = sums[4]
    in_rows = w_in.shape[2] // width
    bias_back = rest[:, :in_rows, local : 2 * local].reshape(1, -1)
    return (home[None], *sums[:4], bias_back, rest[:, :8, :local])


def solution(mesh):
    in_specs = (
        P("section", None, ("wt", "ctx"), None),
        P(),
        P(None, ("wt", "ctx")),
        P("section", "wt", None),
        P("section", "wt", None),
        P("section", "wt", None),
        P("section", "wt", None),
        P("section", "wt"),
        P("section", None, "wt"),
    )
    out_specs = (
        P("section", None, ("wt", "ctx"), None),
        P("section", "wt", None),
        P("section", "wt", None),
        P("section", "wt", None),
        P("section", "wt", None),
        P("section", "wt"),
        P("section", None, "wt"),
    )
    square = mesh.shape["ctx"] == mesh.shape["wt"] == 4
    return jax.shard_map(relay if square else shards, mesh=mesh, in_specs=in_specs, out_specs=out_specs, check_vma=False)
```

```python
import functools

import jax
import jax.numpy as jnp
from jax import lax
from jax.experimental import pallas as pl
from jax.experimental.pallas import tpu as pltpu
from jax.sharding import PartitionSpec as P

HEADS = 16
LOSS_SCALE = 1024


def shifted(block, axis, distance):
    devices = range(lax.axis_size(axis))
    route = [(i - distance, i) for i in devices if i - distance in devices]
    return lax.ppermute(block, axis, route)


def as_sent(x):

    def short(part):
        return part.astype(jnp.bfloat16) if part.dtype == jnp.float32 else part

    return jax.tree.map(short, x)


def layer_norm(values, gain, shift):
    center = jnp.mean(values, axis=-1, keepdims=True)
    offset = values - center
    spread = jnp.mean(offset * offset, axis=-1, keepdims=True)
    return offset * lax.rsqrt(spread + 1e-05) * gain + shift


def exact_gelu(values):
    return jax.nn.gelu(values, approximate=False)


def dealt_ids(length_row, pack_size, ctx_count):
    ends = jnp.cumsum(length_row)
    places = jnp.arange(pack_size, dtype=jnp.int32)
    natural = jnp.sum((places[:, None] >= ends[None, :]).astype(jnp.int32), axis=1)
    return natural.reshape(pack_size // ctx_count, ctx_count).T.reshape(pack_size)


def split_blocks(full_kv, ids_keys):
    block = min(512, full_kv.shape[0])
    count_blocks = full_kv.shape[0] // block
    return (
        full_kv.reshape(count_blocks, block, full_kv.shape[1]),
        ids_keys.reshape(count_blocks, block),
    )


def split_kv(block_kv, heads):
    half = block_kv.shape[1] // 2
    keys = block_kv[:, :half].reshape(block_kv.shape[0], heads, -1)
    values = block_kv[:, half:].reshape(block_kv.shape[0], heads, -1)
    return (keys, values)


def block_scores(queries, keys, ids_query, ids_keys, scale):
    scores = jnp.einsum("qhd,khd->hqk", queries, keys, preferred_element_type=jnp.float32) * scale
    same = ids_query[:, None] == ids_keys[None, :]
    return jnp.where(same[None], scores, -1000000000.0)


def attend_forward(queries, full_kv, ids_query, ids_keys, heads, scale):
    blocks, id_blocks = split_blocks(full_kv, ids_keys)
    query_rows = queries.shape[0]

    def total_step(carry, items):
        run_max, run_sum = carry
        keys, values = split_kv(items[0], heads)
        scores = block_scores(queries, keys, ids_query, items[1], scale)
        new_max = jnp.maximum(run_max, jnp.max(scores, axis=-1))
        run_sum = run_sum * jnp.exp(run_max - new_max) + jnp.sum(
            jnp.exp(scores - new_max[..., None]), axis=-1
        )
        return ((new_max, run_sum), None)

    start = (
        jnp.full((heads, query_rows), -1e30, jnp.float32),
        jnp.zeros((heads, query_rows), jnp.float32),
    )
    (run_max, run_sum), _ = lax.scan(total_step, start, (blocks, id_blocks))
    log_total = run_max + jnp.log(run_sum)

    def mix_step(carry, items):
        keys, values = split_kv(items[0], heads)
        scores = block_scores(queries, keys, ids_query, items[1], scale)
        probs = jnp.exp(scores - log_total[..., None]).astype(jnp.bfloat16)
        return (
            carry + jnp.einsum("hqk,khd->qhd", probs, values, preferred_element_type=jnp.float32),
            None,
        )

    mixed, _ = lax.scan(mix_step, jnp.zeros(queries.shape, jnp.float32), (blocks, id_blocks))
    return (mixed.reshape(query_rows, -1), log_total)


def attend_backward(queries, full_kv, ids_query, ids_keys, mixed_grad, log_total, heads, scale):
    blocks, id_blocks = split_blocks(full_kv, ids_keys)
    grad_heads = mixed_grad.reshape(queries.shape)

    def inner_step(carry, items):
        keys, values = split_kv(items[0], heads)
        scores = block_scores(queries, keys, ids_query, items[1], scale)
        probs = jnp.exp(scores - log_total[..., None])
        prob_grad = jnp.einsum(
            "qhd,khd->hqk", grad_heads, values, preferred_element_type=jnp.float32
        )
        return (carry + jnp.sum(probs * prob_grad, axis=-1), None)

    inner, _ = lax.scan(inner_step, jnp.zeros(log_total.shape, jnp.float32), (blocks, id_blocks))

    def grad_step(carry, items):
        keys, values = split_kv(items[0], heads)
        scores = block_scores(queries, keys, ids_query, items[1], scale)
        probs = jnp.exp(scores - log_total[..., None])
        prob_grad = jnp.einsum(
            "qhd,khd->hqk", grad_heads, values, preferred_element_type=jnp.float32
        )
        score_grad = (probs * (prob_grad - inner[..., None])).astype(jnp.bfloat16)
        carry = (
            carry
            + jnp.einsum("hqk,khd->qhd", score_grad, keys, preferred_element_type=jnp.float32)
            * scale
        )
        key_grad = (
            jnp.einsum("hqk,qhd->khd", score_grad, queries, preferred_element_type=jnp.float32)
            * scale
        )
        value_grad = jnp.einsum(
            "hqk,qhd->khd",
            probs.astype(jnp.bfloat16),
            grad_heads,
            preferred_element_type=jnp.float32,
        )
        block = keys.shape[0]
        return (
            carry,
            jnp.concatenate([key_grad.reshape(block, -1), value_grad.reshape(block, -1)], axis=1),
        )

    query_grad, partial_kv = lax.scan(
        grad_step, jnp.zeros(queries.shape, jnp.float32), (blocks, id_blocks)
    )
    query_grad = query_grad.reshape(queries.shape[0], -1)
    return (query_grad, partial_kv.reshape(-1, partial_kv.shape[-1]), inner)


def shards(boundary, lengths, valid, w_qkv, w_out, w_in, w_down, bias_in, vectors):
    section_at = lax.axis_index("section")
    ctx_count = lax.axis_size("ctx")
    ctx_at = lax.axis_index("ctx")
    wt_at = lax.axis_index("wt")
    micro_count = boundary.shape[1]
    row_count = boundary.shape[2]
    width = boundary.shape[3]
    pack_size = row_count * ctx_count
    head_size = width // HEADS
    scale = head_size ** (-0.5)
    gathered = (
        lax.all_gather(w_qkv[0], "wt", axis=0, tiled=True),
        lax.all_gather(w_out[0], "wt", axis=0, tiled=True),
        lax.all_gather(w_in[0], "wt", axis=0, tiled=True),
        lax.all_gather(w_down[0], "wt", axis=0, tiled=True),
        lax.all_gather(bias_in[0], "wt", axis=0, tiled=True),
        lax.all_gather(vectors[0], "wt", axis=1, tiled=True),
    )
    weight_qkv, weight_out, weight_in, weight_down, in_bias, vector_rows = gathered
    in_bias = in_bias.astype(jnp.float32)
    vector_rows = vector_rows.astype(jnp.float32)
    qkv_bias = jnp.concatenate([vector_rows[0], jnp.zeros((width,), jnp.float32), vector_rows[1]])
    my_lengths = lax.dynamic_index_in_dim(lengths, wt_at, 1, keepdims=False)

    def ids_of(length_row):
        return dealt_ids(length_row, pack_size, ctx_count)

    pack_ids = jax.vmap(ids_of)(my_lengths)
    query_ids = lax.dynamic_slice_in_dim(pack_ids, ctx_at * row_count, row_count, 1)
    count = lax.psum(jnp.sum(valid.astype(jnp.float32)), ("ctx", "wt"))
    factor = LOSS_SCALE / count
    empty_rows = jnp.zeros((row_count, width), jnp.bfloat16)
    arriving = empty_rows
    kept_list = []
    cotangents = []
    final_states = []
    for tick_at in range(micro_count + 1):
        own_input = boundary[0, tick_at] if tick_at < micro_count else empty_rows
        inputs = jnp.where(section_at == 0, own_input, arriving)
        micro_here = jnp.clip(tick_at - section_at, 0, micro_count - 1)
        ids_keys = lax.dynamic_index_in_dim(pack_ids, micro_here, 0, keepdims=False)
        ids_query = lax.dynamic_index_in_dim(query_ids, micro_here, 0, keepdims=False)
        residual = inputs.astype(jnp.float32)
        projected = jnp.dot(inputs, weight_qkv, preferred_element_type=jnp.float32) + qkv_bias
        layer_queries = (
            projected[:, :width].astype(jnp.bfloat16).reshape(row_count, HEADS, head_size)
        )
        layer_local_kv = projected[:, width:].astype(jnp.bfloat16)
        layer_full_kv = lax.all_gather(layer_local_kv, "ctx", axis=0, tiled=True)
        mixed, layer_log_total = attend_forward(
            layer_queries, layer_full_kv, ids_query, ids_keys, HEADS, scale
        )
        layer_mixed_low = mixed.astype(jnp.bfloat16)
        branch = (
            jnp.dot(layer_mixed_low, weight_out, preferred_element_type=jnp.float32)
            + vector_rows[2]
        )
        layer_summed = residual + branch
        first = layer_norm(layer_summed, vector_rows[3], vector_rows[4])
        layer_first_low = first.astype(jnp.bfloat16)
        layer_hidden_pre = (
            jnp.dot(layer_first_low, weight_in, preferred_element_type=jnp.float32) + in_bias
        )
        layer_hidden_low = exact_gelu(layer_hidden_pre).astype(jnp.bfloat16)
        layer_second = first + (
            jnp.dot(layer_hidden_low, weight_down, preferred_element_type=jnp.float32)
            + vector_rows[5]
        )
        output = layer_norm(layer_second, vector_rows[6], vector_rows[7])
        layer_kept = (
            inputs,
            layer_queries,
            layer_local_kv,
            layer_full_kv,
            layer_mixed_low,
            layer_log_total,
            layer_summed,
            layer_first_low,
            layer_hidden_pre,
            layer_hidden_low,
            layer_second,
            ids_keys,
            ids_query,
        )
        output, kept = (output, layer_kept)
        kept_list.append(kept)
        if tick_at > 0:
            teacher = boundary[0, tick_at - 1].astype(jnp.float32)
            covered = valid[tick_at - 1].astype(jnp.float32)[:, None]
            cotangents.append(factor * covered * (output - teacher))
            final_states.append(output.astype(jnp.bfloat16))
        else:
            cotangents.append(jnp.zeros((row_count, width), jnp.float32))
        if tick_at < micro_count:
            arriving = shifted(output.astype(jnp.bfloat16), "section", 1)
    returning = empty_rows
    totals = None
    input_grads = [None] * micro_count
    for back_at in range(micro_count + 1):
        forward_at = micro_count - back_at
        grad_output = jnp.where(
            section_at == 1, cotangents[forward_at], returning.astype(jnp.float32)
        )
        (
            layer_inputs,
            queries,
            local_kv,
            full_kv,
            mixed_low,
            log_total,
            summed,
            first_low,
            hidden_pre,
            hidden_low,
            second,
            layer_ids_keys,
            layer_ids_query,
        ) = kept_list[forward_at]
        full_kv = lax.all_gather(local_kv, "ctx", axis=0, tiled=True)
        _, pull_last = jax.vjp(layer_norm, second, vector_rows[6], vector_rows[7])
        grad_second, grad_gain_two, grad_shift_two = pull_last(grad_output)
        down_low = grad_second.astype(jnp.bfloat16)
        layer_grad_down = jnp.einsum(
            "rf,rd->fd", hidden_low, down_low, preferred_element_type=jnp.float32
        )
        grad_bias_two = jnp.sum(down_low.astype(jnp.float32), axis=0)
        _, pull_gelu = jax.vjp(exact_gelu, hidden_pre)
        (grad_pre,) = pull_gelu(
            jnp.einsum("rd,fd->rf", down_low, weight_down, preferred_element_type=jnp.float32)
        )
        pre_low = grad_pre.astype(jnp.bfloat16)
        layer_grad_in = jnp.einsum(
            "rd,rf->df", first_low, pre_low, preferred_element_type=jnp.float32
        )
        layer_grad_bias_in = jnp.sum(pre_low.astype(jnp.float32), axis=0)
        grad_first = grad_second + jnp.einsum(
            "rf,df->rd", pre_low, weight_in, preferred_element_type=jnp.float32
        )
        _, pull_first = jax.vjp(layer_norm, summed, vector_rows[3], vector_rows[4])
        grad_summed, grad_gain_one, grad_shift_one = pull_first(grad_first)
        branch_low = grad_summed.astype(jnp.bfloat16)
        layer_grad_out = jnp.einsum(
            "rd,re->de", mixed_low, branch_low, preferred_element_type=jnp.float32
        )
        grad_bias_out = jnp.sum(branch_low.astype(jnp.float32), axis=0)
        mixed_grad = jnp.einsum(
            "re,de->rd", branch_low, weight_out, preferred_element_type=jnp.float32
        ).astype(jnp.bfloat16)
        query_grad, partial_kv, inner = attend_backward(
            queries, full_kv, layer_ids_query, layer_ids_keys, mixed_grad, log_total, HEADS, scale
        )
        kv_grad = lax.psum_scatter(
            partial_kv.astype(jnp.bfloat16), "ctx", scatter_dimension=0, tiled=True
        )
        query_low = query_grad.astype(jnp.bfloat16)
        projected_grad = jnp.concatenate([query_low, kv_grad], axis=1)
        layer_grad_qkv = jnp.einsum(
            "rd,re->de", layer_inputs, projected_grad, preferred_element_type=jnp.float32
        )
        vector_grad = jnp.stack(
            [
                jnp.sum(query_low.astype(jnp.float32), axis=0),
                jnp.sum(kv_grad[:, width:].astype(jnp.float32), axis=0),
                grad_bias_out,
                grad_gain_one,
                grad_shift_one,
                grad_bias_two,
                grad_gain_two,
                grad_shift_two,
            ]
        )
        grad_inputs = grad_summed + jnp.einsum(
            "re,de->rd", projected_grad, weight_qkv, preferred_element_type=jnp.float32
        )
        grad_inputs, grads = (
            grad_inputs,
            (
                layer_grad_qkv,
                layer_grad_out,
                layer_grad_in,
                layer_grad_down,
                layer_grad_bias_in,
                vector_grad,
            ),
        )
        totals = grads if totals is None else jax.tree.map(jnp.add, totals, grads)
        if forward_at < micro_count:
            input_grads[forward_at] = grad_inputs
        if back_at < micro_count:
            returning = shifted(grad_inputs.astype(jnp.bfloat16), "section", -1)
    results = jnp.stack(
        [
            jnp.where(section_at == 0, input_grads[index].astype(jnp.bfloat16), final_states[index])
            for index in range(micro_count)
        ]
    )[None]
    shares = (
        lax.psum_scatter(
            totals[0].astype(jnp.bfloat16), "wt", scatter_dimension=0, tiled=True
        ).astype(jnp.float32),
        lax.psum_scatter(
            totals[1].astype(jnp.bfloat16), "wt", scatter_dimension=0, tiled=True
        ).astype(jnp.float32),
        lax.psum_scatter(
            totals[2].astype(jnp.bfloat16), "wt", scatter_dimension=0, tiled=True
        ).astype(jnp.float32),
        lax.psum_scatter(
            totals[3].astype(jnp.bfloat16), "wt", scatter_dimension=0, tiled=True
        ).astype(jnp.float32),
        lax.psum_scatter(
            totals[4].astype(jnp.bfloat16), "wt", scatter_dimension=0, tiled=True
        ).astype(jnp.float32),
        lax.psum_scatter(
            totals[5].astype(jnp.bfloat16), "wt", scatter_dimension=1, tiled=True
        ).astype(jnp.float32),
    )
    shares = jax.tree.map(lambda part: part.astype(jnp.float32), lax.psum(as_sent(shares), "ctx"))
    grad_qkv, grad_out, grad_in, grad_down, grad_bias_in, grad_vectors = shares
    return (
        results,
        grad_qkv[None],
        grad_out[None],
        grad_in[None],
        grad_down[None],
        grad_bias_in[None],
        grad_vectors[None],
    )


PAIR = 128
FAR = -1000000000.0
MESH = pl.DeviceIdType.MESH


def dot(left, right, dims=((1,), (0,))):
    return lax.dot_general(left, right, (dims, ((), ())), preferred_element_type=jnp.float32)


def head_lanes(size):
    lane = lax.broadcasted_iota(jnp.int32, (1, PAIR), 1)
    return [lane // size == index for index in range(PAIR // size)]


def only(mask, values):
    return jnp.where(mask, values, jnp.zeros_like(values))


def normal_tail(values):
    size = jnp.abs(values)
    bell = jnp.exp(-0.5 * values * values)
    t = 1.0 / (1.0 + 0.3275911 * (2.0**-0.5) * size)
    poly = t * (
        0.254829592
        + t * (-0.284496736 + t * (1.421413741 + t * (-1.453152027 + t * 1.061405429)))
    )
    tail = 0.5 * poly * bell
    return (jnp.where(values >= 0, 1.0 - tail, tail), bell)


def gelu_both(values):
    below, bell = normal_tail(values)
    return (values * below, below + values * bell * 0.3989422804014327)


def norm_parts(values):
    center = jnp.mean(values, axis=-1, keepdims=True)
    offset = values - center
    spread = jnp.mean(offset * offset, axis=-1, keepdims=True)
    inverse = lax.rsqrt(spread + 1e-05)
    return (offset * inverse, inverse)


def norm_back(grad, gain, normal, inverse):
    inner = grad * gain
    mean = jnp.mean(inner, axis=-1, keepdims=True)
    along = jnp.mean(inner * normal, axis=-1, keepdims=True)
    return inverse * (inner - mean - normal * along)


class Wires:
    def __init__(self, sems):
        self.sems = sems
        self.places = {}

    def at(self, *key):
        return self.sems.at[self.places.setdefault(key, len(self.places))]

    def remote(self, key, source, target, **where):
        return pltpu.make_async_remote_copy(
            source,
            target,
            self.at(key, "send"),
            self.at(key, "recv"),
            device_id=where,
            device_id_type=MESH,
        )

    def local(self, key, source, target):
        return pltpu.make_async_copy(source, target, self.at(key, "local"))


def wt_places():
    w = lax.axis_index("wt")
    core = lax.rem(w, 2)
    sibling = w + 1 - 2 * core
    across = lax.rem(w + 2, 4)
    return w, sibling, across, lax.rem(sibling + 2, 4)


def turned(place):
    return 2 * lax.rem(place, 2) + place // 2


def stripe_of(z, w):
    return 2 * lax.rem(w, 2) + lax.rem(w // 2 + z, 2)


def plane_place(z, w):
    plane = turned(w)
    return dict(ctx=plane, wt=2 * lax.rem(z + plane, 2) + z // 2)


def home_place(z, w):
    return dict(ctx=stripe_of(z, w), wt=turned(z))


def is_moving(z, w):
    place = home_place(z, w)
    return (place["ctx"] != z) | (place["wt"] != w)


def greet(partners, extra, meanwhile=lambda: None):
    barrier = pltpu.get_barrier_semaphore()
    for partner in partners:
        pl.semaphore_signal(barrier, 1, device_id=partner, device_id_type=MESH)
    waits = len(partners)
    for here, partner in extra:

        @pl.when(here)
        def _():
            pl.semaphore_signal(barrier, 1, device_id=partner, device_id_type=MESH)

        waits = waits + here.astype(jnp.int32)
    meanwhile()
    pl.semaphore_wait(barrier, waits)


def same_document(lengths, m, rows):
    z = lax.axis_index("ctx")
    pack = turned(z)
    ends = [lengths[m, pack, 0]]
    for document in range(1, lengths.shape[2]):
        ends.append(ends[-1] + lengths[m, pack, document])

    def ids(axis):
        shape = (rows, 1) if axis == 0 else (1, rows)
        first = lax.broadcasted_iota(jnp.int32, shape, axis) * 4
        place = jnp.concatenate([first + stripe_of(z, j) for j in range(4)], axis=axis)
        return sum((place >= end).astype(jnp.int32) for end in ends)

    return ids(0) == ids(1)


def attend_pack(size, same, qkv, mixed):
    local = mixed.shape[1]
    masks = head_lanes(size)
    for pair in range(local // PAIR):
        at = pair * PAIR
        q = qkv[:, at : at + PAIR] * jnp.bfloat16(size**-0.5)
        k = qkv[:, local + at : local + at + PAIR]
        v = qkv[:, 2 * local + at : 2 * local + at + PAIR]
        total = None
        for mask in masks:
            scores = jnp.where(same, dot(only(mask, k), q, ((1,), (1,))), FAR)
            probs = jnp.exp(scores - jnp.max(scores, axis=0, keepdims=True))
            scale = 1.0 / jnp.sum(probs, axis=0, keepdims=True)
            low = (probs * scale).astype(jnp.bfloat16)
            term = dot(only(mask, v), low, ((0,), (0,)))
            total = term if total is None else total + term
        mixed[:, at : at + PAIR] = total.T.astype(jnp.bfloat16)


def attend_pack_back(size, same, qkv, grad_heads, projected_grad):
    local = grad_heads.shape[1]
    masks = head_lanes(size)
    for pair in range(local // PAIR):
        at = pair * PAIR
        q = qkv[:, at : at + PAIR] * jnp.bfloat16(size**-0.5)
        k = qkv[:, local + at : local + at + PAIR]
        v = qkv[:, 2 * local + at : 2 * local + at + PAIR]
        grad = grad_heads[:, at : at + PAIR]
        totals = [None] * 3
        for mask in masks:
            own_k = only(mask, k)
            scores = jnp.where(same, dot(own_k, q, ((1,), (1,))), FAR)
            probs = jnp.exp(scores - jnp.max(scores, axis=0, keepdims=True))
            probs = probs * (1.0 / jnp.sum(probs, axis=0, keepdims=True))
            prob_grad = dot(only(mask, v), grad, ((1,), (1,)))
            inner = jnp.sum(probs * prob_grad, axis=0, keepdims=True)
            score_grad = (probs * (prob_grad - inner)).astype(jnp.bfloat16)
            terms = (
                dot(own_k, score_grad, ((0,), (0,))),
                dot(score_grad, only(mask, q)),
                dot(probs.astype(jnp.bfloat16), only(mask, grad)),
            )
            totals = [t if o is None else o + t for o, t in zip(totals, terms)]
        query_grad = totals[0].T * size**-0.5
        projected_grad[:, at : at + PAIR] = query_grad.astype(jnp.bfloat16)
        projected_grad[:, local + at : local + at + PAIR] = totals[1].astype(jnp.bfloat16)
        projected_grad[:, 2 * local + at : 2 * local + at + PAIR] = totals[2].astype(jnp.bfloat16)


class Spread:
    def __init__(self, wires, full, mixed, mixed_rows, rows, local):
        self.wires, self.full, self.mixed, self.mixed_rows = wires, full, mixed, mixed_rows
        self.rows, self.local = rows, local
        self.w, self.sibling, self.across, self.across_sibling = wt_places()

    def stripe(self, m, j):
        return self.full.at[m, pl.ds(j * self.rows, self.rows), :]

    def to_sibling(self, m):
        own = self.stripe(m, self.w)
        return self.wires.remote(("sibling", m), own, own, wt=self.sibling)

    def to_across(self, m):
        own = self.stripe(m, self.w)
        return self.wires.remote(("across", m), own, own, wt=self.across)

    def passed(self, m):
        block = self.stripe(m, self.across)
        return self.wires.remote(("passed", m), block, block, wt=self.sibling)

    def send(self, m):
        self.to_across(m).start()
        self.to_sibling(m).start()

    def hand_on(self, m):
        self.to_across(m).wait_recv()
        self.passed(m).start()

    def settle(self, m):
        self.to_sibling(m).wait_recv()
        self.passed(m).wait_recv()

    def back(self, m):
        heads = pl.ds(self.w * self.local, self.local)
        target = self.mixed_rows.at[pl.ds(m * self.rows, self.rows), heads]
        for index, partner in enumerate((self.across, self.across_sibling, self.sibling)):
            block = self.mixed.at[m, pl.ds(partner * self.rows, self.rows), :]
            yield self.wires.remote(("back", m, index), block, target, wt=partner)

    def send_back(self, m):
        for copy in self.back(m):
            copy.start()
        self.own_back(m).start()

    def own_back(self, m):
        heads = pl.ds(self.w * self.local, self.local)
        return self.wires.local(
            ("back", m),
            self.mixed.at[m, pl.ds(self.w * self.rows, self.rows), :],
            self.mixed_rows.at[pl.ds(m * self.rows, self.rows), heads],
        )

    def arrived_back(self, m):
        for copy in self.back(m):
            copy.wait_recv()
        self.own_back(m).wait()

    def end(self, m):
        for copy in (self.to_sibling(m), self.to_across(m), self.passed(m)):
            copy.wait_send()
        for copy in self.back(m):
            copy.wait_send()


def project(full, weight, bias, qkv):
    qkv[...] = (dot(full[...], weight[...]) + bias).astype(jnp.bfloat16)


def bias_of(rows):
    return jnp.concatenate([rows[0:1], jnp.zeros_like(rows[0:1]), rows[1:2]], axis=1)


BLOCK = 512


def feed_start(states, mixed, weight_out, rows):
    summed = states.astype(jnp.float32) + (dot(mixed, weight_out) + rows[2:3, :])
    normal, inverse = norm_parts(summed)
    return normal, inverse, normal * rows[3:4, :] + rows[4:5, :]


def feed_forward(at, states, mixed, weights, rows, in_bias, kept):
    weight_out, weight_in, weight_down = weights
    normal, inverse, first = feed_start(states, mixed, weight_out[...], rows)
    kept["normal_one"][at, :] = normal
    kept["inverse_one"][at, :] = inverse
    low = first.astype(jnp.bfloat16)
    kept["first"][at, :] = low
    total = first + rows[5:6, :]
    for column in range(0, weight_in.shape[1], BLOCK):
        columns = pl.ds(column, BLOCK)
        hidden, slope = gelu_both(dot(low, weight_in[:, columns]) + in_bias[:, columns])
        hidden = hidden.astype(jnp.bfloat16)
        kept["hidden"][at, columns] = hidden
        kept["slope"][at, columns] = slope.astype(jnp.bfloat16)
        total = total + dot(hidden, weight_down[columns, :])
    normal, inverse = norm_parts(total)
    kept["normal_two"][at, :] = normal
    kept["inverse_two"][at, :] = inverse
    return normal * rows[6:7, :] + rows[7:8, :]


def feed_backward(at, grad, weights, rows, kept):
    weight_out, weight_in, weight_down = weights
    total = norm_back(grad, rows[6:7, :], kept["normal_two"][at, :], kept["inverse_two"][at, :])
    low = total.astype(jnp.bfloat16)
    for column in range(0, weight_in.shape[1], BLOCK):
        columns = pl.ds(column, BLOCK)
        inner = dot(low, weight_down[columns, :], ((1,), (1,)))
        inner = (inner * kept["slope"][at, columns].astype(jnp.float32)).astype(jnp.bfloat16)
        total = total + dot(inner, weight_in[:, columns], ((1,), (1,)))
    total = norm_back(total, rows[3:4, :], kept["normal_one"][at, :], kept["inverse_one"][at, :])
    branch = total.astype(jnp.bfloat16)
    return total, dot(branch, weight_out[...], ((1,), (1,))).astype(jnp.bfloat16)


def first_kernel(size, *refs):
    block, shard_qkv, shard_out, shard_in, shard_down, vectors, own_bias, valid = refs[:8]
    lengths = refs[8]
    own, weight, kept_out, kept_in, kept_down, layer_rows, in_bias, own_marks, count = refs[9:18]
    leaving, full, qkv, mixed, marks_wt, marks_ctx = refs[18:24]
    whole_out, whole_in, whole_down, smalls, mixed_rows, first, inner, total = refs[24:32]
    small, marks, sems = refs[32:]
    micro, rows, width = block.shape
    local = small.shape[1]
    hidden = shard_in.shape[1]
    half = local // 2
    deep = shard_down.shape[0] // 8
    wires = Wires(sems)
    z = lax.axis_index("ctx")
    spread = Spread(wires, full, mixed, mixed_rows, rows, local)
    w, sibling, across, across_sibling = wt_places()
    partners = (across, across_sibling, sibling)
    level = lax.rem(z, 2)
    neighbor = z + 1 - 2 * level
    moves, place = is_moving(z, w), plane_place(z, w)
    others = [lax.rem(z + step, 4) for step in (1, 2, 3)]

    def own_parts():
        small[...] = jnp.zeros_like(small)
        small[:8, :] = vectors[...].astype(jnp.float32)
        for row in range(own_bias.shape[1] // local):
            at = pl.ds(row * local, local)
            small[8 + row : 9 + row, :] = own_bias[:, at].astype(jnp.float32)
        marks[...] = jnp.zeros_like(marks)
        marks[: valid.shape[0], :] = valid[...].astype(jnp.float32)

    greet(
        [{"wt": partner} for partner in partners] + [{"ctx": other} for other in others],
        [(moves, place), (moves, home_place(z, w))],
        own_parts,
    )
    bias = bias_of(small)

    def swap(m):
        return wires.remote(
            ("swap", m), block.at[m], spread.stripe(m, place["wt"]), **place
        )

    def stay(m):
        return wires.local(("stay", m), block.at[m], spread.stripe(m, w))

    def swap_marks():
        return wires.remote("swap marks", marks, own_marks, **place)

    def head_copy(part, index):
        column = part * width + partners[index] * local
        return wires.remote(
            ("heads", part, index),
            shard_qkv.at[:, pl.ds(column, local)],
            weight.at[pl.ds(w * local, local), pl.ds(part * local, local)],
            wt=partners[index],
        )

    def head_own(part):
        return wires.local(
            ("heads", part),
            shard_qkv.at[:, pl.ds(part * width + w * local, local)],
            weight.at[pl.ds(w * local, local), pl.ds(part * local, local)],
        )

    def small_copy(index):
        return wires.remote(("small", index), small, smalls.at[w], wt=partners[index])

    def marks_copy(index):
        return wires.remote(("marks", index), marks, marks_wt.at[index], wt=partners[index])

    def count_copy(index):
        return wires.remote(("count", index), count, marks_ctx.at[index], ctx=others[index])

    columns = hidden // width
    chunks = 1 + columns + 4

    def piece(k, level):
        if k == 0:
            return shard_out, whole_out, local, level * half, half, 0
        if k <= columns:
            return shard_in, whole_in, local, level * half, half, (k - 1) * width
        at = (level * 4 + k - 1 - columns) * deep
        return shard_down, whole_down, 4 * deep * 2, at, deep, 0

    def from_shard(k, level):
        shard, _, _, at, size, column = piece(k, level)
        return shard.at[pl.ds(at, size), pl.ds(column, width)]

    def in_whole(k, level, j):
        _, whole, stride, at, size, column = piece(k, level)
        return whole.at[pl.ds(j * stride + at, size), pl.ds(column, width)]

    def y_copy(k):
        return wires.remote(
            ("y", k), from_shard(k, level), in_whole(k, level, w), wt=across
        )

    def z_copy(k):
        block = in_whole(k, level, across)
        return wires.remote(("z", k), block, block, ctx=neighbor)

    def core_copy(k, side):
        block = in_whole(k, level if side == 0 else 1 - level, across)
        return wires.remote(("core", k, side), block, block, wt=sibling)

    def shard_sibling(index):
        shard, whole = ((shard_out, whole_out), (shard_in, whole_in), (shard_down, whole_down))[
            index
        ]
        size = shard.shape[0]
        return wires.remote(
            ("shard", index), shard, whole.at[pl.ds(w * size, size), :], wt=sibling
        )

    def shard_own(index):
        shard, whole = ((shard_out, whole_out), (shard_in, whole_in), (shard_down, whole_down))[
            index
        ]
        size = shard.shape[0]
        return wires.local(("shard", index), shard, whole.at[pl.ds(w * size, size), :])

    def shard_ready(index):
        shard_own(index).wait()
        shard_sibling(index).wait_recv()

    @pl.when(moves)
    def _():
        swap(0).start()
        swap_marks().start()

    @pl.when(jnp.logical_not(moves))
    def _():
        for m in range(micro):
            stay(m).start()
        own_marks[...] = marks[...]

    for part in range(3):
        for index in range(3):
            head_copy(part, index).start()
        head_own(part).start()
    for index in range(3):
        small_copy(index).start()
        marks_copy(index).start()
    smalls[w] = small[...]

    def arrive(m):
        @pl.when(moves)
        def _():
            swap(m).wait_recv()

        @pl.when(jnp.logical_not(moves))
        def _():
            stay(m).wait()

    def own_copy(m):
        return wires.local(("own", m), spread.stripe(m, w), own.at[m])

    @pl.when(moves)
    def _():
        swap(0).wait_send()
        for m in range(1, micro):
            swap(m).start()

    for m in range(micro):
        arrive(m)
        spread.send(m)
        own_copy(m).start()
    for k in range(micro):
        y_copy(k).start()
    for index in range(3):
        shard_sibling(index).start()
        shard_own(index).start()
    for index in range(3):
        marks_copy(index).wait_recv()
    count[...] = marks[...] + marks_wt[0] + marks_wt[1] + marks_wt[2]
    for index in range(3):
        count_copy(index).start()
    for part in range(3):
        for index in range(3):
            head_copy(part, index).wait_recv()
        head_own(part).wait()
    def passing(k):
        y_copy(k).wait_recv()
        if k + micro < chunks:
            y_copy(k + micro).start()
        z_copy(k).start()
        core_copy(k, 0).start()

    def passed(k):
        z_copy(k).wait_recv()
        core_copy(k, 1).start()

    def stored(k):
        if k == 0:
            return [wires.local(("stored", k), whole_out, kept_out)]
        if k <= columns:
            at = pl.ds((k - 1) * width, width)
            return [wires.local(("stored", k), whole_in.at[:, at], kept_in.at[:, at])]
        return [
            wires.local(("stored", k, row), whole_down.at[at, :], kept_down.at[at, :])
            for row, at in pair_rows(k)
        ]

    def pair_rows(k):
        if (k - columns) % 2 == 1:
            return []
        first_row = (k - 2 - columns) * deep
        return [
            (row, pl.ds(row, 2 * deep)) for row in range(first_row, hidden, 4 * deep)
        ]

    def compute(k):
        core_copy(k, 0).wait_recv()
        core_copy(k, 1).wait_recv()
        if k == 0:
            shard_ready(0)
            for m in range(micro):
                spread.arrived_back(m)
            states = [spread.stripe(m, w)[...] for m in range(micro)]
            states = jnp.concatenate(states, axis=0)
            values = feed_start(states, mixed_rows[...], whole_out[...], layer_rows)[2]
            first[...] = values.astype(jnp.bfloat16)
            total[...] = values + layer_rows[5:6, :]
        elif k <= columns:
            if k == 1:
                shard_ready(1)
            for column in range((k - 1) * width, k * width, BLOCK):
                at = pl.ds(column, BLOCK)
                values = gelu_both(dot(first[...], whole_in[:, at]) + in_bias[:, at])[0]
                inner[:, at] = values.astype(jnp.bfloat16)
        else:
            if k == columns + 1:
                shard_ready(2)
            for _, at in pair_rows(k):
                total[...] += dot(inner[:, at], whole_down[at, :])
        for copy in stored(k):
            copy.start()

    for index in range(3):
        small_copy(index).wait_recv()
    for j in range(4):
        at = pl.ds(j * local, local)
        layer_rows[:, at] = smalls[j, :8, :]
        for row in range(columns):
            at = pl.ds(j * 8 * deep + row * local, local)
            in_bias[:, at] = smalls[j, 8 + row : 9 + row, :]
    for m in range(micro):
        spread.hand_on(m)
        spread.settle(m)
        project(full.at[m], weight, bias, qkv.at[0])
        attend_pack(size, same_document(lengths, m, rows), qkv.at[0], mixed.at[m])
        spread.send_back(m)
        passing(m)
    passed(0)
    for k in range(micro, chunks):
        passing(k)
        passed(k - 2)
        if k >= micro + 2:
            compute(k - micro - 2)
    passed(chunks - 2)
    for k in range(chunks - micro - 2, chunks):
        if k == chunks - 2:
            passed(chunks - 1)
        compute(k)
    values = norm_parts(total[...])[0] * layer_rows[6:7, :] + layer_rows[7:8, :]
    leaving[...] = values.astype(jnp.bfloat16)
    for index in range(3):
        count_copy(index).wait()
    count[...] = count[...] + marks_ctx[0] + marks_ctx[1] + marks_ctx[2]
    for m in range(micro):
        spread.end(m)
        own_copy(m).wait()
    for part in range(3):
        for index in range(3):
            head_copy(part, index).wait_send()
    for index in range(3):
        small_copy(index).wait_send()
        marks_copy(index).wait_send()
        shard_sibling(index).wait_send()
    for k in range(chunks):
        y_copy(k).wait_send()
        z_copy(k).wait_send()
        for side in range(2):
            core_copy(k, side).wait_send()
        for copy in stored(k):
            copy.wait()

    @pl.when(moves)
    def _():
        for m in range(1, micro):
            swap(m).wait_send()
        swap_marks().wait()


def first_pass(block, shards, vectors, bias, valid, lengths, size):
    micro, rows, width = block.shape
    local = vectors.shape[1]
    pack = 4 * rows
    marks = (8, rows)
    tokens, hidden = micro * rows, shards[2].shape[1]
    anywhere = pl.BlockSpec(memory_space=pl.ANY)
    inside = pl.BlockSpec(memory_space=pltpu.VMEM)
    low = lambda *shape: jax.ShapeDtypeStruct(shape, jnp.bfloat16)
    word = lambda *shape: jax.ShapeDtypeStruct(shape, jnp.float32)
    room = lambda *shape: pltpu.VMEM(shape, jnp.bfloat16)
    return pl.pallas_call(
        functools.partial(first_kernel, size),
        in_specs=[anywhere] * 5 + [inside] * 3 + [pl.BlockSpec(memory_space=pltpu.SMEM)],
        out_specs=[anywhere, inside] + [anywhere] * 3 + [inside] * 5,
        out_shape=[
            low(micro, rows, width),
            low(width, 3 * local),
            low(width, width),
            low(width, hidden),
            low(hidden, width),
            word(8, width),
            word(1, hidden),
            word(*marks),
            word(*marks),
            low(tokens, width),
        ],
        scratch_shapes=[
            room(micro, pack, width),
            room(1, pack, 3 * local),
            room(micro, pack, local),
            pltpu.VMEM((3,) + marks, jnp.float32),
            pltpu.VMEM((3,) + marks, jnp.float32),
            room(width, width),
            room(width, hidden),
            room(hidden, width),
            pltpu.VMEM((4, 16, local), jnp.float32),
            room(tokens, width),
            room(tokens, width),
            room(tokens, hidden),
            pltpu.VMEM((tokens, width), jnp.float32),
            pltpu.VMEM((16, local), jnp.float32),
            pltpu.VMEM(marks, jnp.float32),
            pltpu.SemaphoreType.DMA((320,)),
        ],
        compiler_params=pltpu.CompilerParams(
            collective_id=2, has_side_effects=True, vmem_limit_bytes=60 * 2**20
        ),
        name="first_pass",
    )(block, *shards, vectors, bias, valid, lengths)


class Back:
    def __init__(self, wires, size, refs):
        self.wires, self.size = wires, size
        self.rows_grad, self.skip, self.qkv, self.weight, self.lengths = refs[:5]
        self.projected, self.grad_states = refs[5:7]
        self.heads_grad, self.part, self.from_sibling, self.far, self.from_across = refs[7:]
        self.micro, self.pack, self.local = self.heads_grad.shape
        self.rows = self.pack // 4
        self.w, self.sibling, self.across, self.across_sibling = wt_places()
        self.partners = (self.across, self.across_sibling, self.sibling)

    def place(self, m):
        return pl.ds(m * self.rows, self.rows)

    def heads_copy(self, m, index):
        column = pl.ds(self.partners[index] * self.local, self.local)
        return self.wires.remote(
            ("heads", m, index),
            self.rows_grad.at[self.place(m), column],
            self.heads_grad.at[m, pl.ds(self.w * self.rows, self.rows), :],
            wt=self.partners[index],
        )

    def heads_own(self, m):
        return self.wires.local(
            ("heads", m),
            self.rows_grad.at[self.place(m), pl.ds(self.w * self.local, self.local)],
            self.heads_grad.at[m, pl.ds(self.w * self.rows, self.rows), :],
        )

    def stripe(self, m, j):
        return self.part.at[m, pl.ds(j * self.rows, self.rows), :]

    def sibling_copy(self, m, index):
        j = (self.across_sibling, self.sibling)[index]
        return self.wires.remote(
            ("to sibling", m, index),
            self.stripe(m, j),
            self.from_sibling.at[m, index],
            wt=self.sibling,
        )

    def across_copy(self, m):
        return self.wires.remote(
            ("to across", m), self.far.at[m], self.from_across.at[m], wt=self.across
        )

    def begin(self, m):
        for index in range(3):
            self.heads_copy(m, index).start()
        self.heads_own(m).start()

    def arrive(self, m):
        for index in range(3):
            self.heads_copy(m, index).wait_recv()
        self.heads_own(m).wait()

    def work(self, m, following=None):
        self.arrive(m)
        if following is not None:
            self.begin(following)
        whole = pl.ds(m * self.pack, self.pack)
        projected = self.projected.at[whole, :]
        same = same_document(self.lengths, m, self.rows)
        qkv = self.qkv(m)
        attend_pack_back(self.size, same, qkv, self.heads_grad.at[m], projected)
        product = dot(projected[...], self.weight[...], ((1,), (1,)))
        self.part[m] = product.astype(jnp.bfloat16)
        for index in range(2):
            self.sibling_copy(m, index).start()

    def cross(self, m):
        for index in range(2):
            self.sibling_copy(m, index).wait_recv()
        total = self.stripe(m, self.across)[...].astype(jnp.float32)
        total = total + self.from_sibling[m, 0].astype(jnp.float32)
        self.far[m] = total.astype(jnp.bfloat16)
        self.across_copy(m).start()

    def finish(self, m):
        self.across_copy(m).wait_recv()
        total = self.skip[self.place(m), :] + self.stripe(m, self.w)[...].astype(jnp.float32)
        total = total + self.from_sibling[m, 1].astype(jnp.float32)
        total = total + self.from_across[m].astype(jnp.float32)
        self.grad_states[self.place(m), :] = total.astype(jnp.bfloat16)

    def end(self, m):
        for index in range(3):
            self.heads_copy(m, index).wait_send()
        for index in range(2):
            self.sibling_copy(m, index).wait_send()
        self.across_copy(m).wait_send()


def back_scratch(micro, pack, local, width):
    block = pltpu.VMEM((micro, pack // 4, width), jnp.bfloat16)
    return [
        pltpu.VMEM((micro, pack, local), jnp.bfloat16),
        pltpu.VMEM((micro, pack, width), jnp.bfloat16),
        pltpu.VMEM((micro, 2, pack // 4, width), jnp.bfloat16),
        block,
        block,
    ]


def swap_back(wires, rows, source, target, m, moves):
    z, w = lax.axis_index("ctx"), lax.axis_index("wt")
    block = source.at[pl.ds(m * rows, rows), :]
    if moves:
        return wires.remote(("home", m), block, target.at[m], **home_place(z, w))
    return wires.local(("home", m), block, target.at[m])


def mid_kernel(size, *refs):
    states, leaving, weight_out, weight_in, weight_down = refs[:5]
    weight, layer_rows, in_bias, marks, count, lengths = refs[5:11]
    outs = refs[11:21]
    inverse_one, inverse_two, returned = refs[21:24]
    held = refs[24:27]
    full, qkv, mixed_rows, mixed = refs[27:31]
    saved = dict(zip(SAVED, refs[31:38]))
    skip, rows_grad, projected, grad_states = refs[38:42]
    micro, rows, width = states.shape
    wires = Wires(refs[-1])
    section = lax.axis_index("section")
    spread = Spread(wires, full, mixed, mixed_rows, rows, weight.shape[1] // 3)
    given = (rows_grad, skip, lambda m: qkv.at[m], weight, lengths)
    back = Back(wires, size, given + (projected, grad_states) + refs[42:-1])
    w = spread.w
    bias = bias_of(layer_rows[:2, pl.ds(w * spread.local, spread.local)])
    kept = dict(saved, inverse_one=inverse_one, inverse_two=inverse_two)

    def stay(m):
        return wires.local(("stay", m), states.at[m], spread.stripe(m, w))

    def teacher_copy(m):
        return wires.local(("teacher", m), states.at[m], grad_states.at[pl.ds(m * rows, rows), :])

    def weight_copies():
        for index, source in enumerate((weight_out, weight_in, weight_down)):
            step = source.shape[0] if index == 0 else source.shape[0] // 4
            for row in range(0, source.shape[0], step):
                at = pl.ds(row, step)
                yield wires.local(("weight", index, row), source.at[at, :], held[index].at[at, :])

    def load_weights(first, last):
        for copy in list(weight_copies())[first:last]:
            copy.start()

    def own_loads():
        @pl.when(section == 0)
        def _():
            for m in range(micro):
                stay(m).start()

        load_weights(0, 3)

    greet(
        [{"wt": partner} for partner in back.partners] + [{"section": 1 - section}],
        [],
        own_loads,
    )

    def relay_copy(m):
        return wires.remote(("relay", m), leaving.at[m], spread.stripe(m, w), section=1 - section)

    @pl.when(section == 0)
    def _():
        for m in range(micro):
            relay_copy(m).start()

    def arrive(m):
        @pl.when(section == 0)
        def _():
            stay(m).wait()

        @pl.when(section == 1)
        def _():
            relay_copy(m).wait_recv()

        spread.send(m)

    def attend(m):
        spread.settle(m)
        project(full.at[m], weight, bias, qkv.at[m])
        attend_pack(size, same_document(lengths, m, rows), qkv.at[m], mixed.at[m])
        spread.send_back(m)
        for name, source in (("full", full), ("qkv", qkv)):
            store(name, m, source.at[m], outs[OUTS.index(name)].at[m]).start()

    def store(name, m, source, target):
        return wires.local(("store", name, m), source, target)

    def stores(m):
        at = pl.ds(m * rows, rows)
        for name, ref in [("mixed", mixed_rows)] + list(saved.items()):
            yield store(name, m, ref.at[at, :], outs[OUTS.index(name)].at[at, :])

    def covered(m):
        total = jnp.sum(jnp.sum(count[...], axis=0, keepdims=True), axis=1, keepdims=True)
        shape = (rows, rows)
        here = lax.broadcasted_iota(jnp.int32, shape, 0) == lax.broadcasted_iota(jnp.int32, shape, 1)
        column = jnp.sum(jnp.where(here, marks[m : m + 1, :], 0.0), axis=1, keepdims=True)
        return LOSS_SCALE / total * column

    def feed(*packs):
        for m in packs:
            spread.arrived_back(m)
            teacher_copy(m).wait()
        at = pl.ds(packs[0] * rows, len(packs) * rows)
        block = jnp.concatenate([spread.stripe(m, w)[...] for m in packs], axis=0)
        output = feed_forward(at, block, mixed_rows[at, :], held, layer_rows, in_bias, kept)
        saved["final"][at, :] = output.astype(jnp.bfloat16)
        factor = jnp.concatenate([covered(m) for m in packs], axis=0)
        grad = factor * (output - grad_states[at, :].astype(jnp.float32))
        saved["grad"][at, :] = grad
        skip[at, :], rows_grad[at, :] = feed_backward(at, grad, held, layer_rows, kept)
        for m in packs:
            for copy in stores(m):
                copy.start()
            back.begin(m)

    def back_copy(m):
        place = back.place(m)
        return wires.remote(
            ("return", m), grad_states.at[place, :], returned.at[place, :], section=1 - section
        )

    def finish(m):
        back.finish(m)

        @pl.when(section == 1)
        def _():
            back_copy(m).start()

    arrive(0)
    load_weights(3, 5)
    arrive(1)
    load_weights(5, 6)
    spread.hand_on(0)
    attend(0)
    arrive(2)
    load_weights(6, 8)
    spread.hand_on(1)
    attend(1)
    load_weights(8, 9)
    for m in range(micro):
        teacher_copy(m).start()
    spread.hand_on(2)
    for copy in weight_copies():
        copy.wait()
    feed(0)
    attend(2)
    feed(1, 2)
    back.work(0)
    back.cross(0)
    back.work(1)
    back.cross(1)
    finish(0)
    back.work(2)
    back.cross(2)
    finish(1)
    finish(2)
    for m in range(micro):
        spread.end(m)
        back.end(m)
        for name, source in (("full", full), ("qkv", qkv)):
            store(name, m, source.at[m], outs[OUTS.index(name)].at[m]).wait()
        for copy in stores(m):
            copy.wait()

        @pl.when(section == 1)
        def _():
            back_copy(m).wait_send()

        @pl.when(section == 0)
        def _():
            relay_copy(m).wait_send()
            back_copy(m).wait_recv()


SAVED = ("normal_one", "first", "hidden", "slope", "normal_two", "final", "grad")
OUTS = ("full", "qkv", "mixed") + SAVED


def mid_pass(states, leaving, weights, weight, layer_rows, in_bias, marks, count, lengths, size):
    micro, rows, width = states.shape
    local = weight.shape[1] // 3
    pack = 4 * rows
    tokens, hidden = micro * rows, weights[1].shape[1]
    anywhere = pl.BlockSpec(memory_space=pl.ANY)
    inside = pl.BlockSpec(memory_space=pltpu.VMEM)
    low = lambda *shape: jax.ShapeDtypeStruct(shape, jnp.bfloat16)
    word = lambda *shape: jax.ShapeDtypeStruct(shape, jnp.float32)
    held = [
        word(tokens, width),
        low(tokens, width),
        low(tokens, hidden),
        low(tokens, hidden),
        word(tokens, width),
        low(tokens, width),
        word(tokens, width),
    ]
    room = lambda shape: pltpu.VMEM(shape.shape, shape.dtype)
    kept = [low(micro, pack, width), low(micro, pack, 3 * local), low(tokens, width)]
    *results, inverse_one, inverse_two, returned = pl.pallas_call(
        functools.partial(mid_kernel, size),
        in_specs=[anywhere] * 5 + [inside] * 5 + [pl.BlockSpec(memory_space=pltpu.SMEM)],
        out_specs=[anywhere] * 10 + [inside] * 3,
        out_shape=kept + held + [word(tokens, 1), word(tokens, 1), low(tokens, width)],
        scratch_shapes=[pltpu.VMEM(part.shape, jnp.bfloat16) for part in weights]
        + [room(shape) for shape in kept]
        + [room(low(micro, pack, local))]
        + [room(shape) for shape in held]
        + [
            room(word(tokens, width)),
            room(low(tokens, width)),
            room(low(micro * pack, 3 * local)),
            room(low(tokens, width)),
        ]
        + back_scratch(micro, pack, local, width)
        + [pltpu.SemaphoreType.DMA((200,))],
        compiler_params=pltpu.CompilerParams(
            collective_id=4, has_side_effects=True, vmem_limit_bytes=62 * 2**20
        ),
        name="mid_pass",
    )(
        states,
        leaving,
        *weights,
        weight,
        layer_rows,
        in_bias,
        marks,
        count,
        lengths,
    )
    return dict(zip(OUTS, results)), inverse_one, inverse_two, returned


CHUNK = 128
RING = 6
TILE = 256
LAGS = (2, 4, 6, 8)
AHEAD = 4


def sum_into(target, parts, rows):
    step = 16

    def one(index, carry):
        at = pl.ds(pl.multiple_of(index * step, step), step)
        total = parts[0][at, :].astype(jnp.float32)
        for part in parts[1:]:
            total = total + part[at, :].astype(jnp.float32)
        target[at, :] = total.astype(jnp.bfloat16)
        return carry

    lax.fori_loop(0, rows // step, one, 0)


def chunk_list(local, width, hidden):
    down = [("down", 0, CHUNK // 4, 0), ("down", CHUNK // 4, CHUNK // 4, 0)]
    down += [("down", CHUNK // 2, CHUNK // 2, 0)]
    down += [("down", row, CHUNK, 0) for row in range(CHUNK, hidden // 4, CHUNK)]
    across = [
        ("in", row, CHUNK, column)
        for column in range(hidden // width)
        for row in range(0, local, CHUNK)
    ]
    out = [("out", row, CHUNK // 2, 0) for row in range(0, local - CHUNK // 2, CHUNK // 2)]
    out += [("out", row, CHUNK // 4, 0) for row in range(local - CHUNK // 2, local, CHUNK // 4)]
    qkv = [("qkv", row, CHUNK, part) for part in range(3) for row in range(0, local, CHUNK)]
    return down + across[:3] + qkv + across[3:] + out + [("rest", 0, 16, 0)]


def starts_of(chunks):
    rows = [chunk[2] for chunk in chunks]
    starts = [sum(rows[:k]) for k in range(len(rows) + 1)]
    return starts, [sum(rows[k % 2 : k : 2]) for k in range(len(rows) + 2)]


def last_kernel(chunks, size, *refs):
    weight, layer_rows, inverse_one, inverse_two, lengths = refs[:5]
    grad, returned, normal_two, normal_one, qkv_all, full_all, slope = refs[5:12]
    weight_out, weight_in, weight_down = refs[12:15]
    hidden, first, mixed, final = refs[15:19]
    home = refs[19]
    results = dict(zip(("qkv", "out", "in", "down", "rest"), refs[20:25]))
    grad_states, projected, full, product = refs[25:29]
    downs, ins, outs, down_both, pre_both, branch_both, rest_in = refs[29:36]
    near, far, across_in, up_in, side_in = refs[36:41]
    skip, normal, slopes, qkv_one, rows_grad, rest = refs[41:47]
    wires = Wires(refs[-1])
    z, section = lax.axis_index("ctx"), lax.axis_index("section")
    tokens, width = final.shape
    count = len(chunks)
    micro = qkv_all.shape[0]

    def qkv_copy(m):
        return wires.local(("pack", m), qkv_all.at[m], qkv_one)

    def qkv_of(m):
        qkv_copy(m).wait()
        return qkv_one

    given = (rows_grad, skip, qkv_of, weight, lengths)
    back = Back(wires, size, given + (projected, grad_states) + refs[47:-1])
    w, sibling, across, across_sibling = wt_places()
    partners = (sibling, across, across_sibling)
    local = back.local
    deep = hidden.shape[1] // 4
    starts, sides_at = starts_of(chunks)
    moves = is_moving(z, w)
    own_rows = pl.ds(0, tokens)
    blocks = hidden.shape[1] // TILE

    def tile_copies(b):
        low = full.at[pl.ds((b % 2) * TILE, TILE), :]
        if b >= blocks:
            source = weight_out.at[pl.ds((b - blocks) * TILE, TILE), :]
            return [wires.local(("tile", b), source, low)]
        columns = pl.ds(b * TILE, TILE)
        wide = full.at[pl.ds(2 * TILE, width), pl.ds((b % 4) * TILE, TILE)]
        return [
            wires.local(("tile", b), weight_down.at[columns, :], low),
            wires.local(("wide", b), weight_in.at[:, columns], wide),
            wires.local(("slope", b), slope.at[:, columns], slopes.at[b % 2]),
        ]

    def start_tiles(b):
        for copy in tile_copies(b):
            copy.start()

    def first_copies():
        return [
            wires.local("grad", grad, skip),
            wires.local("returned", returned, rows_grad),
            wires.local("normal two", normal_two, normal),
        ]

    def normal_copy():
        return wires.local("normal", normal_one, normal)

    def own_loads():
        for copy in first_copies():
            copy.start()
        start_tiles(0)
        start_tiles(1)
        qkv_copy(0).start()

    greet(
        [{"wt": partner} for partner in partners],
        [
            (moves, home_place(z, w)),
            (moves, plane_place(z, w)),
            (z > 0, {"ctx": z - 1}),
            (z < 3, {"ctx": z + 1}),
        ],
        own_loads,
    )

    def step_first():
        for copy in first_copies():
            copy.wait()

        @pl.when(section == 0)
        def _():
            skip[...] = rows_grad[...].astype(jnp.float32)

        values = skip[...]
        rest_rows[6] = jnp.sum(values * normal[...], axis=0, keepdims=True)
        rest_rows[7] = jnp.sum(values, axis=0, keepdims=True)
        values = norm_back(values, layer_rows[6:7, :], normal[...], inverse_two[...])
        skip[...] = values
        low = values.astype(jnp.bfloat16)
        down_both[own_rows, :] = low
        to_sibling("down", down_both, 0).start()
        rest_rows[5] = dot(jnp.ones((16, tokens), jnp.bfloat16), low)[:1]
        for r, row in rest_rows.items():
            for j in range(4):
                rest[j * 16 + r : j * 16 + r + 1, :local] = row[:, j * local : (j + 1) * local]
        normal_copy().start()

    rest_rows = {}

    def step_back(b):
        for copy in tile_copies(b):
            copy.wait()
        columns = pl.ds(b * TILE, TILE)
        low = full[pl.ds((b % 2) * TILE, TILE), :]
        wide = full[pl.ds(2 * TILE, width), pl.ds((b % 4) * TILE, TILE)]
        grad = dot(down_both[own_rows, :], low, ((1,), (1,)))
        grad = (grad * slopes[b % 2].astype(jnp.float32)).astype(jnp.bfloat16)
        pre_both[own_rows, columns] = grad
        skip[...] += dot(grad, wide, ((1,), (1,)))
        start_tiles(b + 2)
        if (b + 1) * TILE % width == 0:
            to_sibling("pre", pre_both, (b + 1) * TILE // width - 1).start()

    def to_sibling(key, array, column):
        at = pl.ds(column * width, width)
        target = array.at[pl.ds(tokens, tokens), at]
        return wires.remote((key, column), array.at[own_rows, at], target, wt=sibling)

    def step_norm():
        normal_copy().wait()
        ones = jnp.ones((16, tokens), jnp.bfloat16)
        grad_first = skip[...]
        rows = {}
        rows[3] = jnp.sum(grad_first * normal[...], axis=0, keepdims=True)
        rows[4] = jnp.sum(grad_first, axis=0, keepdims=True)
        grad_summed = norm_back(grad_first, layer_rows[3:4, :], normal[...], inverse_one[...])
        skip[...] = grad_summed
        branch = grad_summed.astype(jnp.bfloat16)
        branch_both[own_rows, :] = branch
        to_sibling("branch", branch_both, 0).start()
        rows[2] = dot(ones, branch)[:1]
        sums = dot(ones, pre_both[own_rows, :])[:1]
        for j in range(4):
            for r, row in rows.items():
                rest[j * 16 + r : j * 16 + r + 1, :local] = row[:, j * local : (j + 1) * local]
            for r in range(deep // local):
                at = j * deep + r * local
                rest[j * 16 + r : j * 16 + r + 1, local : 2 * local] = sums[:, at : at + local]
        for copy in rest_copies():
            copy.start()

    def step_out(b):
        for copy in tile_copies(b):
            copy.wait()
        tile = full[pl.ds((b % 2) * TILE, TILE), :]
        grad = dot(branch_both[own_rows, :], tile, ((1,), (1,))).astype(jnp.bfloat16)
        rows_grad[:, pl.ds((b - blocks) * TILE, TILE)] = grad
        if b + 2 < blocks + width // TILE:
            start_tiles(b + 2)

    def last_out():
        for b in range(blocks, blocks + width // TILE):
            step_out(b)
        full_copy().start()
        for m in range(micro):
            back.begin(m)

    def both(key, source, target, at, columns, theirs):
        mine = (pl.ds(0, tokens), at)
        other = (pl.ds(tokens, tokens), at)
        return (
            wires.local(key, source.at[:, columns], target.at[mine]),
            wires.remote(key, source.at[:, theirs], target.at[other], wt=sibling),
        )

    def sides(key, source, block, target):
        for side, (j, k) in enumerate(((w, sibling), (across, across_sibling))):
            yield from both(
                key + (side,),
                source,
                target,
                pl.ds(side * CHUNK, CHUNK),
                pl.ds(block(j), CHUNK),
                pl.ds(block(k), CHUNK),
            )

    def down_block(index):
        return sides(
            ("down", index), hidden, lambda j: j * deep + index * CHUNK, downs.at[index]
        )

    def in_block(half):
        return sides(("in", half), first, lambda j: j * local + half * CHUNK, ins.at[half])

    def out_block(half):
        return sides(("out", half), mixed, lambda j: j * local + half * CHUNK, outs.at[half])

    def rest_copies():
        for side, k in enumerate((sibling, across_sibling)):
            yield wires.remote(
                ("rest", side), rest.at[pl.ds(k * 16, 16), :], rest_in.at[side], wt=sibling
            )

    halves = local // CHUNK
    columns = hidden.shape[1] // width
    loads = [lambda index=index: down_block(index) for index in range(deep // CHUNK)]
    loads += [lambda half=half: in_block(half) for half in range(halves)]
    loads += [lambda half=half: out_block(half) for half in range(halves)]

    def full_copy():
        return wires.local("full", full_all, full)

    def needs(k):
        kind, row, _, column = chunks[k]
        index = row // CHUNK
        copies = []
        if kind == "down":
            if index == 0:
                to_sibling("down", down_both, 0).wait_recv()
            copies += down_block(index)
        elif kind == "in":
            if column == 0:
                copies += in_block(index)
            if index == 0:
                to_sibling("pre", pre_both, column).wait_recv()
        else:
            copies += out_block(index)
            if index == 0:
                to_sibling("branch", branch_both, 0).wait_recv()
        for index, copy in enumerate(copies):
            (copy.wait if index % 2 == 0 else copy.wait_recv)()

    def operands(k):
        kind, row, _, column = chunks[k]
        index = row // CHUNK
        if kind == "down":
            return downs[index], down_both[...]
        if kind == "in":
            return ins[index], pre_both[:, column * width : (column + 1) * width]
        return outs[index], branch_both[...]

    def is_piece(k):
        return chunks[k][0] == "qkv"

    def rows_of(k):
        return chunks[k][2]

    def slot(buffer, k):
        return buffer.at[pl.ds(starts[k], rows_of(k)), :]

    def beside_slot(k):
        return side_in.at[pl.ds(sides_at[k], rows_of(k)), :]

    def result(k):
        kind, row, rows, column = chunks[k]
        if kind == "rest":
            return results["rest"]
        return results[kind].at[pl.ds(row, rows), pl.ds(column * width, width)]

    def piece(k, j):
        _, row, rows, part = chunks[k]
        return product.at[part, pl.ds(j * local + row, rows), :]

    def piece_place(k):
        return near.at[pl.ds(starts[k], rows_of(k)), pl.ds(w * local, local)]

    def piece_copy(k, index):
        place = piece_place(k)
        return wires.remote(
            ("piece", k, index), piece(k, partners[index]), place, wt=partners[index]
        )

    def piece_own(k):
        return wires.local(("piece", k), piece(k, w), piece_place(k))

    direct = [k for k in range(count) if not is_piece(k)]
    bases = [k for k in direct if chunks[k][1] % CHUNK == 0]

    def base_of(k):
        return max(base for base in bases if base <= k)

    def far_slot(k, rows):
        return far.at[bases.index(base_of(k)) % RING, pl.ds(chunks[k][1] % CHUNK, rows), :]

    def across_copy(k):
        source = far_slot(k, rows_of(k))
        return wires.remote(("chunk", k), source, slot(across_in, k), wt=across)

    def place_of(k, role):
        return role if k % 2 == 0 else 3 - role

    def up_copy(k, role):
        target = place_of(k, 1 if role == 0 else 2)
        return wires.remote(("up", k), slot(near, k), slot(up_in, k), ctx=target)

    def side_copy(k):
        return wires.remote(("side", k), slot(near, k), beside_slot(k), ctx=place_of(k, 1))

    def down_copy(k, role):
        origin = result(k) if role == 3 else slot(near, k)
        return pltpu.make_async_remote_copy(
            origin,
            result(k),
            wires.at("down send", k, 1 if role == 2 else 0),
            wires.at("down recv", k),
            device_id={"ctx": place_of(k, role)},
            device_id_type=MESH,
        )

    def keep_copy(k):
        return wires.local(("keep", k), slot(near, k), result(k))

    def on(k, role, step):
        pl.when(z == place_of(k, role))(step)

    def summands(k):
        if is_piece(k):
            return [slot(near, k)]
        return [slot(near, k), slot(across_in, k)]

    def begin(k):
        kind, row, _, column = chunks[k]
        if is_piece(k):
            if row == 0:
                at = pl.ds(column * local, local)
                grad = dot(full[...], projected[:, at], ((0,), (0,)))
                product[column] = grad.astype(jnp.bfloat16)
            for partner in range(3):
                piece_copy(k, partner).start()
            piece_own(k).start()
            return
        if k in bases:
            order = bases.index(k)
            for old in direct:
                if order >= RING and base_of(old) == bases[order - RING]:
                    across_copy(old).wait_send()
        if kind == "rest":
            for copy in rest_copies():
                copy.wait_recv()
            ones = jnp.ones((16, projected.shape[0]), jnp.bfloat16)
            sums = dot(ones, projected[...])
            row = lax.broadcasted_iota(jnp.int32, (16, local), 0)
            own = jnp.where(row == 0, sums[:, :local], 0.0)
            own = own + jnp.where(row == 1, sums[:, 2 * local :], 0.0)
            own = jnp.concatenate([own, jnp.zeros((16, width - local), jnp.float32)], axis=1)
            own = own + rest[pl.ds(w * 16, 16), :] + rest_in[0]
            other = rest[pl.ds(across * 16, 16), :] + rest_in[1]
            slot(near, k)[...] = own.astype(jnp.bfloat16)
            far_slot(k, 16)[...] = other.astype(jnp.bfloat16)
        elif k in bases:
            needs(k)
            left, right = operands(k)
            grad = dot(left, right, ((0,), (0,))).astype(jnp.bfloat16)
            near[pl.ds(starts[k], CHUNK), :] = grad[:CHUNK]
            far_slot(k, CHUNK)[...] = grad[CHUNK:]
        across_copy(k).start()

    def settle(k):
        if is_piece(k):
            for index in range(3):
                piece_copy(k, index).wait_recv()
            piece_own(k).wait()
        else:
            across_copy(k).wait_recv()
        for role in (0, 3):

            def step(role=role):
                if not is_piece(k):
                    sum_into(slot(near, k), summands(k), rows_of(k))
                up_copy(k, role).start()

            on(k, role, step)

    def aside(k):
        def step():
            up_copy(k, 3).wait_recv()
            sum_into(slot(near, k), summands(k) + [slot(up_in, k)], rows_of(k))
            side_copy(k).start()

        on(k, 2, step)

    def finish(k):
        def step():
            up_copy(k, 0).wait_recv()
            side_copy(k).wait_recv()
            parts = summands(k) + [slot(up_in, k), beside_slot(k)]
            sum_into(slot(near, k), parts, rows_of(k))
            down_copy(k, 0).start()
            down_copy(k, 2).start()
            keep_copy(k).start()

        on(k, 1, step)

    def forward(k):
        def step():
            down_copy(k, 2).wait_recv()
            down_copy(k, 3).start()

        on(k, 2, step)

    def go_home(m, source, here, do):
        @pl.when(moves & here)
        def _():
            do(swap_back(wires, back.rows, source, home, m, True))

        @pl.when(jnp.logical_not(moves) & here)
        def _():
            do(swap_back(wires, back.rows, source, home, m, False))

    def done(m):
        back.finish(m)
        go_home(m, grad_states, section == 0, lambda copy: copy.start())

    def final_home(m):
        go_home(m, final, section == 1, lambda copy: copy.start())

    beside = {
        9: [lambda: back.work(0), lambda: qkv_copy(1).start()],
        10: [lambda: back.work(1), lambda: qkv_copy(2).start()],
        11: [lambda: back.work(2)],
        17: [lambda: final_home(0)],
        18: [lambda: final_home(1)],
        19: [lambda: final_home(2)],
        20: [lambda: back.cross(0)],
        22: [lambda: back.cross(1)],
        24: [lambda: back.cross(2), lambda: done(0)],
        26: [lambda: done(1)],
        28: [lambda: done(2)],
        7: [step_norm, last_out],
    }
    steps = iter(range(blocks))
    for tick, many in enumerate((0, 0, 2, 3, 3, 4, 4)):
        beside[tick] = [functools.partial(step_back, next(steps)) for _ in range(many)]

    for load in loads:
        for copy in load():
            copy.start()
    rest[...] = jnp.zeros_like(rest)
    step_first()
    stages = (settle, aside, finish, forward)
    begun, first_piece = 0, min(k for k in range(count) if is_piece(k))
    for tick in range(count + LAGS[-1]):
        for lag, stage in reversed(list(zip(LAGS, stages))):
            if 0 <= tick - lag < count:
                stage(tick - lag)
        while begun < min(count, tick + 1 + max(0, min(AHEAD, tick - 11))):
            if begun == first_piece:
                full_copy().wait()
            begin(begun)
            begun += 1
        for step in beside.get(tick, []):
            step()
    for m in range(back.micro):
        back.end(m)
        go_home(m, grad_states, z >= 0, lambda copy: copy.wait())
    for copy in rest_copies():
        copy.wait_send()
    for load in loads:
        for index, copy in enumerate(load()):
            if index % 2 == 1:
                copy.wait_send()
    for column in range(columns):
        to_sibling("pre", pre_both, column).wait_send()
    to_sibling("branch", branch_both, 0).wait_send()
    to_sibling("down", down_both, 0).wait_send()
    for k in direct:
        if base_of(k) in bases[-RING:]:
            across_copy(k).wait_send()
    for k in range(count):
        if is_piece(k):
            for index in range(3):
                piece_copy(k, index).wait_send()

        def ends(role):
            up_copy(k, role).wait_send()
            down_copy(k, role).wait_recv()

        def middle():
            side_copy(k).wait_send()
            down_copy(k, 3).wait_send()

        def owner():
            down_copy(k, 0).wait_send()
            down_copy(k, 2).wait_send()
            keep_copy(k).wait()

        on(k, 0, lambda: ends(0))
        on(k, 3, lambda: ends(3))
        on(k, 2, middle)
        on(k, 1, owner)


def last_pass(weight, layer_rows, inverses, lengths, arrays, weights, operands, size):
    micro, pack, local = arrays[4].shape
    local = local // 3
    tokens, width = operands[3].shape
    hidden = operands[0].shape[1]
    chunks = chunk_list(local, width, hidden)
    count = len(chunks)
    starts, sides_at = starts_of(chunks)
    inside = pl.BlockSpec(memory_space=pltpu.VMEM)
    anywhere = pl.BlockSpec(memory_space=pl.ANY)
    low = lambda *shape: jax.ShapeDtypeStruct(shape, jnp.bfloat16)
    room = lambda *shape: pltpu.VMEM(shape, jnp.bfloat16)
    halves = local // CHUNK
    return pl.pallas_call(
        functools.partial(last_kernel, chunks, size),
        in_specs=[inside] * 4 + [pl.BlockSpec(memory_space=pltpu.SMEM)] + [anywhere] * 14,
        out_specs=[anywhere] * 6,
        out_shape=[
            low(micro, pack // 4, width),
            low(local, 3 * width),
            low(local, width),
            low(local, hidden),
            low(hidden // 4, width),
            low(16, width),
        ],
        scratch_shapes=[
            room(tokens, width),
            room(micro * pack, 3 * local),
            room(micro * pack, width),
            room(3, width, local),
            room(hidden // 4 // CHUNK, 2 * tokens, 2 * CHUNK),
            room(halves, 2 * tokens, 2 * CHUNK),
            room(halves, 2 * tokens, 2 * CHUNK),
            room(2 * tokens, width),
            room(2 * tokens, hidden),
            room(2 * tokens, width),
            pltpu.VMEM((2, 16, width), jnp.float32),
            room(starts[count], width),
            room(RING, CHUNK, width),
            room(starts[count], width),
            room(starts[count], width),
            room(max(sides_at[count:]), width),
            pltpu.VMEM((tokens, width), jnp.float32),
            pltpu.VMEM((tokens, width), jnp.float32),
            room(2, tokens, TILE),
            room(pack, 3 * local),
            room(tokens, width),
            pltpu.VMEM((64, width), jnp.float32),
        ]
        + back_scratch(micro, pack, local, width)
        + [pltpu.SemaphoreType.DMA((900,))],
        compiler_params=pltpu.CompilerParams(
            collective_id=1, has_side_effects=True, vmem_limit_bytes=63 * 2**20
        ),
        name="last_pass",
    )(
        weight,
        layer_rows,
        *inverses,
        lengths,
        *arrays,
        *weights,
        *operands,
    )


def widen_kernel(*refs):
    count = len(refs) // 2
    for source, target in zip(refs[: count - 1], refs[count:]):
        target[0] = source[...].astype(jnp.float32)
    rest, (bias, rows) = refs[count - 1], refs[-2:]
    local = rows.shape[2]
    rows[0] = rest[:8, :local].astype(jnp.float32)
    for row in range(bias.shape[1] // local):
        part = rest[row : row + 1, local : 2 * local]
        bias[:, row * local : (row + 1) * local] = part.astype(jnp.float32)


def widen(sums, steps=8):
    *sums, rest = sums
    local = sums[1].shape[0]
    cut = lambda part: (part.shape[0] // steps, part.shape[1])
    word = lambda *shape: jax.ShapeDtypeStruct(shape, jnp.float32)
    still = lambda *shape: pl.BlockSpec(shape, lambda step: (0,) * len(shape))
    return pl.pallas_call(
        widen_kernel,
        grid=(steps,),
        in_specs=[pl.BlockSpec(cut(part), lambda step: (step, 0)) for part in sums]
        + [still(*rest.shape)],
        out_specs=[pl.BlockSpec((1,) + cut(part), lambda step: (0, step, 0)) for part in sums]
        + [still(1, sums[3].shape[0]), still(1, 8, local)],
        out_shape=[word(1, *part.shape) for part in sums]
        + [word(1, sums[3].shape[0]), word(1, 8, local)],
        name="widen",
    )(*sums, rest)


def relay(boundary, lengths, valid, w_qkv, w_out, w_in, w_down, bias_in, vectors):
    micro, rows, width = boundary.shape[1:]
    size = width // HEADS
    local = vectors.shape[2]
    shards = (w_qkv[0], w_out[0], w_in[0], w_down[0])
    own, weight_qkv, *weights, layer_rows, in_bias, marks, count, leaving = first_pass(
        boundary[0], shards, vectors[0], bias_in, valid, lengths, size
    )
    leaving = leaving.reshape(micro, rows, width)
    kept, inverse_one, inverse_two, returned = mid_pass(
        own, leaving, weights, weight_qkv, layer_rows, in_bias, marks, count, lengths, size
    )
    home, *sums = last_pass(
        weight_qkv,
        layer_rows,
        (inverse_one, inverse_two),
        lengths,
        (
            kept["grad"],
            returned,
            kept["normal_two"],
            kept["normal_one"],
            kept["qkv"],
            kept["full"].reshape(-1, width),
            kept["slope"],
        ),
        weights,
        (kept["hidden"], kept["first"], kept["mixed"], kept["final"]),
        size,
    )
    return (home[None], *widen(sums))


def solution(mesh):
    in_specs = (
        P("section", None, ("wt", "ctx"), None),
        P(),
        P(None, ("wt", "ctx")),
        P("section", "wt", None),
        P("section", "wt", None),
        P("section", "wt", None),
        P("section", "wt", None),
        P("section", "wt"),
        P("section", None, "wt"),
    )
    out_specs = (
        P("section", None, ("wt", "ctx"), None),
        P("section", "wt", None),
        P("section", "wt", None),
        P("section", "wt", None),
        P("section", "wt", None),
        P("section", "wt"),
        P("section", None, "wt"),
    )
    square = mesh.shape["ctx"] == mesh.shape["wt"] == 4
    return jax.shard_map(relay if square else shards, mesh=mesh, in_specs=in_specs, out_specs=out_specs, check_vma=False)
```

```python
import functools

import jax
import jax.numpy as jnp
from jax import lax
from jax.experimental import pallas as pl
from jax.experimental.pallas import tpu as pltpu
from jax.sharding import PartitionSpec as P

HEADS = 16
LOSS_SCALE = 1024


def shifted(block, axis, distance):
    devices = range(lax.axis_size(axis))
    route = [(i - distance, i) for i in devices if i - distance in devices]
    return lax.ppermute(block, axis, route)


def as_sent(x):

    def short(part):
        return part.astype(jnp.bfloat16) if part.dtype == jnp.float32 else part

    return jax.tree.map(short, x)


def layer_norm(values, gain, shift):
    center = jnp.mean(values, axis=-1, keepdims=True)
    offset = values - center
    spread = jnp.mean(offset * offset, axis=-1, keepdims=True)
    return offset * lax.rsqrt(spread + 1e-05) * gain + shift


def exact_gelu(values):
    return jax.nn.gelu(values, approximate=False)


def dealt_ids(length_row, pack_size, ctx_count):
    ends = jnp.cumsum(length_row)
    places = jnp.arange(pack_size, dtype=jnp.int32)
    natural = jnp.sum((places[:, None] >= ends[None, :]).astype(jnp.int32), axis=1)
    return natural.reshape(pack_size // ctx_count, ctx_count).T.reshape(pack_size)


def split_blocks(full_kv, ids_keys):
    block = min(512, full_kv.shape[0])
    count_blocks = full_kv.shape[0] // block
    return (
        full_kv.reshape(count_blocks, block, full_kv.shape[1]),
        ids_keys.reshape(count_blocks, block),
    )


def split_kv(block_kv, heads):
    half = block_kv.shape[1] // 2
    keys = block_kv[:, :half].reshape(block_kv.shape[0], heads, -1)
    values = block_kv[:, half:].reshape(block_kv.shape[0], heads, -1)
    return (keys, values)


def block_scores(queries, keys, ids_query, ids_keys, scale):
    scores = jnp.einsum("qhd,khd->hqk", queries, keys, preferred_element_type=jnp.float32) * scale
    same = ids_query[:, None] == ids_keys[None, :]
    return jnp.where(same[None], scores, -1000000000.0)


def attend_forward(queries, full_kv, ids_query, ids_keys, heads, scale):
    blocks, id_blocks = split_blocks(full_kv, ids_keys)
    query_rows = queries.shape[0]

    def total_step(carry, items):
        run_max, run_sum = carry
        keys, values = split_kv(items[0], heads)
        scores = block_scores(queries, keys, ids_query, items[1], scale)
        new_max = jnp.maximum(run_max, jnp.max(scores, axis=-1))
        run_sum = run_sum * jnp.exp(run_max - new_max) + jnp.sum(
            jnp.exp(scores - new_max[..., None]), axis=-1
        )
        return ((new_max, run_sum), None)

    start = (
        jnp.full((heads, query_rows), -1e30, jnp.float32),
        jnp.zeros((heads, query_rows), jnp.float32),
    )
    (run_max, run_sum), _ = lax.scan(total_step, start, (blocks, id_blocks))
    log_total = run_max + jnp.log(run_sum)

    def mix_step(carry, items):
        keys, values = split_kv(items[0], heads)
        scores = block_scores(queries, keys, ids_query, items[1], scale)
        probs = jnp.exp(scores - log_total[..., None]).astype(jnp.bfloat16)
        return (
            carry + jnp.einsum("hqk,khd->qhd", probs, values, preferred_element_type=jnp.float32),
            None,
        )

    mixed, _ = lax.scan(mix_step, jnp.zeros(queries.shape, jnp.float32), (blocks, id_blocks))
    return (mixed.reshape(query_rows, -1), log_total)


def attend_backward(queries, full_kv, ids_query, ids_keys, mixed_grad, log_total, heads, scale):
    blocks, id_blocks = split_blocks(full_kv, ids_keys)
    grad_heads = mixed_grad.reshape(queries.shape)

    def inner_step(carry, items):
        keys, values = split_kv(items[0], heads)
        scores = block_scores(queries, keys, ids_query, items[1], scale)
        probs = jnp.exp(scores - log_total[..., None])
        prob_grad = jnp.einsum(
            "qhd,khd->hqk", grad_heads, values, preferred_element_type=jnp.float32
        )
        return (carry + jnp.sum(probs * prob_grad, axis=-1), None)

    inner, _ = lax.scan(inner_step, jnp.zeros(log_total.shape, jnp.float32), (blocks, id_blocks))

    def grad_step(carry, items):
        keys, values = split_kv(items[0], heads)
        scores = block_scores(queries, keys, ids_query, items[1], scale)
        probs = jnp.exp(scores - log_total[..., None])
        prob_grad = jnp.einsum(
            "qhd,khd->hqk", grad_heads, values, preferred_element_type=jnp.float32
        )
        score_grad = (probs * (prob_grad - inner[..., None])).astype(jnp.bfloat16)
        carry = (
            carry
            + jnp.einsum("hqk,khd->qhd", score_grad, keys, preferred_element_type=jnp.float32)
            * scale
        )
        key_grad = (
            jnp.einsum("hqk,qhd->khd", score_grad, queries, preferred_element_type=jnp.float32)
            * scale
        )
        value_grad = jnp.einsum(
            "hqk,qhd->khd",
            probs.astype(jnp.bfloat16),
            grad_heads,
            preferred_element_type=jnp.float32,
        )
        block = keys.shape[0]
        return (
            carry,
            jnp.concatenate([key_grad.reshape(block, -1), value_grad.reshape(block, -1)], axis=1),
        )

    query_grad, partial_kv = lax.scan(
        grad_step, jnp.zeros(queries.shape, jnp.float32), (blocks, id_blocks)
    )
    query_grad = query_grad.reshape(queries.shape[0], -1)
    return (query_grad, partial_kv.reshape(-1, partial_kv.shape[-1]), inner)


def shards(boundary, lengths, valid, w_qkv, w_out, w_in, w_down, bias_in, vectors):
    section_at = lax.axis_index("section")
    ctx_count = lax.axis_size("ctx")
    ctx_at = lax.axis_index("ctx")
    wt_at = lax.axis_index("wt")
    micro_count = boundary.shape[1]
    row_count = boundary.shape[2]
    width = boundary.shape[3]
    pack_size = row_count * ctx_count
    head_size = width // HEADS
    scale = head_size ** (-0.5)
    gathered = (
        lax.all_gather(w_qkv[0], "wt", axis=0, tiled=True),
        lax.all_gather(w_out[0], "wt", axis=0, tiled=True),
        lax.all_gather(w_in[0], "wt", axis=0, tiled=True),
        lax.all_gather(w_down[0], "wt", axis=0, tiled=True),
        lax.all_gather(bias_in[0], "wt", axis=0, tiled=True),
        lax.all_gather(vectors[0], "wt", axis=1, tiled=True),
    )
    weight_qkv, weight_out, weight_in, weight_down, in_bias, vector_rows = gathered
    in_bias = in_bias.astype(jnp.float32)
    vector_rows = vector_rows.astype(jnp.float32)
    qkv_bias = jnp.concatenate([vector_rows[0], jnp.zeros((width,), jnp.float32), vector_rows[1]])
    my_lengths = lax.dynamic_index_in_dim(lengths, wt_at, 1, keepdims=False)

    def ids_of(length_row):
        return dealt_ids(length_row, pack_size, ctx_count)

    pack_ids = jax.vmap(ids_of)(my_lengths)
    query_ids = lax.dynamic_slice_in_dim(pack_ids, ctx_at * row_count, row_count, 1)
    count = lax.psum(jnp.sum(valid.astype(jnp.float32)), ("ctx", "wt"))
    factor = LOSS_SCALE / count
    empty_rows = jnp.zeros((row_count, width), jnp.bfloat16)
    arriving = empty_rows
    kept_list = []
    cotangents = []
    final_states = []
    for tick_at in range(micro_count + 1):
        own_input = boundary[0, tick_at] if tick_at < micro_count else empty_rows
        inputs = jnp.where(section_at == 0, own_input, arriving)
        micro_here = jnp.clip(tick_at - section_at, 0, micro_count - 1)
        ids_keys = lax.dynamic_index_in_dim(pack_ids, micro_here, 0, keepdims=False)
        ids_query = lax.dynamic_index_in_dim(query_ids, micro_here, 0, keepdims=False)
        residual = inputs.astype(jnp.float32)
        projected = jnp.dot(inputs, weight_qkv, preferred_element_type=jnp.float32) + qkv_bias
        layer_queries = (
            projected[:, :width].astype(jnp.bfloat16).reshape(row_count, HEADS, head_size)
        )
        layer_local_kv = projected[:, width:].astype(jnp.bfloat16)
        layer_full_kv = lax.all_gather(layer_local_kv, "ctx", axis=0, tiled=True)
        mixed, layer_log_total = attend_forward(
            layer_queries, layer_full_kv, ids_query, ids_keys, HEADS, scale
        )
        layer_mixed_low = mixed.astype(jnp.bfloat16)
        branch = (
            jnp.dot(layer_mixed_low, weight_out, preferred_element_type=jnp.float32)
            + vector_rows[2]
        )
        layer_summed = residual + branch
        first = layer_norm(layer_summed, vector_rows[3], vector_rows[4])
        layer_first_low = first.astype(jnp.bfloat16)
        layer_hidden_pre = (
            jnp.dot(layer_first_low, weight_in, preferred_element_type=jnp.float32) + in_bias
        )
        layer_hidden_low = exact_gelu(layer_hidden_pre).astype(jnp.bfloat16)
        layer_second = first + (
            jnp.dot(layer_hidden_low, weight_down, preferred_element_type=jnp.float32)
            + vector_rows[5]
        )
        output = layer_norm(layer_second, vector_rows[6], vector_rows[7])
        layer_kept = (
            inputs,
            layer_queries,
            layer_local_kv,
            layer_full_kv,
            layer_mixed_low,
            layer_log_total,
            layer_summed,
            layer_first_low,
            layer_hidden_pre,
            layer_hidden_low,
            layer_second,
            ids_keys,
            ids_query,
        )
        output, kept = (output, layer_kept)
        kept_list.append(kept)
        if tick_at > 0:
            teacher = boundary[0, tick_at - 1].astype(jnp.float32)
            covered = valid[tick_at - 1].astype(jnp.float32)[:, None]
            cotangents.append(factor * covered * (output - teacher))
            final_states.append(output.astype(jnp.bfloat16))
        else:
            cotangents.append(jnp.zeros((row_count, width), jnp.float32))
        if tick_at < micro_count:
            arriving = shifted(output.astype(jnp.bfloat16), "section", 1)
    returning = empty_rows
    totals = None
    input_grads = [None] * micro_count
    for back_at in range(micro_count + 1):
        forward_at = micro_count - back_at
        grad_output = jnp.where(
            section_at == 1, cotangents[forward_at], returning.astype(jnp.float32)
        )
        (
            layer_inputs,
            queries,
            local_kv,
            full_kv,
            mixed_low,
            log_total,
            summed,
            first_low,
            hidden_pre,
            hidden_low,
            second,
            layer_ids_keys,
            layer_ids_query,
        ) = kept_list[forward_at]
        full_kv = lax.all_gather(local_kv, "ctx", axis=0, tiled=True)
        _, pull_last = jax.vjp(layer_norm, second, vector_rows[6], vector_rows[7])
        grad_second, grad_gain_two, grad_shift_two = pull_last(grad_output)
        down_low = grad_second.astype(jnp.bfloat16)
        layer_grad_down = jnp.einsum(
            "rf,rd->fd", hidden_low, down_low, preferred_element_type=jnp.float32
        )
        grad_bias_two = jnp.sum(down_low.astype(jnp.float32), axis=0)
        _, pull_gelu = jax.vjp(exact_gelu, hidden_pre)
        (grad_pre,) = pull_gelu(
            jnp.einsum("rd,fd->rf", down_low, weight_down, preferred_element_type=jnp.float32)
        )
        pre_low = grad_pre.astype(jnp.bfloat16)
        layer_grad_in = jnp.einsum(
            "rd,rf->df", first_low, pre_low, preferred_element_type=jnp.float32
        )
        layer_grad_bias_in = jnp.sum(pre_low.astype(jnp.float32), axis=0)
        grad_first = grad_second + jnp.einsum(
            "rf,df->rd", pre_low, weight_in, preferred_element_type=jnp.float32
        )
        _, pull_first = jax.vjp(layer_norm, summed, vector_rows[3], vector_rows[4])
        grad_summed, grad_gain_one, grad_shift_one = pull_first(grad_first)
        branch_low = grad_summed.astype(jnp.bfloat16)
        layer_grad_out = jnp.einsum(
            "rd,re->de", mixed_low, branch_low, preferred_element_type=jnp.float32
        )
        grad_bias_out = jnp.sum(branch_low.astype(jnp.float32), axis=0)
        mixed_grad = jnp.einsum(
            "re,de->rd", branch_low, weight_out, preferred_element_type=jnp.float32
        ).astype(jnp.bfloat16)
        query_grad, partial_kv, inner = attend_backward(
            queries, full_kv, layer_ids_query, layer_ids_keys, mixed_grad, log_total, HEADS, scale
        )
        kv_grad = lax.psum_scatter(
            partial_kv.astype(jnp.bfloat16), "ctx", scatter_dimension=0, tiled=True
        )
        query_low = query_grad.astype(jnp.bfloat16)
        projected_grad = jnp.concatenate([query_low, kv_grad], axis=1)
        layer_grad_qkv = jnp.einsum(
            "rd,re->de", layer_inputs, projected_grad, preferred_element_type=jnp.float32
        )
        vector_grad = jnp.stack(
            [
                jnp.sum(query_low.astype(jnp.float32), axis=0),
                jnp.sum(kv_grad[:, width:].astype(jnp.float32), axis=0),
                grad_bias_out,
                grad_gain_one,
                grad_shift_one,
                grad_bias_two,
                grad_gain_two,
                grad_shift_two,
            ]
        )
        grad_inputs = grad_summed + jnp.einsum(
            "re,de->rd", projected_grad, weight_qkv, preferred_element_type=jnp.float32
        )
        grad_inputs, grads = (
            grad_inputs,
            (
                layer_grad_qkv,
                layer_grad_out,
                layer_grad_in,
                layer_grad_down,
                layer_grad_bias_in,
                vector_grad,
            ),
        )
        totals = grads if totals is None else jax.tree.map(jnp.add, totals, grads)
        if forward_at < micro_count:
            input_grads[forward_at] = grad_inputs
        if back_at < micro_count:
            returning = shifted(grad_inputs.astype(jnp.bfloat16), "section", -1)
    results = jnp.stack(
        [
            jnp.where(section_at == 0, input_grads[index].astype(jnp.bfloat16), final_states[index])
            for index in range(micro_count)
        ]
    )[None]
    shares = (
        lax.psum_scatter(
            totals[0].astype(jnp.bfloat16), "wt", scatter_dimension=0, tiled=True
        ).astype(jnp.float32),
        lax.psum_scatter(
            totals[1].astype(jnp.bfloat16), "wt", scatter_dimension=0, tiled=True
        ).astype(jnp.float32),
        lax.psum_scatter(
            totals[2].astype(jnp.bfloat16), "wt", scatter_dimension=0, tiled=True
        ).astype(jnp.float32),
        lax.psum_scatter(
            totals[3].astype(jnp.bfloat16), "wt", scatter_dimension=0, tiled=True
        ).astype(jnp.float32),
        lax.psum_scatter(
            totals[4].astype(jnp.bfloat16), "wt", scatter_dimension=0, tiled=True
        ).astype(jnp.float32),
        lax.psum_scatter(
            totals[5].astype(jnp.bfloat16), "wt", scatter_dimension=1, tiled=True
        ).astype(jnp.float32),
    )
    shares = jax.tree.map(lambda part: part.astype(jnp.float32), lax.psum(as_sent(shares), "ctx"))
    grad_qkv, grad_out, grad_in, grad_down, grad_bias_in, grad_vectors = shares
    return (
        results,
        grad_qkv[None],
        grad_out[None],
        grad_in[None],
        grad_down[None],
        grad_bias_in[None],
        grad_vectors[None],
    )


PAIR = 128
FAR = -1000000000.0
MESH = pl.DeviceIdType.MESH


def dot(left, right, dims=((1,), (0,))):
    return lax.dot_general(left, right, (dims, ((), ())), preferred_element_type=jnp.float32)


def head_lanes(size):
    lane = lax.broadcasted_iota(jnp.int32, (1, PAIR), 1)
    return [lane // size == index for index in range(PAIR // size)]


def only(mask, values):
    return jnp.where(mask, values, jnp.zeros_like(values))


def normal_tail(values):
    size = jnp.abs(values)
    bell = jnp.exp(-0.5 * values * values)
    t = 1.0 / (1.0 + 0.3275911 * (2.0**-0.5) * size)
    poly = t * (
        0.254829592
        + t * (-0.284496736 + t * (1.421413741 + t * (-1.453152027 + t * 1.061405429)))
    )
    tail = 0.5 * poly * bell
    return (jnp.where(values >= 0, 1.0 - tail, tail), bell)


def gelu_both(values):
    below, bell = normal_tail(values)
    return (values * below, below + values * bell * 0.3989422804014327)


def norm_parts(values):
    center = jnp.mean(values, axis=-1, keepdims=True)
    offset = values - center
    spread = jnp.mean(offset * offset, axis=-1, keepdims=True)
    inverse = lax.rsqrt(spread + 1e-05)
    return (offset * inverse, inverse)


def norm_back(grad, gain, normal, inverse):
    inner = grad * gain
    mean = jnp.mean(inner, axis=-1, keepdims=True)
    along = jnp.mean(inner * normal, axis=-1, keepdims=True)
    return inverse * (inner - mean - normal * along)


class Wires:
    def __init__(self, sems):
        self.sems = sems
        self.places = {}

    def at(self, *key):
        return self.sems.at[self.places.setdefault(key, len(self.places))]

    def remote(self, key, source, target, **where):
        return pltpu.make_async_remote_copy(
            source,
            target,
            self.at(key, "send"),
            self.at(key, "recv"),
            device_id=where,
            device_id_type=MESH,
        )

    def local(self, key, source, target):
        return pltpu.make_async_copy(source, target, self.at(key, "local"))


def wt_places():
    w = lax.axis_index("wt")
    core = lax.rem(w, 2)
    sibling = w + 1 - 2 * core
    across = lax.rem(w + 2, 4)
    return w, sibling, across, lax.rem(sibling + 2, 4)


def turned(place):
    return 2 * lax.rem(place, 2) + place // 2


def stripe_of(z, w):
    return 2 * lax.rem(w, 2) + lax.rem(w // 2 + z, 2)


def plane_place(z, w):
    plane = turned(w)
    return dict(ctx=plane, wt=2 * lax.rem(z + plane, 2) + z // 2)


def home_place(z, w):
    return dict(ctx=stripe_of(z, w), wt=turned(z))


def is_moving(z, w):
    place = home_place(z, w)
    return (place["ctx"] != z) | (place["wt"] != w)


def greet(partners, extra, meanwhile=lambda: None):
    barrier = pltpu.get_barrier_semaphore()
    for partner in partners:
        pl.semaphore_signal(barrier, 1, device_id=partner, device_id_type=MESH)
    waits = len(partners)
    for here, partner in extra:

        @pl.when(here)
        def _():
            pl.semaphore_signal(barrier, 1, device_id=partner, device_id_type=MESH)

        waits = waits + here.astype(jnp.int32)
    meanwhile()
    pl.semaphore_wait(barrier, waits)


def same_document(lengths, m, rows):
    z = lax.axis_index("ctx")
    pack = turned(z)
    ends = [lengths[m, pack, 0]]
    for document in range(1, lengths.shape[2]):
        ends.append(ends[-1] + lengths[m, pack, document])

    def ids(axis):
        shape = (rows, 1) if axis == 0 else (1, rows)
        first = lax.broadcasted_iota(jnp.int32, shape, axis) * 4
        place = jnp.concatenate([first + stripe_of(z, j) for j in range(4)], axis=axis)
        return sum((place >= end).astype(jnp.int32) for end in ends)

    return ids(0) == ids(1)


def attend_pack(size, same, qkv, mixed):
    local = mixed.shape[1]
    masks = head_lanes(size)
    for pair in range(local // PAIR):
        at = pair * PAIR
        q = qkv[:, at : at + PAIR] * jnp.bfloat16(size**-0.5)
        k = qkv[:, local + at : local + at + PAIR]
        v = qkv[:, 2 * local + at : 2 * local + at + PAIR]
        total = None
        for mask in masks:
            scores = jnp.where(same, dot(only(mask, k), q, ((1,), (1,))), FAR)
            probs = jnp.exp(scores - jnp.max(scores, axis=0, keepdims=True))
            scale = 1.0 / jnp.sum(probs, axis=0, keepdims=True)
            low = (probs * scale).astype(jnp.bfloat16)
            term = dot(only(mask, v), low, ((0,), (0,)))
            total = term if total is None else total + term
        mixed[:, at : at + PAIR] = total.T.astype(jnp.bfloat16)


def attend_pack_back(size, same, qkv, grad_heads, projected_grad):
    local = grad_heads.shape[1]
    masks = head_lanes(size)
    for pair in range(local // PAIR):
        at = pair * PAIR
        q = qkv[:, at : at + PAIR] * jnp.bfloat16(size**-0.5)
        k = qkv[:, local + at : local + at + PAIR]
        v = qkv[:, 2 * local + at : 2 * local + at + PAIR]
        grad = grad_heads[:, at : at + PAIR]
        totals = [None] * 3
        for mask in masks:
            own_k = only(mask, k)
            scores = jnp.where(same, dot(own_k, q, ((1,), (1,))), FAR)
            probs = jnp.exp(scores - jnp.max(scores, axis=0, keepdims=True))
            probs = probs * (1.0 / jnp.sum(probs, axis=0, keepdims=True))
            prob_grad = dot(only(mask, v), grad, ((1,), (1,)))
            inner = jnp.sum(probs * prob_grad, axis=0, keepdims=True)
            score_grad = (probs * (prob_grad - inner)).astype(jnp.bfloat16)
            terms = (
                dot(own_k, score_grad, ((0,), (0,))),
                dot(score_grad, only(mask, q)),
                dot(probs.astype(jnp.bfloat16), only(mask, grad)),
            )
            totals = [t if o is None else o + t for o, t in zip(totals, terms)]
        query_grad = totals[0].T * size**-0.5
        projected_grad[:, at : at + PAIR] = query_grad.astype(jnp.bfloat16)
        projected_grad[:, local + at : local + at + PAIR] = totals[1].astype(jnp.bfloat16)
        projected_grad[:, 2 * local + at : 2 * local + at + PAIR] = totals[2].astype(jnp.bfloat16)


class Spread:
    def __init__(self, wires, full, mixed, mixed_rows, rows, local):
        self.wires, self.full, self.mixed, self.mixed_rows = wires, full, mixed, mixed_rows
        self.rows, self.local = rows, local
        self.w, self.sibling, self.across, self.across_sibling = wt_places()

    def stripe(self, m, j):
        return self.full.at[m, pl.ds(j * self.rows, self.rows), :]

    def to_sibling(self, m):
        own = self.stripe(m, self.w)
        return self.wires.remote(("sibling", m), own, own, wt=self.sibling)

    def to_across(self, m):
        own = self.stripe(m, self.w)
        return self.wires.remote(("across", m), own, own, wt=self.across)

    def passed(self, m):
        block = self.stripe(m, self.across)
        return self.wires.remote(("passed", m), block, block, wt=self.sibling)

    def send(self, m):
        self.to_across(m).start()
        self.to_sibling(m).start()

    def hand_on(self, m):
        self.to_across(m).wait_recv()
        self.passed(m).start()

    def settle(self, m):
        self.to_sibling(m).wait_recv()
        self.passed(m).wait_recv()

    def back(self, m):
        heads = pl.ds(self.w * self.local, self.local)
        target = self.mixed_rows.at[pl.ds(m * self.rows, self.rows), heads]
        for index, partner in enumerate((self.across, self.across_sibling, self.sibling)):
            block = self.mixed.at[m, pl.ds(partner * self.rows, self.rows), :]
            yield self.wires.remote(("back", m, index), block, target, wt=partner)

    def send_back(self, m):
        for copy in self.back(m):
            copy.start()
        self.own_back(m).start()

    def own_back(self, m):
        heads = pl.ds(self.w * self.local, self.local)
        return self.wires.local(
            ("back", m),
            self.mixed.at[m, pl.ds(self.w * self.rows, self.rows), :],
            self.mixed_rows.at[pl.ds(m * self.rows, self.rows), heads],
        )

    def arrived_back(self, m):
        for copy in self.back(m):
            copy.wait_recv()
        self.own_back(m).wait()

    def end(self, m):
        for copy in (self.to_sibling(m), self.to_across(m), self.passed(m)):
            copy.wait_send()
        for copy in self.back(m):
            copy.wait_send()


def project(full, weight, bias, qkv):
    qkv[...] = (dot(full[...], weight[...]) + bias).astype(jnp.bfloat16)


def bias_of(rows):
    return jnp.concatenate([rows[0:1], jnp.zeros_like(rows[0:1]), rows[1:2]], axis=1)


BLOCK = 512


def feed_start(states, mixed, weight_out, rows):
    summed = states.astype(jnp.float32) + (dot(mixed, weight_out) + rows[2:3, :])
    normal, inverse = norm_parts(summed)
    return normal, inverse, normal * rows[3:4, :] + rows[4:5, :]


def feed_forward(at, states, mixed, weights, rows, in_bias, kept):
    weight_out, weight_in, weight_down = weights
    normal, inverse, first = feed_start(states, mixed, weight_out[...], rows)
    kept["normal_one"][at, :] = normal
    kept["inverse_one"][at, :] = inverse
    low = first.astype(jnp.bfloat16)
    kept["first"][at, :] = low
    total = first + rows[5:6, :]
    for column in range(0, weight_in.shape[1], BLOCK):
        columns = pl.ds(column, BLOCK)
        hidden, slope = gelu_both(dot(low, weight_in[:, columns]) + in_bias[:, columns])
        hidden = hidden.astype(jnp.bfloat16)
        kept["hidden"][at, columns] = hidden
        kept["slope"][at, columns] = slope.astype(jnp.bfloat16)
        total = total + dot(hidden, weight_down[columns, :])
    normal, inverse = norm_parts(total)
    kept["normal_two"][at, :] = normal
    kept["inverse_two"][at, :] = inverse
    return normal * rows[6:7, :] + rows[7:8, :]


def feed_backward(at, grad, weights, rows, kept):
    weight_out, weight_in, weight_down = weights
    total = norm_back(grad, rows[6:7, :], kept["normal_two"][at, :], kept["inverse_two"][at, :])
    low = total.astype(jnp.bfloat16)
    for column in range(0, weight_in.shape[1], BLOCK):
        columns = pl.ds(column, BLOCK)
        inner = dot(low, weight_down[columns, :], ((1,), (1,)))
        inner = (inner * kept["slope"][at, columns].astype(jnp.float32)).astype(jnp.bfloat16)
        total = total + dot(inner, weight_in[:, columns], ((1,), (1,)))
    total = norm_back(total, rows[3:4, :], kept["normal_one"][at, :], kept["inverse_one"][at, :])
    branch = total.astype(jnp.bfloat16)
    return total, dot(branch, weight_out[...], ((1,), (1,))).astype(jnp.bfloat16)


def first_kernel(size, *refs):
    block, shard_qkv, shard_out, shard_in, shard_down, vectors, own_bias, valid = refs[:8]
    lengths = refs[8]
    own, weight, kept_out, kept_in, kept_down, layer_rows, in_bias, own_marks, count = refs[9:18]
    leaving, full, qkv, mixed, marks_wt, marks_ctx = refs[18:24]
    whole_out, whole_in, whole_down, smalls, mixed_rows, first, inner, total = refs[24:32]
    small, marks, sems = refs[32:]
    micro, rows, width = block.shape
    local = small.shape[1]
    hidden = shard_in.shape[1]
    half = local // 2
    deep = shard_down.shape[0] // 8
    wires = Wires(sems)
    z = lax.axis_index("ctx")
    spread = Spread(wires, full, mixed, mixed_rows, rows, local)
    w, sibling, across, across_sibling = wt_places()
    partners = (across, across_sibling, sibling)
    level = lax.rem(z, 2)
    neighbor = z + 1 - 2 * level
    moves, place = is_moving(z, w), plane_place(z, w)
    others = [lax.rem(z + step, 4) for step in (1, 2, 3)]

    def own_parts():
        small[...] = jnp.zeros_like(small)
        small[:8, :] = vectors[...].astype(jnp.float32)
        for row in range(own_bias.shape[1] // local):
            at = pl.ds(row * local, local)
            small[8 + row : 9 + row, :] = own_bias[:, at].astype(jnp.float32)
        marks[...] = jnp.zeros_like(marks)
        marks[: valid.shape[0], :] = valid[...].astype(jnp.float32)

    greet(
        [{"wt": partner} for partner in partners] + [{"ctx": other} for other in others],
        [(moves, place), (moves, home_place(z, w))],
        own_parts,
    )
    bias = bias_of(small)

    def swap(m):
        return wires.remote(
            ("swap", m), block.at[m], spread.stripe(m, place["wt"]), **place
        )

    def stay(m):
        return wires.local(("stay", m), block.at[m], spread.stripe(m, w))

    def swap_marks():
        return wires.remote("swap marks", marks, own_marks, **place)

    def head_copy(part, index):
        column = part * width + partners[index] * local
        return wires.remote(
            ("heads", part, index),
            shard_qkv.at[:, pl.ds(column, local)],
            weight.at[pl.ds(w * local, local), pl.ds(part * local, local)],
            wt=partners[index],
        )

    def head_own(part):
        return wires.local(
            ("heads", part),
            shard_qkv.at[:, pl.ds(part * width + w * local, local)],
            weight.at[pl.ds(w * local, local), pl.ds(part * local, local)],
        )

    def small_copy(index):
        return wires.remote(("small", index), small, smalls.at[w], wt=partners[index])

    def marks_copy(index):
        return wires.remote(("marks", index), marks, marks_wt.at[index], wt=partners[index])

    def count_copy(index):
        return wires.remote(("count", index), count, marks_ctx.at[index], ctx=others[index])

    columns = hidden // width
    chunks = 1 + columns + 4

    def piece(k, level):
        if k == 0:
            return shard_out, whole_out, local, level * half, half, 0
        if k <= columns:
            return shard_in, whole_in, local, level * half, half, (k - 1) * width
        at = (level * 4 + k - 1 - columns) * deep
        return shard_down, whole_down, 4 * deep * 2, at, deep, 0

    def from_shard(k, level):
        shard, _, _, at, size, column = piece(k, level)
        return shard.at[pl.ds(at, size), pl.ds(column, width)]

    def in_whole(k, level, j):
        _, whole, stride, at, size, column = piece(k, level)
        return whole.at[pl.ds(j * stride + at, size), pl.ds(column, width)]

    def y_copy(k):
        return wires.remote(
            ("y", k), from_shard(k, level), in_whole(k, level, w), wt=across
        )

    def z_copy(k):
        block = in_whole(k, level, across)
        return wires.remote(("z", k), block, block, ctx=neighbor)

    def core_copy(k, side):
        block = in_whole(k, level if side == 0 else 1 - level, across)
        return wires.remote(("core", k, side), block, block, wt=sibling)

    def shard_sibling(index):
        shard, whole = ((shard_out, whole_out), (shard_in, whole_in), (shard_down, whole_down))[
            index
        ]
        size = shard.shape[0]
        return wires.remote(
            ("shard", index), shard, whole.at[pl.ds(w * size, size), :], wt=sibling
        )

    def shard_own(index):
        shard, whole = ((shard_out, whole_out), (shard_in, whole_in), (shard_down, whole_down))[
            index
        ]
        size = shard.shape[0]
        return wires.local(("shard", index), shard, whole.at[pl.ds(w * size, size), :])

    def shard_ready(index):
        shard_own(index).wait()
        shard_sibling(index).wait_recv()

    @pl.when(moves)
    def _():
        swap(0).start()
        swap_marks().start()

    @pl.when(jnp.logical_not(moves))
    def _():
        for m in range(micro):
            stay(m).start()
        own_marks[...] = marks[...]

    for part in range(3):
        for index in range(3):
            head_copy(part, index).start()
        head_own(part).start()
    for index in range(3):
        small_copy(index).start()
        marks_copy(index).start()
    smalls[w] = small[...]

    def arrive(m):
        @pl.when(moves)
        def _():
            swap(m).wait_recv()

        @pl.when(jnp.logical_not(moves))
        def _():
            stay(m).wait()

    def own_copy(m):
        return wires.local(("own", m), spread.stripe(m, w), own.at[m])

    @pl.when(moves)
    def _():
        swap(0).wait_send()
        for m in range(1, micro):
            swap(m).start()

    for m in range(micro):
        arrive(m)
        spread.send(m)
        own_copy(m).start()
    for k in range(micro):
        y_copy(k).start()
    for index in range(3):
        shard_sibling(index).start()
        shard_own(index).start()
    for index in range(3):
        marks_copy(index).wait_recv()
    count[...] = marks[...] + marks_wt[0] + marks_wt[1] + marks_wt[2]
    for index in range(3):
        count_copy(index).start()
    for part in range(3):
        for index in range(3):
            head_copy(part, index).wait_recv()
        head_own(part).wait()
    def passing(k):
        y_copy(k).wait_recv()
        if k + micro < chunks:
            y_copy(k + micro).start()
        z_copy(k).start()
        core_copy(k, 0).start()

    def passed(k):
        z_copy(k).wait_recv()
        core_copy(k, 1).start()

    def stored(k):
        if k == 0:
            return [wires.local(("stored", k), whole_out, kept_out)]
        if k <= columns:
            at = pl.ds((k - 1) * width, width)
            return [wires.local(("stored", k), whole_in.at[:, at], kept_in.at[:, at])]
        return [
            wires.local(("stored", k, row), whole_down.at[at, :], kept_down.at[at, :])
            for row, at in pair_rows(k)
        ]

    def pair_rows(k):
        if (k - columns) % 2 == 1:
            return []
        first_row = (k - 2 - columns) * deep
        return [
            (row, pl.ds(row, 2 * deep)) for row in range(first_row, hidden, 4 * deep)
        ]

    def compute(k):
        core_copy(k, 0).wait_recv()
        core_copy(k, 1).wait_recv()
        if k == 0:
            shard_ready(0)
            for m in range(micro):
                spread.arrived_back(m)
            states = [spread.stripe(m, w)[...] for m in range(micro)]
            states = jnp.concatenate(states, axis=0)
            values = feed_start(states, mixed_rows[...], whole_out[...], layer_rows)[2]
            first[...] = values.astype(jnp.bfloat16)
            total[...] = values + layer_rows[5:6, :]
        elif k <= columns:
            if k == 1:
                shard_ready(1)
            for column in range((k - 1) * width, k * width, BLOCK):
                at = pl.ds(column, BLOCK)
                values = gelu_both(dot(first[...], whole_in[:, at]) + in_bias[:, at])[0]
                inner[:, at] = values.astype(jnp.bfloat16)
        else:
            if k == columns + 1:
                shard_ready(2)
            for _, at in pair_rows(k):
                total[...] += dot(inner[:, at], whole_down[at, :])
        for copy in stored(k):
            copy.start()

    for index in range(3):
        small_copy(index).wait_recv()
    for j in range(4):
        at = pl.ds(j * local, local)
        layer_rows[:, at] = smalls[j, :8, :]
        for row in range(columns):
            at = pl.ds(j * 8 * deep + row * local, local)
            in_bias[:, at] = smalls[j, 8 + row : 9 + row, :]
    for m in range(micro):
        spread.hand_on(m)
        spread.settle(m)
        project(full.at[m], weight, bias, qkv.at[0])
        attend_pack(size, same_document(lengths, m, rows), qkv.at[0], mixed.at[m])
        spread.send_back(m)
        passing(m)
    passed(0)
    for k in range(micro, chunks):
        passing(k)
        passed(k - 2)
        if k >= micro + 2:
            compute(k - micro - 2)
    passed(chunks - 2)
    for k in range(chunks - micro - 2, chunks):
        if k == chunks - 2:
            passed(chunks - 1)
        compute(k)
    values = norm_parts(total[...])[0] * layer_rows[6:7, :] + layer_rows[7:8, :]
    leaving[...] = values.astype(jnp.bfloat16)
    for index in range(3):
        count_copy(index).wait()
    count[...] = count[...] + marks_ctx[0] + marks_ctx[1] + marks_ctx[2]
    for m in range(micro):
        spread.end(m)
        own_copy(m).wait()
    for part in range(3):
        for index in range(3):
            head_copy(part, index).wait_send()
    for index in range(3):
        small_copy(index).wait_send()
        marks_copy(index).wait_send()
        shard_sibling(index).wait_send()
    for k in range(chunks):
        y_copy(k).wait_send()
        z_copy(k).wait_send()
        for side in range(2):
            core_copy(k, side).wait_send()
        for copy in stored(k):
            copy.wait()

    @pl.when(moves)
    def _():
        for m in range(1, micro):
            swap(m).wait_send()
        swap_marks().wait()


def first_pass(block, shards, vectors, bias, valid, lengths, size):
    micro, rows, width = block.shape
    local = vectors.shape[1]
    pack = 4 * rows
    marks = (8, rows)
    tokens, hidden = micro * rows, shards[2].shape[1]
    anywhere = pl.BlockSpec(memory_space=pl.ANY)
    inside = pl.BlockSpec(memory_space=pltpu.VMEM)
    low = lambda *shape: jax.ShapeDtypeStruct(shape, jnp.bfloat16)
    word = lambda *shape: jax.ShapeDtypeStruct(shape, jnp.float32)
    room = lambda *shape: pltpu.VMEM(shape, jnp.bfloat16)
    return pl.pallas_call(
        functools.partial(first_kernel, size),
        in_specs=[anywhere] * 5 + [inside] * 3 + [pl.BlockSpec(memory_space=pltpu.SMEM)],
        out_specs=[anywhere, inside] + [anywhere] * 3 + [inside] * 5,
        out_shape=[
            low(micro, rows, width),
            low(width, 3 * local),
            low(width, width),
            low(width, hidden),
            low(hidden, width),
            word(8, width),
            word(1, hidden),
            word(*marks),
            word(*marks),
            low(tokens, width),
        ],
        scratch_shapes=[
            room(micro, pack, width),
            room(1, pack, 3 * local),
            room(micro, pack, local),
            pltpu.VMEM((3,) + marks, jnp.float32),
            pltpu.VMEM((3,) + marks, jnp.float32),
            room(width, width),
            room(width, hidden),
            room(hidden, width),
            pltpu.VMEM((4, 16, local), jnp.float32),
            room(tokens, width),
            room(tokens, width),
            room(tokens, hidden),
            pltpu.VMEM((tokens, width), jnp.float32),
            pltpu.VMEM((16, local), jnp.float32),
            pltpu.VMEM(marks, jnp.float32),
            pltpu.SemaphoreType.DMA((320,)),
        ],
        compiler_params=pltpu.CompilerParams(
            collective_id=2, has_side_effects=True, vmem_limit_bytes=60 * 2**20
        ),
        name="first_pass",
    )(block, *shards, vectors, bias, valid, lengths)


class Back:
    def __init__(self, wires, size, refs):
        self.wires, self.size = wires, size
        self.rows_grad, self.skip, self.qkv, self.weight, self.lengths = refs[:5]
        self.projected, self.grad_states = refs[5:7]
        self.heads_grad, self.part, self.from_sibling, self.far, self.from_across = refs[7:]
        self.micro, self.pack, self.local = self.heads_grad.shape
        self.rows = self.pack // 4
        self.w, self.sibling, self.across, self.across_sibling = wt_places()
        self.partners = (self.across, self.across_sibling, self.sibling)

    def place(self, m):
        return pl.ds(m * self.rows, self.rows)

    def heads_copy(self, m, index):
        column = pl.ds(self.partners[index] * self.local, self.local)
        return self.wires.remote(
            ("heads", m, index),
            self.rows_grad.at[self.place(m), column],
            self.heads_grad.at[m, pl.ds(self.w * self.rows, self.rows), :],
            wt=self.partners[index],
        )

    def heads_own(self, m):
        return self.wires.local(
            ("heads", m),
            self.rows_grad.at[self.place(m), pl.ds(self.w * self.local, self.local)],
            self.heads_grad.at[m, pl.ds(self.w * self.rows, self.rows), :],
        )

    def stripe(self, m, j):
        return self.part.at[m, pl.ds(j * self.rows, self.rows), :]

    def sibling_copy(self, m, index):
        j = (self.across_sibling, self.sibling)[index]
        return self.wires.remote(
            ("to sibling", m, index),
            self.stripe(m, j),
            self.from_sibling.at[m, index],
            wt=self.sibling,
        )

    def half(self, part):
        return pl.ds(part * (self.rows // 2), self.rows // 2)

    def across_copy(self, m, part):
        source, target = self.far.at[m, self.half(part), :], self.from_across.at[m, self.half(part), :]
        return self.wires.remote(("to across", m, part), source, target, wt=self.across)

    def begin(self, m):
        for index in range(3):
            self.heads_copy(m, index).start()
        self.heads_own(m).start()

    def arrive(self, m):
        for index in range(3):
            self.heads_copy(m, index).wait_recv()
        self.heads_own(m).wait()

    def work(self, m, following=None):
        self.arrive(m)
        if following is not None:
            self.begin(following)
        whole = pl.ds(m * self.pack, self.pack)
        projected = self.projected.at[whole, :]
        same = same_document(self.lengths, m, self.rows)
        qkv = self.qkv(m)
        attend_pack_back(self.size, same, qkv, self.heads_grad.at[m], projected)
        product = dot(projected[...], self.weight[...], ((1,), (1,)))
        self.part[m] = product.astype(jnp.bfloat16)
        for index in range(2):
            self.sibling_copy(m, index).start()

    def cross(self, m):
        for index in range(2):
            self.sibling_copy(m, index).wait_recv()
        total = self.stripe(m, self.across)[...].astype(jnp.float32)
        total = total + self.from_sibling[m, 0].astype(jnp.float32)
        self.far[m] = total.astype(jnp.bfloat16)
        for part in range(2):
            self.across_copy(m, part).start()

    def finish(self, m, then=lambda part: None):
        half = self.rows // 2
        for part in range(2):
            self.across_copy(m, part).wait_recv()
            at = self.half(part)
            place = pl.ds(m * self.rows + part * half, half)
            own = self.part.at[m, pl.ds(self.w * self.rows + part * half, half), :]
            total = self.skip[place, :] + own[...].astype(jnp.float32)
            total = total + self.from_sibling[m, 1, at, :].astype(jnp.float32)
            total = total + self.from_across[m, at, :].astype(jnp.float32)
            self.grad_states[place, :] = total.astype(jnp.bfloat16)
            then(part)

    def end(self, m):
        for index in range(3):
            self.heads_copy(m, index).wait_send()
        for index in range(2):
            self.sibling_copy(m, index).wait_send()
        for part in range(2):
            self.across_copy(m, part).wait_send()


def back_scratch(micro, pack, local, width):
    block = pltpu.VMEM((micro, pack // 4, width), jnp.bfloat16)
    return [
        pltpu.VMEM((micro, pack, local), jnp.bfloat16),
        pltpu.VMEM((micro, pack, width), jnp.bfloat16),
        pltpu.VMEM((micro, 2, pack // 4, width), jnp.bfloat16),
        block,
        block,
    ]


def swap_back(wires, rows, source, target, m, moves):
    z, w = lax.axis_index("ctx"), lax.axis_index("wt")
    block = source.at[pl.ds(m * rows, rows), :]
    if moves:
        return wires.remote(("home", m), block, target.at[m], **home_place(z, w))
    return wires.local(("home", m), block, target.at[m])


def mid_kernel(size, *refs):
    states, leaving, weight_out, weight_in, weight_down = refs[:5]
    weight, layer_rows, in_bias, marks, count, lengths = refs[5:11]
    outs = refs[11:21]
    inverse_one, inverse_two, returned = refs[21:24]
    held = refs[24:27]
    full, qkv, mixed_rows, mixed = refs[27:31]
    saved = dict(zip(SAVED, refs[31:38]))
    skip, rows_grad, projected, grad_states = refs[38:42]
    micro, rows, width = states.shape
    wires = Wires(refs[-1])
    section = lax.axis_index("section")
    spread = Spread(wires, full, mixed, mixed_rows, rows, weight.shape[1] // 3)
    given = (rows_grad, skip, lambda m: qkv.at[m], weight, lengths)
    back = Back(wires, size, given + (projected, grad_states) + refs[42:-1])
    w = spread.w
    bias = bias_of(layer_rows[:2, pl.ds(w * spread.local, spread.local)])
    kept = dict(saved, inverse_one=inverse_one, inverse_two=inverse_two)

    def stay(m):
        return wires.local(("stay", m), states.at[m], spread.stripe(m, w))

    def teacher_copy(m):
        return wires.local(("teacher", m), states.at[m], grad_states.at[pl.ds(m * rows, rows), :])

    def weight_copies():
        for index, source in enumerate((weight_out, weight_in, weight_down)):
            step = source.shape[0] if index == 0 else source.shape[0] // 4
            for row in range(0, source.shape[0], step):
                at = pl.ds(row, step)
                yield wires.local(("weight", index, row), source.at[at, :], held[index].at[at, :])

    def load_weights(first, last):
        for copy in list(weight_copies())[first:last]:
            copy.start()

    def own_loads():
        @pl.when(section == 0)
        def _():
            for m in range(micro):
                stay(m).start()

        load_weights(0, 3)

    greet(
        [{"wt": partner} for partner in back.partners] + [{"section": 1 - section}],
        [],
        own_loads,
    )

    def relay_copy(m):
        return wires.remote(("relay", m), leaving.at[m], spread.stripe(m, w), section=1 - section)

    @pl.when(section == 0)
    def _():
        for m in range(micro):
            relay_copy(m).start()

    def arrive(m):
        @pl.when(section == 0)
        def _():
            stay(m).wait()

        @pl.when(section == 1)
        def _():
            relay_copy(m).wait_recv()

        spread.send(m)

    def attend(m):
        spread.settle(m)
        project(full.at[m], weight, bias, qkv.at[m])
        attend_pack(size, same_document(lengths, m, rows), qkv.at[m], mixed.at[m])
        spread.send_back(m)
        for name, source in (("full", full), ("qkv", qkv)):
            store(name, m, source.at[m], outs[OUTS.index(name)].at[m]).start()

    def store(name, m, source, target):
        return wires.local(("store", name, m), source, target)

    def stores(m):
        at = pl.ds(m * rows, rows)
        for name, ref in [("mixed", mixed_rows)] + list(saved.items()):
            yield store(name, m, ref.at[at, :], outs[OUTS.index(name)].at[at, :])

    def covered(m):
        total = jnp.sum(jnp.sum(count[...], axis=0, keepdims=True), axis=1, keepdims=True)
        shape = (rows, rows)
        here = lax.broadcasted_iota(jnp.int32, shape, 0) == lax.broadcasted_iota(jnp.int32, shape, 1)
        column = jnp.sum(jnp.where(here, marks[m : m + 1, :], 0.0), axis=1, keepdims=True)
        return LOSS_SCALE / total * column

    def feed(*packs):
        for m in packs:
            spread.arrived_back(m)
            teacher_copy(m).wait()
        at = pl.ds(packs[0] * rows, len(packs) * rows)
        block = jnp.concatenate([spread.stripe(m, w)[...] for m in packs], axis=0)
        output = feed_forward(at, block, mixed_rows[at, :], held, layer_rows, in_bias, kept)
        saved["final"][at, :] = output.astype(jnp.bfloat16)
        factor = jnp.concatenate([covered(m) for m in packs], axis=0)
        grad = factor * (output - grad_states[at, :].astype(jnp.float32))
        saved["grad"][at, :] = grad
        skip[at, :], rows_grad[at, :] = feed_backward(at, grad, held, layer_rows, kept)
        for m in packs:
            for copy in stores(m):
                copy.start()
            back.begin(m)

    def back_copy(m, part):
        place = pl.ds(m * rows + part * (rows // 2), rows // 2)
        source, target = grad_states.at[place, :], returned.at[place, :]
        return wires.remote(("return", m, part), source, target, section=1 - section)

    def finish(m):
        def then(part):
            @pl.when(section == 1)
            def _():
                back_copy(m, part).start()

        back.finish(m, then)

    arrive(0)
    load_weights(3, 5)
    arrive(1)
    load_weights(5, 6)
    spread.hand_on(0)
    attend(0)
    arrive(2)
    load_weights(6, 8)
    spread.hand_on(1)
    attend(1)
    load_weights(8, 9)
    for m in range(micro):
        teacher_copy(m).start()
    spread.hand_on(2)
    for copy in weight_copies():
        copy.wait()
    feed(0)
    attend(2)
    feed(1, 2)
    back.work(0)
    back.cross(0)
    back.work(1)
    back.cross(1)
    finish(0)
    back.work(2)
    back.cross(2)
    finish(1)
    finish(2)
    for m in range(micro):
        spread.end(m)
        back.end(m)
        for name, source in (("full", full), ("qkv", qkv)):
            store(name, m, source.at[m], outs[OUTS.index(name)].at[m]).wait()
        for copy in stores(m):
            copy.wait()

        @pl.when(section == 1)
        def _():
            for part in range(2):
                back_copy(m, part).wait_send()

        @pl.when(section == 0)
        def _():
            relay_copy(m).wait_send()
            for part in range(2):
                back_copy(m, part).wait_recv()


SAVED = ("normal_one", "first", "hidden", "slope", "normal_two", "final", "grad")
OUTS = ("full", "qkv", "mixed") + SAVED


def mid_pass(states, leaving, weights, weight, layer_rows, in_bias, marks, count, lengths, size):
    micro, rows, width = states.shape
    local = weight.shape[1] // 3
    pack = 4 * rows
    tokens, hidden = micro * rows, weights[1].shape[1]
    anywhere = pl.BlockSpec(memory_space=pl.ANY)
    inside = pl.BlockSpec(memory_space=pltpu.VMEM)
    low = lambda *shape: jax.ShapeDtypeStruct(shape, jnp.bfloat16)
    word = lambda *shape: jax.ShapeDtypeStruct(shape, jnp.float32)
    held = [
        word(tokens, width),
        low(tokens, width),
        low(tokens, hidden),
        low(tokens, hidden),
        word(tokens, width),
        low(tokens, width),
        word(tokens, width),
    ]
    room = lambda shape: pltpu.VMEM(shape.shape, shape.dtype)
    kept = [low(micro, pack, width), low(micro, pack, 3 * local), low(tokens, width)]
    *results, inverse_one, inverse_two, returned = pl.pallas_call(
        functools.partial(mid_kernel, size),
        in_specs=[anywhere] * 5 + [inside] * 5 + [pl.BlockSpec(memory_space=pltpu.SMEM)],
        out_specs=[anywhere] * 10 + [inside] * 3,
        out_shape=kept + held + [word(tokens, 1), word(tokens, 1), low(tokens, width)],
        scratch_shapes=[pltpu.VMEM(part.shape, jnp.bfloat16) for part in weights]
        + [room(shape) for shape in kept]
        + [room(low(micro, pack, local))]
        + [room(shape) for shape in held]
        + [
            room(word(tokens, width)),
            room(low(tokens, width)),
            room(low(micro * pack, 3 * local)),
            room(low(tokens, width)),
        ]
        + back_scratch(micro, pack, local, width)
        + [pltpu.SemaphoreType.DMA((200,))],
        compiler_params=pltpu.CompilerParams(
            collective_id=4, has_side_effects=True, vmem_limit_bytes=62 * 2**20
        ),
        name="mid_pass",
    )(
        states,
        leaving,
        *weights,
        weight,
        layer_rows,
        in_bias,
        marks,
        count,
        lengths,
    )
    return dict(zip(OUTS, results)), inverse_one, inverse_two, returned


CHUNK = 128
RING = 6
TILE = 256
LAGS = (2, 4, 6, 8)
AHEAD = 4


def sum_into(target, parts, rows):
    step = 16

    def one(index, carry):
        at = pl.ds(pl.multiple_of(index * step, step), step)
        total = parts[0][at, :].astype(jnp.float32)
        for part in parts[1:]:
            total = total + part[at, :].astype(jnp.float32)
        target[at, :] = total.astype(jnp.bfloat16)
        return carry

    lax.fori_loop(0, rows // step, one, 0)


def chunk_list(local, width, hidden):
    down = [("down", 0, CHUNK // 4, 0), ("down", CHUNK // 4, CHUNK // 4, 0)]
    down += [("down", CHUNK // 2, CHUNK // 2, 0)]
    down += [("down", row, CHUNK, 0) for row in range(CHUNK, hidden // 4, CHUNK)]
    across = [
        ("in", row, CHUNK, column)
        for column in range(hidden // width)
        for row in range(0, local, CHUNK)
    ]
    out = [("out", row, CHUNK // 2, 0) for row in range(0, local - CHUNK // 2, CHUNK // 2)]
    out += [("out", row, CHUNK // 4, 0) for row in range(local - CHUNK // 2, local, CHUNK // 4)]
    qkv = [("qkv", row, CHUNK, part) for part in range(3) for row in range(0, local, CHUNK)]
    return down + across[:3] + qkv + across[3:] + out + [("rest", 0, 16, 0)]


def starts_of(chunks):
    rows = [chunk[2] for chunk in chunks]
    starts = [sum(rows[:k]) for k in range(len(rows) + 1)]
    return starts, [sum(rows[k % 2 : k : 2]) for k in range(len(rows) + 2)]


def last_kernel(chunks, size, *refs):
    weight, layer_rows, inverse_one, inverse_two, lengths = refs[:5]
    grad, returned, normal_two, normal_one, qkv_all, full_all, slope = refs[5:12]
    weight_out, weight_in, weight_down = refs[12:15]
    hidden, first, mixed, final = refs[15:19]
    home = refs[19]
    results = dict(zip(("qkv", "out", "in", "down", "rest"), refs[20:25]))
    grad_states, projected, full, product = refs[25:29]
    downs, ins, outs, down_both, pre_both, branch_both, rest_in = refs[29:36]
    near, far, across_in, up_in, side_in = refs[36:41]
    skip, normal, slopes, qkv_one, rows_grad, rest = refs[41:47]
    wires = Wires(refs[-1])
    z, section = lax.axis_index("ctx"), lax.axis_index("section")
    tokens, width = final.shape
    count = len(chunks)
    micro = qkv_all.shape[0]

    def qkv_copy(m):
        return wires.local(("pack", m), qkv_all.at[m], qkv_one)

    def qkv_of(m):
        qkv_copy(m).wait()
        return qkv_one

    given = (rows_grad, skip, qkv_of, weight, lengths)
    back = Back(wires, size, given + (projected, grad_states) + refs[47:-1])
    w, sibling, across, across_sibling = wt_places()
    partners = (sibling, across, across_sibling)
    local = back.local
    deep = hidden.shape[1] // 4
    starts, sides_at = starts_of(chunks)
    moves = is_moving(z, w)
    own_rows = pl.ds(0, tokens)
    blocks = hidden.shape[1] // TILE

    def tile_copies(b):
        low = full.at[pl.ds((b % 2) * TILE, TILE), :]
        if b >= blocks:
            source = weight_out.at[pl.ds((b - blocks) * TILE, TILE), :]
            return [wires.local(("tile", b), source, low)]
        columns = pl.ds(b * TILE, TILE)
        wide = full.at[pl.ds(2 * TILE, width), pl.ds((b % 4) * TILE, TILE)]
        return [
            wires.local(("tile", b), weight_down.at[columns, :], low),
            wires.local(("wide", b), weight_in.at[:, columns], wide),
            wires.local(("slope", b), slope.at[:, columns], slopes.at[b % 2]),
        ]

    def start_tiles(b):
        for copy in tile_copies(b):
            copy.start()

    def first_copies():
        return [
            wires.local("grad", grad, skip),
            wires.local("returned", returned, rows_grad),
            wires.local("normal two", normal_two, normal),
        ]

    def normal_copy():
        return wires.local("normal", normal_one, normal)

    def own_loads():
        for copy in first_copies():
            copy.start()
        start_tiles(0)
        start_tiles(1)
        qkv_copy(0).start()

    greet(
        [{"wt": partner} for partner in partners],
        [
            (moves, home_place(z, w)),
            (moves, plane_place(z, w)),
            (z > 0, {"ctx": z - 1}),
            (z < 3, {"ctx": z + 1}),
        ],
        own_loads,
    )

    def step_first():
        for copy in first_copies():
            copy.wait()

        @pl.when(section == 0)
        def _():
            skip[...] = rows_grad[...].astype(jnp.float32)

        values = skip[...]
        rest_rows[6] = jnp.sum(values * normal[...], axis=0, keepdims=True)
        rest_rows[7] = jnp.sum(values, axis=0, keepdims=True)
        values = norm_back(values, layer_rows[6:7, :], normal[...], inverse_two[...])
        skip[...] = values
        low = values.astype(jnp.bfloat16)
        down_both[own_rows, :] = low
        to_sibling("down", down_both, 0).start()
        rest_rows[5] = dot(jnp.ones((16, tokens), jnp.bfloat16), low)[:1]
        for r, row in rest_rows.items():
            for j in range(4):
                rest[j * 16 + r : j * 16 + r + 1, :local] = row[:, j * local : (j + 1) * local]
        normal_copy().start()

    rest_rows = {}

    def step_back(b):
        for copy in tile_copies(b):
            copy.wait()
        columns = pl.ds(b * TILE, TILE)
        low = full[pl.ds((b % 2) * TILE, TILE), :]
        wide = full[pl.ds(2 * TILE, width), pl.ds((b % 4) * TILE, TILE)]
        grad = dot(down_both[own_rows, :], low, ((1,), (1,)))
        grad = (grad * slopes[b % 2].astype(jnp.float32)).astype(jnp.bfloat16)
        pre_both[own_rows, columns] = grad
        skip[...] += dot(grad, wide, ((1,), (1,)))
        start_tiles(b + 2)
        if (b + 1) * TILE % width == 0:
            to_sibling("pre", pre_both, (b + 1) * TILE // width - 1).start()

    def to_sibling(key, array, column):
        at = pl.ds(column * width, width)
        target = array.at[pl.ds(tokens, tokens), at]
        return wires.remote((key, column), array.at[own_rows, at], target, wt=sibling)

    def step_norm():
        normal_copy().wait()
        ones = jnp.ones((16, tokens), jnp.bfloat16)
        grad_first = skip[...]
        rows = {}
        rows[3] = jnp.sum(grad_first * normal[...], axis=0, keepdims=True)
        rows[4] = jnp.sum(grad_first, axis=0, keepdims=True)
        grad_summed = norm_back(grad_first, layer_rows[3:4, :], normal[...], inverse_one[...])
        skip[...] = grad_summed
        branch = grad_summed.astype(jnp.bfloat16)
        branch_both[own_rows, :] = branch
        to_sibling("branch", branch_both, 0).start()
        rows[2] = dot(ones, branch)[:1]
        sums = dot(ones, pre_both[own_rows, :])[:1]
        for j in range(4):
            for r, row in rows.items():
                rest[j * 16 + r : j * 16 + r + 1, :local] = row[:, j * local : (j + 1) * local]
            for r in range(deep // local):
                at = j * deep + r * local
                rest[j * 16 + r : j * 16 + r + 1, local : 2 * local] = sums[:, at : at + local]
        for copy in rest_copies():
            copy.start()

    def step_out(b):
        for copy in tile_copies(b):
            copy.wait()
        tile = full[pl.ds((b % 2) * TILE, TILE), :]
        grad = dot(branch_both[own_rows, :], tile, ((1,), (1,))).astype(jnp.bfloat16)
        rows_grad[:, pl.ds((b - blocks) * TILE, TILE)] = grad
        if b + 2 < blocks + width // TILE:
            start_tiles(b + 2)

    def last_out():
        for b in range(blocks, blocks + width // TILE):
            step_out(b)
        full_copy().start()
        for m in range(micro):
            back.begin(m)

    def both(key, source, target, at, columns, theirs):
        mine = (pl.ds(0, tokens), at)
        other = (pl.ds(tokens, tokens), at)
        return (
            wires.local(key, source.at[:, columns], target.at[mine]),
            wires.remote(key, source.at[:, theirs], target.at[other], wt=sibling),
        )

    def sides(key, source, block, target):
        for side, (j, k) in enumerate(((w, sibling), (across, across_sibling))):
            yield from both(
                key + (side,),
                source,
                target,
                pl.ds(side * CHUNK, CHUNK),
                pl.ds(block(j), CHUNK),
                pl.ds(block(k), CHUNK),
            )

    def down_block(index):
        return sides(
            ("down", index), hidden, lambda j: j * deep + index * CHUNK, downs.at[index]
        )

    def in_block(half):
        return sides(("in", half), first, lambda j: j * local + half * CHUNK, ins.at[half])

    def out_block(half):
        return sides(("out", half), mixed, lambda j: j * local + half * CHUNK, outs.at[half])

    def rest_copies():
        for side, k in enumerate((sibling, across_sibling)):
            yield wires.remote(
                ("rest", side), rest.at[pl.ds(k * 16, 16), :], rest_in.at[side], wt=sibling
            )

    halves = local // CHUNK
    columns = hidden.shape[1] // width
    loads = [lambda index=index: down_block(index) for index in range(deep // CHUNK)]
    loads += [lambda half=half: in_block(half) for half in range(halves)]
    loads += [lambda half=half: out_block(half) for half in range(halves)]

    def full_copy():
        return wires.local("full", full_all, full)

    def needs(k):
        kind, row, _, column = chunks[k]
        index = row // CHUNK
        copies = []
        if kind == "down":
            if index == 0:
                to_sibling("down", down_both, 0).wait_recv()
            copies += down_block(index)
        elif kind == "in":
            if column == 0:
                copies += in_block(index)
            if index == 0:
                to_sibling("pre", pre_both, column).wait_recv()
        else:
            copies += out_block(index)
            if index == 0:
                to_sibling("branch", branch_both, 0).wait_recv()
        for index, copy in enumerate(copies):
            (copy.wait if index % 2 == 0 else copy.wait_recv)()

    def operands(k):
        kind, row, _, column = chunks[k]
        index = row // CHUNK
        if kind == "down":
            return downs[index], down_both[...]
        if kind == "in":
            return ins[index], pre_both[:, column * width : (column + 1) * width]
        return outs[index], branch_both[...]

    def is_piece(k):
        return chunks[k][0] == "qkv"

    def rows_of(k):
        return chunks[k][2]

    def slot(buffer, k):
        return buffer.at[pl.ds(starts[k], rows_of(k)), :]

    def beside_slot(k):
        return side_in.at[pl.ds(sides_at[k], rows_of(k)), :]

    def result(k):
        kind, row, rows, column = chunks[k]
        if kind == "rest":
            return results["rest"]
        return results[kind].at[pl.ds(row, rows), pl.ds(column * width, width)]

    def piece(k, j):
        _, row, rows, part = chunks[k]
        return product.at[part, pl.ds(j * local + row, rows), :]

    def piece_place(k):
        return near.at[pl.ds(starts[k], rows_of(k)), pl.ds(w * local, local)]

    def piece_copy(k, index):
        place = piece_place(k)
        return wires.remote(
            ("piece", k, index), piece(k, partners[index]), place, wt=partners[index]
        )

    def piece_own(k):
        return wires.local(("piece", k), piece(k, w), piece_place(k))

    direct = [k for k in range(count) if not is_piece(k)]
    bases = [k for k in direct if chunks[k][1] % CHUNK == 0]

    def base_of(k):
        return max(base for base in bases if base <= k)

    def far_slot(k, rows):
        return far.at[bases.index(base_of(k)) % RING, pl.ds(chunks[k][1] % CHUNK, rows), :]

    def across_copy(k):
        source = far_slot(k, rows_of(k))
        return wires.remote(("chunk", k), source, slot(across_in, k), wt=across)

    def place_of(k, role):
        return role if k % 2 == 0 else 3 - role

    def up_copy(k, role):
        target = place_of(k, 1 if role == 0 else 2)
        return wires.remote(("up", k), slot(near, k), slot(up_in, k), ctx=target)

    def side_copy(k):
        return wires.remote(("side", k), slot(near, k), beside_slot(k), ctx=place_of(k, 1))

    def down_copy(k, role):
        origin = result(k) if role == 3 else slot(near, k)
        return pltpu.make_async_remote_copy(
            origin,
            result(k),
            wires.at("down send", k, 1 if role == 2 else 0),
            wires.at("down recv", k),
            device_id={"ctx": place_of(k, role)},
            device_id_type=MESH,
        )

    def keep_copy(k):
        return wires.local(("keep", k), slot(near, k), result(k))

    def on(k, role, step):
        pl.when(z == place_of(k, role))(step)

    def summands(k):
        if is_piece(k):
            return [slot(near, k)]
        return [slot(near, k), slot(across_in, k)]

    def begin(k):
        kind, row, _, column = chunks[k]
        if is_piece(k):
            if row == 0:
                at = pl.ds(column * local, local)
                grad = dot(full[...], projected[:, at], ((0,), (0,)))
                product[column] = grad.astype(jnp.bfloat16)
            for partner in range(3):
                piece_copy(k, partner).start()
            piece_own(k).start()
            return
        if k in bases:
            order = bases.index(k)
            for old in direct:
                if order >= RING and base_of(old) == bases[order - RING]:
                    across_copy(old).wait_send()
        if kind == "rest":
            for copy in rest_copies():
                copy.wait_recv()
            ones = jnp.ones((16, projected.shape[0]), jnp.bfloat16)
            sums = dot(ones, projected[...])
            row = lax.broadcasted_iota(jnp.int32, (16, local), 0)
            own = jnp.where(row == 0, sums[:, :local], 0.0)
            own = own + jnp.where(row == 1, sums[:, 2 * local :], 0.0)
            own = jnp.concatenate([own, jnp.zeros((16, width - local), jnp.float32)], axis=1)
            own = own + rest[pl.ds(w * 16, 16), :] + rest_in[0]
            other = rest[pl.ds(across * 16, 16), :] + rest_in[1]
            slot(near, k)[...] = own.astype(jnp.bfloat16)
            far_slot(k, 16)[...] = other.astype(jnp.bfloat16)
        elif k in bases:
            needs(k)
            left, right = operands(k)
            grad = dot(left, right, ((0,), (0,))).astype(jnp.bfloat16)
            near[pl.ds(starts[k], CHUNK), :] = grad[:CHUNK]
            far_slot(k, CHUNK)[...] = grad[CHUNK:]
        across_copy(k).start()

    def settle(k):
        if is_piece(k):
            for index in range(3):
                piece_copy(k, index).wait_recv()
            piece_own(k).wait()
        else:
            across_copy(k).wait_recv()
        for role in (0, 3):

            def step(role=role):
                if not is_piece(k):
                    sum_into(slot(near, k), summands(k), rows_of(k))
                up_copy(k, role).start()

            on(k, role, step)

    def aside(k):
        def step():
            up_copy(k, 3).wait_recv()
            sum_into(slot(near, k), summands(k) + [slot(up_in, k)], rows_of(k))
            side_copy(k).start()

        on(k, 2, step)

    def finish(k):
        def step():
            up_copy(k, 0).wait_recv()
            side_copy(k).wait_recv()
            parts = summands(k) + [slot(up_in, k), beside_slot(k)]
            sum_into(slot(near, k), parts, rows_of(k))
            down_copy(k, 0).start()
            down_copy(k, 2).start()
            keep_copy(k).start()

        on(k, 1, step)

    def forward(k):
        def step():
            down_copy(k, 2).wait_recv()
            down_copy(k, 3).start()

        on(k, 2, step)

    def go_home(m, source, here, do):
        @pl.when(moves & here)
        def _():
            do(swap_back(wires, back.rows, source, home, m, True))

        @pl.when(jnp.logical_not(moves) & here)
        def _():
            do(swap_back(wires, back.rows, source, home, m, False))

    def done(m):
        back.finish(m)
        go_home(m, grad_states, section == 0, lambda copy: copy.start())

    def final_home(m):
        go_home(m, final, section == 1, lambda copy: copy.start())

    beside = {
        9: [lambda: back.work(0), lambda: qkv_copy(1).start()],
        10: [lambda: back.work(1), lambda: qkv_copy(2).start()],
        11: [lambda: back.work(2)],
        17: [lambda: final_home(0)],
        18: [lambda: final_home(1)],
        19: [lambda: final_home(2)],
        20: [lambda: back.cross(0)],
        22: [lambda: back.cross(1)],
        24: [lambda: back.cross(2), lambda: done(0)],
        26: [lambda: done(1)],
        28: [lambda: done(2)],
        7: [step_norm, last_out],
    }
    steps = iter(range(blocks))
    for tick, many in enumerate((0, 0, 2, 3, 3, 4, 4)):
        beside[tick] = [functools.partial(step_back, next(steps)) for _ in range(many)]

    for load in loads:
        for copy in load():
            copy.start()
    rest[...] = jnp.zeros_like(rest)
    step_first()
    stages = (settle, aside, finish, forward)
    begun, first_piece = 0, min(k for k in range(count) if is_piece(k))
    for tick in range(count + LAGS[-1]):
        for lag, stage in reversed(list(zip(LAGS, stages))):
            if 0 <= tick - lag < count:
                stage(tick - lag)
        while begun < min(count, tick + 1 + max(0, min(AHEAD, tick - 11))):
            if begun == first_piece:
                full_copy().wait()
            begin(begun)
            begun += 1
        for step in beside.get(tick, []):
            step()
    for m in range(back.micro):
        back.end(m)
        go_home(m, grad_states, z >= 0, lambda copy: copy.wait())
    for copy in rest_copies():
        copy.wait_send()
    for load in loads:
        for index, copy in enumerate(load()):
            if index % 2 == 1:
                copy.wait_send()
    for column in range(columns):
        to_sibling("pre", pre_both, column).wait_send()
    to_sibling("branch", branch_both, 0).wait_send()
    to_sibling("down", down_both, 0).wait_send()
    for k in direct:
        if base_of(k) in bases[-RING:]:
            across_copy(k).wait_send()
    for k in range(count):
        if is_piece(k):
            for index in range(3):
                piece_copy(k, index).wait_send()

        def ends(role):
            up_copy(k, role).wait_send()
            down_copy(k, role).wait_recv()

        def middle():
            side_copy(k).wait_send()
            down_copy(k, 3).wait_send()

        def owner():
            down_copy(k, 0).wait_send()
            down_copy(k, 2).wait_send()
            keep_copy(k).wait()

        on(k, 0, lambda: ends(0))
        on(k, 3, lambda: ends(3))
        on(k, 2, middle)
        on(k, 1, owner)


def last_pass(weight, layer_rows, inverses, lengths, arrays, weights, operands, size):
    micro, pack, local = arrays[4].shape
    local = local // 3
    tokens, width = operands[3].shape
    hidden = operands[0].shape[1]
    chunks = chunk_list(local, width, hidden)
    count = len(chunks)
    starts, sides_at = starts_of(chunks)
    inside = pl.BlockSpec(memory_space=pltpu.VMEM)
    anywhere = pl.BlockSpec(memory_space=pl.ANY)
    low = lambda *shape: jax.ShapeDtypeStruct(shape, jnp.bfloat16)
    room = lambda *shape: pltpu.VMEM(shape, jnp.bfloat16)
    halves = local // CHUNK
    return pl.pallas_call(
        functools.partial(last_kernel, chunks, size),
        in_specs=[inside] * 4 + [pl.BlockSpec(memory_space=pltpu.SMEM)] + [anywhere] * 14,
        out_specs=[anywhere] * 6,
        out_shape=[
            low(micro, pack // 4, width),
            low(local, 3 * width),
            low(local, width),
            low(local, hidden),
            low(hidden // 4, width),
            low(16, width),
        ],
        scratch_shapes=[
            room(tokens, width),
            room(micro * pack, 3 * local),
            room(micro * pack, width),
            room(3, width, local),
            room(hidden // 4 // CHUNK, 2 * tokens, 2 * CHUNK),
            room(halves, 2 * tokens, 2 * CHUNK),
            room(halves, 2 * tokens, 2 * CHUNK),
            room(2 * tokens, width),
            room(2 * tokens, hidden),
            room(2 * tokens, width),
            pltpu.VMEM((2, 16, width), jnp.float32),
            room(starts[count], width),
            room(RING, CHUNK, width),
            room(starts[count], width),
            room(starts[count], width),
            room(max(sides_at[count:]), width),
            pltpu.VMEM((tokens, width), jnp.float32),
            pltpu.VMEM((tokens, width), jnp.float32),
            room(2, tokens, TILE),
            room(pack, 3 * local),
            room(tokens, width),
            pltpu.VMEM((64, width), jnp.float32),
        ]
        + back_scratch(micro, pack, local, width)
        + [pltpu.SemaphoreType.DMA((900,))],
        compiler_params=pltpu.CompilerParams(
            collective_id=1, has_side_effects=True, vmem_limit_bytes=63 * 2**20
        ),
        name="last_pass",
    )(
        weight,
        layer_rows,
        *inverses,
        lengths,
        *arrays,
        *weights,
        *operands,
    )


def widen_kernel(*refs):
    count = len(refs) // 2
    for source, target in zip(refs[: count - 1], refs[count:]):
        target[0] = source[...].astype(jnp.float32)
    rest, (bias, rows) = refs[count - 1], refs[-2:]
    local = rows.shape[2]
    rows[0] = rest[:8, :local].astype(jnp.float32)
    for row in range(bias.shape[1] // local):
        part = rest[row : row + 1, local : 2 * local]
        bias[:, row * local : (row + 1) * local] = part.astype(jnp.float32)


def widen(sums, steps=8):
    *sums, rest = sums
    local = sums[1].shape[0]
    cut = lambda part: (part.shape[0] // steps, part.shape[1])
    word = lambda *shape: jax.ShapeDtypeStruct(shape, jnp.float32)
    still = lambda *shape: pl.BlockSpec(shape, lambda step: (0,) * len(shape))
    return pl.pallas_call(
        widen_kernel,
        grid=(steps,),
        in_specs=[pl.BlockSpec(cut(part), lambda step: (step, 0)) for part in sums]
        + [still(*rest.shape)],
        out_specs=[pl.BlockSpec((1,) + cut(part), lambda step: (0, step, 0)) for part in sums]
        + [still(1, sums[3].shape[0]), still(1, 8, local)],
        out_shape=[word(1, *part.shape) for part in sums]
        + [word(1, sums[3].shape[0]), word(1, 8, local)],
        name="widen",
    )(*sums, rest)


def relay(boundary, lengths, valid, w_qkv, w_out, w_in, w_down, bias_in, vectors):
    micro, rows, width = boundary.shape[1:]
    size = width // HEADS
    local = vectors.shape[2]
    shards = (w_qkv[0], w_out[0], w_in[0], w_down[0])
    own, weight_qkv, *weights, layer_rows, in_bias, marks, count, leaving = first_pass(
        boundary[0], shards, vectors[0], bias_in, valid, lengths, size
    )
    leaving = leaving.reshape(micro, rows, width)
    kept, inverse_one, inverse_two, returned = mid_pass(
        own, leaving, weights, weight_qkv, layer_rows, in_bias, marks, count, lengths, size
    )
    home, *sums = last_pass(
        weight_qkv,
        layer_rows,
        (inverse_one, inverse_two),
        lengths,
        (
            kept["grad"],
            returned,
            kept["normal_two"],
            kept["normal_one"],
            kept["qkv"],
            kept["full"].reshape(-1, width),
            kept["slope"],
        ),
        weights,
        (kept["hidden"], kept["first"], kept["mixed"], kept["final"]),
        size,
    )
    return (home[None], *widen(sums))


def solution(mesh):
    in_specs = (
        P("section", None, ("wt", "ctx"), None),
        P(),
        P(None, ("wt", "ctx")),
        P("section", "wt", None),
        P("section", "wt", None),
        P("section", "wt", None),
        P("section", "wt", None),
        P("section", "wt"),
        P("section", None, "wt"),
    )
    out_specs = (
        P("section", None, ("wt", "ctx"), None),
        P("section", "wt", None),
        P("section", "wt", None),
        P("section", "wt", None),
        P("section", "wt", None),
        P("section", "wt"),
        P("section", None, "wt"),
    )
    square = mesh.shape["ctx"] == mesh.shape["wt"] == 4
    return jax.shard_map(relay if square else shards, mesh=mesh, in_specs=in_specs, out_specs=out_specs, check_vma=False)
```
